32 devices in a mesh: groups: 2 (over y), tensor: 4 (over z), dp: 2 (over x), query: 2 (over core).
Axes of the slice: x: 2, y: 2, z: 4, core: 2. Of those that a mesh axis runs over, the one named last changes fastest.
Arguments:
- inputs: bfloat16 [8, 512, 8192], P(('groups', 'dp', 'query'), None, 'tensor'), parts along dimension 0, may hold values from -6 to 6
- residual: bfloat16 [8, 512, 8192], P(('groups', 'dp', 'query'), 'tensor'), parts along dimension 0, may hold values from -4 to 4
- out_grad: bfloat16 [8, 512, 8192], P(('groups', 'dp', 'query'), 'tensor'), parts along dimension 0, may hold values from -6 to 6
- norm_gain: bfloat16 [8192], replicated, may hold values from 0.099609375 to 1.8984375
- w_out: bfloat16 [8192, 8192], P('tensor'), may hold values from -0.0625 to 0.0625
- proj_in: bfloat16 [64, 8192], P(None, 'tensor'), may hold values from -0.0625 to 0.0625
- proj_out: bfloat16 [64, 8192], replicated, may hold values from -0.0625 to 0.0625
- queries: bfloat16 [1024, 4096], P('query', 'tensor'), may hold values from -0.0078125 to 0.0078125
- segment_ids: int32 [8, 512], P(('groups', 'dp', 'query')), parts along dimension 0, may hold values from 0 to 3, never falling along the last dimension, each value on 1 to 256 neighbouring positions
Outputs:
- input_grad: bfloat16 [8, 512, 8192], P(('groups', 'dp', 'query'), None, 'tensor'), parts along dimension 0
- scores: float32 [32, 1024], P(('groups', 'dp'), 'query'), parts along dimension 0
The draws below stay inside these ranges and needn't reach their ends.
There are 2 independent parts, one for each index of `groups`. The reference program is written for one: setup_inputs(seed, part) draws one part's arguments, and reference() takes and returns one part's arrays. A program takes and returns all parts, laid end to end along the dimension named above; an argument that names none is the same for every part. Nothing has to cross between parts.
Inputs may be any that keep to these rules, and one draw needn't show every extreme that they name: `segment_ids`: within each row of 512 tokens the example numbers never fall and every example number has at least one token.
All inputs are finite; a program needn't handle non-finite values.
Results may differ from the reference program's by a relative error of at most 0.015.
Values may be sent and summed in bfloat16 or wider, within the bound.
No kernel may reach another device: no remote copies, remote signals or barrier semaphores. Data moves between devices by JAX's collectives and lax.ppermute only.
A program may use at most 128 MiB of HBM per device.

```python
import math
import jax
import jax.numpy as jnp
import numpy as np
from jax import lax

D = 8192
KP = 64
NQ = 1024
TOK_DEV = 512
EX_DEV = 4
SKETCH = 4096
N_TENSOR = 4
N_DP = 2
N_QUERY = 2


def common_field(key):
    values = jax.random.normal(key, (N_DP * N_QUERY, TOK_DEV, D), jnp.float32)
    return jnp.clip(values, -4.0, 4.0)


def draw_residual(key, part):
    common = common_field(key)
    return common.astype(jnp.bfloat16)


def draw_out_grad(key, part):
    common = common_field(key)
    key = jax.random.fold_in(key, 23)
    noise = jnp.clip(jax.random.normal(key, (N_DP * N_QUERY, TOK_DEV, D), jnp.float32), -4.0, 4.0)
    return (0.8 * common + 0.6 * noise).astype(jnp.bfloat16)


def levels(rng, dims, split, least, high):
    gain = 1.0
    for axis_at, shards_of in split:
        heights = jax.random.uniform(jax.random.fold_in(jax.random.fold_in(rng, 6), axis_at), (shards_of,), jnp.float32, least / len(split), high / len(split))
        gain = gain * jnp.repeat(jnp.exp(heights), dims[axis_at] // shards_of).reshape((-1,) + (1,) * (len(dims) - 1 - axis_at))
    return gain


def length_profile(count, total, reach, lean):
    weights = [(1 << 20) // math.isqrt(standing ** lean) + 1 for standing in range(2, count + 1)]
    spare, counts = total - reach - (count - 1), [1] * (count - 1)
    while spare > 0:
        candidates = [i for i in range(count - 1) if counts[i] < reach]
        pool, remaining = sum([weights[i] for i in candidates]), spare
        for i in candidates:
            more = min(reach - counts[i], max(1, remaining * weights[i] // pool), spare)
            counts[i] = counts[i] + more
            spare = spare - more
    return np.array([reach] + counts)


def uneven_parts(own_key, number_of, total, bound, lean):
    if number_of == 2:
        one = jax.random.randint(own_key, (), max(1, total - bound), min(bound, total - 1) + 1)
        return jnp.stack([one, total - one])
    tallies = jnp.asarray(length_profile(number_of, total, bound, lean), jnp.int32)
    pairs = (number_of - 1) // 2
    donor, receiver = tallies[1:1 + 2 * pairs:2], tallies[2:2 + 2 * pairs:2]
    room = jnp.minimum(donor - 1, bound - receiver)
    moved = jax.random.randint(jax.random.fold_in(own_key, 1), (pairs,), 0, 1 << 20) % (room + 1)
    tallies = tallies.at[1:1 + 2 * pairs:2].set(donor - moved).at[2:2 + 2 * pairs:2].set(receiver + moved)
    return tallies[jax.random.permutation(jax.random.fold_in(own_key, 2), number_of)]


def normal_values(own_key, dims, scale, reach, split=(), kind=jnp.bfloat16):
    entries = jax.random.normal(own_key, dims, jnp.float32) * scale
    if len(split) > 0:
        entries = levels(own_key, dims, split, -0.22, 0.18) * entries
    return jnp.clip(entries, min=-reach, max=reach).astype(kind)


def setup_inputs(seed: int = 0, part: int = 0) -> dict:
    keys = jax.random.split(jax.random.key(seed), 10)
    part_splits = jax.random.split(jax.random.fold_in(keys[9], part), 10)
    return {
        "inputs": normal_values(part_splits[0], (N_DP * N_QUERY, TOK_DEV, D), 1.0, 6.0, ((0, 4), (2, 4))),
        "residual": draw_residual(jax.random.fold_in(jax.random.fold_in(keys[9], part), 71), part),
        "out_grad": draw_out_grad(jax.random.fold_in(jax.random.fold_in(keys[9], part), 71), part),
        "norm_gain": jnp.clip(1.0 + 0.18 * jax.random.normal(keys[3], (D,), jnp.float32), 0.099609375, 1.8984375).astype(jnp.bfloat16),
        "w_out": normal_values(keys[4], (D, D), D ** -0.5, 0.0625, ((0, 4),)),
        "proj_in": normal_values(keys[5], (KP, D), D ** -0.5, 0.0625, ((1, 4),)),
        "proj_out": normal_values(keys[6], (KP, D), D ** -0.5, 0.0625),
        "queries": normal_values(keys[7], (NQ, SKETCH), (KP * KP * TOK_DEV // EX_DEV) ** -0.5, 0.0078125, ((0, 2), (1, 4))),
        "segment_ids": jax.vmap(lambda own: jnp.searchsorted(jnp.cumsum(uneven_parts(own, EX_DEV, TOK_DEV, TOK_DEV // 2, 0)), jnp.arange(TOK_DEV), side="right"))(jax.random.split(part_splits[8], (N_DP * N_QUERY))).reshape((N_DP * N_QUERY, TOK_DEV)).astype(jnp.int32),
    }


EPS = 1e-05

def reference(inputs, residual, out_grad, norm_gain, w_out, proj_in, proj_out, queries, segment_ids):
    batches = N_DP * N_QUERY
    rows = inputs.reshape(batches * TOK_DEV, D)
    width = D // N_TENSOR

    def add_block(total, index):
        block = lax.dynamic_slice_in_dim(rows, index * width, width, 1)
        weights = lax.dynamic_slice_in_dim(w_out, index * width, width, 0)
        term = jnp.dot(block, weights, preferred_element_type=jnp.float32).astype(jnp.bfloat16)
        term = lax.optimization_barrier(term)
        return (total + term.astype(jnp.float32), None)
    start = jnp.zeros((batches * TOK_DEV, D), jnp.float32)
    proj, _ = lax.scan(add_block, start, jnp.arange(N_TENSOR, dtype=jnp.int32))
    z = residual.reshape(batches * TOK_DEV, D).astype(jnp.float32) + proj
    inv = lax.rsqrt(lax.optimization_barrier(jnp.mean(z * z, axis=-1, keepdims=True)) + EPS)
    scaled = norm_gain.astype(jnp.float32) * out_grad.reshape(batches * TOK_DEV, D).astype(jnp.float32)
    center = lax.optimization_barrier(jnp.mean(scaled * z, axis=-1, keepdims=True))
    dproj = (inv * scaled - z * inv * inv * inv * center).astype(jnp.bfloat16)
    input_grad = lax.dot_general(dproj, w_out, (((1,), (1,)), ((), ())), preferred_element_type=jnp.float32)
    input_grad = input_grad.astype(jnp.bfloat16).reshape(batches, TOK_DEV, D)
    proj_a = lax.dot_general(rows, proj_in, (((1,), (1,)), ((), ())), preferred_element_type=jnp.float32)
    proj_b = lax.dot_general(dproj, proj_out, (((1,), (1,)), ((), ())), preferred_element_type=jnp.float32)
    proj_a = proj_a.reshape(batches, TOK_DEV, KP)
    proj_b = proj_b.reshape(batches, TOK_DEV, KP)
    onehot = (segment_ids[:, :, None] == jnp.arange(EX_DEV, dtype=jnp.int32)[None, None, :]).astype(jnp.float32)
    weighted = (onehot[:, :, :, None] * proj_b[:, :, None, :]).reshape(batches, TOK_DEV, EX_DEV * KP)
    sketch = jnp.einsum('ntf,ntq->nfq', weighted, proj_a, precision=lax.Precision.HIGHEST)
    sketch = sketch.reshape(batches * EX_DEV, KP * KP)
    scores = jnp.dot(sketch, queries.astype(jnp.float32).T, precision=lax.Precision.HIGHEST)
    return (input_grad, scores)
```

```python
import jax
import jax.numpy as jnp
from jax import lax
from jax.sharding import PartitionSpec as P

EX_DEV = 4
EPS = 1e-05
CHUNKS = 4
HALVES = 2


def norm_backward(proj_rows, resid_rows, grad_rows, norm_gain):
    z = resid_rows.astype(jnp.float32) + proj_rows
    inv = lax.rsqrt(jnp.mean(z * z, axis=-1, keepdims=True) + EPS)
    scaled = norm_gain.astype(jnp.float32) * grad_rows.astype(jnp.float32)
    center = jnp.mean(scaled * z, axis=-1, keepdims=True)
    return (inv * scaled - z * inv * inv * inv * center).astype(jnp.bfloat16)


def project_rows(values, matrix):
    return lax.dot_general(
        values, matrix, (((1,), (1,)), ((), ())), preferred_element_type=jnp.float32
    )


def hop(value, pairs):
    return lax.ppermute(value, "tensor", pairs)


def reduce_line(partial, rank, parts):
    def block(index):
        return lax.dynamic_index_in_dim(partial, jnp.clip(index, 0, parts - 1), 0, keepdims=False)

    right = left = None
    for far in range(parts - 1, 0, -1):
        out_right, out_left = block(rank + far), block(rank - far)
        if right is not None:
            out_right = (out_right.astype(jnp.float32) + right.astype(jnp.float32)).astype(jnp.bfloat16)
            out_left = (out_left.astype(jnp.float32) + left.astype(jnp.float32)).astype(jnp.bfloat16)
        right = hop(out_right, [(d, d + 1) for d in range(parts - far)])
        left = hop(out_left, [(d, d - 1) for d in range(far, parts)])
    return (
        block(rank).astype(jnp.float32) + right.astype(jnp.float32) + left.astype(jnp.float32)
    )


def gather_line(own, rank, parts):
    right = left = own
    rights, lefts = [], []
    for far in range(1, parts):
        right = hop(right, [(d, d + 1) for d in range(far - 1, parts - 1)])
        left = hop(left, [(d, d - 1) for d in range(1, parts - far + 1)])
        rights.append(right)
        lefts.append(left)
    blocks = [own]
    for far in range(1, parts):
        blocks.append(jnp.where(rank >= far, rights[far - 1], lefts[parts - far - 1]))
    return blocks


def exchange(value_of, axis, size, rank):
    first = value_of(rank)
    out = jnp.zeros((size,) + first.shape, first.dtype)
    out = lax.dynamic_update_index_in_dim(out, first, rank, 0)
    for shift in range(1, size):
        got = lax.ppermute(
            value_of((rank + shift) % size), axis, [(d, (d + shift) % size) for d in range(size)]
        )
        out = lax.dynamic_update_index_in_dim(out, got, (rank - shift + size) % size, 0)
    return out


def body(inputs, residual, out_grad, norm_gain, w_out, proj_in, proj_out, queries, segment_ids):
    parts = lax.axis_size("tensor")
    rank = lax.axis_index("tensor")
    queriers = lax.axis_size("query")
    q_rank = lax.axis_index("query")
    tok_rows = inputs.reshape(inputs.shape[1], inputs.shape[2])
    tokens, width = tok_rows.shape[0], w_out.shape[1]
    share = tokens // parts
    chunks = max(1, min(CHUNKS, share // 16))
    rows = share // chunks
    by_share = tok_rows.reshape(parts, chunks, rows, tok_rows.shape[1])
    half = width // HALVES

    partial_in = project_rows(tok_rows, proj_in)
    in_rows = lax.psum_scatter(
        partial_in.astype(jnp.bfloat16), "tensor", scatter_dimension=0, tiled=True
    ).astype(jnp.float32)

    grads, outs = [], []
    for c in range(chunks):
        here = by_share[:, c].reshape(parts * rows, -1)
        sums = []
        for h in range(HALVES):
            cols = w_out[:, h * half : (h + 1) * half]
            part = jnp.dot(here, cols, preferred_element_type=jnp.float32).astype(jnp.bfloat16)
            sums.append(reduce_line(part.reshape(parts, rows, half), rank, parts))
        proj_rows = jnp.concatenate(sums, axis=1)
        own = slice(c * rows, (c + 1) * rows)
        dproj_rows = norm_backward(proj_rows, residual[0, own], out_grad[0, own], norm_gain)
        grads.append(dproj_rows)
        halves = [
            gather_line(dproj_rows[:, h * half : (h + 1) * half], rank, parts) for h in range(HALVES)
        ]
        ordered = []
        for h in range(HALVES):
            stack = jnp.zeros((parts, rows, half), jnp.bfloat16)
            for far in range(parts):
                stack = lax.dynamic_update_index_in_dim(
                    stack, halves[h][far], (rank - far + parts) % parts, 0
                )
            ordered.append(stack.reshape(parts * rows, half))
        total = None
        for h in range(HALVES):
            term = project_rows(ordered[h], w_out[:, h * half : (h + 1) * half])
            total = term if total is None else total + term
        outs.append(total.astype(jnp.bfloat16).reshape(parts, 1, rows, -1))
    input_grad = jnp.concatenate(outs, axis=1).reshape(1, tokens, -1)

    dproj_own = jnp.concatenate(grads, axis=0)
    out_rows = project_rows(dproj_own, proj_out)
    kp = out_rows.shape[1]
    segs = lax.dynamic_slice_in_dim(segment_ids[0], rank * share, share, 0)
    member = (segs[None, :] == jnp.arange(EX_DEV, dtype=jnp.int32)[:, None]).astype(jnp.float32)
    weighted = member[:, :, None] * out_rows[None]
    sketch_part = lax.dot_general(
        weighted,
        jnp.broadcast_to(in_rows[None], (EX_DEV,) + in_rows.shape),
        (((1,), (1,)), ((0,), (0,))),
        precision=lax.Precision.HIGHEST,
    )
    sketch_part = sketch_part.reshape(EX_DEV, parts, kp * kp // parts).astype(jnp.bfloat16)
    got = exchange(
        lambda at: lax.dynamic_index_in_dim(sketch_part, at, 1, keepdims=False), "tensor", parts, rank
    )
    sketch_cols = jnp.sum(got.astype(jnp.float32), axis=0)
    paired = exchange(lambda at: sketch_cols, "query", queriers, q_rank)
    paired = paired.reshape(queriers * EX_DEV, sketch_cols.shape[1])
    score_part = lax.dot_general(
        paired,
        queries.astype(jnp.float32),
        (((1,), (1,)), ((), ())),
        precision=lax.Precision.HIGHEST,
    )
    scores = jnp.sum(exchange(lambda at: score_part, "tensor", parts, rank), axis=0)
    return (input_grad, scores)


def solution(mesh):
    return jax.shard_map(
        body,
        mesh=mesh,
        in_specs=(
            P(("groups", "dp", "query"), None, "tensor"),
            P(("groups", "dp", "query"), "tensor", None),
            P(("groups", "dp", "query"), "tensor", None),
            P(),
            P("tensor", None),
            P(None, "tensor"),
            P(),
            P("query", "tensor"),
            P(("groups", "dp", "query"), None),
        ),
        out_specs=(P(("groups", "dp", "query"), None, "tensor"), P(("groups", "dp"), "query")),
        check_vma=False,
    )
```

```python
import functools

import jax
import jax.numpy as jnp
from jax import lax
from jax.experimental import pallas as pl
from jax.experimental.pallas import tpu as pltpu
from jax.sharding import PartitionSpec as P

EX_DEV = 4
EPS = 1e-05
CHUNKS = 4
PIECES = 4
LIMIT = 48 * 1024 * 1024

F32, BF16 = jnp.float32, jnp.bfloat16
ANY = pl.BlockSpec(memory_space=pl.ANY)
TOKEN = jax.ShapeDtypeStruct((8, 128), F32)
TOKEN_SPEC = pl.BlockSpec((8, 128), lambda *_: (0, 0))


def divisor(total, wanted):
    size = min(total, wanted)
    while total % size:
        size //= 2
    return size


def cost(flops, moved):
    return pl.CostEstimate(flops=flops, bytes_accessed=moved, transcendentals=0)


def project_rows(values, matrix):
    return lax.dot_general(
        values, matrix, (((1,), (1,)), ((), ())), preferred_element_type=F32
    )


def forward_piece(by_share, w_out, chunk, piece, pieces, held, after):
    parts, _, rows, depth = by_share.shape
    width = w_out.shape[1]
    span = width // pieces
    cols = divisor(span, 512)
    steps = span // cols

    def kernel(x_ref, w_ref, *refs):
        out_ref, tok_ref = refs[-2:]
        x = x_ref[...].reshape(parts * rows, depth)
        y = jnp.dot(x, w_ref[...], preferred_element_type=F32).astype(BF16)
        out_ref[...] = y.reshape(parts, rows, cols)
        tok_ref[...] = jnp.zeros_like(tok_ref)

    extra = ([] if held is None else [held]) + after
    return pl.pallas_call(
        kernel,
        grid=(steps,),
        in_specs=[
            pl.BlockSpec((parts, None, rows, depth), lambda i: (0, chunk, 0, 0)),
            pl.BlockSpec((depth, cols), lambda i: (0, piece * steps + i)),
        ]
        + [ANY] * len(extra),
        out_specs=[pl.BlockSpec((parts, rows, cols), lambda i: (0, 0, piece * steps + i)), TOKEN_SPEC],
        out_shape=[jax.ShapeDtypeStruct((parts, rows, width), BF16), TOKEN],
        input_output_aliases={} if held is None else {2: 0},
        compiler_params=pltpu.CompilerParams(vmem_limit_bytes=LIMIT),
        cost_estimate=cost(2 * parts * rows * depth * span, 2 * depth * span),
        name="forward_piece",
    )(by_share, w_out, *extra)


def backward_piece(gathered, w_out, chunk, chunks, piece, pieces, held, after):
    parts, rows, width = gathered.shape
    depth = w_out.shape[0]
    span = depth // pieces
    cols = divisor(span, 256)
    steps = span // cols

    def kernel(g_ref, w_ref, *refs):
        out_ref, tok_ref = refs[-2:]
        g = g_ref[...].reshape(parts * rows, width)
        y = project_rows(g, w_ref[...]).astype(BF16)
        out_ref[...] = y.reshape(parts, rows, cols)
        tok_ref[...] = jnp.zeros_like(tok_ref)

    extra = ([] if held is None else [held]) + after
    return pl.pallas_call(
        kernel,
        grid=(steps,),
        in_specs=[
            pl.BlockSpec((parts, rows, width), lambda i: (0, 0, 0)),
            pl.BlockSpec((cols, width), lambda i: (piece * steps + i, 0)),
        ]
        + [ANY] * len(extra),
        out_specs=[
            pl.BlockSpec((parts, None, rows, cols), lambda i: (0, chunk, 0, piece * steps + i)),
            TOKEN_SPEC,
        ],
        out_shape=[jax.ShapeDtypeStruct((parts, chunks, rows, depth), BF16), TOKEN],
        input_output_aliases={} if held is None else {2: 0},
        compiler_params=pltpu.CompilerParams(vmem_limit_bytes=LIMIT),
        cost_estimate=cost(2 * parts * rows * width * span, 2 * width * span),
        name="backward_piece",
    )(gathered, w_out, *extra)


def add_term(where, partial, came, after):
    parts, rows, width = partial.shape
    cols = divisor(width, 4096)

    def kernel(where_ref, p_ref, *refs):
        out_ref = refs[-1]
        if came is None:
            out_ref[...] = p_ref[...]
            return
        came_ref = refs[0]

        @pl.when(where_ref[1] == 1)
        def _():
            out_ref[...] = (came_ref[...].astype(F32) + p_ref[...].astype(F32)).astype(BF16)

        @pl.when(where_ref[1] == 0)
        def _():
            out_ref[...] = came_ref[...]

    line = pl.BlockSpec((rows, cols), lambda i, w: (0, i))
    first = [] if came is None else [came]
    return pl.pallas_call(
        kernel,
        grid_spec=pltpu.PrefetchScalarGridSpec(
            num_scalar_prefetch=1,
            grid=(width // cols,),
            in_specs=[pl.BlockSpec((None, rows, cols), lambda i, w: (w[0], 0, i))]
            + [line] * len(first)
            + [ANY] * len(after),
            out_specs=line,
        ),
        out_shape=jax.ShapeDtypeStruct((rows, width), BF16),
        compiler_params=pltpu.CompilerParams(vmem_limit_bytes=LIMIT),
        cost_estimate=cost(rows * width, 6 * rows * width),
        name="add_term",
    )(where, partial, *first, *after)


def norm_backward(rank, partial, from_a, from_b, residual, out_grad, norm_gain, chunk, after):
    parts, rows, width = partial.shape
    cols = divisor(width, 1024)
    count = width // cols

    def kernel(rank_ref, p_ref, a_ref, b_ref, res_ref, grad_ref, gain_ref, *refs):
        out_ref, z_ref, s_ref = refs[-3:]

        def first(i, sums):
            at = pl.ds(pl.multiple_of(i * cols, cols), cols)
            proj = p_ref[:, at].astype(F32) + a_ref[:, at].astype(F32) + b_ref[:, at].astype(F32)
            z = res_ref[:, at].astype(F32) + proj
            scaled = gain_ref[:, at].astype(F32) * grad_ref[:, at].astype(F32)
            z_ref[:, at] = z
            s_ref[:, at] = scaled
            square, cross = sums
            for j in range(0, cols, 128):
                zj = z[:, j : j + 128]
                square = square + zj * zj
                cross = cross + zj * scaled[:, j : j + 128]
            return square, cross

        zero = jnp.zeros((rows, 128), F32)
        square, cross = lax.fori_loop(0, count, first, (zero, zero))
        inv = lax.rsqrt(jnp.sum(square, axis=-1, keepdims=True) / width + EPS)
        center = jnp.sum(cross, axis=-1, keepdims=True) / width
        slope = inv * inv * inv * center

        def second(i, carry):
            at = pl.ds(pl.multiple_of(i * cols, cols), cols)
            out_ref[:, at] = (inv * s_ref[:, at] - z_ref[:, at] * slope).astype(BF16)
            return carry

        lax.fori_loop(0, count, second, 0)

    whole = pl.BlockSpec((rows, width), lambda i, r: (0, 0))
    own = pl.BlockSpec((None, rows, width), lambda i, r: (0, chunk, 0))
    return pl.pallas_call(
        kernel,
        grid_spec=pltpu.PrefetchScalarGridSpec(
            num_scalar_prefetch=1,
            grid=(1,),
            in_specs=[
                pl.BlockSpec((None, rows, width), lambda i, r: (r[0], 0, 0)),
                whole,
                whole,
                own,
                own,
                pl.BlockSpec((1, width), lambda i, r: (0, 0)),
            ]
            + [ANY] * len(after),
            out_specs=whole,
            scratch_shapes=[pltpu.VMEM((rows, width), F32), pltpu.VMEM((rows, width), F32)],
        ),
        out_shape=jax.ShapeDtypeStruct((rows, width), BF16),
        compiler_params=pltpu.CompilerParams(vmem_limit_bytes=LIMIT),
        cost_estimate=cost(20 * rows * width, 12 * rows * width),
        name="norm_backward",
    )(rank, partial, from_a, from_b, residual, out_grad, norm_gain, *after)


def put_in_order(place, own, from_a, from_b):
    rows, width = own.shape
    parts = len(from_a) + 1

    def kernel(place_ref, *refs):
        own_ref, a_refs, b_refs = refs[0], refs[1:parts], refs[parts : 2 * parts - 1]
        out_ref, sems = refs[-2:]
        rank, way, behind = place_ref[0], place_ref[1], place_ref[2]
        copies = [(None, pltpu.make_async_copy(own_ref, out_ref.at[rank], sems.at[0]))]
        for j in range(1, parts):
            low = lax.clamp(0, rank - way * j, parts - 1)
            high = lax.clamp(0, rank + way * j, parts - 1)
            copies.append(
                (j <= behind, pltpu.make_async_copy(a_refs[j - 1], out_ref.at[low], sems.at[j]))
            )
            copies.append(
                (
                    j <= parts - 1 - behind,
                    pltpu.make_async_copy(b_refs[j - 1], out_ref.at[high], sems.at[parts - 1 + j]),
                )
            )
        for phase in ("start", "wait"):
            for test, copy in copies:
                if test is None:
                    getattr(copy, phase)()
                else:
                    pl.when(test)(getattr(copy, phase))

    return pl.pallas_call(
        kernel,
        grid_spec=pltpu.PrefetchScalarGridSpec(
            num_scalar_prefetch=1,
            grid=(1,),
            in_specs=[ANY] * (2 * parts - 1),
            out_specs=ANY,
            scratch_shapes=[pltpu.SemaphoreType.DMA((2 * parts - 1,))],
        ),
        out_shape=jax.ShapeDtypeStruct((parts, rows, width), BF16),
        compiler_params=pltpu.CompilerParams(vmem_limit_bytes=LIMIT),
        cost_estimate=cost(0, 4 * parts * rows * width),
        name="put_in_order",
    )(place, own, *from_a, *from_b)


def exchange(value_of, axis, size, rank):
    first = value_of(rank)
    out = jnp.zeros((size,) + first.shape, first.dtype)
    out = lax.dynamic_update_index_in_dim(out, first, rank, 0)
    for shift in range(1, size):
        got = lax.ppermute(
            value_of((rank + shift) % size), axis, [(d, (d + shift) % size) for d in range(size)]
        )
        out = lax.dynamic_update_index_in_dim(out, got, (rank - shift + size) % size, 0)
    return out


def body(inputs, residual, out_grad, norm_gain, w_out, proj_in, proj_out, queries, segment_ids):
    parts = lax.axis_size("tensor")
    rank = lax.axis_index("tensor")
    queriers = lax.axis_size("query")
    q_rank = lax.axis_index("query")
    tokens = inputs.shape[1]
    share = tokens // parts
    chunks = max(1, min(CHUNKS, share // 16))
    rows = share // chunks
    by_share = inputs.reshape(parts, chunks, rows, inputs.shape[2])
    gain = norm_gain.reshape(1, -1)

    partial_in = project_rows(inputs.reshape(tokens, -1), proj_in)
    in_rows = lax.psum_scatter(
        partial_in.astype(BF16), "tensor", scatter_dimension=0, tiled=True
    ).astype(F32)

    up = 1 - 2 * (q_rank % 2)
    ways = (up, -up)
    spots = [jnp.where(way == 1, rank, parts - 1 - rank) for way in ways]
    rank_at = jnp.stack([rank]).astype(jnp.int32)
    place = jnp.stack([rank, ways[0], spots[0]]).astype(jnp.int32)

    def pairs(flow, low, high):
        out = []
        for q in range(queriers):
            way = 1 if (q % 2 == 0) == (flow == 0) else -1
            for t in range(parts):
                spot = t if way == 1 else parts - 1 - t
                if low <= spot <= min(high, parts - 2):
                    out.append((t * queriers + q, (t + way) * queriers + q))
        return out

    work, tokens_made = [], []
    partials = {}
    result = [None]

    def forward(chunk, piece, pieces, after):
        partials[chunk], tok = forward_piece(
            by_share, w_out, chunk, piece, pieces, partials.get(chunk), after
        )
        return tok

    def backward(chunk, gathered, piece, pieces, after):
        result[0], tok = backward_piece(
            gathered, w_out, chunk, chunks, piece, pieces, result[0], after
        )
        return tok

    def do_one(x):
        if work:
            tokens_made[:] = [work.pop(0)([x])]

    forward(0, 0, 1, [])
    for c in range(1, chunks):
        for piece in range(PIECES):
            work.append(functools.partial(forward, c, piece, PIECES))
    grads = []
    for slot in range(chunks + 1):
        rs = slot < chunks
        ag = slot > 0
        came = [None, None]
        gathered = [[], []]
        if rs:
            while slot not in partials or any(
                w.func is forward and w.args[0] <= slot for w in work
            ):
                tokens_made[:] = [work.pop(0)([])]
        for k in range(parts):
            gather_now = ag and k <= parts - 2
            reduce_now = rs and k >= 1
            if not gather_now and not reduce_now:
                continue
            for flow in range(2):
                if k == 0:
                    x = grads[slot - 1]
                elif reduce_now:
                    at = jnp.clip(rank + ways[flow] * (parts - k), 0, parts - 1)
                    adds = spots[flow] <= k - 1
                    x = add_term(
                        jnp.stack([at, adds.astype(at.dtype)]).astype(jnp.int32),
                        partials[slot],
                        came[flow],
                        list(tokens_made),
                    )
                else:
                    x = came[flow]
                low = 0 if reduce_now else k
                high = parts - 2 if gather_now else k - 1
                came[flow] = lax.ppermute(x, ("tensor", "query"), pairs(flow, low, high))
                if gather_now:
                    gathered[flow].append(came[flow])
                do_one(x)
        if rs:
            grads.append(
                norm_backward(
                    rank_at, partials[slot], *came, residual, out_grad, gain, slot, list(tokens_made)
                )
            )
        if ag:
            ready = put_in_order(place, grads[slot - 1], *gathered)
            if slot == chunks:
                while work:
                    work.pop(0)([])
                backward(slot - 1, ready, 0, 1, [])
            else:
                for piece in range(PIECES):
                    work.append(functools.partial(backward, slot - 1, ready, piece, PIECES))
    input_grad = result[0].reshape(1, tokens, -1)

    dproj_own = jnp.concatenate(grads, axis=0)
    out_rows = project_rows(dproj_own, proj_out)
    kp = out_rows.shape[1]
    segs = lax.dynamic_slice_in_dim(segment_ids[0], rank * share, share, 0)
    member = (segs[None, :] == jnp.arange(EX_DEV, dtype=jnp.int32)[:, None]).astype(F32)
    weighted = member[:, :, None] * out_rows[None]
    sketch_part = lax.dot_general(
        weighted,
        jnp.broadcast_to(in_rows[None], (EX_DEV,) + in_rows.shape),
        (((1,), (1,)), ((0,), (0,))),
        precision=lax.Precision.HIGHEST,
    )
    sketch_part = sketch_part.reshape(EX_DEV, parts, kp * kp // parts).astype(BF16)
    got = exchange(
        lambda at: lax.dynamic_index_in_dim(sketch_part, at, 1, keepdims=False), "tensor", parts, rank
    )
    sketch_cols = jnp.sum(got.astype(F32), axis=0)
    paired = exchange(lambda at: sketch_cols, "query", queriers, q_rank)
    paired = paired.reshape(queriers * EX_DEV, sketch_cols.shape[1])
    score_part = lax.dot_general(
        paired,
        queries.astype(F32),
        (((1,), (1,)), ((), ())),
        precision=lax.Precision.HIGHEST,
    )
    scores = jnp.sum(exchange(lambda at: score_part, "tensor", parts, rank), axis=0)
    return (input_grad, scores)


def solution(mesh):
    return jax.shard_map(
        body,
        mesh=mesh,
        in_specs=(
            P(("groups", "dp", "query"), None, "tensor"),
            P(("groups", "dp", "query"), "tensor", None),
            P(("groups", "dp", "query"), "tensor", None),
            P(),
            P("tensor", None),
            P(None, "tensor"),
            P(),
            P("query", "tensor"),
            P(("groups", "dp", "query"), None),
        ),
        out_specs=(P(("groups", "dp", "query"), None, "tensor"), P(("groups", "dp"), "query")),
        check_vma=False,
    )
```

```python
import functools

import jax
import jax.numpy as jnp
from jax import lax
from jax.experimental import pallas as pl
from jax.experimental.pallas import tpu as pltpu
from jax.sharding import PartitionSpec as P

EX_DEV = 4
EPS = 1e-05
CHUNKS = 2
HALVES = 2
PIECES = 4
SPLIT = 4
SHORT, LONG = 0.2, 5.0
LIMIT = 28 * 1024 * 1024

F32, BF16 = jnp.float32, jnp.bfloat16
ANY = pl.BlockSpec(memory_space=pl.ANY)
TOKEN = jax.ShapeDtypeStruct((8, 128), F32)
TOKEN_SPEC = pl.BlockSpec((8, 128), lambda *_: (0, 0))


def divisor(total, wanted):
    size = min(total, wanted)
    while total % size:
        size //= 2
    return size


def cost(microseconds):
    return pl.CostEstimate(flops=0, bytes_accessed=int(microseconds * 3.6e6), transcendentals=0)


def project_rows(values, matrix):
    return lax.dot_general(
        values, matrix, (((1,), (1,)), ((), ())), preferred_element_type=F32
    )


def project_inputs(tok_rows, proj_in, after):
    tokens, depth = tok_rows.shape
    width = proj_in.shape[0]

    def kernel(x_ref, p_ref, *refs):
        refs[-1][...] = project_rows(x_ref[...], p_ref[...]).astype(BF16)

    return pl.pallas_call(
        kernel,
        grid=(1,),
        in_specs=[
            pl.BlockSpec((tokens, depth), lambda i: (0, 0)),
            pl.BlockSpec((width, depth), lambda i: (0, 0)),
        ]
        + [ANY] * len(after),
        out_specs=pl.BlockSpec((tokens, width), lambda i: (0, 0)),
        out_shape=jax.ShapeDtypeStruct((tokens, width), BF16),
        compiler_params=pltpu.CompilerParams(vmem_limit_bytes=LIMIT),
        cost_estimate=cost(SHORT),
        name="project_inputs",
    )(tok_rows, proj_in, *after)


def forward_piece(by_share, w_out, chunk, halves, half_at, piece, pieces, held, after):
    parts, _, rows, depth = by_share.shape
    half = w_out.shape[1] // halves
    span = half // pieces
    cols = divisor(span, 512)
    steps = span // cols
    base = (half_at * half + piece * span) // cols
    cut = depth // SPLIT

    def kernel(x_ref, *refs):
        out_ref, tok_ref = refs[-2:]
        x = x_ref[...].reshape(parts * rows, depth)
        y = None
        for s in range(SPLIT):
            term = jnp.dot(x[:, s * cut : (s + 1) * cut], refs[s][...], preferred_element_type=F32)
            y = term if y is None else y + term
        out_ref[...] = y.astype(BF16).reshape(parts, rows, cols)
        tok_ref[...] = jnp.zeros_like(tok_ref)

    extra = ([] if held is None else [held]) + after
    return pl.pallas_call(
        kernel,
        grid=(steps,),
        in_specs=[pl.BlockSpec((parts, None, rows, depth), lambda i: (0, chunk, 0, 0))]
        + [pl.BlockSpec((cut, cols), lambda i, s=s: (s, base + i)) for s in range(SPLIT)]
        + [ANY] * len(extra),
        out_specs=[
            pl.BlockSpec((parts, rows, cols), lambda i: (0, 0, piece * steps + i)),
            TOKEN_SPEC,
        ],
        out_shape=[jax.ShapeDtypeStruct((parts, rows, half), BF16), TOKEN],
        input_output_aliases={} if held is None else {1 + SPLIT: 0},
        compiler_params=pltpu.CompilerParams(vmem_limit_bytes=LIMIT),
        cost_estimate=cost(SHORT),
        name="forward_piece",
    )(by_share, *([w_out] * SPLIT), *extra)


def backward_piece(blocks, w_out, chunk, chunks, halves, piece, pieces, total, last, held, after):
    parts, rows, half = blocks[0][1].shape
    depth = w_out.shape[0]
    span = depth // pieces
    cols = divisor(span, 256)
    steps = span // cols
    cut = half // SPLIT
    n = len(blocks)

    def kernel(*refs):
        out_ref, tok_ref = refs[-2:]
        y = None if total is None else refs[n + n * SPLIT][...].reshape(parts * rows, cols)
        for b in range(n):
            g = refs[b][...].reshape(parts * rows, half)
            for s in range(SPLIT):
                term = project_rows(g[:, s * cut : (s + 1) * cut], refs[n + b * SPLIT + s][...])
                y = term if y is None else y + term
        out_ref[...] = y.astype(out_ref.dtype).reshape(parts, rows, cols)
        tok_ref[...] = jnp.zeros_like(tok_ref)

    here = pl.BlockSpec((parts, rows, cols), lambda i: (0, 0, piece * steps + i))
    if last:
        out_spec = pl.BlockSpec((parts, None, rows, cols), lambda i: (0, chunk, 0, piece * steps + i))
        out_shape = jax.ShapeDtypeStruct((parts, chunks, rows, depth), BF16)
    else:
        out_spec, out_shape = here, jax.ShapeDtypeStruct((parts, rows, depth), F32)
    weights = [
        pl.BlockSpec((cols, cut), lambda i, at=at * SPLIT + s: (piece * steps + i, at))
        for at, _ in blocks
        for s in range(SPLIT)
    ]
    sums = [] if total is None else [total]
    extra = ([] if held is None else [held]) + after
    return pl.pallas_call(
        kernel,
        grid=(steps,),
        in_specs=[pl.BlockSpec((parts, rows, half), lambda i: (0, 0, 0))] * n
        + weights
        + [here] * len(sums)
        + [ANY] * len(extra),
        out_specs=[out_spec, TOKEN_SPEC],
        out_shape=[out_shape, TOKEN],
        input_output_aliases={} if held is None else {n + n * SPLIT + len(sums): 0},
        compiler_params=pltpu.CompilerParams(vmem_limit_bytes=LIMIT),
        cost_estimate=cost(SHORT),
        name="backward_piece",
    )(*[g for _, g in blocks], *([w_out] * (n * SPLIT)), *sums, *extra)


def relay(where, partial, came, held, after):
    rows, width = came.shape
    n_in = 1 + (partial is not None) + (held is not None) + len(after)

    def kernel(where_ref, *refs):
        came_ref, x_ref = refs[0], refs[n_in]
        if held is not None:
            store = pltpu.make_async_copy(came_ref, refs[n_in + 1].at[where_ref[2]], refs[-1])
            pl.when(where_ref[3] == 1)(store.start)
        if partial is not None:

            @pl.when(where_ref[1] == 1)
            def _():
                x_ref[...] = (came_ref[...].astype(F32) + refs[1][...].astype(F32)).astype(BF16)

            @pl.when(where_ref[1] == 0)
            def _():
                x_ref[...] = came_ref[...]

        if held is not None:
            pl.when(where_ref[3] == 1)(store.wait)

    line = jax.ShapeDtypeStruct((rows, width), BF16)
    args, out_shape, alias = [came], [line], {}
    if partial is not None:
        whole = pl.BlockSpec((rows, width), lambda i, w: (0, 0))
        specs, out_specs = [whole, pl.BlockSpec((None, rows, width), lambda i, w: (w[0], 0, 0))], [whole]
        args.append(partial)
    else:
        specs, out_specs, alias = [ANY], [ANY], {1: 0}
    if held is not None:
        alias[1 + len(args)] = 1
        specs.append(ANY)
        args.append(held)
        out_specs.append(ANY)
        out_shape.append(jax.ShapeDtypeStruct(held.shape, BF16))
    outs = pl.pallas_call(
        kernel,
        grid_spec=pltpu.PrefetchScalarGridSpec(
            num_scalar_prefetch=1,
            grid=(1,),
            in_specs=specs + [ANY] * len(after),
            out_specs=out_specs,
            scratch_shapes=[pltpu.SemaphoreType.DMA] if held is not None else [],
        ),
        out_shape=out_shape,
        input_output_aliases=alias,
        compiler_params=pltpu.CompilerParams(vmem_limit_bytes=LIMIT),
        cost_estimate=cost(LONG),
        name="relay",
    )(where, *args, *after)
    return outs[0], (outs[1] if held is not None else None)


def take_block(partial, at):
    return lax.dynamic_index_in_dim(partial, at, 0, keepdims=False)


def norm_terms(p_ref, a_ref, b_ref, res_ref, grad_ref, gain_ref, at):
    proj = p_ref[:, at].astype(F32) + a_ref[:, at].astype(F32) + b_ref[:, at].astype(F32)
    z = res_ref[:, at].astype(F32) + proj
    scaled = gain_ref[:, at].astype(F32) * grad_ref[:, at].astype(F32)
    return z, scaled


def norm_specs(rows, half, chunk, at):
    whole = pl.BlockSpec((rows, half), lambda i, r: (0, 0))
    own = pl.BlockSpec((None, rows, half), lambda i, r: (0, chunk, at))
    mine = pl.BlockSpec((None, rows, half), lambda i, r: (r[0], 0, 0))
    return [mine, whole, whole, own, own, pl.BlockSpec((1, half), lambda i, r: (0, at))]


def norm_sums(rank, ins, chunk, at, sums, after):
    parts, rows, half = ins[0].shape
    cols = divisor(half, 1024)

    def kernel(rank_ref, *refs):
        square_ref, cross_ref = refs[-2:]

        def step(i, sums):
            z, scaled = norm_terms(*refs[:6], pl.ds(pl.multiple_of(i * cols, cols), cols))
            square, cross = sums
            for j in range(0, cols, 128):
                zj = z[:, j : j + 128]
                square = square + zj * zj
                cross = cross + zj * scaled[:, j : j + 128]
            return square, cross

        zero = jnp.zeros((rows, 128), F32)
        start = (zero, zero) if sums is None else (refs[6][...], refs[7][...])
        square_ref[...], cross_ref[...] = lax.fori_loop(0, half // cols, step, start)

    stat = pl.BlockSpec((rows, 128), lambda i, r: (0, 0))
    before = [] if sums is None else list(sums)
    return pl.pallas_call(
        kernel,
        grid_spec=pltpu.PrefetchScalarGridSpec(
            num_scalar_prefetch=1,
            grid=(1,),
            in_specs=norm_specs(rows, half, chunk, at) + [stat] * len(before) + [ANY] * len(after),
            out_specs=[stat, stat],
        ),
        out_shape=[jax.ShapeDtypeStruct((rows, 128), F32)] * 2,
        compiler_params=pltpu.CompilerParams(vmem_limit_bytes=LIMIT),
        cost_estimate=cost(LONG),
        name="norm_sums",
    )(rank, *ins, *before, *after)


def norm_out(rank, ins, chunk, at, sums, width, after):
    parts, rows, half = ins[0].shape
    cols = divisor(half, 1024)

    def kernel(rank_ref, *refs):
        out_ref, held_ref, sem = refs[-3:]
        inv = lax.rsqrt(jnp.sum(refs[6][...], axis=-1, keepdims=True) / width + EPS)
        slope = inv * inv * inv * (jnp.sum(refs[7][...], axis=-1, keepdims=True) / width)

        def step(i, carry):
            here = pl.ds(pl.multiple_of(i * cols, cols), cols)
            z, scaled = norm_terms(*refs[:6], here)
            out_ref[:, here] = (inv * scaled - z * slope).astype(BF16)
            return carry

        lax.fori_loop(0, half // cols, step, 0)
        own = pltpu.make_async_copy(out_ref, held_ref.at[rank_ref[0]], sem)
        own.start()
        own.wait()

    stat = pl.BlockSpec((rows, 128), lambda i, r: (0, 0))
    return pl.pallas_call(
        kernel,
        grid_spec=pltpu.PrefetchScalarGridSpec(
            num_scalar_prefetch=1,
            grid=(1,),
            in_specs=norm_specs(rows, half, chunk, at) + [stat, stat] + [ANY] * len(after),
            out_specs=[pl.BlockSpec((rows, half), lambda i, r: (0, 0)), ANY],
            scratch_shapes=[pltpu.SemaphoreType.DMA],
        ),
        out_shape=[
            jax.ShapeDtypeStruct((rows, half), BF16),
            jax.ShapeDtypeStruct((parts, rows, half), BF16),
        ],
        compiler_params=pltpu.CompilerParams(vmem_limit_bytes=LIMIT),
        cost_estimate=cost(SHORT),
        name="norm_out",
    )(rank, *ins, *sums, *after)


def project_grads(grads, proj_out, after):
    blocks = [block for grad in grads for block in grad]
    rows, half = blocks[0].shape
    halves = len(grads[0])
    width = proj_out.shape[0]

    def kernel(*refs):
        out_ref, p_ref = refs[-1], refs[len(blocks)]
        for c in range(len(grads)):
            y = None
            for h in range(halves):
                term = project_rows(refs[c * halves + h][...], p_ref[:, h * half : (h + 1) * half])
                y = term if y is None else y + term
            out_ref[c * rows : (c + 1) * rows, :] = y

    return pl.pallas_call(
        kernel,
        grid=(1,),
        in_specs=[pl.BlockSpec((rows, half), lambda i: (0, 0))] * len(blocks)
        + [pl.BlockSpec(proj_out.shape, lambda i: (0, 0))]
        + [ANY] * len(after),
        out_specs=pl.BlockSpec((len(grads) * rows, width), lambda i: (0, 0)),
        out_shape=jax.ShapeDtypeStruct((len(grads) * rows, width), F32),
        compiler_params=pltpu.CompilerParams(vmem_limit_bytes=LIMIT),
        cost_estimate=cost(SHORT),
        name="project_grads",
    )(*blocks, proj_out, *after)


def tie(value, after):
    def kernel(value_ref, *refs):
        refs[-1][...] = value_ref[...]

    whole = pl.BlockSpec(value.shape, lambda i: (0,) * value.ndim)
    return pl.pallas_call(
        kernel,
        grid=(1,),
        in_specs=[whole] + [ANY] * len(after),
        out_specs=whole,
        out_shape=jax.ShapeDtypeStruct(value.shape, value.dtype),
        compiler_params=pltpu.CompilerParams(vmem_limit_bytes=LIMIT),
        cost_estimate=cost(SHORT),
        name="tie",
    )(value, *after)


def exchange(value_of, axis, size, rank):
    first = value_of(rank)
    out = jnp.zeros((size,) + first.shape, first.dtype)
    out = lax.dynamic_update_index_in_dim(out, first, rank, 0)
    for shift in range(1, size):
        got = lax.ppermute(
            value_of((rank + shift) % size), axis, [(d, (d + shift) % size) for d in range(size)]
        )
        out = lax.dynamic_update_index_in_dim(out, got, (rank - shift + size) % size, 0)
    return out


def body(inputs, residual, out_grad, norm_gain, w_out, proj_in, proj_out, queries, segment_ids):
    parts = lax.axis_size("tensor")
    rank = lax.axis_index("tensor")
    queriers = lax.axis_size("query")
    q_rank = lax.axis_index("query")
    tokens = inputs.shape[1]
    share = tokens // parts
    chunks = max(1, min(CHUNKS, share // 16))
    rows = share // chunks
    by_share = inputs.reshape(parts, chunks, rows, inputs.shape[2])
    gain = norm_gain.reshape(1, -1)
    half = w_out.shape[1] // HALVES

    up = 1 - 2 * (q_rank % 2)
    ways = (up, -up)
    spots = [jnp.where(way == 1, rank, parts - 1 - rank) for way in ways]
    rank_at = jnp.stack([rank]).astype(jnp.int32)

    def pairs(flow, low, high):
        out = []
        for q in range(queriers):
            way = 1 if (q % 2 == 0) == (flow == 0) else -1
            for t in range(parts):
                spot = t if way == 1 else parts - 1 - t
                if low <= spot <= min(high, parts - 2):
                    out.append((t * queriers + q, (t + way) * queriers + q))
        return out

    def where(flow, k):
        at = jnp.clip(rank + ways[flow] * (parts - k), 0, parts - 1)
        origin = jnp.clip(rank - ways[flow] * k, 0, parts - 1)
        return jnp.stack([at, spots[flow] <= k - 1, origin, spots[flow] >= k]).astype(jnp.int32)

    work, marks = [], []
    partials, totals, result = {}, {}, [None]

    def forward(c, h, piece, pieces, after):
        partials[c, h], mark = forward_piece(
            by_share, w_out, c, HALVES, h, piece, pieces, partials.get((c, h)), after
        )
        return mark

    def backward(c, blocks, total, last, piece, pieces, after):
        held = result[0] if last else totals.get(c)
        done, mark = backward_piece(
            blocks, w_out, c, chunks, HALVES, piece, pieces, total, last, held, after
        )
        if last:
            result[0] = done
        else:
            totals[c] = done
        return mark

    def do_one(x):
        if work:
            marks[:] = [work.pop(0)[1]([x])]

    def finish(key):
        while any(k == key for k, _ in work):
            marks[:] = [work.pop(0)[1](list(marks))]

    def add_forward(c, h, pieces):
        for piece in range(pieces):
            work.append(((c, h), functools.partial(forward, c, h, piece, pieces)))

    add_forward(0, 0, 1)
    finish((0, 0))
    in_rows = None
    grads = []
    for slot in range(chunks + 1):
        rs, ag = slot < chunks, slot > 0
        came, held, sent, marked, before = {}, {}, {}, {}, None
        if ag:
            grad = [None] * HALVES
            ins = [
                [partials[slot - 1, h], arrived[h, 0], arrived[h, 1], residual, out_grad, gain]
                for h in range(HALVES)
            ]
            sums = None
            for h in range(HALVES):
                extra = [in_rows] if slot == chunks and h == 0 else []
                sums = norm_sums(rank_at, ins[h], slot - 1, h, sums, list(marks) + extra)
            grad[0], held[0] = norm_out(rank_at, ins[0], slot - 1, 0, sums, w_out.shape[1], [])
        for k in range(parts):
            gather_now, reduce_now = ag and k <= parts - 2, rs and k >= 1
            if not gather_now and not reduce_now:
                continue
            for h in range(HALVES):
                if k == 0 and h > 0:
                    if rs:
                        add_forward(slot, h, PIECES)
                    for _ in range(PIECES):
                        do_one(sent[h - 1, 1])
                    grad[h], held[h] = norm_out(
                        rank_at, ins[h], slot - 1, h, sums, w_out.shape[1], list(marks)
                    )
                if reduce_now:
                    if slot == 0 and k == 1 and h > 0:
                        add_forward(0, h, 1)
                        marks[:] = [work.pop(0)[1]([sent[h - 1, 1]])]
                    finish((slot, h))
                for flow in range(2):
                    if k == 0:
                        x = grad[h]
                    elif (h, flow) not in came:
                        x = take_block(
                            partials[slot, h], jnp.clip(rank + ways[flow] * (parts - k), 0, parts - 1)
                        )
                    else:
                        after = list(marks) + ([] if before is None else [before])
                        if slot == 1 and k == 2 and h == 0 and flow == 0:
                            in_part = project_inputs(inputs.reshape(tokens, -1), proj_in, [before])
                            in_part = in_part.reshape(parts, share, -1)
                            in_rows = jnp.sum(
                                exchange(lambda at: take_block(in_part, at), "tensor", parts, rank).astype(F32),
                                axis=0,
                            )
                        x, held[h] = relay(
                            where(flow, k),
                            partials[slot, h] if reduce_now else None,
                            came[h, flow],
                            held.get(h),
                            after,
                        )
                        before = x
                    came[h, flow] = lax.ppermute(
                        x,
                        ("tensor", "query"),
                        pairs(flow, 0 if reduce_now else k, parts - 2 if gather_now else k - 1),
                    )
                    sent[h, flow] = x
                    marked[k] = x
                    if not (k == 0 or (slot == 0 and k == 1 and h == 0)):
                        do_one(x)
            if slot == 0 and k == 1:
                add_forward(1, 0, PIECES) if chunks > 1 else None
        if ag:
            grads.append(grad)
            if slot + 1 < chunks:
                add_forward(slot + 1, 0, PIECES)
            if rs:
                blocks = list(enumerate(held[h] for h in range(HALVES)))
                pieces = min(PIECES * HALVES, max(1, w_out.shape[0] // 128))
                for piece in range(pieces):
                    work.append(
                        (
                            ("b", slot - 1),
                            functools.partial(backward, slot - 1, blocks, None, True, piece, pieces),
                        )
                    )
            else:
                while work:
                    marks[:] = [work.pop(0)[1](list(marks))]
                for h in range(HALVES):
                    for flow in range(2):
                        _, held[h] = relay(where(flow, parts - 1), None, came[h, flow], held[h], list(marks))
                    backward(
                        slot - 1, [(h, held[h])], totals.get(slot - 1), h == HALVES - 1, 0, 1, list(marks)
                    )
        arrived = came
    input_grad = result[0].reshape(1, tokens, -1)

    out_rows = project_grads(grads, proj_out, [marked[1]])
    in_rows = in_rows.astype(F32)
    kp = out_rows.shape[1]
    segs = lax.dynamic_slice_in_dim(segment_ids[0], rank * share, share, 0)
    member = (segs[None, :] == jnp.arange(EX_DEV, dtype=jnp.int32)[:, None]).astype(F32)
    weighted = member[:, :, None] * out_rows[None]
    sketch_part = lax.dot_general(
        weighted,
        jnp.broadcast_to(in_rows[None], (EX_DEV,) + in_rows.shape),
        (((1,), (1,)), ((0,), (0,))),
        precision=lax.Precision.HIGHEST,
    )
    sketch_part = sketch_part.reshape(EX_DEV, parts, kp * kp // parts).astype(BF16)
    got = exchange(
        lambda at: lax.dynamic_index_in_dim(sketch_part, at, 1, keepdims=False), "tensor", parts, rank
    )
    sketch_cols = jnp.sum(tie(got, [marked[parts - 2]]).astype(F32), axis=0)
    paired = exchange(lambda at: sketch_cols, "query", queriers, q_rank)
    paired = tie(paired, [came[0, 0]]).reshape(queriers * EX_DEV, sketch_cols.shape[1])
    score_part = lax.dot_general(
        paired,
        queries.astype(F32),
        (((1,), (1,)), ((), ())),
        precision=lax.Precision.HIGHEST,
    )
    scores = jnp.sum(exchange(lambda at: score_part, "tensor", parts, rank), axis=0)
    return (input_grad, scores)


def solution(mesh):
    return jax.shard_map(
        body,
        mesh=mesh,
        in_specs=(
            P(("groups", "dp", "query"), None, "tensor"),
            P(("groups", "dp", "query"), "tensor", None),
            P(("groups", "dp", "query"), "tensor", None),
            P(),
            P("tensor", None),
            P(None, "tensor"),
            P(),
            P("query", "tensor"),
            P(("groups", "dp", "query"), None),
        ),
        out_specs=(P(("groups", "dp", "query"), None, "tensor"), P(("groups", "dp"), "query")),
        check_vma=False,
    )
```

```python
import functools

import jax
import jax.numpy as jnp
from jax import lax
from jax.experimental import pallas as pl
from jax.experimental.pallas import tpu as pltpu
from jax.sharding import PartitionSpec as P

EX_DEV = 4
EPS = 1e-05
CHUNKS = 2
HALVES = 2
PIECES = 2
SPLIT = 4
SHORT, LONG = 0.2, 5.0
LIMIT = 28 * 1024 * 1024

F32, BF16 = jnp.float32, jnp.bfloat16
ANY = pl.BlockSpec(memory_space=pl.ANY)
TOKEN = jax.ShapeDtypeStruct((8, 128), F32)
TOKEN_SPEC = pl.BlockSpec((8, 128), lambda *_: (0, 0))


def divisor(total, wanted):
    size = min(total, wanted)
    while total % size:
        size //= 2
    return size


def cost(microseconds):
    return pl.CostEstimate(flops=0, bytes_accessed=int(microseconds * 3.6e6), transcendentals=0)


def project_rows(values, matrix):
    return lax.dot_general(
        values, matrix, (((1,), (1,)), ((), ())), preferred_element_type=F32
    )


def spread(values, first):
    k = values.shape[1]
    row = lax.broadcasted_iota(jnp.int32, (k, 2 * k), 0)
    col = lax.broadcasted_iota(jnp.int32, (k, 2 * k), 1)
    return jnp.dot(values, jnp.where(col == row + first, 1.0, 0.0).astype(BF16), preferred_element_type=F32)


def forward_extra(by_share, proj_in, chunk, held, after):
    parts, _, rows, depth = by_share.shape
    extra = 2 * proj_in.shape[0]
    at = held.shape[2] // extra - 1

    def kernel(x_ref, p_ref, *refs):
        part = project_rows(x_ref[...].reshape(parts * rows, depth), p_ref[...]).astype(BF16)
        refs[-1][...] = spread(part, 0).astype(BF16).reshape(parts, rows, extra)

    return pl.pallas_call(
        kernel,
        grid=(1,),
        in_specs=[
            pl.BlockSpec((parts, None, rows, depth), lambda i: (0, chunk, 0, 0)),
            pl.BlockSpec(proj_in.shape, lambda i: (0, 0)),
        ]
        + [ANY] * (1 + len(after)),
        out_specs=pl.BlockSpec((parts, rows, extra), lambda i: (0, 0, at)),
        out_shape=jax.ShapeDtypeStruct(held.shape, BF16),
        input_output_aliases={2: 0},
        compiler_params=pltpu.CompilerParams(vmem_limit_bytes=LIMIT),
        cost_estimate=cost(SHORT),
        name="forward_extra",
    )(by_share, proj_in, held, *after)


def forward_piece(by_share, w_out, chunk, halves, half_at, extra, piece, pieces, held, after):
    parts, _, rows, depth = by_share.shape
    half = w_out.shape[1] // halves
    span = half // pieces
    cols = divisor(span, 512)
    steps = span // cols
    base = (half_at * half + piece * span) // cols
    cut = depth // SPLIT

    def kernel(x_ref, *refs):
        out_ref, tok_ref = refs[-2:]
        x = x_ref[...].reshape(parts * rows, depth)
        y = None
        for s in range(SPLIT):
            term = jnp.dot(x[:, s * cut : (s + 1) * cut], refs[s][...], preferred_element_type=F32)
            y = term if y is None else y + term
        out_ref[...] = y.astype(BF16).reshape(parts, rows, cols)
        tok_ref[...] = jnp.zeros_like(tok_ref)

    more = ([] if held is None else [held]) + after
    return pl.pallas_call(
        kernel,
        grid=(steps,),
        in_specs=[pl.BlockSpec((parts, None, rows, depth), lambda i: (0, chunk, 0, 0))]
        + [pl.BlockSpec((cut, cols), lambda i, s=s: (s, base + i)) for s in range(SPLIT)]
        + [ANY] * len(more),
        out_specs=[
            pl.BlockSpec((parts, rows, cols), lambda i: (0, 0, piece * steps + i)),
            TOKEN_SPEC,
        ],
        out_shape=[jax.ShapeDtypeStruct((parts, rows, half + extra), BF16), TOKEN],
        input_output_aliases={} if held is None else {1 + SPLIT: 0},
        compiler_params=pltpu.CompilerParams(vmem_limit_bytes=LIMIT),
        cost_estimate=cost(SHORT),
        name="forward_piece",
    )(by_share, *([w_out] * SPLIT), *more)


def backward_piece(blocks, w_out, chunk, chunks, halves, piece, pieces, total, last, held, after):
    parts, rows, _ = blocks[0][1].shape
    half = w_out.shape[1] // halves
    depth = w_out.shape[0]
    span = depth // pieces
    cols = divisor(span, 256)
    steps = span // cols
    cut = half // SPLIT
    n = len(blocks)

    def kernel(*refs):
        out_ref, tok_ref = refs[-2:]
        y = None if total is None else refs[n + n * SPLIT][...].reshape(parts * rows, cols)
        for b in range(n):
            g = refs[b][...].reshape(parts * rows, half)
            for s in range(SPLIT):
                term = project_rows(g[:, s * cut : (s + 1) * cut], refs[n + b * SPLIT + s][...])
                y = term if y is None else y + term
        out_ref[...] = y.astype(out_ref.dtype).reshape(parts, rows, cols)
        tok_ref[...] = jnp.zeros_like(tok_ref)

    here = pl.BlockSpec((parts, rows, cols), lambda i: (0, 0, piece * steps + i))
    if last:
        out_spec = pl.BlockSpec((parts, None, rows, cols), lambda i: (0, chunk, 0, piece * steps + i))
        out_shape = jax.ShapeDtypeStruct((parts, chunks, rows, depth), BF16)
    else:
        out_spec, out_shape = here, jax.ShapeDtypeStruct((parts, rows, depth), F32)
    weights = [
        pl.BlockSpec((cols, cut), lambda i, at=at * SPLIT + s: (piece * steps + i, at))
        for at, _ in blocks
        for s in range(SPLIT)
    ]
    sums = [] if total is None else [total]
    extra = ([] if held is None else [held]) + after
    return pl.pallas_call(
        kernel,
        grid=(steps,),
        in_specs=[pl.BlockSpec((parts, rows, half), lambda i: (0, 0, 0))] * n
        + weights
        + [here] * len(sums)
        + [ANY] * len(extra),
        out_specs=[out_spec, TOKEN_SPEC],
        out_shape=[out_shape, TOKEN],
        input_output_aliases={} if held is None else {n + n * SPLIT + len(sums): 0},
        compiler_params=pltpu.CompilerParams(vmem_limit_bytes=LIMIT),
        cost_estimate=cost(SHORT),
        name="backward_piece",
    )(*[g for _, g in blocks], *([w_out] * (n * SPLIT)), *sums, *extra)


def relay(pos, flow, k, partial, came, held, after):
    rows, width = came.shape
    parts = (partial if held is None else held).shape[0]
    n_in = 1 + (partial is not None) + (held is not None) + len(after)

    def far(pos_ref, steps):
        way = pos_ref[1] if flow == 0 else -pos_ref[1]
        return lax.clamp(0, pos_ref[0] + way * steps, parts - 1)

    def kernel(pos_ref, *refs):
        came_ref, x_ref = refs[0], refs[n_in]
        place = pos_ref[2] if flow == 0 else parts - 1 - pos_ref[2]
        if held is not None:
            store = pltpu.make_async_copy(came_ref, refs[n_in + 1].at[far(pos_ref, -k)], refs[-1])
            pl.when(place >= k)(store.start)
        if partial is not None:

            @pl.when(place < k)
            def _():
                x_ref[...] = (came_ref[...].astype(F32) + refs[1][...].astype(F32)).astype(BF16)

            @pl.when(place >= k)
            def _():
                x_ref[...] = came_ref[...]

        if held is not None:
            pl.when(place >= k)(store.wait)

    line = jax.ShapeDtypeStruct((rows, width), BF16)
    args, out_shape, alias = [came], [line], {}
    if partial is not None:
        whole = pl.BlockSpec((rows, width), lambda i, w: (0, 0))
        term = pl.BlockSpec((None, rows, width), lambda i, w: (far(w, parts - k), 0, 0))
        specs, out_specs = [whole, term], [whole]
        args.append(partial)
    else:
        specs, out_specs, alias = [ANY], [ANY], {1: 0}
    if held is not None:
        alias[1 + len(args)] = 1
        specs.append(ANY)
        args.append(held)
        out_specs.append(ANY)
        out_shape.append(jax.ShapeDtypeStruct(held.shape, BF16))
    outs = pl.pallas_call(
        kernel,
        grid_spec=pltpu.PrefetchScalarGridSpec(
            num_scalar_prefetch=1,
            grid=(1,),
            in_specs=specs + [ANY] * len(after),
            out_specs=out_specs,
            scratch_shapes=[pltpu.SemaphoreType.DMA] if held is not None else [],
        ),
        out_shape=out_shape,
        input_output_aliases=alias,
        compiler_params=pltpu.CompilerParams(vmem_limit_bytes=LIMIT),
        cost_estimate=cost(LONG),
        name="relay",
    )(pos, *args, *after)
    return outs[0], (outs[1] if held is not None else None)


def take_block(partial, at):
    return lax.dynamic_index_in_dim(partial, at, 0, keepdims=False)


def norm_terms(p_ref, a_ref, b_ref, res_ref, grad_ref, gain_ref, at):
    proj = p_ref[:, at].astype(F32) + a_ref[:, at].astype(F32) + b_ref[:, at].astype(F32)
    z = res_ref[:, at].astype(F32) + proj
    scaled = gain_ref[:, at].astype(F32) * grad_ref[:, at].astype(F32)
    return z, scaled


def norm_specs(ins, half, chunk, at):
    _, rows, wide = ins[0].shape
    whole = pl.BlockSpec((rows, wide), lambda i, r: (0, 0))
    own = pl.BlockSpec((None, rows, half), lambda i, r: (0, chunk, at))
    mine = pl.BlockSpec((None, rows, wide), lambda i, r: (r[0], 0, 0))
    return [mine, whole, whole, own, own, pl.BlockSpec((1, half), lambda i, r: (0, at))]


def norm_sums(pos, ins, half, chunk, at, sums, after):
    rows = ins[0].shape[1]
    cols = divisor(half, 1024)

    def kernel(pos_ref, *refs):
        square_ref, cross_ref = refs[-2:]

        def step(i, sums):
            z, scaled = norm_terms(*refs[:6], pl.ds(pl.multiple_of(i * cols, cols), cols))
            square, cross = sums
            for j in range(0, cols, 128):
                zj = z[:, j : j + 128]
                square = square + zj * zj
                cross = cross + zj * scaled[:, j : j + 128]
            return square, cross

        zero = jnp.zeros((rows, 128), F32)
        start = (zero, zero) if sums is None else (refs[6][...], refs[7][...])
        square_ref[...], cross_ref[...] = lax.fori_loop(0, half // cols, step, start)

    stat = pl.BlockSpec((rows, 128), lambda i, r: (0, 0))
    before = [] if sums is None else list(sums)
    return pl.pallas_call(
        kernel,
        grid_spec=pltpu.PrefetchScalarGridSpec(
            num_scalar_prefetch=1,
            grid=(1,),
            in_specs=norm_specs(ins, half, chunk, at) + [stat] * len(before) + [ANY] * len(after),
            out_specs=[stat, stat],
        ),
        out_shape=[jax.ShapeDtypeStruct((rows, 128), F32)] * 2,
        compiler_params=pltpu.CompilerParams(vmem_limit_bytes=LIMIT),
        cost_estimate=cost(LONG),
        name="norm_sums",
    )(pos, *ins, *before, *after)


def norm_out(pos, ins, half, chunk, sums, proj_out, after):
    parts, rows, wide = ins[0][1][0].shape
    cols = divisor(half, 1024)
    n, kp, width = len(ins), proj_out.shape[0], proj_out.shape[1]
    with_b = proj_out if wide > half else None

    def kernel(pos_ref, *refs):
        square_ref, cross_ref = refs[6 * n], refs[6 * n + 1]
        if with_b is None:
            out_ref, held_ref, sem = refs[-3:]
        else:
            out_ref, held_ref, rest_ref, sem = refs[-4:]
        inv = lax.rsqrt(jnp.sum(square_ref[...], axis=-1, keepdims=True) / width + EPS)
        slope = inv * inv * inv * (jnp.sum(cross_ref[...], axis=-1, keepdims=True) / width)
        for j in range(n):
            to_ref = out_ref if j == 0 else rest_ref.at[j - 1]

            def step(i, carry):
                here = pl.ds(pl.multiple_of(i * cols, cols), cols)
                z, scaled = norm_terms(*refs[6 * j : 6 * j + 6], here)
                to_ref[:, here] = (inv * scaled - z * slope).astype(BF16)
                return carry

            lax.fori_loop(0, half // cols, step, 0)
        if with_b is not None:
            p_ref = refs[6 * n + 2]
            b = project_rows(out_ref[:, :half], p_ref[:, :half])
            for j in range(1, n):
                b = b + project_rows(rest_ref[j - 1], p_ref[:, j * half : (j + 1) * half])
            a = sum(refs[j][:, half:].astype(F32) for j in range(3))
            out_ref[:, half:] = (a + spread(b.astype(BF16), kp)).astype(BF16)
        own = pltpu.make_async_copy(out_ref, held_ref.at[pos_ref[0]], sem)
        own.start()
        own.wait()

    stat = pl.BlockSpec((rows, 128), lambda i, r: (0, 0))
    specs, args = [], []
    for at, one in ins:
        specs += norm_specs(one, half, chunk, at)
        args += one
    specs, args = specs + [stat, stat], args + list(sums)
    scratch = [pltpu.SemaphoreType.DMA]
    if with_b is not None:
        specs.append(pl.BlockSpec(proj_out.shape, lambda i, r: (0, 0)))
        args.append(proj_out)
        scratch = [pltpu.VMEM((max(1, n - 1), rows, half), BF16)] + scratch
    return pl.pallas_call(
        kernel,
        grid_spec=pltpu.PrefetchScalarGridSpec(
            num_scalar_prefetch=1,
            grid=(1,),
            in_specs=specs + [ANY] * len(after),
            out_specs=[pl.BlockSpec((rows, wide), lambda i, r: (0, 0)), ANY],
            scratch_shapes=scratch,
        ),
        out_shape=[
            jax.ShapeDtypeStruct((rows, wide), BF16),
            jax.ShapeDtypeStruct((parts, rows, wide), BF16),
        ],
        compiler_params=pltpu.CompilerParams(vmem_limit_bytes=LIMIT),
        cost_estimate=cost(SHORT),
        name="norm_out",
    )(pos, *args, *after)


def exchange(value_of, axis, size, rank):
    first = value_of(rank)
    out = jnp.zeros((size,) + first.shape, first.dtype)
    out = lax.dynamic_update_index_in_dim(out, first, rank, 0)
    for shift in range(1, size):
        got = lax.ppermute(
            value_of(lax.rem(rank + shift, size)), axis, [(d, (d + shift) % size) for d in range(size)]
        )
        out = lax.dynamic_update_index_in_dim(out, got, lax.rem(rank - shift + size, size), 0)
    return out


def body(inputs, residual, out_grad, norm_gain, w_out, proj_in, proj_out, queries, segment_ids):
    parts = lax.axis_size("tensor")
    rank = lax.axis_index("tensor")
    queriers = lax.axis_size("query")
    q_rank = lax.axis_index("query")
    tokens = inputs.shape[1]
    share = tokens // parts
    chunks = max(1, min(CHUNKS, share // 16))
    rows = share // chunks
    by_share = inputs.reshape(parts, chunks, rows, inputs.shape[2])
    gain = norm_gain.reshape(1, -1)
    half = w_out.shape[1] // HALVES
    kp = proj_out.shape[0]

    up = 1 - 2 * lax.rem(q_rank, 2)
    pos = jnp.stack([rank, up, jnp.where(up == 1, rank, parts - 1 - rank)]).astype(jnp.int32)

    def pairs(flow, low, high):
        out = []
        for q in range(queriers):
            way = 1 if (q % 2 == 0) == (flow == 0) else -1
            for t in range(parts):
                spot = t if way == 1 else parts - 1 - t
                if low <= spot <= min(high, parts - 2):
                    out.append((t * queriers + q, (t + way) * queriers + q))
        return out

    work, marks = [], []
    partials, totals, result = {}, {}, [None]

    def forward(c, h, piece, pieces, after):
        partials[c, h], mark = forward_piece(
            by_share,
            w_out,
            c,
            HALVES,
            h,
            2 * kp if h == 0 else 0,
            piece,
            pieces,
            partials.get((c, h)),
            after,
        )
        if h == 0 and piece == pieces - 1:
            partials[c, h] = forward_extra(by_share, proj_in, c, partials[c, h], [mark])
        return mark

    def backward(c, blocks, total, last, piece, pieces, after):
        held = result[0] if last else totals.get(c)
        done, mark = backward_piece(
            blocks, w_out, c, chunks, HALVES, piece, pieces, total, last, held, after
        )
        if last:
            result[0] = done
        else:
            totals[c] = done
        return mark

    def do_one(after):
        if work:
            marks[:] = [work.pop(0)[1](after)]

    def finish(key):
        while any(k == key for k, _ in work):
            do_one(list(marks))

    def add_forward(c, h, pieces):
        for piece in range(pieces):
            work.append(((c, h), functools.partial(forward, c, h, piece, pieces)))

    add_forward(0, 0, 1)
    finish((0, 0))
    gathered = []
    for slot in range(chunks + 1):
        rs, ag = slot < chunks, slot > 0
        came, held, sent, before = {}, {}, {}, None
        if ag:
            ins = [
                [partials[slot - 1, h], arrived[h, 0], arrived[h, 1], residual, out_grad, gain]
                for h in range(HALVES)
            ]
            sums = None
            for h in range(HALVES):
                sums = norm_sums(pos, ins[h], half, slot - 1, h, sums, list(marks))
            grad = [None] * HALVES
            grad[0], held[0] = norm_out(
                pos, list(enumerate(ins)), half, slot - 1, sums, proj_out, []
            )
        for k in range(parts):
            gather_now, reduce_now = ag and k <= parts - 2, rs and k >= 1
            if not gather_now and not reduce_now:
                continue
            for h in range(HALVES):
                if k == 0 and h > 0:
                    if rs:
                        add_forward(slot, h, 1)
                    do_one([sent[h - 1, 1]])
                    grad[h], held[h] = norm_out(
                        pos, [(h, ins[h])], half, slot - 1, sums, proj_out, list(marks)
                    )
                if reduce_now:
                    if slot == 0 and k == 1 and h > 0:
                        add_forward(0, h, 1)
                        do_one([sent[h - 1, 1]])
                    finish((slot, h))
                for flow in range(2):
                    if k == 0:
                        x = before = grad[h]
                    elif (h, flow) not in came:
                        way = up if flow == 0 else -up
                        x = take_block(
                            partials[slot, h], jnp.clip(rank + way * (parts - k), 0, parts - 1)
                        )
                    else:
                        x, held[h] = relay(
                            pos,
                            flow,
                            k,
                            partials[slot, h] if reduce_now else None,
                            came[h, flow],
                            held.get(h),
                            list(marks) + ([] if before is None else [before]),
                        )
                        before = x
                    came[h, flow] = lax.ppermute(
                        x,
                        ("tensor", "query"),
                        pairs(flow, 0 if reduce_now else k, parts - 2 if gather_now else k - 1),
                    )
                    sent[h, flow] = x
                    if k > 0 and (slot > 0 or k > 1):
                        do_one([x])
            if slot == 0 and k == 1 and chunks > 1:
                add_forward(1, 0, PIECES)
        if ag:
            if slot + 1 < chunks:
                add_forward(slot + 1, 0, PIECES)
            if rs:
                blocks = [(h, held[h]) for h in range(HALVES)]
                for piece in range(PIECES):
                    work.append(
                        (
                            ("b", slot - 1),
                            functools.partial(backward, slot - 1, blocks, None, True, piece, PIECES),
                        )
                    )
            else:
                while work:
                    do_one(list(marks))
                for h in range(HALVES):
                    for flow in range(2):
                        _, held[h] = relay(
                            pos, flow, parts - 1, None, came[h, flow], held[h], list(marks)
                        )
                    if h < HALVES - 1:
                        blocks = [(h, held[h])]
                        marks[:] = [backward(slot - 1, blocks, totals.get(slot - 1), False, 0, 1, [])]
            gathered.append(held[0][:, :, half:])
        arrived = came
    both = jnp.stack(gathered, axis=1).reshape(tokens, 2 * kp)
    member = segment_ids[0][None, :] == jnp.arange(EX_DEV, dtype=jnp.int32)[:, None]
    weighted = jnp.where(member[:, :, None], both[None, :, kp:], 0)
    sketch = lax.dot_general(
        weighted,
        jnp.broadcast_to(both[None, :, :kp], (EX_DEV, tokens, kp)),
        (((1,), (1,)), ((0,), (0,))),
        preferred_element_type=F32,
    )
    sketch_cols = lax.dynamic_slice_in_dim(sketch, rank * (kp // parts), kp // parts, 1)
    sketch_cols = sketch_cols.reshape(EX_DEV, kp // parts * kp)
    paired = exchange(lambda at: sketch_cols, "query", queriers, q_rank)
    paired = paired.reshape(queriers * EX_DEV, sketch_cols.shape[1])
    score_part = lax.dot_general(
        paired,
        queries.astype(F32),
        (((1,), (1,)), ((), ())),
        precision=lax.Precision.HIGHEST,
    )
    scores = jnp.sum(exchange(lambda at: score_part, "tensor", parts, rank), axis=0)
    blocks = [(HALVES - 1, held[HALVES - 1])]
    for piece in range(PIECES):
        after = [scores] if piece == PIECES - 1 else []
        backward(chunks - 1, blocks, totals.get(chunks - 1), True, piece, PIECES, after)
    return (result[0].reshape(1, tokens, -1), scores)


def solution(mesh):
    return jax.shard_map(
        body,
        mesh=mesh,
        in_specs=(
            P(("groups", "dp", "query"), None, "tensor"),
            P(("groups", "dp", "query"), "tensor", None),
            P(("groups", "dp", "query"), "tensor", None),
            P(),
            P("tensor", None),
            P(None, "tensor"),
            P(),
            P("query", "tensor"),
            P(("groups", "dp", "query"), None),
        ),
        out_specs=(P(("groups", "dp", "query"), None, "tensor"), P(("groups", "dp"), "query")),
        check_vma=False,
    )
```

```python
import functools

import jax
import jax.numpy as jnp
from jax import lax
from jax.experimental import pallas as pl
from jax.experimental.pallas import tpu as pltpu
from jax.sharding import PartitionSpec as P

EX_DEV = 4
EPS = 1e-05
CHUNKS = 2
HALVES = 2
PIECES = 2
SPLIT = 4
SHORT, LONG = 0.2, 5.0
LIMIT = 28 * 1024 * 1024

F32, BF16 = jnp.float32, jnp.bfloat16
ANY = pl.BlockSpec(memory_space=pl.ANY)
TOKEN = jax.ShapeDtypeStruct((8, 128), F32)
TOKEN_SPEC = pl.BlockSpec((8, 128), lambda *_: (0, 0))


def divisor(total, wanted):
    size = min(total, wanted)
    while total % size:
        size //= 2
    return size


def cost(microseconds):
    return pl.CostEstimate(flops=0, bytes_accessed=int(microseconds * 3.6e6), transcendentals=0)


def project_rows(values, matrix):
    return lax.dot_general(
        values, matrix, (((1,), (1,)), ((), ())), preferred_element_type=F32
    )


def spread(values, first):
    k = values.shape[1]
    row = lax.broadcasted_iota(jnp.int32, (k, 2 * k), 0)
    col = lax.broadcasted_iota(jnp.int32, (k, 2 * k), 1)
    return jnp.dot(values, jnp.where(col == row + first, 1.0, 0.0).astype(BF16), preferred_element_type=F32)


def forward_extra(by_share, proj_in, chunk, held, after):
    parts, _, rows, depth = by_share.shape
    extra = 2 * proj_in.shape[0]
    at = held.shape[2] // extra - 1

    def kernel(x_ref, p_ref, *refs):
        part = project_rows(x_ref[...].reshape(parts * rows, depth), p_ref[...]).astype(BF16)
        refs[-1][...] = spread(part, 0).astype(BF16).reshape(parts, rows, extra)

    return pl.pallas_call(
        kernel,
        grid=(1,),
        in_specs=[
            pl.BlockSpec((parts, None, rows, depth), lambda i: (0, chunk, 0, 0)),
            pl.BlockSpec(proj_in.shape, lambda i: (0, 0)),
        ]
        + [ANY] * (1 + len(after)),
        out_specs=pl.BlockSpec((parts, rows, extra), lambda i: (0, 0, at)),
        out_shape=jax.ShapeDtypeStruct(held.shape, BF16),
        input_output_aliases={2: 0},
        compiler_params=pltpu.CompilerParams(vmem_limit_bytes=LIMIT),
        cost_estimate=cost(SHORT),
        name="forward_extra",
    )(by_share, proj_in, held, *after)


def forward_piece(by_share, w_out, chunk, halves, half_at, extra, piece, pieces, held, after):
    parts, _, rows, depth = by_share.shape
    half = w_out.shape[1] // halves
    span = half // pieces
    cols = divisor(span, 512)
    steps = span // cols
    base = (half_at * half + piece * span) // cols
    cut = depth // SPLIT

    def kernel(x_ref, *refs):
        out_ref, tok_ref = refs[-2:]
        x = x_ref[...].reshape(parts * rows, depth)
        y = None
        for s in range(SPLIT):
            term = jnp.dot(x[:, s * cut : (s + 1) * cut], refs[s][...], preferred_element_type=F32)
            y = term if y is None else y + term
        out_ref[...] = y.astype(BF16).reshape(parts, rows, cols)
        tok_ref[...] = jnp.zeros_like(tok_ref)

    more = ([] if held is None else [held]) + after
    return pl.pallas_call(
        kernel,
        grid=(steps,),
        in_specs=[pl.BlockSpec((parts, None, rows, depth), lambda i: (0, chunk, 0, 0))]
        + [pl.BlockSpec((cut, cols), lambda i, s=s: (s, base + i)) for s in range(SPLIT)]
        + [ANY] * len(more),
        out_specs=[
            pl.BlockSpec((parts, rows, cols), lambda i: (0, 0, piece * steps + i)),
            TOKEN_SPEC,
        ],
        out_shape=[jax.ShapeDtypeStruct((parts, rows, half + extra), BF16), TOKEN],
        input_output_aliases={} if held is None else {1 + SPLIT: 0},
        compiler_params=pltpu.CompilerParams(vmem_limit_bytes=LIMIT),
        cost_estimate=cost(SHORT),
        name="forward_piece",
    )(by_share, *([w_out] * SPLIT), *more)


def backward_piece(blocks, w_out, chunk, chunks, halves, piece, pieces, total, last, held, after):
    parts, rows, _ = blocks[0][1].shape
    half = w_out.shape[1] // halves
    depth = w_out.shape[0]
    span = depth // pieces
    cols = divisor(span, 256)
    steps = span // cols
    cut = half // SPLIT
    n = len(blocks)

    def kernel(*refs):
        out_ref, tok_ref = refs[-2:]
        y = None if total is None else refs[n + n * SPLIT][...].reshape(parts * rows, cols)
        for b in range(n):
            g = refs[b][...].reshape(parts * rows, half)
            for s in range(SPLIT):
                term = project_rows(g[:, s * cut : (s + 1) * cut], refs[n + b * SPLIT + s][...])
                y = term if y is None else y + term
        out_ref[...] = y.astype(out_ref.dtype).reshape(parts, rows, cols)
        tok_ref[...] = jnp.zeros_like(tok_ref)

    here = pl.BlockSpec((parts, rows, cols), lambda i: (0, 0, piece * steps + i))
    if last:
        out_spec = pl.BlockSpec((parts, None, rows, cols), lambda i: (0, chunk, 0, piece * steps + i))
        out_shape = jax.ShapeDtypeStruct((parts, chunks, rows, depth), BF16)
    else:
        out_spec, out_shape = here, jax.ShapeDtypeStruct((parts, rows, depth), F32)
    weights = [
        pl.BlockSpec((cols, cut), lambda i, at=at * SPLIT + s: (piece * steps + i, at))
        for at, _ in blocks
        for s in range(SPLIT)
    ]
    sums = [] if total is None else [total]
    extra = ([] if held is None else [held]) + after
    return pl.pallas_call(
        kernel,
        grid=(steps,),
        in_specs=[pl.BlockSpec((parts, rows, half), lambda i: (0, 0, 0))] * n
        + weights
        + [here] * len(sums)
        + [ANY] * len(extra),
        out_specs=[out_spec, TOKEN_SPEC],
        out_shape=[out_shape, TOKEN],
        input_output_aliases={} if held is None else {n + n * SPLIT + len(sums): 0},
        compiler_params=pltpu.CompilerParams(vmem_limit_bytes=LIMIT),
        cost_estimate=cost(SHORT),
        name="backward_piece",
    )(*[g for _, g in blocks], *([w_out] * (n * SPLIT)), *sums, *extra)


def relay(pos, flow, k, partial, came, held, after):
    rows, width = came.shape
    parts = (partial if held is None else held).shape[0]
    n_in = 1 + (partial is not None) + (held is not None) + len(after)

    def far(pos_ref, steps):
        way = pos_ref[1] if flow == 0 else -pos_ref[1]
        return lax.clamp(0, pos_ref[0] + way * steps, parts - 1)

    def kernel(pos_ref, *refs):
        came_ref, x_ref = refs[0], refs[n_in]
        place = pos_ref[2] if flow == 0 else parts - 1 - pos_ref[2]
        if held is not None:
            store = pltpu.make_async_copy(came_ref, refs[n_in + 1].at[far(pos_ref, -k)], refs[-1])
            pl.when(place >= k)(store.start)
        if partial is not None:

            @pl.when(place < k)
            def _():
                x_ref[...] = (came_ref[...].astype(F32) + refs[1][...].astype(F32)).astype(BF16)

            @pl.when(place >= k)
            def _():
                x_ref[...] = came_ref[...]

        else:
            x_ref[...] = came_ref[...]
        if held is not None:
            pl.when(place >= k)(store.wait)

    line = jax.ShapeDtypeStruct((rows, width), BF16)
    whole = pl.BlockSpec((rows, width), lambda i, w: (0, 0))
    args, specs, out_specs, out_shape, alias = [came], [whole], [whole], [line], {}
    if partial is not None:
        specs.append(pl.BlockSpec((None, rows, width), lambda i, w: (far(w, parts - k), 0, 0)))
        args.append(partial)
    if held is not None:
        alias[1 + len(args)] = 1
        specs.append(ANY)
        args.append(held)
        out_specs.append(ANY)
        out_shape.append(jax.ShapeDtypeStruct(held.shape, BF16))
    outs = pl.pallas_call(
        kernel,
        grid_spec=pltpu.PrefetchScalarGridSpec(
            num_scalar_prefetch=1,
            grid=(1,),
            in_specs=specs + [ANY] * len(after),
            out_specs=out_specs,
            scratch_shapes=[pltpu.SemaphoreType.DMA] if held is not None else [],
        ),
        out_shape=out_shape,
        input_output_aliases=alias,
        compiler_params=pltpu.CompilerParams(vmem_limit_bytes=LIMIT),
        cost_estimate=cost(LONG),
        name="relay",
    )(pos, *args, *after)
    return outs[0], (outs[1] if held is not None else None)


def take_block(partial, at):
    return lax.dynamic_index_in_dim(partial, at, 0, keepdims=False)


def norm_terms(p_ref, a_ref, b_ref, res_ref, grad_ref, gain_ref, at):
    proj = p_ref[:, at].astype(F32) + a_ref[:, at].astype(F32) + b_ref[:, at].astype(F32)
    z = res_ref[:, at].astype(F32) + proj
    scaled = gain_ref[:, at].astype(F32) * grad_ref[:, at].astype(F32)
    return z, scaled


def norm_specs(ins, half, chunk, at):
    _, rows, wide = ins[0].shape
    whole = pl.BlockSpec((rows, wide), lambda i, r: (0, 0))
    own = pl.BlockSpec((None, rows, half), lambda i, r: (0, chunk, at))
    mine = pl.BlockSpec((None, rows, wide), lambda i, r: (r[0], 0, 0))
    return [mine, whole, whole, own, own, pl.BlockSpec((1, half), lambda i, r: (0, at))]


def norm_sums(pos, ins, half, chunk, at, sums, after):
    rows = ins[0].shape[1]
    cols = divisor(half, 1024)

    def kernel(pos_ref, *refs):
        square_ref, cross_ref = refs[-2:]

        def step(i, sums):
            z, scaled = norm_terms(*refs[:6], pl.ds(pl.multiple_of(i * cols, cols), cols))
            square, cross = sums
            for j in range(0, cols, 128):
                zj = z[:, j : j + 128]
                square = square + zj * zj
                cross = cross + zj * scaled[:, j : j + 128]
            return square, cross

        zero = jnp.zeros((rows, 128), F32)
        start = (zero, zero) if sums is None else (refs[6][...], refs[7][...])
        square_ref[...], cross_ref[...] = lax.fori_loop(0, half // cols, step, start)

    stat = pl.BlockSpec((rows, 128), lambda i, r: (0, 0))
    before = [] if sums is None else list(sums)
    return pl.pallas_call(
        kernel,
        grid_spec=pltpu.PrefetchScalarGridSpec(
            num_scalar_prefetch=1,
            grid=(1,),
            in_specs=norm_specs(ins, half, chunk, at) + [stat] * len(before) + [ANY] * len(after),
            out_specs=[stat, stat],
        ),
        out_shape=[jax.ShapeDtypeStruct((rows, 128), F32)] * 2,
        compiler_params=pltpu.CompilerParams(vmem_limit_bytes=LIMIT),
        cost_estimate=cost(LONG),
        name="norm_sums",
    )(pos, *ins, *before, *after)


def norm_out(pos, ins, half, chunk, sums, proj_out, after):
    parts, rows, wide = ins[0][1][0].shape
    cols = divisor(half, 1024)
    n, width = len(ins), ins[0][1][3].shape[2]
    with_b = proj_out

    def kernel(pos_ref, *refs):
        square_ref, cross_ref = refs[6 * n], refs[6 * n + 1]
        if with_b is None:
            out_ref, held_ref, sem = refs[-3:]
        else:
            out_ref, held_ref, rest_ref, sem = refs[-4:]
        inv = lax.rsqrt(jnp.sum(square_ref[...], axis=-1, keepdims=True) / width + EPS)
        slope = inv * inv * inv * (jnp.sum(cross_ref[...], axis=-1, keepdims=True) / width)
        for j in range(n):
            to_ref = out_ref if j == 0 else rest_ref.at[j - 1]

            def step(i, carry):
                here = pl.ds(pl.multiple_of(i * cols, cols), cols)
                z, scaled = norm_terms(*refs[6 * j : 6 * j + 6], here)
                to_ref[:, here] = (inv * scaled - z * slope).astype(BF16)
                return carry

            lax.fori_loop(0, half // cols, step, 0)
        if with_b is not None:
            p_ref = refs[6 * n + 2]
            b = project_rows(out_ref[:, :half], p_ref[:, :half])
            for j in range(1, n):
                b = b + project_rows(rest_ref[j - 1], p_ref[:, j * half : (j + 1) * half])
            a = sum(refs[j][:, half:].astype(F32) for j in range(3))
            out_ref[:, half:] = (a + spread(b.astype(BF16), b.shape[1])).astype(BF16)
        else:
            out_ref[:, half:] = jnp.zeros((rows, wide - half), BF16)
        own = pltpu.make_async_copy(out_ref, held_ref.at[pos_ref[0]], sem)
        own.start()
        own.wait()

    stat = pl.BlockSpec((rows, 128), lambda i, r: (0, 0))
    specs, args = [], []
    for at, one in ins:
        specs += norm_specs(one, half, chunk, at)
        args += one
    specs, args = specs + [stat, stat], args + list(sums)
    scratch = [pltpu.SemaphoreType.DMA]
    if with_b is not None:
        specs.append(pl.BlockSpec(proj_out.shape, lambda i, r: (0, 0)))
        args.append(proj_out)
        scratch = [pltpu.VMEM((max(1, n - 1), rows, half), BF16)] + scratch
    return pl.pallas_call(
        kernel,
        grid_spec=pltpu.PrefetchScalarGridSpec(
            num_scalar_prefetch=1,
            grid=(1,),
            in_specs=specs + [ANY] * len(after),
            out_specs=[pl.BlockSpec((rows, wide), lambda i, r: (0, 0)), ANY],
            scratch_shapes=scratch,
        ),
        out_shape=[
            jax.ShapeDtypeStruct((rows, wide), BF16),
            jax.ShapeDtypeStruct((parts, rows, wide), BF16),
        ],
        compiler_params=pltpu.CompilerParams(vmem_limit_bytes=LIMIT),
        cost_estimate=cost(SHORT),
        name="norm_out",
    )(pos, *args, *after)


def tie(value, after):
    def kernel(value_ref, *refs):
        refs[-1][...] = value_ref[...]

    whole = pl.BlockSpec(value.shape, lambda i: (0,) * value.ndim)
    return pl.pallas_call(
        kernel,
        grid=(1,),
        in_specs=[whole] + [ANY] * len(after),
        out_specs=whole,
        out_shape=jax.ShapeDtypeStruct(value.shape, value.dtype),
        compiler_params=pltpu.CompilerParams(vmem_limit_bytes=LIMIT),
        cost_estimate=cost(SHORT),
        name="tie",
    )(value, *after)


def touch(x):
    def kernel(x_ref, out_ref):
        out_ref[...] = jnp.zeros_like(out_ref)

    return pl.pallas_call(
        kernel,
        grid=(1,),
        in_specs=[ANY],
        out_specs=TOKEN_SPEC,
        out_shape=TOKEN,
        compiler_params=pltpu.CompilerParams(vmem_limit_bytes=LIMIT),
        cost_estimate=cost(SHORT),
        name="touch",
    )(x)


def exchange(value_of, axis, size, rank):
    first = value_of(rank)
    out = jnp.zeros((size,) + first.shape, first.dtype)
    out = lax.dynamic_update_index_in_dim(out, first, rank, 0)
    for shift in range(1, size):
        got = lax.ppermute(
            value_of(lax.rem(rank + shift, size)), axis, [(d, (d + shift) % size) for d in range(size)]
        )
        out = lax.dynamic_update_index_in_dim(out, got, lax.rem(rank - shift + size, size), 0)
    return out


def body(inputs, residual, out_grad, norm_gain, w_out, proj_in, proj_out, queries, segment_ids):
    parts = lax.axis_size("tensor")
    rank = lax.axis_index("tensor")
    queriers = lax.axis_size("query")
    q_rank = lax.axis_index("query")
    tokens = inputs.shape[1]
    share = tokens // parts
    chunks = max(1, min(CHUNKS, share // 16))
    rows = share // chunks
    by_share = inputs.reshape(parts, chunks, rows, inputs.shape[2])
    gain = norm_gain.reshape(1, -1)
    half = w_out.shape[1] // HALVES
    kp = proj_out.shape[0]

    up = 1 - 2 * lax.rem(q_rank, 2)
    pos = jnp.stack([rank, up, jnp.where(up == 1, rank, parts - 1 - rank)]).astype(jnp.int32)

    def pairs(flow, low, high):
        out = []
        for q in range(queriers):
            way = 1 if (q % 2 == 0) == (flow == 0) else -1
            for t in range(parts):
                spot = t if way == 1 else parts - 1 - t
                if low <= spot <= min(high, parts - 2):
                    out.append((t * queriers + q, (t + way) * queriers + q))
        return out

    work, marks = [], []
    partials, totals, result = {}, {}, [None]

    def forward(c, h, piece, pieces, after):
        partials[c, h], mark = forward_piece(
            by_share,
            w_out,
            c,
            HALVES,
            h,
            2 * kp,
            piece,
            pieces,
            partials.get((c, h)),
            after,
        )
        if h == 0 and piece == pieces - 1:
            partials[c, h] = forward_extra(by_share, proj_in, c, partials[c, h], [mark])
        return mark

    def backward(c, blocks, total, last, piece, pieces, after):
        held = result[0] if last else totals.get(c)
        done, mark = backward_piece(
            blocks, w_out, c, chunks, HALVES, piece, pieces, total, last, held, after
        )
        if last:
            result[0] = done
        else:
            totals[c] = done
        return mark

    def do_one(after, touching=False):
        if work:
            marks[:] = [work.pop(0)[1](after)]
        elif touching:
            marks[:] = [touch(after[0])]

    def finish(key, after):
        while any(k == key for k, _ in work):
            do_one(list(marks) + after)

    def add_forward(c, h, pieces):
        for piece in range(pieces):
            work.append(((c, h), functools.partial(forward, c, h, piece, pieces)))

    add_forward(0, 0, 1)
    finish((0, 0), [])
    gathered = []
    for slot in range(chunks + 1):
        rs, ag = slot < chunks, slot > 0
        came, held, sent, before = {}, {}, {}, None
        if ag:
            ins = [
                [partials[slot - 1, h], arrived[h, 0], arrived[h, 1], residual, out_grad, gain]
                for h in range(HALVES)
            ]
            sums = None
            for h in range(HALVES):
                sums = norm_sums(pos, ins[h], half, slot - 1, h, sums, list(marks))
            grad = [None] * HALVES
            grad[0], held[0] = norm_out(
                pos, list(enumerate(ins)), half, slot - 1, sums, proj_out, []
            )
        for k in range(parts):
            gather_now, reduce_now = ag and k <= parts - 2, rs and k >= 1
            if not gather_now and not reduce_now:
                continue
            for h in range(HALVES):
                if k == 0 and h > 0:
                    if rs:
                        add_forward(slot, h, PIECES)
                    do_one([sent[h - 1, 1]])
                    grad[h], held[h] = norm_out(
                        pos, [(h, ins[h])], half, slot - 1, sums, None, list(marks)
                    )
                if reduce_now:
                    if slot == 0 and k == 1 and h > 0:
                        add_forward(0, h, 1)
                        do_one([sent[h - 1, 1]])
                    finish((slot, h), [sent[h - 1, 1]] if h > 0 else [])
                for flow in range(2):
                    if k == 0:
                        x = before = grad[h]
                    elif (h, flow) not in came:
                        way = up if flow == 0 else -up
                        x = take_block(
                            partials[slot, h], jnp.clip(rank + way * (parts - k), 0, parts - 1)
                        )
                    else:
                        x, held[h] = relay(
                            pos,
                            flow,
                            k,
                            partials[slot, h] if reduce_now else None,
                            came[h, flow],
                            held.get(h),
                            list(marks) + ([] if before is None else [before]),
                        )
                        before = x
                    came[h, flow] = lax.ppermute(
                        x,
                        ("tensor", "query"),
                        pairs(flow, 0 if reduce_now else k, parts - 2 if gather_now else k - 1),
                    )
                    sent[h, flow] = x
                    if slot == 0 and k == parts - 1 and (h, flow) == (HALVES - 1, 1) and chunks > 1:
                        add_forward(1, 0, 1)
                    if k > 0 and (slot > 0 or k > 1) and not (slot == 1 and work and k == 1 and flow == 0):
                        do_one([x], slot == chunks)
                if k == 0 and slot == chunks and h == HALVES - 1:
                    marks[:] = [touch(sent[h, 1])]
        if ag:
            if slot + 1 < chunks:
                add_forward(slot + 1, 0, PIECES)
            if rs:
                blocks = [(h, held[h]) for h in range(HALVES)]
                for piece in range(PIECES):
                    work.append(
                        (
                            ("b", slot - 1),
                            functools.partial(backward, slot - 1, blocks, None, True, piece, PIECES),
                        )
                    )
            else:
                while work:
                    do_one(list(marks))
                for flow in range(2):
                    _, held[0] = relay(pos, flow, parts - 1, None, came[0, flow], held[0], list(marks))
            gathered.append(held[0][:, :, half:])
        arrived = came
    both = jnp.stack(gathered, axis=1).reshape(tokens, 2 * kp)
    member = segment_ids[0][None, :] == jnp.arange(EX_DEV, dtype=jnp.int32)[:, None]
    weighted = jnp.where(member[:, :, None], both[None, :, kp:], 0)
    sketch = lax.dot_general(
        weighted,
        jnp.broadcast_to(both[None, :, :kp], (EX_DEV, tokens, kp)),
        (((1,), (1,)), ((0,), (0,))),
        preferred_element_type=F32,
    )
    sketch_cols = lax.dynamic_slice_in_dim(sketch, rank * (kp // parts), kp // parts, 1)
    sketch_cols = sketch_cols.reshape(EX_DEV, kp // parts * kp)

    last = chunks - 1
    marks[:] = [backward(last, [(0, held[0])], None, HALVES == 1, 0, 1, [sketch_cols])]
    for h in range(1, HALVES):
        for flow in range(2):
            _, held[h] = relay(pos, flow, parts - 1, None, came[h, flow], held[h], list(marks))
    paired = exchange(lambda at: sketch_cols, "query", queriers, q_rank)
    paired = tie(paired, list(marks)).reshape(queriers * EX_DEV, sketch_cols.shape[1])
    score_part = lax.dot_general(
        paired,
        queries.astype(F32),
        (((1,), (1,)), ((), ())),
        precision=lax.Precision.HIGHEST,
    )
    for h in range(1, HALVES):
        marks[:] = [
            backward(last, [(h, held[h])], totals.get(last), h == HALVES - 1, 0, 1, [score_part])
        ]
    scores = jnp.sum(tie(exchange(lambda at: score_part, "tensor", parts, rank), list(marks)), axis=0)
    return (result[0].reshape(1, tokens, -1), scores)


def solution(mesh):
    return jax.shard_map(
        body,
        mesh=mesh,
        in_specs=(
            P(("groups", "dp", "query"), None, "tensor"),
            P(("groups", "dp", "query"), "tensor", None),
            P(("groups", "dp", "query"), "tensor", None),
            P(),
            P("tensor", None),
            P(None, "tensor"),
            P(),
            P("query", "tensor"),
            P(("groups", "dp", "query"), None),
        ),
        out_specs=(P(("groups", "dp", "query"), None, "tensor"), P(("groups", "dp"), "query")),
        check_vma=False,
    )
```

```python
import functools

import jax
import jax.numpy as jnp
from jax import lax
from jax.experimental import pallas as pl
from jax.experimental.pallas import tpu as pltpu
from jax.sharding import PartitionSpec as P

EX_DEV = 4
EPS = 1e-05
CHUNKS = 2
HALVES = 2
PIECES = 2
SPLIT = 4
SHORT, LONG = 0.2, 5.0
LIMIT = 20 * 1024 * 1024

F32, BF16 = jnp.float32, jnp.bfloat16
ANY = pl.BlockSpec(memory_space=pl.ANY)
TOKEN = jax.ShapeDtypeStruct((8, 128), F32)
TOKEN_SPEC = pl.BlockSpec((8, 128), lambda *_: (0, 0))


def divisor(total, wanted):
    size = min(total, wanted)
    while total % size:
        size //= 2
    return size


def cost(microseconds):
    return pl.CostEstimate(flops=0, bytes_accessed=int(microseconds * 3.6e6), transcendentals=0)


def in_hbm(x):
    return pltpu.with_memory_space_constraint(x, pltpu.HBM)


def project_rows(values, matrix):
    return lax.dot_general(
        values, matrix, (((1,), (1,)), ((), ())), preferred_element_type=F32
    )


def spread(values, first):
    k = values.shape[1]
    row = lax.broadcasted_iota(jnp.int32, (k, 2 * k), 0)
    col = lax.broadcasted_iota(jnp.int32, (k, 2 * k), 1)
    return jnp.dot(values, jnp.where(col == row + first, 1.0, 0.0).astype(BF16), preferred_element_type=F32)


def forward_extra(by_share, proj_in, chunk, held, after):
    parts, _, rows, depth = by_share.shape
    extra = 2 * proj_in.shape[0]
    at = held.shape[2] // extra - 1

    def kernel(x_ref, p_ref, *refs):
        part = project_rows(x_ref[...].reshape(parts * rows, depth), p_ref[...]).astype(BF16)
        refs[-1][...] = spread(part, 0).astype(BF16).reshape(parts, rows, extra)

    return pl.pallas_call(
        kernel,
        grid=(1,),
        in_specs=[
            pl.BlockSpec((parts, None, rows, depth), lambda i: (0, chunk, 0, 0)),
            pl.BlockSpec(proj_in.shape, lambda i: (0, 0)),
        ]
        + [ANY] * (1 + len(after)),
        out_specs=pl.BlockSpec((parts, rows, extra), lambda i: (0, 0, at)),
        out_shape=jax.ShapeDtypeStruct(held.shape, BF16),
        input_output_aliases={2: 0},
        compiler_params=pltpu.CompilerParams(vmem_limit_bytes=LIMIT),
        cost_estimate=cost(SHORT),
        name="forward_extra",
    )(by_share, proj_in, held, *after)


def forward_piece(by_share, w_out, chunk, halves, half_at, extra, piece, pieces, held, after):
    parts, _, rows, depth = by_share.shape
    half = w_out.shape[1] // halves
    span = half // pieces
    cols = divisor(span, 512)
    steps = span // cols
    base = (half_at * half + piece * span) // cols
    cut = depth // SPLIT

    def kernel(x_ref, *refs):
        out_ref, tok_ref = refs[-2:]
        x = x_ref[...].reshape(parts * rows, depth)
        y = None
        for s in range(SPLIT):
            term = jnp.dot(x[:, s * cut : (s + 1) * cut], refs[s][...], preferred_element_type=F32)
            y = term if y is None else y + term
        out_ref[...] = y.astype(BF16).reshape(parts, rows, cols)
        tok_ref[...] = jnp.zeros_like(tok_ref)

    more = ([] if held is None else [held]) + after
    return pl.pallas_call(
        kernel,
        grid=(steps,),
        in_specs=[pl.BlockSpec((parts, None, rows, depth), lambda i: (0, chunk, 0, 0))]
        + [pl.BlockSpec((cut, cols), lambda i, s=s: (s, base + i)) for s in range(SPLIT)]
        + [ANY] * len(more),
        out_specs=[
            pl.BlockSpec((parts, rows, cols), lambda i: (0, 0, piece * steps + i)),
            TOKEN_SPEC,
        ],
        out_shape=[jax.ShapeDtypeStruct((parts, rows, half + extra), BF16), TOKEN],
        input_output_aliases={} if held is None else {1 + SPLIT: 0},
        compiler_params=pltpu.CompilerParams(vmem_limit_bytes=LIMIT),
        cost_estimate=cost(SHORT),
        name="forward_piece",
    )(by_share, *([in_hbm(w_out)] * SPLIT), *more)


def backward_piece(blocks, w_out, chunk, chunks, halves, piece, pieces, total, last, held, after):
    parts, rows, _ = blocks[0][1].shape
    half = w_out.shape[1] // halves
    depth = w_out.shape[0]
    span = depth // pieces
    cols = divisor(span, 256)
    steps = span // cols
    cut = half // SPLIT
    n = len(blocks)

    def kernel(*refs):
        out_ref, tok_ref = refs[-2:]
        y = None if total is None else refs[n + n * SPLIT][...].reshape(parts * rows, cols)
        for b in range(n):
            g = refs[b][...].reshape(parts * rows, half)
            for s in range(SPLIT):
                term = project_rows(g[:, s * cut : (s + 1) * cut], refs[n + b * SPLIT + s][...])
                y = term if y is None else y + term
        out_ref[...] = y.astype(out_ref.dtype).reshape(parts, rows, cols)
        tok_ref[...] = jnp.zeros_like(tok_ref)

    here = pl.BlockSpec((parts, rows, cols), lambda i: (0, 0, piece * steps + i))
    if last:
        out_spec = pl.BlockSpec((parts, None, rows, cols), lambda i: (0, chunk, 0, piece * steps + i))
        out_shape = jax.ShapeDtypeStruct((parts, chunks, rows, depth), BF16)
    else:
        out_spec, out_shape = here, jax.ShapeDtypeStruct((parts, rows, depth), F32)
    weights = [
        pl.BlockSpec((cols, cut), lambda i, at=at * SPLIT + s: (piece * steps + i, at))
        for at, _ in blocks
        for s in range(SPLIT)
    ]
    sums = [] if total is None else [total]
    extra = ([] if held is None else [held]) + after
    return pl.pallas_call(
        kernel,
        grid=(steps,),
        in_specs=[pl.BlockSpec((parts, rows, half), lambda i: (0, 0, 0))] * n
        + weights
        + [here] * len(sums)
        + [ANY] * len(extra),
        out_specs=[out_spec, TOKEN_SPEC],
        out_shape=[out_shape, TOKEN],
        input_output_aliases={} if held is None else {n + n * SPLIT + len(sums): 0},
        compiler_params=pltpu.CompilerParams(vmem_limit_bytes=LIMIT),
        cost_estimate=cost(SHORT),
        name="backward_piece",
    )(*[in_hbm(g) for _, g in blocks], *([in_hbm(w_out)] * (n * SPLIT)), *sums, *extra)


def relay(pos, flow, k, partial, came, held, after):
    rows, width = came.shape
    parts = (partial if held is None else held).shape[0]
    n_in = 1 + (partial is not None) + (held is not None) + len(after)

    def far(pos_ref, steps):
        way = pos_ref[1] if flow == 0 else -pos_ref[1]
        return lax.clamp(0, pos_ref[0] + way * steps, parts - 1)

    def kernel(pos_ref, *refs):
        came_ref, x_ref = refs[0], refs[n_in]
        place = pos_ref[2] if flow == 0 else parts - 1 - pos_ref[2]
        if held is not None:
            store = pltpu.make_async_copy(came_ref, refs[n_in + 1].at[far(pos_ref, -k)], refs[-1])
            pl.when(place >= k)(store.start)
        if partial is not None:

            @pl.when(place < k)
            def _():
                x_ref[...] = (came_ref[...].astype(F32) + refs[1][...].astype(F32)).astype(BF16)

            @pl.when(place >= k)
            def _():
                x_ref[...] = came_ref[...]

        else:
            x_ref[...] = came_ref[...]
        if held is not None:
            pl.when(place >= k)(store.wait)

    line = jax.ShapeDtypeStruct((rows, width), BF16)
    whole = pl.BlockSpec((rows, width), lambda i, w: (0, 0))
    args, specs, out_specs, out_shape, alias = [came], [whole], [whole], [line], {}
    if partial is not None:
        specs.append(pl.BlockSpec((None, rows, width), lambda i, w: (far(w, parts - k), 0, 0)))
        args.append(partial)
    if held is not None:
        alias[1 + len(args)] = 1
        specs.append(ANY)
        args.append(in_hbm(held))
        out_specs.append(ANY)
        out_shape.append(jax.ShapeDtypeStruct(held.shape, BF16))
    outs = pl.pallas_call(
        kernel,
        grid_spec=pltpu.PrefetchScalarGridSpec(
            num_scalar_prefetch=1,
            grid=(1,),
            in_specs=specs + [ANY] * len(after),
            out_specs=out_specs,
            scratch_shapes=[pltpu.SemaphoreType.DMA] if held is not None else [],
        ),
        out_shape=out_shape,
        input_output_aliases=alias,
        compiler_params=pltpu.CompilerParams(vmem_limit_bytes=LIMIT),
        cost_estimate=cost(LONG),
        name="relay",
    )(pos, *args, *after)
    return outs[0], (outs[1] if held is not None else None)


def store_last(pos, came, held, after):
    parts = held.shape[0]

    def kernel(pos_ref, a_ref, b_ref, *refs):
        out_ref, sem = refs[-2:]
        rank, way, place = pos_ref[0], pos_ref[1], pos_ref[2]
        ends = (
            (place == parts - 1, a_ref, rank - way * (parts - 1)),
            (place == 0, b_ref, rank + way * (parts - 1)),
        )
        for at_end, came_ref, at in ends:
            copy = pltpu.make_async_copy(came_ref, out_ref.at[lax.clamp(0, at, parts - 1)], sem)

            @pl.when(at_end)
            def _():
                copy.start()
                copy.wait()

    return pl.pallas_call(
        kernel,
        grid_spec=pltpu.PrefetchScalarGridSpec(
            num_scalar_prefetch=1,
            grid=(1,),
            in_specs=[ANY] * (3 + len(after)),
            out_specs=ANY,
            scratch_shapes=[pltpu.SemaphoreType.DMA],
        ),
        out_shape=jax.ShapeDtypeStruct(held.shape, BF16),
        input_output_aliases={3: 0},
        compiler_params=pltpu.CompilerParams(vmem_limit_bytes=LIMIT),
        cost_estimate=cost(SHORT),
        name="store_last",
    )(pos, *came, in_hbm(held), *after)


def take_block(partial, at):
    return lax.dynamic_index_in_dim(partial, at, 0, keepdims=False)


def norm_terms(p_ref, a_ref, b_ref, res_ref, grad_ref, gain_ref, at):
    proj = p_ref[:, at].astype(F32) + a_ref[:, at].astype(F32) + b_ref[:, at].astype(F32)
    z = res_ref[:, at].astype(F32) + proj
    scaled = gain_ref[:, at].astype(F32) * grad_ref[:, at].astype(F32)
    return z, scaled


def norm_specs(ins, half, chunk, at):
    _, rows, wide = ins[0].shape
    whole = pl.BlockSpec((rows, wide), lambda i, r: (0, 0))
    own = pl.BlockSpec((None, rows, half), lambda i, r: (0, chunk, at))
    mine = pl.BlockSpec((None, rows, wide), lambda i, r: (r[0], 0, 0))
    return [mine, whole, whole, own, own, pl.BlockSpec((1, half), lambda i, r: (0, at))]


def norm_sums(pos, ins, half, chunk, at, sums, after):
    rows = ins[0].shape[1]
    cols = divisor(half, 1024)

    def kernel(pos_ref, *refs):
        square_ref, cross_ref = refs[-2:]

        def step(i, sums):
            z, scaled = norm_terms(*refs[:6], pl.ds(pl.multiple_of(i * cols, cols), cols))
            square, cross = sums
            for j in range(0, cols, 128):
                zj = z[:, j : j + 128]
                square = square + zj * zj
                cross = cross + zj * scaled[:, j : j + 128]
            return square, cross

        zero = jnp.zeros((rows, 128), F32)
        start = (zero, zero) if sums is None else (refs[6][...], refs[7][...])
        square_ref[...], cross_ref[...] = lax.fori_loop(0, half // cols, step, start)

    stat = pl.BlockSpec((rows, 128), lambda i, r: (0, 0))
    before = [] if sums is None else list(sums)
    return pl.pallas_call(
        kernel,
        grid_spec=pltpu.PrefetchScalarGridSpec(
            num_scalar_prefetch=1,
            grid=(1,),
            in_specs=norm_specs(ins, half, chunk, at) + [stat] * len(before) + [ANY] * len(after),
            out_specs=[stat, stat],
        ),
        out_shape=[jax.ShapeDtypeStruct((rows, 128), F32)] * 2,
        compiler_params=pltpu.CompilerParams(vmem_limit_bytes=LIMIT),
        cost_estimate=cost(LONG),
        name="norm_sums",
    )(pos, *ins, *before, *after)


def norm_out(pos, ins, half, chunk, sums, proj_out, after):
    parts, rows, wide = ins[0][1][0].shape
    cols = divisor(half, 1024)
    n, width = len(ins), ins[0][1][3].shape[2]
    with_b = proj_out

    def kernel(pos_ref, *refs):
        square_ref, cross_ref = refs[6 * n], refs[6 * n + 1]
        if with_b is None:
            out_ref, held_ref, sem = refs[-3:]
        else:
            out_ref, held_ref, rest_ref, sem = refs[-4:]
        inv = lax.rsqrt(jnp.sum(square_ref[...], axis=-1, keepdims=True) / width + EPS)
        slope = inv * inv * inv * (jnp.sum(cross_ref[...], axis=-1, keepdims=True) / width)
        for j in range(n):
            to_ref = out_ref if j == 0 else rest_ref.at[j - 1]

            def step(i, carry):
                here = pl.ds(pl.multiple_of(i * cols, cols), cols)
                z, scaled = norm_terms(*refs[6 * j : 6 * j + 6], here)
                to_ref[:, here] = (inv * scaled - z * slope).astype(BF16)
                return carry

            lax.fori_loop(0, half // cols, step, 0)
        if with_b is not None:
            p_ref = refs[6 * n + 2]
            b = project_rows(out_ref[:, :half], p_ref[:, :half])
            for j in range(1, n):
                b = b + project_rows(rest_ref[j - 1], p_ref[:, j * half : (j + 1) * half])
            a = sum(refs[j][:, half:].astype(F32) for j in range(3))
            out_ref[:, half:] = (a + spread(b.astype(BF16), b.shape[1])).astype(BF16)
        else:
            out_ref[:, half:] = jnp.zeros((rows, wide - half), BF16)
        own = pltpu.make_async_copy(out_ref, held_ref.at[pos_ref[0]], sem)
        own.start()
        own.wait()

    stat = pl.BlockSpec((rows, 128), lambda i, r: (0, 0))
    specs, args = [], []
    for at, one in ins:
        specs += norm_specs(one, half, chunk, at)
        args += one
    specs, args = specs + [stat, stat], args + list(sums)
    scratch = [pltpu.SemaphoreType.DMA]
    if with_b is not None:
        specs.append(pl.BlockSpec(proj_out.shape, lambda i, r: (0, 0)))
        args.append(proj_out)
        scratch = [pltpu.VMEM((max(1, n - 1), rows, half), BF16)] + scratch
    return pl.pallas_call(
        kernel,
        grid_spec=pltpu.PrefetchScalarGridSpec(
            num_scalar_prefetch=1,
            grid=(1,),
            in_specs=specs + [ANY] * len(after),
            out_specs=[pl.BlockSpec((rows, wide), lambda i, r: (0, 0)), ANY],
            scratch_shapes=scratch,
        ),
        out_shape=[
            jax.ShapeDtypeStruct((rows, wide), BF16),
            pltpu.HBM((parts, rows, wide), BF16),
        ],
        compiler_params=pltpu.CompilerParams(vmem_limit_bytes=LIMIT),
        cost_estimate=cost(SHORT),
        name="norm_out",
    )(pos, *args, *after)


def tie(value, after):
    def kernel(value_ref, *refs):
        refs[-1][...] = value_ref[...]

    whole = pl.BlockSpec(value.shape, lambda i: (0,) * value.ndim)
    return pl.pallas_call(
        kernel,
        grid=(1,),
        in_specs=[whole] + [ANY] * len(after),
        out_specs=whole,
        out_shape=jax.ShapeDtypeStruct(value.shape, value.dtype),
        compiler_params=pltpu.CompilerParams(vmem_limit_bytes=LIMIT),
        cost_estimate=cost(SHORT),
        name="tie",
    )(value, *after)


def touch(x):
    def kernel(x_ref, out_ref):
        out_ref[...] = jnp.zeros_like(out_ref)

    return pl.pallas_call(
        kernel,
        grid=(1,),
        in_specs=[ANY],
        out_specs=TOKEN_SPEC,
        out_shape=TOKEN,
        compiler_params=pltpu.CompilerParams(vmem_limit_bytes=LIMIT),
        cost_estimate=cost(SHORT),
        name="touch",
    )(x)


def exchange(value_of, axis, size, rank):
    first = value_of(rank)
    out = jnp.zeros((size,) + first.shape, first.dtype)
    out = lax.dynamic_update_index_in_dim(out, first, rank, 0)
    for shift in range(1, size):
        got = lax.ppermute(
            value_of(lax.rem(rank + shift, size)), axis, [(d, (d + shift) % size) for d in range(size)]
        )
        out = lax.dynamic_update_index_in_dim(out, got, lax.rem(rank - shift + size, size), 0)
    return out


def body(inputs, residual, out_grad, norm_gain, w_out, proj_in, proj_out, queries, segment_ids):
    parts = lax.axis_size("tensor")
    rank = lax.axis_index("tensor")
    queriers = lax.axis_size("query")
    q_rank = lax.axis_index("query")
    tokens = inputs.shape[1]
    share = tokens // parts
    chunks = max(1, min(CHUNKS, share // 16))
    rows = share // chunks
    by_share = inputs.reshape(parts, chunks, rows, inputs.shape[2])
    gain = norm_gain.reshape(1, -1)
    half = w_out.shape[1] // HALVES
    kp = proj_out.shape[0]

    up = 1 - 2 * lax.rem(q_rank, 2)
    pos = jnp.stack([rank, up, jnp.where(up == 1, rank, parts - 1 - rank)]).astype(jnp.int32)

    def pairs(flow, low, high):
        out = []
        for q in range(queriers):
            way = 1 if (q % 2 == 0) == (flow == 0) else -1
            for t in range(parts):
                spot = t if way == 1 else parts - 1 - t
                if low <= spot <= min(high, parts - 2):
                    out.append((t * queriers + q, (t + way) * queriers + q))
        return out

    work, marks = [], []
    partials, totals, result = {}, {}, [None]

    def forward(c, h, piece, pieces, after):
        partials[c, h], mark = forward_piece(
            by_share,
            w_out,
            c,
            HALVES,
            h,
            2 * kp,
            piece,
            pieces,
            partials.get((c, h)),
            after,
        )
        if h == 0 and piece == pieces - 1:
            partials[c, h] = forward_extra(by_share, proj_in, c, partials[c, h], [mark])
        return mark

    def backward(c, blocks, total, last, piece, pieces, after):
        held = result[0] if last else totals.get(c)
        done, mark = backward_piece(
            blocks, w_out, c, chunks, HALVES, piece, pieces, total, last, held, after
        )
        if last:
            result[0] = done
        else:
            totals[c] = done
        return mark

    def do_one(after, touching=False):
        if work:
            marks[:] = [work.pop(0)[1](after)]
        elif touching:
            marks[:] = [touch(after[0])]

    def finish(key, after):
        while any(k == key for k, _ in work):
            do_one(list(marks) + after)

    def add_forward(c, h, pieces):
        for piece in range(pieces):
            work.append(((c, h), functools.partial(forward, c, h, piece, pieces)))

    add_forward(0, 0, 1)
    finish((0, 0), [])
    gathered = []
    for slot in range(chunks + 1):
        rs, ag = slot < chunks, slot > 0
        came, held, sent, before = {}, {}, {}, None
        if ag:
            ins = [
                [partials[slot - 1, h], arrived[h, 0], arrived[h, 1], residual, out_grad, gain]
                for h in range(HALVES)
            ]
            sums = None
            for h in range(HALVES):
                sums = norm_sums(pos, ins[h], half, slot - 1, h, sums, list(marks))
            grad = [None] * HALVES
            grad[0], held[0] = norm_out(
                pos, list(enumerate(ins)), half, slot - 1, sums, proj_out, []
            )
        for k in range(parts):
            gather_now, reduce_now = ag and k <= parts - 2, rs and k >= 1
            if not gather_now and not reduce_now:
                continue
            for h in range(HALVES):
                if k == 0 and h > 0:
                    if rs:
                        add_forward(slot, h, PIECES)
                    do_one([sent[h - 1, 1]])
                    grad[h], held[h] = norm_out(
                        pos, [(h, ins[h])], half, slot - 1, sums, None, list(marks)
                    )
                if reduce_now:
                    if slot == 0 and k == 1 and h > 0:
                        add_forward(0, h, 1)
                        do_one([sent[h - 1, 1]])
                    finish((slot, h), [sent[h - 1, 1]] if h > 0 else [])
                for flow in range(2):
                    if k == 0:
                        x = before = grad[h]
                    elif (h, flow) not in came:
                        way = up if flow == 0 else -up
                        x = take_block(
                            partials[slot, h], jnp.clip(rank + way * (parts - k), 0, parts - 1)
                        )
                    else:
                        x, held[h] = relay(
                            pos,
                            flow,
                            k,
                            partials[slot, h] if reduce_now else None,
                            came[h, flow],
                            held.get(h),
                            list(marks) + ([] if before is None else [before]),
                        )
                        before = x
                    came[h, flow] = lax.ppermute(
                        x,
                        ("tensor", "query"),
                        pairs(flow, 0 if reduce_now else k, parts - 2 if gather_now else k - 1),
                    )
                    sent[h, flow] = x
                    if slot == 0 and k == parts - 1 and (h, flow) == (HALVES - 1, 1) and chunks > 1:
                        add_forward(1, 0, 1)
                    if k > 0 and (slot > 0 or k > 1) and not (slot == 1 and work and k == 1 and flow == 0):
                        do_one([x], slot == chunks)
                if k == 0 and slot == chunks and h == HALVES - 1:
                    marks[:] = [touch(sent[h, 1])]
        if ag:
            if slot + 1 < chunks:
                add_forward(slot + 1, 0, PIECES)
            if rs:
                blocks = [(h, held[h]) for h in range(HALVES)]
                for piece in range(PIECES):
                    work.append(
                        (
                            ("b", slot - 1),
                            functools.partial(backward, slot - 1, blocks, None, True, piece, PIECES),
                        )
                    )
            else:
                while work:
                    do_one(list(marks))
                marks[:] = [touch(came[0, 0])]
                held[0] = store_last(pos, (came[0, 0], came[0, 1]), held[0], list(marks))
            gathered.append(held[0][:, :, half:])
        arrived = came
    both = jnp.stack(gathered, axis=1).reshape(tokens, 2 * kp)
    member = segment_ids[0][None, :] == jnp.arange(EX_DEV, dtype=jnp.int32)[:, None]
    weighted = jnp.where(member[:, :, None], both[None, :, kp:], 0)
    sketch = lax.dot_general(
        weighted,
        jnp.broadcast_to(both[None, :, :kp], (EX_DEV, tokens, kp)),
        (((1,), (1,)), ((0,), (0,))),
        preferred_element_type=F32,
    )
    sketch_cols = lax.dynamic_slice_in_dim(sketch, rank * (kp // parts), kp // parts, 1)
    sketch_cols = sketch_cols.reshape(EX_DEV, kp // parts * kp)

    last = chunks - 1
    marks[:] = [backward(last, [(0, held[0])], None, HALVES == 1, 0, 1, [sketch_cols])]
    for h in range(1, HALVES):
        marks[:] = [tie(marks[0], [came[h, 0]])]
        held[h] = store_last(pos, (came[h, 0], came[h, 1]), held[h], list(marks))
    paired = exchange(lambda at: sketch_cols, "query", queriers, q_rank)
    paired = tie(paired, list(marks)).reshape(queriers * EX_DEV, sketch_cols.shape[1])
    score_part = lax.dot_general(
        paired,
        queries.astype(F32),
        (((1,), (1,)), ((), ())),
        precision=lax.Precision.HIGHEST,
    )
    for h in range(1, HALVES):
        marks[:] = [
            backward(last, [(h, held[h])], totals.get(last), h == HALVES - 1, 0, 1, [score_part])
        ]
    scores = jnp.sum(tie(exchange(lambda at: score_part, "tensor", parts, rank), list(marks)), axis=0)
    return (result[0].reshape(1, tokens, -1), scores)


def solution(mesh):
    return jax.shard_map(
        body,
        mesh=mesh,
        in_specs=(
            P(("groups", "dp", "query"), None, "tensor"),
            P(("groups", "dp", "query"), "tensor", None),
            P(("groups", "dp", "query"), "tensor", None),
            P(),
            P("tensor", None),
            P(None, "tensor"),
            P(),
            P("query", "tensor"),
            P(("groups", "dp", "query"), None),
        ),
        out_specs=(P(("groups", "dp", "query"), None, "tensor"), P(("groups", "dp"), "query")),
        check_vma=False,
    )
```

```python
import functools

import jax
import jax.numpy as jnp
from jax import lax
from jax.experimental import pallas as pl
from jax.experimental.pallas import tpu as pltpu
from jax.sharding import PartitionSpec as P

EX_DEV = 4
EPS = 1e-05
CHUNKS = 2
HALVES = 2
PIECES = 2
SPLIT = 4
SHORT, LONG = 0.2, 5.0
LIMIT = 20 * 1024 * 1024

F32, BF16 = jnp.float32, jnp.bfloat16
ANY = pl.BlockSpec(memory_space=pl.ANY)
TOKEN = jax.ShapeDtypeStruct((8, 128), F32)
TOKEN_SPEC = pl.BlockSpec((8, 128), lambda *_: (0, 0))


def divisor(total, wanted):
    size = min(total, wanted)
    while total % size:
        size //= 2
    return size


def cost(microseconds):
    return pl.CostEstimate(flops=0, bytes_accessed=int(microseconds * 3.6e6), transcendentals=0)


def in_hbm(x):
    return pltpu.with_memory_space_constraint(x, pltpu.HBM)


def project_rows(values, matrix):
    return lax.dot_general(
        values, matrix, (((1,), (1,)), ((), ())), preferred_element_type=F32
    )


def spread(values, first):
    k = values.shape[1]
    row = lax.broadcasted_iota(jnp.int32, (k, 2 * k), 0)
    col = lax.broadcasted_iota(jnp.int32, (k, 2 * k), 1)
    return jnp.dot(values, jnp.where(col == row + first, 1.0, 0.0).astype(BF16), preferred_element_type=F32)


def forward_extra(by_share, proj_in, chunk, held, after):
    parts, _, rows, depth = by_share.shape
    extra = 2 * proj_in.shape[0]
    at = held.shape[2] // extra - 1

    def kernel(x_ref, p_ref, *refs):
        part = project_rows(x_ref[...].reshape(parts * rows, depth), p_ref[...]).astype(BF16)
        refs[-1][...] = spread(part, 0).astype(BF16).reshape(parts, rows, extra)

    return pl.pallas_call(
        kernel,
        grid=(1,),
        in_specs=[
            pl.BlockSpec((parts, None, rows, depth), lambda i: (0, chunk, 0, 0)),
            pl.BlockSpec(proj_in.shape, lambda i: (0, 0)),
        ]
        + [ANY] * (1 + len(after)),
        out_specs=pl.BlockSpec((parts, rows, extra), lambda i: (0, 0, at)),
        out_shape=jax.ShapeDtypeStruct(held.shape, BF16),
        input_output_aliases={2: 0},
        compiler_params=pltpu.CompilerParams(vmem_limit_bytes=LIMIT),
        cost_estimate=cost(SHORT),
        name="forward_extra",
    )(by_share, proj_in, held, *after)


def forward_piece(by_share, w_out, chunk, halves, half_at, extra, piece, pieces, held, after):
    parts, _, rows, depth = by_share.shape
    half = w_out.shape[1] // halves
    span = half // pieces
    cols = divisor(span, 512)
    steps = span // cols
    base = (half_at * half + piece * span) // cols
    cut = depth // SPLIT

    def kernel(x_ref, *refs):
        out_ref, tok_ref = refs[-2:]
        x = x_ref[...].reshape(parts * rows, depth)
        y = None
        for s in range(SPLIT):
            term = jnp.dot(x[:, s * cut : (s + 1) * cut], refs[s][...], preferred_element_type=F32)
            y = term if y is None else y + term
        out_ref[...] = y.astype(BF16).reshape(parts, rows, cols)
        tok_ref[...] = jnp.zeros_like(tok_ref)

    more = ([] if held is None else [held]) + after
    return pl.pallas_call(
        kernel,
        grid=(steps,),
        in_specs=[pl.BlockSpec((parts, None, rows, depth), lambda i: (0, chunk, 0, 0))]
        + [pl.BlockSpec((cut, cols), lambda i, s=s: (s, base + i)) for s in range(SPLIT)]
        + [ANY] * len(more),
        out_specs=[
            pl.BlockSpec((parts, rows, cols), lambda i: (0, 0, piece * steps + i)),
            TOKEN_SPEC,
        ],
        out_shape=[jax.ShapeDtypeStruct((parts, rows, half + extra), BF16), TOKEN],
        input_output_aliases={} if held is None else {1 + SPLIT: 0},
        compiler_params=pltpu.CompilerParams(vmem_limit_bytes=LIMIT),
        cost_estimate=cost(SHORT),
        name="forward_piece",
    )(by_share, *([in_hbm(w_out)] * SPLIT), *more)


def backward_piece(blocks, w_out, chunk, chunks, halves, piece, pieces, total, last, held, after):
    parts, rows, _ = blocks[0][1].shape
    half = w_out.shape[1] // halves
    depth = w_out.shape[0]
    span = depth // pieces
    cols = divisor(span, 256)
    steps = span // cols
    cut = half // SPLIT
    n = len(blocks)

    def kernel(*refs):
        out_ref, tok_ref = refs[-2:]
        y = None if total is None else refs[n + n * SPLIT][...].reshape(parts * rows, cols)
        for b in range(n):
            g = refs[b][...].reshape(parts * rows, half)
            for s in range(SPLIT):
                term = project_rows(g[:, s * cut : (s + 1) * cut], refs[n + b * SPLIT + s][...])
                y = term if y is None else y + term
        out_ref[...] = y.astype(out_ref.dtype).reshape(parts, rows, cols)
        tok_ref[...] = jnp.zeros_like(tok_ref)

    here = pl.BlockSpec((parts, rows, cols), lambda i: (0, 0, piece * steps + i))
    if last:
        out_spec = pl.BlockSpec((parts, None, rows, cols), lambda i: (0, chunk, 0, piece * steps + i))
        out_shape = jax.ShapeDtypeStruct((parts, chunks, rows, depth), BF16)
    else:
        out_spec, out_shape = here, jax.ShapeDtypeStruct((parts, rows, depth), F32)
    weights = [
        pl.BlockSpec((cols, cut), lambda i, at=at * SPLIT + s: (piece * steps + i, at))
        for at, _ in blocks
        for s in range(SPLIT)
    ]
    sums = [] if total is None else [total]
    extra = ([] if held is None else [held]) + after
    return pl.pallas_call(
        kernel,
        grid=(steps,),
        in_specs=[pl.BlockSpec((parts, rows, half), lambda i: (0, 0, 0))] * n
        + weights
        + [here] * len(sums)
        + [ANY] * len(extra),
        out_specs=[out_spec, TOKEN_SPEC],
        out_shape=[out_shape, TOKEN],
        input_output_aliases={} if held is None else {n + n * SPLIT + len(sums): 0},
        compiler_params=pltpu.CompilerParams(vmem_limit_bytes=LIMIT),
        cost_estimate=cost(SHORT),
        name="backward_piece",
    )(*[g for _, g in blocks], *([in_hbm(w_out)] * (n * SPLIT)), *sums, *extra)


def relay(pos, flow, k, partial, came, held, after):
    rows, width = came.shape
    parts = (partial if held is None else held).shape[0]
    n_in = 1 + (partial is not None) + (held is not None) + len(after)

    def far(pos_ref, steps):
        way = pos_ref[1] if flow == 0 else -pos_ref[1]
        return lax.clamp(0, pos_ref[0] + way * steps, parts - 1)

    def kernel(pos_ref, *refs):
        came_ref, x_ref = refs[0], refs[n_in]
        place = pos_ref[2] if flow == 0 else parts - 1 - pos_ref[2]
        if held is not None:
            store = pltpu.make_async_copy(came_ref, refs[n_in + 1].at[far(pos_ref, -k)], refs[-1])
            pl.when(place >= k)(store.start)
        if partial is not None:

            @pl.when(place < k)
            def _():
                x_ref[...] = (came_ref[...].astype(F32) + refs[1][...].astype(F32)).astype(BF16)

            @pl.when(place >= k)
            def _():
                x_ref[...] = came_ref[...]

        else:
            x_ref[...] = came_ref[...]
        if held is not None:
            pl.when(place >= k)(store.wait)

    line = jax.ShapeDtypeStruct((rows, width), BF16)
    whole = pl.BlockSpec((rows, width), lambda i, w: (0, 0))
    args, specs, out_specs, out_shape, alias = [came], [whole], [whole], [line], {}
    if partial is not None:
        specs.append(pl.BlockSpec((None, rows, width), lambda i, w: (far(w, parts - k), 0, 0)))
        args.append(partial)
    if held is not None:
        alias[1 + len(args)] = 1
        specs.append(ANY)
        args.append(held)
        out_specs.append(ANY)
        out_shape.append(jax.ShapeDtypeStruct(held.shape, BF16))
    outs = pl.pallas_call(
        kernel,
        grid_spec=pltpu.PrefetchScalarGridSpec(
            num_scalar_prefetch=1,
            grid=(1,),
            in_specs=specs + [ANY] * len(after),
            out_specs=out_specs,
            scratch_shapes=[pltpu.SemaphoreType.DMA] if held is not None else [],
        ),
        out_shape=out_shape,
        input_output_aliases=alias,
        compiler_params=pltpu.CompilerParams(vmem_limit_bytes=LIMIT),
        cost_estimate=cost(LONG),
        name="relay",
    )(pos, *args, *after)
    return outs[0], (outs[1] if held is not None else None)


def store_last(pos, came, held, after):
    parts = held.shape[0]

    def kernel(pos_ref, a_ref, b_ref, *refs):
        out_ref, sem = refs[-2:]
        rank, way, place = pos_ref[0], pos_ref[1], pos_ref[2]
        ends = (
            (place == parts - 1, a_ref, rank - way * (parts - 1)),
            (place == 0, b_ref, rank + way * (parts - 1)),
        )
        for at_end, came_ref, at in ends:
            copy = pltpu.make_async_copy(came_ref, out_ref.at[lax.clamp(0, at, parts - 1)], sem)

            @pl.when(at_end)
            def _():
                copy.start()
                copy.wait()

    return pl.pallas_call(
        kernel,
        grid_spec=pltpu.PrefetchScalarGridSpec(
            num_scalar_prefetch=1,
            grid=(1,),
            in_specs=[pl.BlockSpec(held.shape[1:], lambda i, w: (0, 0))] * 2 + [ANY] * (1 + len(after)),
            out_specs=ANY,
            scratch_shapes=[pltpu.SemaphoreType.DMA],
        ),
        out_shape=jax.ShapeDtypeStruct(held.shape, BF16),
        input_output_aliases={3: 0},
        compiler_params=pltpu.CompilerParams(vmem_limit_bytes=LIMIT),
        cost_estimate=cost(SHORT),
        name="store_last",
    )(pos, *came, held, *after)


def first_block(pos, flow, partial):
    parts, rows, width = partial.shape

    def there(i, w):
        way = w[1] if flow == 0 else -w[1]
        return lax.clamp(0, w[0] + way * (parts - 1), parts - 1), 0, 0

    def kernel(pos_ref, p_ref, out_ref):
        out_ref[...] = p_ref[...]

    return pl.pallas_call(
        kernel,
        grid_spec=pltpu.PrefetchScalarGridSpec(
            num_scalar_prefetch=1,
            grid=(1,),
            in_specs=[pl.BlockSpec((None, rows, width), there)],
            out_specs=pl.BlockSpec((rows, width), lambda i, w: (0, 0)),
        ),
        out_shape=jax.ShapeDtypeStruct((rows, width), BF16),
        compiler_params=pltpu.CompilerParams(vmem_limit_bytes=LIMIT),
        cost_estimate=cost(SHORT),
        name="first_block",
    )(pos, partial)


def norm_terms(p_ref, a_ref, b_ref, res_ref, grad_ref, gain_ref, at):
    proj = p_ref[:, at].astype(F32) + a_ref[:, at].astype(F32) + b_ref[:, at].astype(F32)
    z = res_ref[:, at].astype(F32) + proj
    scaled = gain_ref[:, at].astype(F32) * grad_ref[:, at].astype(F32)
    return z, scaled


def norm_specs(ins, half, chunk, at):
    _, rows, wide = ins[0].shape
    whole = pl.BlockSpec((rows, wide), lambda i, r: (0, 0))
    own = pl.BlockSpec((None, rows, half), lambda i, r: (0, chunk, at))
    mine = pl.BlockSpec((None, rows, wide), lambda i, r: (r[0], 0, 0))
    return [mine, whole, whole, own, own, pl.BlockSpec((1, half), lambda i, r: (0, at))]


def norm_sums(pos, ins, half, chunk, at, sums, after):
    rows = ins[0].shape[1]
    cols = divisor(half, 1024)

    def kernel(pos_ref, *refs):
        square_ref, cross_ref = refs[-2:]

        def step(i, sums):
            z, scaled = norm_terms(*refs[:6], pl.ds(pl.multiple_of(i * cols, cols), cols))
            square, cross = sums
            for j in range(0, cols, 128):
                zj = z[:, j : j + 128]
                square = square + zj * zj
                cross = cross + zj * scaled[:, j : j + 128]
            return square, cross

        zero = jnp.zeros((rows, 128), F32)
        start = (zero, zero) if sums is None else (refs[6][...], refs[7][...])
        square_ref[...], cross_ref[...] = lax.fori_loop(0, half // cols, step, start)

    stat = pl.BlockSpec((rows, 128), lambda i, r: (0, 0))
    before = [] if sums is None else list(sums)
    return pl.pallas_call(
        kernel,
        grid_spec=pltpu.PrefetchScalarGridSpec(
            num_scalar_prefetch=1,
            grid=(1,),
            in_specs=norm_specs(ins, half, chunk, at) + [stat] * len(before) + [ANY] * len(after),
            out_specs=[stat, stat],
        ),
        out_shape=[jax.ShapeDtypeStruct((rows, 128), F32)] * 2,
        compiler_params=pltpu.CompilerParams(vmem_limit_bytes=LIMIT),
        cost_estimate=cost(LONG),
        name="norm_sums",
    )(pos, *ins, *before, *after)


def norm_out(pos, ins, half, chunk, sums, proj_out, after):
    parts, rows, wide = ins[0][1][0].shape
    cols = divisor(half, 1024)
    n, width = len(ins), ins[0][1][3].shape[2]
    with_b = proj_out

    def kernel(pos_ref, *refs):
        square_ref, cross_ref = refs[6 * n], refs[6 * n + 1]
        if with_b is None:
            out_ref, held_ref, sem = refs[-3:]
        else:
            out_ref, held_ref, rest_ref, sem = refs[-4:]
        inv = lax.rsqrt(jnp.sum(square_ref[...], axis=-1, keepdims=True) / width + EPS)
        slope = inv * inv * inv * (jnp.sum(cross_ref[...], axis=-1, keepdims=True) / width)
        for j in range(n):
            to_ref = out_ref if j == 0 else rest_ref.at[j - 1]

            def step(i, carry):
                here = pl.ds(pl.multiple_of(i * cols, cols), cols)
                z, scaled = norm_terms(*refs[6 * j : 6 * j + 6], here)
                to_ref[:, here] = (inv * scaled - z * slope).astype(BF16)
                return carry

            lax.fori_loop(0, half // cols, step, 0)
        if with_b is not None:
            p_ref = refs[6 * n + 2]
            b = project_rows(out_ref[:, :half], p_ref[:, :half])
            for j in range(1, n):
                b = b + project_rows(rest_ref[j - 1], p_ref[:, j * half : (j + 1) * half])
            a = sum(refs[j][:, half:].astype(F32) for j in range(3))
            out_ref[:, half:] = (a + spread(b.astype(BF16), b.shape[1])).astype(BF16)
        else:
            out_ref[:, half:] = jnp.zeros((rows, wide - half), BF16)
        own = pltpu.make_async_copy(out_ref, held_ref.at[pos_ref[0]], sem)
        own.start()
        own.wait()

    stat = pl.BlockSpec((rows, 128), lambda i, r: (0, 0))
    specs, args = [], []
    for at, one in ins:
        specs += norm_specs(one, half, chunk, at)
        args += one
    specs, args = specs + [stat, stat], args + list(sums)
    scratch = [pltpu.SemaphoreType.DMA]
    if with_b is not None:
        specs.append(pl.BlockSpec(proj_out.shape, lambda i, r: (0, 0)))
        args.append(proj_out)
        scratch = [pltpu.VMEM((max(1, n - 1), rows, half), BF16)] + scratch
    return pl.pallas_call(
        kernel,
        grid_spec=pltpu.PrefetchScalarGridSpec(
            num_scalar_prefetch=1,
            grid=(1,),
            in_specs=specs + [ANY] * len(after),
            out_specs=[pl.BlockSpec((rows, wide), lambda i, r: (0, 0)), ANY],
            scratch_shapes=scratch,
        ),
        out_shape=[
            jax.ShapeDtypeStruct((rows, wide), BF16),
            jax.ShapeDtypeStruct((parts, rows, wide), BF16),
        ],
        compiler_params=pltpu.CompilerParams(vmem_limit_bytes=LIMIT),
        cost_estimate=cost(SHORT),
        name="norm_out",
    )(pos, *args, *after)


def tie(value, after):
    def kernel(value_ref, *refs):
        refs[-1][...] = value_ref[...]

    whole = pl.BlockSpec(value.shape, lambda i: (0,) * value.ndim)
    return pl.pallas_call(
        kernel,
        grid=(1,),
        in_specs=[whole] + [ANY] * len(after),
        out_specs=whole,
        out_shape=jax.ShapeDtypeStruct(value.shape, value.dtype),
        compiler_params=pltpu.CompilerParams(vmem_limit_bytes=LIMIT),
        cost_estimate=cost(SHORT),
        name="tie",
    )(value, *after)


def touch(x):
    def kernel(x_ref, out_ref):
        out_ref[...] = jnp.zeros_like(out_ref)

    return pl.pallas_call(
        kernel,
        grid=(1,),
        in_specs=[ANY],
        out_specs=TOKEN_SPEC,
        out_shape=TOKEN,
        compiler_params=pltpu.CompilerParams(vmem_limit_bytes=LIMIT),
        cost_estimate=cost(SHORT),
        name="touch",
    )(x)


def from_others(value, axis, size):
    return [value] + [
        lax.ppermute(value, axis, [(d, (d + shift) % size) for d in range(size)])
        for shift in range(1, size)
    ]


def sketch_slice(pos, gathered, segment_ids, kp, after):
    parts, rows, wide = gathered[0].shape
    extra, mine = 2 * kp, kp // parts
    chunks, tokens = len(gathered), segment_ids.shape[1]

    def kernel(pos_ref, *refs):
        out_ref, sum_ref = refs[-2:]
        example = lax.broadcasted_iota(jnp.int32, (8, tokens), 0)
        by_row = jnp.where(refs[chunks][...] == example, 1.0, 0.0).astype(BF16)
        same = lax.broadcasted_iota(jnp.int32, (tokens, tokens), 0) == lax.broadcasted_iota(
            jnp.int32, (tokens, tokens), 1
        )
        weights = project_rows(jnp.where(same, 1.0, 0.0).astype(BF16), by_row)
        weights = weights.reshape(parts, chunks, rows, 8)
        for e in range(EX_DEV):
            total = None
            for c in range(chunks):
                both = refs[c][...].reshape(parts * rows, extra)
                weight = weights[:, c].reshape(parts * rows, 8)[:, e : e + 1]
                part = (both.astype(F32) * weight).astype(BF16)
                term = lax.dot_general(
                    part, both, (((0,), (0,)), ((), ())), preferred_element_type=F32
                )
                total = term if total is None else total + term
            sum_ref[e] = total
        low = lax.broadcasted_iota(jnp.int32, (1, extra), 1) < kp
        for r in range(parts):

            @pl.when(pos_ref[0] == r)
            def _():
                for e in range(EX_DEV):
                    for i in range(mine // 2):
                        at = kp + r * mine + 2 * i
                        left, right = sum_ref[e, at : at + 1, :], sum_ref[e, at + 1 : at + 2, :]
                        out_ref[e : e + 1, i * extra : (i + 1) * extra] = jnp.where(
                            low, left, pltpu.roll(right, kp, 1)
                        )

    return pl.pallas_call(
        kernel,
        grid_spec=pltpu.PrefetchScalarGridSpec(
            num_scalar_prefetch=1,
            grid=(1,),
            in_specs=[pl.BlockSpec((parts, rows, extra), lambda i, w: (0, 0, wide // extra - 1))] * chunks
            + [pl.BlockSpec(segment_ids.shape, lambda i, w: (0, 0))]
            + [ANY] * len(after),
            out_specs=pl.BlockSpec((EX_DEV, mine * kp), lambda i, w: (0, 0)),
            scratch_shapes=[pltpu.VMEM((EX_DEV, extra, extra), F32)],
        ),
        out_shape=jax.ShapeDtypeStruct((EX_DEV, mine * kp), F32),
        compiler_params=pltpu.CompilerParams(vmem_limit_bytes=LIMIT),
        cost_estimate=cost(SHORT),
        name="sketch_slice",
    )(pos, *gathered, segment_ids, *after)


def score_terms(pos, sketches, queries, after):
    size = len(sketches)
    n, depth = queries.shape

    def kernel(pos_ref, *refs):
        out_ref, all_ref = refs[-2:]
        for back in range(size):
            all_ref[lax.rem(pos_ref[3] - back + size, size)] = refs[back][...]
        q = refs[size][...].astype(F32)
        for d in range(size):
            out_ref[d * EX_DEV : (d + 1) * EX_DEV, :] = lax.dot_general(
                all_ref[d],
                q,
                (((1,), (1,)), ((), ())),
                precision=lax.Precision.HIGHEST,
                preferred_element_type=F32,
            )

    return pl.pallas_call(
        kernel,
        grid_spec=pltpu.PrefetchScalarGridSpec(
            num_scalar_prefetch=1,
            grid=(1,),
            in_specs=[pl.BlockSpec((EX_DEV, depth), lambda i, w: (0, 0))] * size
            + [pl.BlockSpec((n, depth), lambda i, w: (0, 0))]
            + [ANY] * len(after),
            out_specs=pl.BlockSpec((size * EX_DEV, n), lambda i, w: (0, 0)),
            scratch_shapes=[pltpu.VMEM((size, EX_DEV, depth), F32)],
        ),
        out_shape=jax.ShapeDtypeStruct((size * EX_DEV, n), F32),
        compiler_params=pltpu.CompilerParams(vmem_limit_bytes=LIMIT),
        cost_estimate=cost(SHORT),
        name="score_terms",
    )(pos, *sketches, queries, *after)


def score_sum(pos, terms, after):
    size = len(terms)
    shape = terms[0].shape

    def kernel(pos_ref, *refs):
        out_ref, all_ref = refs[-2:]
        for back in range(size):
            all_ref[lax.rem(pos_ref[0] - back + size, size)] = refs[back][...]
        total = all_ref[0]
        for d in range(1, size):
            total = total + all_ref[d]
        out_ref[...] = total

    whole = pl.BlockSpec(shape, lambda i, w: (0, 0))
    return pl.pallas_call(
        kernel,
        grid_spec=pltpu.PrefetchScalarGridSpec(
            num_scalar_prefetch=1,
            grid=(1,),
            in_specs=[whole] * size + [ANY] * len(after),
            out_specs=whole,
            scratch_shapes=[pltpu.VMEM((size,) + shape, F32)],
        ),
        out_shape=jax.ShapeDtypeStruct(shape, F32),
        compiler_params=pltpu.CompilerParams(vmem_limit_bytes=LIMIT),
        cost_estimate=cost(SHORT),
        name="score_sum",
    )(pos, *terms, *after)


def body(inputs, residual, out_grad, norm_gain, w_out, proj_in, proj_out, queries, segment_ids):
    parts = lax.axis_size("tensor")
    rank = lax.axis_index("tensor")
    queriers = lax.axis_size("query")
    q_rank = lax.axis_index("query")
    tokens = inputs.shape[1]
    share = tokens // parts
    chunks = max(1, min(CHUNKS, share // 16))
    rows = share // chunks
    by_share = inputs.reshape(parts, chunks, rows, inputs.shape[2])
    gain = norm_gain.reshape(1, -1)
    half = w_out.shape[1] // HALVES
    kp = proj_out.shape[0]

    up = 1 - 2 * lax.rem(q_rank, 2)
    pos = jnp.stack([rank, up, jnp.where(up == 1, rank, parts - 1 - rank), q_rank]).astype(jnp.int32)

    def pairs(flow, low, high):
        out = []
        for q in range(queriers):
            way = 1 if (q % 2 == 0) == (flow == 0) else -1
            for t in range(parts):
                spot = t if way == 1 else parts - 1 - t
                if low <= spot <= min(high, parts - 2):
                    out.append((t * queriers + q, (t + way) * queriers + q))
        return out

    work, marks = [], []
    partials, totals, result = {}, {}, [None]

    def forward(c, h, piece, pieces, after):
        partials[c, h], mark = forward_piece(
            by_share,
            w_out,
            c,
            HALVES,
            h,
            2 * kp,
            piece,
            pieces,
            partials.get((c, h)),
            after,
        )
        if h == 0 and piece == pieces - 1:
            partials[c, h] = forward_extra(by_share, proj_in, c, partials[c, h], [mark])
        return mark

    def backward(c, blocks, total, last, piece, pieces, after):
        held = result[0] if last else totals.get(c)
        done, mark = backward_piece(
            blocks, w_out, c, chunks, HALVES, piece, pieces, total, last, held, after
        )
        if last:
            result[0] = done
        else:
            totals[c] = done
        return mark

    def do_one(after, touching=False):
        if work:
            marks[:] = [work.pop(0)[1](after)]
        elif touching:
            marks[:] = [touch(after[0])]

    def finish(key, after):
        while any(k == key for k, _ in work):
            do_one(list(marks) + after)

    def add_forward(c, h, pieces):
        for piece in range(pieces):
            work.append(((c, h), functools.partial(forward, c, h, piece, pieces)))

    add_forward(0, 0, 1)
    finish((0, 0), [])
    gathered = []
    for slot in range(chunks + 1):
        rs, ag = slot < chunks, slot > 0
        came, held, sent, before = {}, {}, {}, None
        if ag:
            ins = [
                [partials[slot - 1, h], arrived[h, 0], arrived[h, 1], residual, out_grad, gain]
                for h in range(HALVES)
            ]
            sums = None
            for h in range(HALVES):
                sums = norm_sums(pos, ins[h], half, slot - 1, h, sums, list(marks))
            grad = [None] * HALVES
            grad[0], held[0] = norm_out(
                pos, list(enumerate(ins)), half, slot - 1, sums, proj_out, []
            )
        for k in range(parts):
            gather_now, reduce_now = ag and k <= parts - 2, rs and k >= 1
            if not gather_now and not reduce_now:
                continue
            for h in range(HALVES):
                if k == 0 and h > 0:
                    if rs and slot > 1:
                        add_forward(slot, h, PIECES)
                    do_one([sent[h - 1, 1]])
                    grad[h], held[h] = norm_out(
                        pos, [(h, ins[h])], half, slot - 1, sums, None, list(marks)
                    )
                if reduce_now:
                    if slot == 0 and k == 1 and h > 0:
                        add_forward(0, h, 1)
                        do_one([sent[h - 1, 1]])
                    finish((slot, h), [sent[h - 1, 1]] if h > 0 else [])
                for flow in range(2):
                    if k == 0:
                        x = before = grad[h]
                    elif (h, flow) not in came:
                        x = first_block(pos, flow, partials[slot, h])
                    else:
                        x, held[h] = relay(
                            pos,
                            flow,
                            k,
                            partials[slot, h] if reduce_now else None,
                            came[h, flow],
                            held.get(h),
                            list(marks) + ([] if before is None else [before]),
                        )
                        before = x
                    came[h, flow] = lax.ppermute(
                        x,
                        ("tensor", "query"),
                        pairs(flow, 0 if reduce_now else k, parts - 2 if gather_now else k - 1),
                    )
                    sent[h, flow] = x
                    if slot == 0 and k == 2 and (h, flow) == (HALVES - 1, 1) and chunks > 1 and HALVES > 1:
                        add_forward(1, 1, PIECES)
                        do_one([x])
                        continue
                    if slot == 0 and k == parts - 1 and (h, flow) == (HALVES - 1, 1) and chunks > 1:
                        work.insert(0, ((1, 0), functools.partial(forward, 1, 0, 0, 1)))
                    if slot == 0 and work and work[0][0] == (1, 1):
                        continue
                    if k > 0 and (slot > 0 or k > 1) and not (slot == 1 and work and k == 1 and flow == 0):
                        do_one([x], slot == chunks)
                if k == 0 and slot == chunks and h == HALVES - 1:
                    marks[:] = [touch(sent[h, 1])]
        if ag:
            if slot + 1 < chunks:
                add_forward(slot + 1, 0, PIECES)
            if rs:
                blocks = [(h, held[h]) for h in range(HALVES)]
                for piece in range(PIECES):
                    work.append(
                        (
                            ("b", slot - 1),
                            functools.partial(backward, slot - 1, blocks, None, True, piece, PIECES),
                        )
                    )
            else:
                while work:
                    do_one(list(marks))
                marks[:] = [touch(came[0, 0])]
                held[0] = store_last(pos, (came[0, 0], came[0, 1]), held[0], list(marks))
            gathered.append(held[0])
        arrived = came
    last = chunks - 1
    sketch = sketch_slice(pos, gathered, segment_ids, kp, [])
    marks[:] = [backward(last, [(0, held[0])], None, HALVES == 1, 0, 1, [sketch])]
    for h in range(1, HALVES):
        marks[:] = [tie(marks[0], [came[h, 0]])]
        held[h] = store_last(pos, (came[h, 0], came[h, 1]), held[h], list(marks))
    terms = score_terms(pos, from_others(sketch, "query", queriers), queries, list(marks))
    for h in range(1, HALVES):
        marks[:] = [backward(last, [(h, held[h])], totals.get(last), h == HALVES - 1, 0, 1, [terms])]
    scores = score_sum(pos, from_others(terms, "tensor", parts), list(marks))
    return (result[0].reshape(1, tokens, -1), scores)


def solution(mesh):
    return jax.shard_map(
        body,
        mesh=mesh,
        in_specs=(
            P(("groups", "dp", "query"), None, "tensor"),
            P(("groups", "dp", "query"), "tensor", None),
            P(("groups", "dp", "query"), "tensor", None),
            P(),
            P("tensor", None),
            P(None, "tensor"),
            P(),
            P("query", "tensor"),
            P(("groups", "dp", "query"), None),
        ),
        out_specs=(P(("groups", "dp", "query"), None, "tensor"), P(("groups", "dp"), "query")),
        check_vma=False,
    )
```

```python
import functools

import jax
import jax.numpy as jnp
from jax import lax
from jax.experimental import pallas as pl
from jax.experimental.pallas import tpu as pltpu
from jax.sharding import PartitionSpec as P

EX_DEV = 4
EPS = 1e-05
CHUNKS = 2
HALVES = 2
PIECES = 2
SPLIT = 4
SHORT, LONG = 0.2, 5.0
SMALL, LIMIT = 6 * 1024 * 1024, 14 * 1024 * 1024
QUARTERS = 4

F32, BF16 = jnp.float32, jnp.bfloat16
ANY = pl.BlockSpec(memory_space=pl.ANY)
TOKEN = jax.ShapeDtypeStruct((8, 128), F32)
TOKEN_SPEC = pl.BlockSpec((8, 128), lambda *_: (0, 0))


def divisor(total, wanted):
    size = min(total, wanted)
    while total % size:
        size //= 2
    return size


def cost(microseconds):
    return pl.CostEstimate(flops=0, bytes_accessed=int(microseconds * 3.6e6), transcendentals=0)


def in_hbm(x):
    return pltpu.with_memory_space_constraint(x, pltpu.HBM)


def project_rows(values, matrix):
    return lax.dot_general(
        values, matrix, (((1,), (1,)), ((), ())), preferred_element_type=F32
    )


def spread(values, first):
    k = values.shape[1]
    row = lax.broadcasted_iota(jnp.int32, (k, 2 * k), 0)
    col = lax.broadcasted_iota(jnp.int32, (k, 2 * k), 1)
    return jnp.dot(values, jnp.where(col == row + first, 1.0, 0.0).astype(BF16), preferred_element_type=F32)


def forward_extra(by_share, proj_in, chunk, held, after):
    parts, _, rows, depth = by_share.shape
    extra = 2 * proj_in.shape[0]
    at = held.shape[2] // extra - 1

    def kernel(x_ref, p_ref, *refs):
        part = project_rows(x_ref[...].reshape(parts * rows, depth), p_ref[...]).astype(BF16)
        refs[-1][...] = spread(part, 0).astype(BF16).reshape(parts, rows, extra)

    return pl.pallas_call(
        kernel,
        grid=(1,),
        in_specs=[
            pl.BlockSpec((parts, None, rows, depth), lambda i: (0, chunk, 0, 0)),
            pl.BlockSpec(proj_in.shape, lambda i: (0, 0)),
        ]
        + [ANY] * (1 + len(after)),
        out_specs=pl.BlockSpec((parts, rows, extra), lambda i: (0, 0, at)),
        out_shape=jax.ShapeDtypeStruct(held.shape, BF16),
        input_output_aliases={2: 0},
        compiler_params=pltpu.CompilerParams(vmem_limit_bytes=LIMIT),
        cost_estimate=cost(SHORT),
        name="forward_extra",
    )(by_share, proj_in, held, *after)


def forward_piece(by_share, w_out, chunk, halves, half_at, extra, piece, pieces, held, after):
    parts, _, rows, depth = by_share.shape
    half = w_out.shape[1] // halves
    span = half // pieces
    cols = divisor(span, 512)
    steps = span // cols
    base = (half_at * half + piece * span) // cols
    cut = depth // SPLIT

    def kernel(x_ref, *refs):
        out_ref, tok_ref = refs[-2:]
        x = x_ref[...].reshape(parts * rows, depth)
        y = None
        for s in range(SPLIT):
            term = jnp.dot(x[:, s * cut : (s + 1) * cut], refs[s][...], preferred_element_type=F32)
            y = term if y is None else y + term
        out_ref[...] = y.astype(BF16).reshape(parts, rows, cols)
        tok_ref[...] = jnp.zeros_like(tok_ref)

    more = ([] if held is None else [held]) + after
    return pl.pallas_call(
        kernel,
        grid=(steps,),
        in_specs=[pl.BlockSpec((parts, None, rows, depth), lambda i: (0, chunk, 0, 0))]
        + [pl.BlockSpec((cut, cols), lambda i, s=s: (s, base + i)) for s in range(SPLIT)]
        + [ANY] * len(more),
        out_specs=[
            pl.BlockSpec((parts, rows, cols), lambda i: (0, 0, piece * steps + i)),
            TOKEN_SPEC,
        ],
        out_shape=[jax.ShapeDtypeStruct((parts, rows, half + extra), BF16), TOKEN],
        input_output_aliases={} if held is None else {1 + SPLIT: 0},
        compiler_params=pltpu.CompilerParams(vmem_limit_bytes=LIMIT),
        cost_estimate=cost(SHORT),
        name="forward_piece",
    )(by_share, *([in_hbm(w_out)] * SPLIT), *more)


def load_weights(w_out, piece, pieces, after):
    rows = w_out.shape[0] // pieces
    width = w_out.shape[1]

    def kernel(w_ref, *refs):
        out_ref, sem = refs[-2:]
        copy = pltpu.make_async_copy(w_ref.at[pl.ds(piece * rows, rows)], out_ref, sem)
        copy.start()
        copy.wait()

    return pl.pallas_call(
        kernel,
        in_specs=[ANY] * (1 + len(after)),
        out_specs=pl.BlockSpec(memory_space=pltpu.VMEM),
        out_shape=pltpu.VMEM((rows, width), BF16),
        scratch_shapes=[pltpu.SemaphoreType.DMA],
        compiler_params=pltpu.CompilerParams(vmem_limit_bytes=SMALL),
        cost_estimate=cost(SHORT),
        name="load_weights",
    )(in_hbm(w_out), *after)


def backward_piece(blocks, weights, chunk, chunks, halves, piece, pieces, total, last, held, after):
    parts, rows, _ = blocks[0][1].shape
    some, width = weights[0].shape
    half, span = width // halves, some * len(weights)
    cols = divisor(some, 256)
    n, m = len(blocks), len(weights)

    def kernel(*refs):
        out_ref, tok_ref = refs[-2:]
        for j in range(m):

            def step(i, carry):
                here = pl.ds(pl.multiple_of(i * cols, cols), cols)
                there = pl.ds(pl.multiple_of(j * some + i * cols, cols), cols)
                y = None if total is None else refs[n + m][:, :, there].reshape(parts * rows, cols)
                for b, (at, _) in enumerate(blocks):
                    g = refs[b][...].reshape(parts * rows, half)
                    term = project_rows(g, refs[n + j][here, at * half : (at + 1) * half])
                    y = term if y is None else y + term
                out_ref[:, :, there] = y.astype(out_ref.dtype).reshape(parts, rows, cols)
                return carry

            lax.fori_loop(0, some // cols, step, 0)
        tok_ref[...] = jnp.zeros_like(tok_ref)

    once = pl.Buffered(1)
    here = pl.BlockSpec((parts, rows, span), lambda i: (0, 0, piece))
    if last:
        out_spec = pl.BlockSpec((parts, None, rows, span), lambda i: (0, chunk, 0, piece))
        out_shape = jax.ShapeDtypeStruct((parts, chunks, rows, span * pieces), BF16)
    else:
        out_spec, out_shape = here, jax.ShapeDtypeStruct((parts, rows, span * pieces), F32)
    sums = [] if total is None else [total]
    extra = ([] if held is None else [held]) + after
    return pl.pallas_call(
        kernel,
        grid=(1,),
        in_specs=[pl.BlockSpec((parts, rows, half), lambda i: (0, 0, 0), pipeline_mode=once)] * n
        + [pl.BlockSpec(memory_space=pltpu.VMEM)] * m
        + [pl.BlockSpec((parts, rows, span), lambda i: (0, 0, piece), pipeline_mode=once)] * len(sums)
        + [ANY] * len(extra),
        out_specs=[out_spec, TOKEN_SPEC],
        out_shape=[out_shape, TOKEN],
        input_output_aliases={} if held is None else {n + m + len(sums): 0},
        compiler_params=pltpu.CompilerParams(vmem_limit_bytes=LIMIT),
        cost_estimate=cost(SHORT),
        name="backward_piece",
    )(
        *[g for _, g in blocks],
        *[pltpu.with_memory_space_constraint(w, pltpu.VMEM) for w in weights],
        *sums,
        *extra,
    )


def relay(pos, flow, k, partial, came, held, after):
    rows, width = came.shape
    parts = (partial if held is None else held).shape[0]
    n_in = 1 + (partial is not None) + (held is not None) + len(after)

    def far(pos_ref, steps):
        way = pos_ref[1] if flow == 0 else -pos_ref[1]
        return lax.clamp(0, pos_ref[0] + way * steps, parts - 1)

    def kernel(pos_ref, *refs):
        came_ref, x_ref = refs[0], refs[n_in]
        place = pos_ref[2] if flow == 0 else parts - 1 - pos_ref[2]
        if held is not None:
            store = pltpu.make_async_copy(came_ref, refs[n_in + 1].at[far(pos_ref, -k)], refs[-1])
            pl.when(place >= k)(store.start)
        if partial is not None:

            @pl.when(place < k)
            def _():
                x_ref[...] = (came_ref[...].astype(F32) + refs[1][...].astype(F32)).astype(BF16)

            @pl.when(place >= k)
            def _():
                x_ref[...] = came_ref[...]

        else:
            x_ref[...] = came_ref[...]
        if held is not None:
            pl.when(place >= k)(store.wait)

    line = jax.ShapeDtypeStruct((rows, width), BF16)
    whole = pl.BlockSpec((rows, width), lambda i, w: (0, 0), pipeline_mode=pl.Buffered(1))
    args, specs, out_specs, out_shape, alias = [came], [whole], [whole], [line], {}
    if partial is not None:
        term = pl.BlockSpec(
            (None, rows, width),
            lambda i, w: (far(w, parts - k), 0, 0),
            pipeline_mode=pl.Buffered(1),
        )
        specs.append(term)
        args.append(partial)
    if held is not None:
        alias[1 + len(args)] = 1
        specs.append(ANY)
        args.append(held)
        out_specs.append(ANY)
        out_shape.append(jax.ShapeDtypeStruct(held.shape, BF16))
    outs = pl.pallas_call(
        kernel,
        grid_spec=pltpu.PrefetchScalarGridSpec(
            num_scalar_prefetch=1,
            grid=(1,),
            in_specs=specs + [ANY] * len(after),
            out_specs=out_specs,
            scratch_shapes=[pltpu.SemaphoreType.DMA] if held is not None else [],
        ),
        out_shape=out_shape,
        input_output_aliases=alias,
        compiler_params=pltpu.CompilerParams(vmem_limit_bytes=SMALL),
        cost_estimate=cost(LONG),
        name="relay",
    )(pos, *args, *after)
    return outs[0], (outs[1] if held is not None else None)


def store_last(pos, came, held, after):
    parts = held.shape[0]

    def kernel(pos_ref, a_ref, b_ref, *refs):
        out_ref, sem = refs[-2:]
        rank, way, place = pos_ref[0], pos_ref[1], pos_ref[2]
        ends = (
            (place == parts - 1, a_ref, rank - way * (parts - 1)),
            (place == 0, b_ref, rank + way * (parts - 1)),
        )
        for at_end, came_ref, at in ends:
            copy = pltpu.make_async_copy(came_ref, out_ref.at[lax.clamp(0, at, parts - 1)], sem)

            @pl.when(at_end)
            def _():
                copy.start()
                copy.wait()

    return pl.pallas_call(
        kernel,
        grid_spec=pltpu.PrefetchScalarGridSpec(
            num_scalar_prefetch=1,
            grid=(1,),
            in_specs=[pl.BlockSpec(held.shape[1:], lambda i, w: (0, 0))] * 2 + [ANY] * (1 + len(after)),
            out_specs=ANY,
            scratch_shapes=[pltpu.SemaphoreType.DMA],
        ),
        out_shape=jax.ShapeDtypeStruct(held.shape, BF16),
        input_output_aliases={3: 0},
        compiler_params=pltpu.CompilerParams(vmem_limit_bytes=SMALL),
        cost_estimate=cost(SHORT),
        name="store_last",
    )(pos, *came, held, *after)


def first_block(pos, flow, partial):
    parts, rows, width = partial.shape

    def there(i, w):
        way = w[1] if flow == 0 else -w[1]
        return lax.clamp(0, w[0] + way * (parts - 1), parts - 1), 0, 0

    def kernel(pos_ref, p_ref, out_ref):
        out_ref[...] = p_ref[...]

    return pl.pallas_call(
        kernel,
        grid_spec=pltpu.PrefetchScalarGridSpec(
            num_scalar_prefetch=1,
            grid=(1,),
            in_specs=[pl.BlockSpec((None, rows, width), there)],
            out_specs=pl.BlockSpec((rows, width), lambda i, w: (0, 0)),
        ),
        out_shape=jax.ShapeDtypeStruct((rows, width), BF16),
        compiler_params=pltpu.CompilerParams(vmem_limit_bytes=SMALL),
        cost_estimate=cost(SHORT),
        name="first_block",
    )(pos, partial)


def norm_terms(p_ref, a_ref, b_ref, res_ref, grad_ref, gain_ref, at):
    proj = p_ref[:, at].astype(F32) + a_ref[:, at].astype(F32) + b_ref[:, at].astype(F32)
    z = res_ref[:, at].astype(F32) + proj
    scaled = gain_ref[:, at].astype(F32) * grad_ref[:, at].astype(F32)
    return z, scaled


def norm_specs(ins, half, chunk, at):
    _, rows, wide = ins[0].shape
    once = pl.Buffered(1)
    whole = pl.BlockSpec((rows, wide), lambda i, r: (0, 0), pipeline_mode=once)
    own = pl.BlockSpec((None, rows, half), lambda i, r: (0, chunk, at), pipeline_mode=once)
    mine = pl.BlockSpec((None, rows, wide), lambda i, r: (r[0], 0, 0), pipeline_mode=once)
    return [mine, whole, whole, own, own, pl.BlockSpec((1, half), lambda i, r: (0, at))]


def norm_sums(pos, ins, half, chunk, at, sums, after):
    rows = ins[0].shape[1]
    cols = divisor(half, 1024)

    def kernel(pos_ref, *refs):
        square_ref, cross_ref = refs[-2:]

        def step(i, sums):
            z, scaled = norm_terms(*refs[:6], pl.ds(pl.multiple_of(i * cols, cols), cols))
            square, cross = sums
            for j in range(0, cols, 128):
                zj = z[:, j : j + 128]
                square = square + zj * zj
                cross = cross + zj * scaled[:, j : j + 128]
            return square, cross

        zero = jnp.zeros((rows, 128), F32)
        start = (zero, zero) if sums is None else (refs[6][...], refs[7][...])
        square_ref[...], cross_ref[...] = lax.fori_loop(0, half // cols, step, start)

    stat = pl.BlockSpec((rows, 128), lambda i, r: (0, 0))
    before = [] if sums is None else list(sums)
    return pl.pallas_call(
        kernel,
        grid_spec=pltpu.PrefetchScalarGridSpec(
            num_scalar_prefetch=1,
            grid=(1,),
            in_specs=norm_specs(ins, half, chunk, at) + [stat] * len(before) + [ANY] * len(after),
            out_specs=[stat, stat],
        ),
        out_shape=[jax.ShapeDtypeStruct((rows, 128), F32)] * 2,
        compiler_params=pltpu.CompilerParams(vmem_limit_bytes=LIMIT),
        cost_estimate=cost(LONG),
        name="norm_sums",
    )(pos, *ins, *before, *after)


def norm_out(pos, ins, half, chunk, sums, proj_out, after):
    parts, rows, wide = ins[0][1][0].shape
    cols = divisor(half, 1024)
    n, width = len(ins), ins[0][1][3].shape[2]
    with_b = proj_out

    def kernel(pos_ref, *refs):
        square_ref, cross_ref = refs[6 * n], refs[6 * n + 1]
        if with_b is None:
            out_ref, held_ref, sem = refs[-3:]
        else:
            out_ref, held_ref, rest_ref, sem = refs[-4:]
        inv = lax.rsqrt(jnp.sum(square_ref[...], axis=-1, keepdims=True) / width + EPS)
        slope = inv * inv * inv * (jnp.sum(cross_ref[...], axis=-1, keepdims=True) / width)
        for j in range(n):
            to_ref = out_ref if j == 0 else rest_ref.at[j - 1]

            def step(i, carry):
                here = pl.ds(pl.multiple_of(i * cols, cols), cols)
                z, scaled = norm_terms(*refs[6 * j : 6 * j + 6], here)
                to_ref[:, here] = (inv * scaled - z * slope).astype(BF16)
                return carry

            lax.fori_loop(0, half // cols, step, 0)
        if with_b is not None:
            p_ref = refs[6 * n + 2]
            b = project_rows(out_ref[:, :half], p_ref[:, :half])
            for j in range(1, n):
                b = b + project_rows(rest_ref[j - 1], p_ref[:, j * half : (j + 1) * half])
            a = sum(refs[j][:, half:].astype(F32) for j in range(3))
            out_ref[:, half:] = (a + spread(b.astype(BF16), b.shape[1])).astype(BF16)
        else:
            out_ref[:, half:] = jnp.zeros((rows, wide - half), BF16)
        own = pltpu.make_async_copy(out_ref, held_ref.at[pos_ref[0]], sem)
        own.start()
        own.wait()

    stat = pl.BlockSpec((rows, 128), lambda i, r: (0, 0))
    specs, args = [], []
    for at, one in ins:
        specs += norm_specs(one, half, chunk, at)
        args += one
    specs, args = specs + [stat, stat], args + list(sums)
    scratch = [pltpu.SemaphoreType.DMA]
    if with_b is not None:
        specs.append(pl.BlockSpec(proj_out.shape, lambda i, r: (0, 0)))
        args.append(proj_out)
        scratch = [pltpu.VMEM((max(1, n - 1), rows, half), BF16)] + scratch
    return pl.pallas_call(
        kernel,
        grid_spec=pltpu.PrefetchScalarGridSpec(
            num_scalar_prefetch=1,
            grid=(1,),
            in_specs=specs + [ANY] * len(after),
            out_specs=[pl.BlockSpec((rows, wide), lambda i, r: (0, 0)), ANY],
            scratch_shapes=scratch,
        ),
        out_shape=[
            jax.ShapeDtypeStruct((rows, wide), BF16),
            jax.ShapeDtypeStruct((parts, rows, wide), BF16),
        ],
        compiler_params=pltpu.CompilerParams(vmem_limit_bytes=LIMIT),
        cost_estimate=cost(SHORT),
        name="norm_out",
    )(pos, *args, *after)


def tie(value, after):
    def kernel(value_ref, *refs):
        refs[-1][...] = value_ref[...]

    whole = pl.BlockSpec(value.shape, lambda i: (0,) * value.ndim)
    return pl.pallas_call(
        kernel,
        grid=(1,),
        in_specs=[whole] + [ANY] * len(after),
        out_specs=whole,
        out_shape=jax.ShapeDtypeStruct(value.shape, value.dtype),
        compiler_params=pltpu.CompilerParams(vmem_limit_bytes=SMALL),
        cost_estimate=cost(SHORT),
        name="tie",
    )(value, *after)


def touch(x):
    def kernel(x_ref, out_ref):
        out_ref[...] = jnp.zeros_like(out_ref)

    return pl.pallas_call(
        kernel,
        grid=(1,),
        in_specs=[ANY],
        out_specs=TOKEN_SPEC,
        out_shape=TOKEN,
        compiler_params=pltpu.CompilerParams(vmem_limit_bytes=SMALL),
        cost_estimate=cost(SHORT),
        name="touch",
    )(x)


def from_others(value, axis, size):
    return [value] + [
        lax.ppermute(value, axis, [(d, (d + shift) % size) for d in range(size)])
        for shift in range(1, size)
    ]


def sketch_slice(pos, gathered, segment_ids, kp, after):
    parts, rows, wide = gathered[0].shape
    extra, mine = 2 * kp, kp // parts
    chunks, tokens = len(gathered), segment_ids.shape[1]

    def kernel(pos_ref, *refs):
        out_ref, sum_ref = refs[-2:]
        example = lax.broadcasted_iota(jnp.int32, (8, tokens), 0)
        by_row = jnp.where(refs[chunks][...] == example, 1.0, 0.0).astype(BF16)
        same = lax.broadcasted_iota(jnp.int32, (tokens, tokens), 0) == lax.broadcasted_iota(
            jnp.int32, (tokens, tokens), 1
        )
        weights = project_rows(jnp.where(same, 1.0, 0.0).astype(BF16), by_row)
        weights = weights.reshape(parts, chunks, rows, 8)
        for e in range(EX_DEV):
            total = None
            for c in range(chunks):
                both = refs[c][...].reshape(parts * rows, extra)
                weight = weights[:, c].reshape(parts * rows, 8)[:, e : e + 1]
                part = (both.astype(F32) * weight).astype(BF16)
                term = lax.dot_general(
                    part, both, (((0,), (0,)), ((), ())), preferred_element_type=F32
                )
                total = term if total is None else total + term
            sum_ref[e] = total
        low = lax.broadcasted_iota(jnp.int32, (1, extra), 1) < kp
        for r in range(parts):

            @pl.when(pos_ref[0] == r)
            def _():
                for e in range(EX_DEV):
                    for i in range(mine // 2):
                        at = kp + r * mine + 2 * i
                        left, right = sum_ref[e, at : at + 1, :], sum_ref[e, at + 1 : at + 2, :]
                        out_ref[e : e + 1, i * extra : (i + 1) * extra] = jnp.where(
                            low, left, pltpu.roll(right, kp, 1)
                        )

    return pl.pallas_call(
        kernel,
        grid_spec=pltpu.PrefetchScalarGridSpec(
            num_scalar_prefetch=1,
            grid=(1,),
            in_specs=[pl.BlockSpec((parts, rows, extra), lambda i, w: (0, 0, wide // extra - 1))] * chunks
            + [pl.BlockSpec(segment_ids.shape, lambda i, w: (0, 0))]
            + [ANY] * len(after),
            out_specs=pl.BlockSpec((EX_DEV, mine * kp), lambda i, w: (0, 0)),
            scratch_shapes=[pltpu.VMEM((EX_DEV, extra, extra), F32)],
        ),
        out_shape=jax.ShapeDtypeStruct((EX_DEV, mine * kp), F32),
        compiler_params=pltpu.CompilerParams(vmem_limit_bytes=LIMIT),
        cost_estimate=cost(SHORT),
        name="sketch_slice",
    )(pos, *gathered, segment_ids, *after)


def score_terms(pos, sketches, queries, after):
    size = len(sketches)
    n, depth = queries.shape

    def kernel(pos_ref, *refs):
        out_ref, all_ref = refs[-2:]
        for back in range(size):
            all_ref[lax.rem(pos_ref[3] - back + size, size)] = refs[back][...]
        for d in range(size):
            rest, total = all_ref[d], None
            for _ in range(3):
                part = rest.astype(BF16)
                rest = rest - part.astype(F32)
                term = project_rows(part, refs[size][...])
                total = term if total is None else total + term
            out_ref[d * EX_DEV : (d + 1) * EX_DEV, :] = total

    return pl.pallas_call(
        kernel,
        grid_spec=pltpu.PrefetchScalarGridSpec(
            num_scalar_prefetch=1,
            grid=(1,),
            in_specs=[pl.BlockSpec((EX_DEV, depth), lambda i, w: (0, 0))] * size
            + [pl.BlockSpec((n, depth), lambda i, w: (0, 0))]
            + [ANY] * len(after),
            out_specs=pl.BlockSpec((size * EX_DEV, n), lambda i, w: (0, 0)),
            scratch_shapes=[pltpu.VMEM((size, EX_DEV, depth), F32)],
        ),
        out_shape=jax.ShapeDtypeStruct((size * EX_DEV, n), F32),
        compiler_params=pltpu.CompilerParams(vmem_limit_bytes=LIMIT),
        cost_estimate=cost(SHORT),
        name="score_terms",
    )(pos, *sketches, queries, *after)


def score_sum(pos, terms, after):
    size = len(terms)
    shape = terms[0].shape

    def kernel(pos_ref, *refs):
        out_ref, all_ref = refs[-2:]
        for back in range(size):
            all_ref[lax.rem(pos_ref[0] - back + size, size)] = refs[back][...]
        total = all_ref[0]
        for d in range(1, size):
            total = total + all_ref[d]
        out_ref[...] = total

    whole = pl.BlockSpec(shape, lambda i, w: (0, 0))
    return pl.pallas_call(
        kernel,
        grid_spec=pltpu.PrefetchScalarGridSpec(
            num_scalar_prefetch=1,
            grid=(1,),
            in_specs=[whole] * size + [ANY] * len(after),
            out_specs=whole,
            scratch_shapes=[pltpu.VMEM((size,) + shape, F32)],
        ),
        out_shape=jax.ShapeDtypeStruct(shape, F32),
        compiler_params=pltpu.CompilerParams(vmem_limit_bytes=SMALL),
        cost_estimate=cost(SHORT),
        name="score_sum",
    )(pos, *terms, *after)


def body(inputs, residual, out_grad, norm_gain, w_out, proj_in, proj_out, queries, segment_ids):
    parts = lax.axis_size("tensor")
    rank = lax.axis_index("tensor")
    queriers = lax.axis_size("query")
    q_rank = lax.axis_index("query")
    tokens = inputs.shape[1]
    share = tokens // parts
    chunks = max(1, min(CHUNKS, share // 16))
    rows = share // chunks
    by_share = inputs.reshape(parts, chunks, rows, inputs.shape[2])
    gain = norm_gain.reshape(1, -1)
    half = w_out.shape[1] // HALVES
    kp = proj_out.shape[0]

    up = 1 - 2 * lax.rem(q_rank, 2)
    pos = jnp.stack([rank, up, jnp.where(up == 1, rank, parts - 1 - rank), q_rank]).astype(jnp.int32)

    def pairs(flow, low, high):
        out = []
        for q in range(queriers):
            way = 1 if (q % 2 == 0) == (flow == 0) else -1
            for t in range(parts):
                spot = t if way == 1 else parts - 1 - t
                if low <= spot <= min(high, parts - 2):
                    out.append((t * queriers + q, (t + way) * queriers + q))
        return out

    work, marks, resident = [], [], []
    partials, totals, result = {}, {}, [None]

    def forward(c, h, piece, pieces, after):
        partials[c, h], mark = forward_piece(
            by_share,
            w_out,
            c,
            HALVES,
            h,
            2 * kp,
            piece,
            pieces,
            partials.get((c, h)),
            after,
        )
        if h == 0 and piece == pieces - 1:
            partials[c, h] = forward_extra(by_share, proj_in, c, partials[c, h], [mark])
        return mark

    def backward(c, blocks, total, last, piece, pieces, after):
        held = result[0] if last else totals.get(c)
        some = resident[piece * QUARTERS // pieces : (piece + 1) * QUARTERS // pieces]
        done, mark = backward_piece(
            blocks, some, c, chunks, HALVES, piece, pieces, total, last, held, after
        )
        if last:
            result[0] = done
        else:
            totals[c] = done
        return mark

    def do_one(after, touching=False):
        if work:
            marks[:] = [work.pop(0)[1](after)]
        elif touching:
            marks[:] = [touch(after[0])]

    def finish(key, after):
        while any(k == key for k, _ in work):
            do_one(list(marks) + after)

    def load(count, after):
        for _ in range(count):
            resident.append(load_weights(w_out, len(resident), QUARTERS, after))
            after = [resident[-1]]
        marks[:] = after

    def add_forward(c, h, pieces):
        for piece in range(pieces):
            work.append(((c, h), functools.partial(forward, c, h, piece, pieces)))

    add_forward(0, 0, 1)
    finish((0, 0), [])
    gathered = []
    for slot in range(chunks + 1):
        rs, ag = slot < chunks, slot > 0
        came, held, sent, before = {}, {}, {}, None
        if ag:
            ins = [
                [partials[slot - 1, h], arrived[h, 0], arrived[h, 1], residual, out_grad, gain]
                for h in range(HALVES)
            ]
            sums = None
            for h in range(HALVES):
                sums = norm_sums(pos, ins[h], half, slot - 1, h, sums, list(marks))
            grad = [None] * HALVES
            grad[0], held[0] = norm_out(
                pos, list(enumerate(ins)), half, slot - 1, sums, proj_out, []
            )
        for k in range(parts):
            gather_now, reduce_now = ag and k <= parts - 2, rs and k >= 1
            if not gather_now and not reduce_now:
                continue
            for h in range(HALVES):
                if k == 0 and h > 0:
                    if rs and slot > 1:
                        add_forward(slot, h, PIECES)
                    do_one([sent[h - 1, 1]])
                    if not rs:
                        finish(("b", slot - 2), [])
                    grad[h], held[h] = norm_out(
                        pos, [(h, ins[h])], half, slot - 1, sums, None, list(marks)
                    )
                if reduce_now:
                    if slot == 0 and k == 1 and h > 0:
                        add_forward(0, h, 1)
                        do_one([sent[h - 1, 1]])
                    finish((slot, h), [sent[h - 1, 1]] if h > 0 else [])
                for flow in range(2):
                    if k == 0:
                        x = before = grad[h]
                    elif (h, flow) not in came:
                        x = first_block(pos, flow, partials[slot, h])
                    else:
                        x, held[h] = relay(
                            pos,
                            flow,
                            k,
                            partials[slot, h] if reduce_now else None,
                            came[h, flow],
                            held.get(h),
                            list(marks) + ([] if before is None else [before]),
                        )
                        before = x
                    came[h, flow] = lax.ppermute(
                        x,
                        ("tensor", "query"),
                        pairs(flow, 0 if reduce_now else k, parts - 2 if gather_now else k - 1),
                    )
                    sent[h, flow] = x
                    if slot == chunks - 1 and flow == 1 and slot > 0:
                        if (k, h) in ((parts - 2, HALVES - 1), (parts - 1, 0)):
                            load(1, [x])
                            continue
                        if (k, h) == (parts - 1, HALVES - 1):
                            load(QUARTERS - len(resident), [x])
                            continue
                    if slot == 0 and k == 2 and (h, flow) == (HALVES - 1, 1) and chunks > 1 and HALVES > 1:
                        add_forward(1, 1, PIECES)
                        do_one([x])
                        continue
                    if slot == 0 and k == parts - 1 and (h, flow) == (HALVES - 1, 1) and chunks > 1:
                        work.insert(0, ((1, 0), functools.partial(forward, 1, 0, 0, 1)))
                    if slot == 0 and work and work[0][0] == (1, 1):
                        continue
                    if k > 0 and (slot > 0 or k > 1) and not (slot == 1 and work and k == 1 and flow == 0):
                        do_one([x], slot == chunks)
                if k == 0 and slot == chunks and h == HALVES - 1:
                    marks[:] = [touch(sent[h, 1])]
        if ag:
            if slot + 1 < chunks:
                add_forward(slot + 1, 0, PIECES)
            if rs:
                blocks = [(h, held[h]) for h in range(HALVES)]
                for piece in range(PIECES):
                    work.append(
                        (
                            ("b", slot - 1),
                            functools.partial(backward, slot - 1, blocks, None, True, piece, PIECES),
                        )
                    )
            else:
                while work:
                    do_one(list(marks))
                marks[:] = [touch(came[0, 0])]
                held[0] = store_last(pos, (came[0, 0], came[0, 1]), held[0], list(marks))
            gathered.append(held[0])
        arrived = came
    last = chunks - 1
    sketch = sketch_slice(pos, gathered, segment_ids, kp, [])
    marks[:] = [backward(last, [(0, held[0])], None, HALVES == 1, 0, 1, [sketch])]
    for h in range(1, HALVES):
        marks[:] = [tie(marks[0], [came[h, 0]])]
        held[h] = store_last(pos, (came[h, 0], came[h, 1]), held[h], list(marks))
    terms = score_terms(pos, from_others(sketch, "query", queriers), queries, list(marks))
    for h in range(1, HALVES):
        marks[:] = [backward(last, [(h, held[h])], totals.get(last), h == HALVES - 1, 0, 1, [terms])]
    scores = score_sum(pos, from_others(terms, "tensor", parts), list(marks))
    return (result[0].reshape(1, tokens, -1), scores)


def solution(mesh):
    return jax.shard_map(
        body,
        mesh=mesh,
        in_specs=(
            P(("groups", "dp", "query"), None, "tensor"),
            P(("groups", "dp", "query"), "tensor", None),
            P(("groups", "dp", "query"), "tensor", None),
            P(),
            P("tensor", None),
            P(None, "tensor"),
            P(),
            P("query", "tensor"),
            P(("groups", "dp", "query"), None),
        ),
        out_specs=(P(("groups", "dp", "query"), None, "tensor"), P(("groups", "dp"), "query")),
        check_vma=False,
    )
```

```python
import functools

import jax
import jax.numpy as jnp
from jax import lax
from jax.experimental import pallas as pl
from jax.experimental.pallas import tpu as pltpu
from jax.sharding import PartitionSpec as P

EX_DEV = 4
EPS = 1e-05
CHUNKS = 2
HALVES = 2
PIECES = 2
SHORT, LONG = 0.2, 5.0
SMALL, LIMIT, LARGE = 6 * 1024 * 1024, 11 * 1024 * 1024, 24 * 1024 * 1024
QUARTERS = 4

F32, BF16 = jnp.float32, jnp.bfloat16
ANY = pl.BlockSpec(memory_space=pl.ANY)
TOKEN = jax.ShapeDtypeStruct((8, 128), F32)
TOKEN_SPEC = pl.BlockSpec((8, 128), lambda *_: (0, 0))


def divisor(total, wanted):
    size = min(total, wanted)
    while total % size:
        size //= 2
    return size


def cost(microseconds):
    return pl.CostEstimate(flops=0, bytes_accessed=int(microseconds * 3.6e6), transcendentals=0)


def in_hbm(x):
    return pltpu.with_memory_space_constraint(x, pltpu.HBM)


def project_rows(values, matrix):
    return lax.dot_general(
        values, matrix, (((1,), (1,)), ((), ())), preferred_element_type=F32
    )


def spread(values, first):
    k = values.shape[1]
    row = lax.broadcasted_iota(jnp.int32, (k, 2 * k), 0)
    col = lax.broadcasted_iota(jnp.int32, (k, 2 * k), 1)
    return jnp.dot(values, jnp.where(col == row + first, 1.0, 0.0).astype(BF16), preferred_element_type=F32)


def forward_extra(by_share, proj_in, chunk, held, after):
    parts, _, rows, depth = by_share.shape
    extra = 2 * proj_in.shape[0]
    at = held.shape[2] // extra - 1

    def kernel(x_ref, p_ref, *refs):
        part = project_rows(x_ref[...].reshape(parts * rows, depth), p_ref[...]).astype(BF16)
        refs[-1][...] = spread(part, 0).astype(BF16).reshape(parts, rows, extra)

    return pl.pallas_call(
        kernel,
        grid=(1,),
        in_specs=[
            pl.BlockSpec((parts, None, rows, depth), lambda i: (0, chunk, 0, 0)),
            pl.BlockSpec(proj_in.shape, lambda i: (0, 0)),
        ]
        + [ANY] * (1 + len(after)),
        out_specs=pl.BlockSpec((parts, rows, extra), lambda i: (0, 0, at)),
        out_shape=jax.ShapeDtypeStruct(held.shape, BF16),
        input_output_aliases={2: 0},
        compiler_params=pltpu.CompilerParams(vmem_limit_bytes=LIMIT),
        cost_estimate=cost(SHORT),
        name="forward_extra",
    )(by_share, proj_in, held, *after)


def forward_piece(by_share, w_out, chunk, halves, half_at, extra, piece, pieces, held, after):
    parts, _, rows, depth = by_share.shape
    half = w_out.shape[1] // halves
    span = half // pieces
    cols = divisor(span, 1024)
    steps = span // cols
    base = half_at * half + piece * span

    def kernel(x_ref, w_ref, *refs):
        out_ref, tok_ref, held_ref, sems = refs[-4:]
        i = pl.program_id(0)

        def copy(j):
            columns = pl.ds(base + j * cols, cols)
            return pltpu.make_async_copy(w_ref.at[:, columns], held_ref.at[j], sems.at[j])

        @pl.when(i == 0)
        def _():
            for j in range(steps):
                copy(j).start()

        for j in range(steps):

            @pl.when(i == j)
            def _():
                copy(j).wait()
                x = x_ref[...].reshape(parts * rows, depth)
                y = jnp.dot(x, held_ref[j], preferred_element_type=F32).astype(BF16)
                out_ref[...] = y.reshape(parts, rows, cols)

        tok_ref[...] = jnp.zeros_like(tok_ref)

    more = ([] if held is None else [held]) + after
    return pl.pallas_call(
        kernel,
        grid=(steps,),
        in_specs=[
            pl.BlockSpec(
                (parts, None, rows, depth), lambda i: (0, chunk, 0, 0), pipeline_mode=pl.Buffered(1)
            )
        ]
        + [ANY] * (1 + len(more)),
        out_specs=[
            pl.BlockSpec((parts, rows, cols), lambda i: (0, 0, piece * steps + i)),
            TOKEN_SPEC,
        ],
        out_shape=[jax.ShapeDtypeStruct((parts, rows, half + extra), BF16), TOKEN],
        scratch_shapes=[pltpu.VMEM((steps, depth, cols), BF16), pltpu.SemaphoreType.DMA((steps,))],
        input_output_aliases={} if held is None else {2: 0},
        compiler_params=pltpu.CompilerParams(vmem_limit_bytes=LARGE),
        cost_estimate=cost(SHORT),
        name="forward_piece",
    )(in_hbm(by_share), in_hbm(w_out), *more)


def load_weights(w_out, piece, pieces, after):
    rows = w_out.shape[0] // pieces
    width = w_out.shape[1]

    def kernel(w_ref, *refs):
        out_ref, sem = refs[-2:]
        copy = pltpu.make_async_copy(w_ref.at[pl.ds(piece * rows, rows)], out_ref, sem)
        copy.start()
        copy.wait()

    return pl.pallas_call(
        kernel,
        in_specs=[ANY] * (1 + len(after)),
        out_specs=pl.BlockSpec(memory_space=pltpu.VMEM),
        out_shape=pltpu.VMEM((rows, width), BF16),
        scratch_shapes=[pltpu.SemaphoreType.DMA],
        compiler_params=pltpu.CompilerParams(vmem_limit_bytes=SMALL),
        cost_estimate=cost(SHORT),
        name="load_weights",
    )(in_hbm(w_out), *after)


def backward_piece(blocks, weights, chunk, chunks, halves, piece, pieces, total, last, held, after):
    parts, rows, _ = blocks[0][1].shape
    some, width = weights[0].shape
    half, span = width // halves, some * len(weights)
    cols = divisor(some, 256)
    n, m = len(blocks), len(weights)

    def kernel(*refs):
        out_ref, tok_ref = refs[-2:]
        for j in range(m):

            def step(i, carry):
                here = pl.ds(pl.multiple_of(i * cols, cols), cols)
                there = pl.ds(pl.multiple_of(j * some + i * cols, cols), cols)
                y = None if total is None else refs[n + m][:, :, there].reshape(parts * rows, cols)
                for b, (at, _) in enumerate(blocks):
                    g = refs[b][...].reshape(parts * rows, half)
                    term = project_rows(g, refs[n + j][here, at * half : (at + 1) * half])
                    y = term if y is None else y + term
                out_ref[:, :, there] = y.astype(out_ref.dtype).reshape(parts, rows, cols)
                return carry

            lax.fori_loop(0, some // cols, step, 0)
        tok_ref[...] = jnp.zeros_like(tok_ref)

    once = pl.Buffered(1)
    here = pl.BlockSpec((parts, rows, span), lambda i: (0, 0, piece))
    if last:
        out_spec = pl.BlockSpec((parts, None, rows, span), lambda i: (0, chunk, 0, piece))
        out_shape = jax.ShapeDtypeStruct((parts, chunks, rows, span * pieces), BF16)
    else:
        out_spec, out_shape = here, jax.ShapeDtypeStruct((parts, rows, span * pieces), F32)
    sums = [] if total is None else [total]
    extra = ([] if held is None else [held]) + after
    return pl.pallas_call(
        kernel,
        grid=(1,),
        in_specs=[pl.BlockSpec((parts, rows, half), lambda i: (0, 0, 0), pipeline_mode=once)] * n
        + [pl.BlockSpec(memory_space=pltpu.VMEM)] * m
        + [pl.BlockSpec((parts, rows, span), lambda i: (0, 0, piece), pipeline_mode=once)] * len(sums)
        + [ANY] * len(extra),
        out_specs=[out_spec, TOKEN_SPEC],
        out_shape=[out_shape, TOKEN],
        input_output_aliases={} if held is None else {n + m + len(sums): 0},
        compiler_params=pltpu.CompilerParams(vmem_limit_bytes=LIMIT),
        cost_estimate=cost(SHORT),
        name="backward_piece",
    )(
        *[g for _, g in blocks],
        *[pltpu.with_memory_space_constraint(w, pltpu.VMEM) for w in weights],
        *sums,
        *extra,
    )


def relay(pos, flow, k, partial, came, held, after):
    rows, width = came.shape
    parts = (partial if held is None else held).shape[0]
    n_in = 1 + (partial is not None) + (held is not None) + len(after)

    def far(pos_ref, steps):
        way = pos_ref[1] if flow == 0 else -pos_ref[1]
        return lax.clamp(0, pos_ref[0] + way * steps, parts - 1)

    def kernel(pos_ref, *refs):
        came_ref, x_ref = refs[0], refs[n_in]
        place = pos_ref[2] if flow == 0 else parts - 1 - pos_ref[2]
        if held is not None:
            store = pltpu.make_async_copy(came_ref, refs[n_in + 1].at[far(pos_ref, -k)], refs[-1])
            pl.when(place >= k)(store.start)
        if partial is not None:

            @pl.when(place < k)
            def _():
                x_ref[...] = (came_ref[...].astype(F32) + refs[1][...].astype(F32)).astype(BF16)

            @pl.when(place >= k)
            def _():
                x_ref[...] = came_ref[...]

        else:
            x_ref[...] = came_ref[...]
        if held is not None:
            pl.when(place >= k)(store.wait)

    line = jax.ShapeDtypeStruct((rows, width), BF16)
    whole = pl.BlockSpec((rows, width), lambda i, w: (0, 0), pipeline_mode=pl.Buffered(1))
    args, specs, out_specs, out_shape, alias = [came], [whole], [whole], [line], {}
    if partial is not None:
        term = pl.BlockSpec(
            (None, rows, width),
            lambda i, w: (far(w, parts - k), 0, 0),
            pipeline_mode=pl.Buffered(1),
        )
        specs.append(term)
        args.append(partial)
    if held is not None:
        alias[1 + len(args)] = 1
        specs.append(ANY)
        args.append(held)
        out_specs.append(ANY)
        out_shape.append(jax.ShapeDtypeStruct(held.shape, BF16))
    outs = pl.pallas_call(
        kernel,
        grid_spec=pltpu.PrefetchScalarGridSpec(
            num_scalar_prefetch=1,
            grid=(1,),
            in_specs=specs + [ANY] * len(after),
            out_specs=out_specs,
            scratch_shapes=[pltpu.SemaphoreType.DMA] if held is not None else [],
        ),
        out_shape=out_shape,
        input_output_aliases=alias,
        compiler_params=pltpu.CompilerParams(vmem_limit_bytes=SMALL),
        cost_estimate=cost(LONG),
        name="relay",
    )(pos, *args, *after)
    return outs[0], (outs[1] if held is not None else None)


def store_last(pos, came, held, after):
    parts = held.shape[0]

    def kernel(pos_ref, a_ref, b_ref, *refs):
        out_ref, sem = refs[-2:]
        rank, way, place = pos_ref[0], pos_ref[1], pos_ref[2]
        ends = (
            (place == parts - 1, a_ref, rank - way * (parts - 1)),
            (place == 0, b_ref, rank + way * (parts - 1)),
        )
        for at_end, came_ref, at in ends:
            copy = pltpu.make_async_copy(came_ref, out_ref.at[lax.clamp(0, at, parts - 1)], sem)

            @pl.when(at_end)
            def _():
                copy.start()
                copy.wait()

    return pl.pallas_call(
        kernel,
        grid_spec=pltpu.PrefetchScalarGridSpec(
            num_scalar_prefetch=1,
            grid=(1,),
            in_specs=[pl.BlockSpec(held.shape[1:], lambda i, w: (0, 0))] * 2 + [ANY] * (1 + len(after)),
            out_specs=ANY,
            scratch_shapes=[pltpu.SemaphoreType.DMA],
        ),
        out_shape=jax.ShapeDtypeStruct(held.shape, BF16),
        input_output_aliases={3: 0},
        compiler_params=pltpu.CompilerParams(vmem_limit_bytes=SMALL),
        cost_estimate=cost(SHORT),
        name="store_last",
    )(pos, *came, held, *after)


def first_block(pos, flow, partial):
    parts, rows, width = partial.shape

    def there(i, w):
        way = w[1] if flow == 0 else -w[1]
        return lax.clamp(0, w[0] + way * (parts - 1), parts - 1), 0, 0

    def kernel(pos_ref, p_ref, out_ref):
        out_ref[...] = p_ref[...]

    return pl.pallas_call(
        kernel,
        grid_spec=pltpu.PrefetchScalarGridSpec(
            num_scalar_prefetch=1,
            grid=(1,),
            in_specs=[pl.BlockSpec((None, rows, width), there)],
            out_specs=pl.BlockSpec((rows, width), lambda i, w: (0, 0)),
        ),
        out_shape=jax.ShapeDtypeStruct((rows, width), BF16),
        compiler_params=pltpu.CompilerParams(vmem_limit_bytes=SMALL),
        cost_estimate=cost(SHORT),
        name="first_block",
    )(pos, partial)


def norm_terms(p_ref, a_ref, b_ref, res_ref, grad_ref, gain_ref, at):
    proj = p_ref[:, at].astype(F32) + a_ref[:, at].astype(F32) + b_ref[:, at].astype(F32)
    z = res_ref[:, at].astype(F32) + proj
    scaled = gain_ref[:, at].astype(F32) * grad_ref[:, at].astype(F32)
    return z, scaled


def norm_specs(ins, half, chunk, at):
    _, rows, wide = ins[0].shape
    once = pl.Buffered(1)
    whole = pl.BlockSpec((rows, wide), lambda i, r: (0, 0), pipeline_mode=once)
    own = pl.BlockSpec((None, rows, half), lambda i, r: (0, chunk, at), pipeline_mode=once)
    mine = pl.BlockSpec((None, rows, wide), lambda i, r: (r[0], 0, 0), pipeline_mode=once)
    return [mine, whole, whole, own, own, pl.BlockSpec((1, half), lambda i, r: (0, at))]


def norm_sums(pos, ins, half, chunk, at, sums, after):
    rows = ins[0].shape[1]
    cols = divisor(half, 1024)

    def kernel(pos_ref, *refs):
        square_ref, cross_ref = refs[-2:]

        def step(i, sums):
            z, scaled = norm_terms(*refs[:6], pl.ds(pl.multiple_of(i * cols, cols), cols))
            square, cross = sums
            for j in range(0, cols, 128):
                zj = z[:, j : j + 128]
                square = square + zj * zj
                cross = cross + zj * scaled[:, j : j + 128]
            return square, cross

        zero = jnp.zeros((rows, 128), F32)
        start = (zero, zero) if sums is None else (refs[6][...], refs[7][...])
        square_ref[...], cross_ref[...] = lax.fori_loop(0, half // cols, step, start)

    stat = pl.BlockSpec((rows, 128), lambda i, r: (0, 0))
    before = [] if sums is None else list(sums)
    return pl.pallas_call(
        kernel,
        grid_spec=pltpu.PrefetchScalarGridSpec(
            num_scalar_prefetch=1,
            grid=(1,),
            in_specs=norm_specs(ins, half, chunk, at) + [stat] * len(before) + [ANY] * len(after),
            out_specs=[stat, stat],
        ),
        out_shape=[jax.ShapeDtypeStruct((rows, 128), F32)] * 2,
        compiler_params=pltpu.CompilerParams(vmem_limit_bytes=LIMIT),
        cost_estimate=cost(LONG),
        name="norm_sums",
    )(pos, *ins, *before, *after)


def norm_out(pos, ins, half, chunk, sums, proj_out, after):
    parts, rows, wide = ins[0][1][0].shape
    cols = divisor(half, 1024)
    n, width = len(ins), ins[0][1][3].shape[2]
    with_b = proj_out

    def kernel(pos_ref, *refs):
        square_ref, cross_ref = refs[6 * n], refs[6 * n + 1]
        if with_b is None:
            out_ref, held_ref, sem = refs[-3:]
        else:
            out_ref, held_ref, rest_ref, sem = refs[-4:]
        inv = lax.rsqrt(jnp.sum(square_ref[...], axis=-1, keepdims=True) / width + EPS)
        slope = inv * inv * inv * (jnp.sum(cross_ref[...], axis=-1, keepdims=True) / width)
        for j in range(n):
            to_ref = out_ref if j == 0 else rest_ref.at[j - 1]

            def step(i, carry):
                here = pl.ds(pl.multiple_of(i * cols, cols), cols)
                z, scaled = norm_terms(*refs[6 * j : 6 * j + 6], here)
                to_ref[:, here] = (inv * scaled - z * slope).astype(BF16)
                return carry

            lax.fori_loop(0, half // cols, step, 0)
        if with_b is not None:
            p_ref = refs[6 * n + 2]
            b = project_rows(out_ref[:, :half], p_ref[:, :half])
            for j in range(1, n):
                b = b + project_rows(rest_ref[j - 1], p_ref[:, j * half : (j + 1) * half])
            a = sum(refs[j][:, half:].astype(F32) for j in range(3))
            out_ref[:, half:] = (a + spread(b.astype(BF16), b.shape[1])).astype(BF16)
        else:
            out_ref[:, half:] = jnp.zeros((rows, wide - half), BF16)
        own = pltpu.make_async_copy(out_ref, held_ref.at[pos_ref[0]], sem)
        own.start()
        own.wait()

    stat = pl.BlockSpec((rows, 128), lambda i, r: (0, 0))
    specs, args = [], []
    for at, one in ins:
        specs += norm_specs(one, half, chunk, at)
        args += one
    specs, args = specs + [stat, stat], args + list(sums)
    scratch = [pltpu.SemaphoreType.DMA]
    if with_b is not None:
        specs.append(pl.BlockSpec(proj_out.shape, lambda i, r: (0, 0)))
        args.append(proj_out)
        scratch = [pltpu.VMEM((max(1, n - 1), rows, half), BF16)] + scratch
    return pl.pallas_call(
        kernel,
        grid_spec=pltpu.PrefetchScalarGridSpec(
            num_scalar_prefetch=1,
            grid=(1,),
            in_specs=specs + [ANY] * len(after),
            out_specs=[pl.BlockSpec((rows, wide), lambda i, r: (0, 0)), ANY],
            scratch_shapes=scratch,
        ),
        out_shape=[
            jax.ShapeDtypeStruct((rows, wide), BF16),
            jax.ShapeDtypeStruct((parts, rows, wide), BF16),
        ],
        compiler_params=pltpu.CompilerParams(vmem_limit_bytes=LIMIT),
        cost_estimate=cost(SHORT),
        name="norm_out",
    )(pos, *args, *after)


def tie(value, after):
    def kernel(value_ref, *refs):
        refs[-1][...] = value_ref[...]

    whole = pl.BlockSpec(value.shape, lambda i: (0,) * value.ndim)
    return pl.pallas_call(
        kernel,
        grid=(1,),
        in_specs=[whole] + [ANY] * len(after),
        out_specs=whole,
        out_shape=jax.ShapeDtypeStruct(value.shape, value.dtype),
        compiler_params=pltpu.CompilerParams(vmem_limit_bytes=SMALL),
        cost_estimate=cost(SHORT),
        name="tie",
    )(value, *after)


def touch(x):
    def kernel(x_ref, out_ref):
        out_ref[...] = jnp.zeros_like(out_ref)

    return pl.pallas_call(
        kernel,
        grid=(1,),
        in_specs=[ANY],
        out_specs=TOKEN_SPEC,
        out_shape=TOKEN,
        compiler_params=pltpu.CompilerParams(vmem_limit_bytes=SMALL),
        cost_estimate=cost(SHORT),
        name="touch",
    )(x)


def from_others(value, axis, size):
    return [value] + [
        lax.ppermute(value, axis, [(d, (d + shift) % size) for d in range(size)])
        for shift in range(1, size)
    ]


def sketch_slice(pos, gathered, segment_ids, kp, after):
    parts, rows, wide = gathered[0].shape
    extra, mine = 2 * kp, kp // parts
    chunks, tokens = len(gathered), segment_ids.shape[1]

    def kernel(pos_ref, *refs):
        out_ref, sum_ref = refs[-2:]
        example = lax.broadcasted_iota(jnp.int32, (8, tokens), 0)
        by_row = jnp.where(refs[chunks][...] == example, 1.0, 0.0).astype(BF16)
        same = lax.broadcasted_iota(jnp.int32, (tokens, tokens), 0) == lax.broadcasted_iota(
            jnp.int32, (tokens, tokens), 1
        )
        weights = project_rows(jnp.where(same, 1.0, 0.0).astype(BF16), by_row)
        weights = weights.reshape(parts, chunks, rows, 8)
        for e in range(EX_DEV):
            total = None
            for c in range(chunks):
                both = refs[c][...].reshape(parts * rows, extra)
                weight = weights[:, c].reshape(parts * rows, 8)[:, e : e + 1]
                part = (both.astype(F32) * weight).astype(BF16)
                term = lax.dot_general(
                    part, both, (((0,), (0,)), ((), ())), preferred_element_type=F32
                )
                total = term if total is None else total + term
            sum_ref[e] = total
        low = lax.broadcasted_iota(jnp.int32, (1, extra), 1) < kp
        for r in range(parts):

            @pl.when(pos_ref[0] == r)
            def _():
                for e in range(EX_DEV):
                    for i in range(mine // 2):
                        at = kp + r * mine + 2 * i
                        left, right = sum_ref[e, at : at + 1, :], sum_ref[e, at + 1 : at + 2, :]
                        out_ref[e : e + 1, i * extra : (i + 1) * extra] = jnp.where(
                            low, left, pltpu.roll(right, kp, 1)
                        )

    return pl.pallas_call(
        kernel,
        grid_spec=pltpu.PrefetchScalarGridSpec(
            num_scalar_prefetch=1,
            grid=(1,),
            in_specs=[pl.BlockSpec((parts, rows, extra), lambda i, w: (0, 0, wide // extra - 1))] * chunks
            + [pl.BlockSpec(segment_ids.shape, lambda i, w: (0, 0))]
            + [ANY] * len(after),
            out_specs=pl.BlockSpec((EX_DEV, mine * kp), lambda i, w: (0, 0)),
            scratch_shapes=[pltpu.VMEM((EX_DEV, extra, extra), F32)],
        ),
        out_shape=jax.ShapeDtypeStruct((EX_DEV, mine * kp), F32),
        compiler_params=pltpu.CompilerParams(vmem_limit_bytes=LIMIT),
        cost_estimate=cost(SHORT),
        name="sketch_slice",
    )(pos, *gathered, segment_ids, *after)


def score_terms(pos, sketches, queries, after):
    size = len(sketches)
    n, depth = queries.shape

    def kernel(pos_ref, *refs):
        out_ref, all_ref = refs[-2:]
        for back in range(size):
            all_ref[lax.rem(pos_ref[3] - back + size, size)] = refs[back][...]
        for d in range(size):
            rest, total = all_ref[d], None
            for _ in range(3):
                part = rest.astype(BF16)
                rest = rest - part.astype(F32)
                term = project_rows(part, refs[size][...])
                total = term if total is None else total + term
            out_ref[d * EX_DEV : (d + 1) * EX_DEV, :] = total

    return pl.pallas_call(
        kernel,
        grid_spec=pltpu.PrefetchScalarGridSpec(
            num_scalar_prefetch=1,
            grid=(1,),
            in_specs=[pl.BlockSpec((EX_DEV, depth), lambda i, w: (0, 0))] * size
            + [pl.BlockSpec((n, depth), lambda i, w: (0, 0))]
            + [ANY] * len(after),
            out_specs=pl.BlockSpec((size * EX_DEV, n), lambda i, w: (0, 0)),
            scratch_shapes=[pltpu.VMEM((size, EX_DEV, depth), F32)],
        ),
        out_shape=jax.ShapeDtypeStruct((size * EX_DEV, n), F32),
        compiler_params=pltpu.CompilerParams(vmem_limit_bytes=LIMIT),
        cost_estimate=cost(SHORT),
        name="score_terms",
    )(pos, *sketches, queries, *after)


def score_sum(pos, terms, after):
    size = len(terms)
    shape = terms[0].shape

    def kernel(pos_ref, *refs):
        out_ref, all_ref = refs[-2:]
        for back in range(size):
            all_ref[lax.rem(pos_ref[0] - back + size, size)] = refs[back][...]
        total = all_ref[0]
        for d in range(1, size):
            total = total + all_ref[d]
        out_ref[...] = total

    whole = pl.BlockSpec(shape, lambda i, w: (0, 0))
    return pl.pallas_call(
        kernel,
        grid_spec=pltpu.PrefetchScalarGridSpec(
            num_scalar_prefetch=1,
            grid=(1,),
            in_specs=[whole] * size + [ANY] * len(after),
            out_specs=whole,
            scratch_shapes=[pltpu.VMEM((size,) + shape, F32)],
        ),
        out_shape=jax.ShapeDtypeStruct(shape, F32),
        compiler_params=pltpu.CompilerParams(vmem_limit_bytes=SMALL),
        cost_estimate=cost(SHORT),
        name="score_sum",
    )(pos, *terms, *after)


def body(inputs, residual, out_grad, norm_gain, w_out, proj_in, proj_out, queries, segment_ids):
    parts = lax.axis_size("tensor")
    rank = lax.axis_index("tensor")
    queriers = lax.axis_size("query")
    q_rank = lax.axis_index("query")
    tokens = inputs.shape[1]
    share = tokens // parts
    chunks = max(1, min(CHUNKS, share // 16))
    rows = share // chunks
    by_share = inputs.reshape(parts, chunks, rows, inputs.shape[2])
    gain = norm_gain.reshape(1, -1)
    residual, out_grad, proj_out = in_hbm(residual), in_hbm(out_grad), in_hbm(proj_out)
    half = w_out.shape[1] // HALVES
    kp = proj_out.shape[0]

    up = 1 - 2 * lax.rem(q_rank, 2)
    pos = jnp.stack([rank, up, jnp.where(up == 1, rank, parts - 1 - rank), q_rank]).astype(jnp.int32)

    def pairs(flow, low, high):
        out = []
        for q in range(queriers):
            way = 1 if (q % 2 == 0) == (flow == 0) else -1
            for t in range(parts):
                spot = t if way == 1 else parts - 1 - t
                if low <= spot <= min(high, parts - 2):
                    out.append((t * queriers + q, (t + way) * queriers + q))
        return out

    work, marks, resident = [], [], []
    partials, totals, result = {}, {}, [None]

    def forward(c, h, piece, pieces, after):
        partials[c, h], mark = forward_piece(
            by_share,
            w_out,
            c,
            HALVES,
            h,
            2 * kp,
            piece,
            pieces,
            partials.get((c, h)),
            after,
        )
        if h == 0 and piece == pieces - 1:
            partials[c, h] = forward_extra(by_share, proj_in, c, partials[c, h], [mark])
        return mark

    def backward(c, blocks, total, last, piece, pieces, after):
        held = result[0] if last else totals.get(c)
        some = resident[piece * QUARTERS // pieces : (piece + 1) * QUARTERS // pieces]
        done, mark = backward_piece(
            blocks, some, c, chunks, HALVES, piece, pieces, total, last, held, after
        )
        if last:
            result[0] = done
        else:
            totals[c] = done
        return mark

    def do_one(after, touching=False):
        if work:
            marks[:] = [work.pop(0)[1](after)]
        elif touching:
            marks[:] = [touch(after[0])]

    def finish(key, after):
        while any(k == key for k, _ in work):
            do_one(list(marks) + after)

    def load(count, after):
        for _ in range(count):
            resident.append(load_weights(w_out, len(resident), QUARTERS, after))
            after = [resident[-1]]
        marks[:] = after

    def add_forward(c, h, pieces):
        for piece in range(pieces):
            work.append(((c, h), functools.partial(forward, c, h, piece, pieces)))

    add_forward(0, 0, 1)
    finish((0, 0), [])
    gathered = []
    for slot in range(chunks + 1):
        rs, ag = slot < chunks, slot > 0
        came, held, sent, before = {}, {}, {}, None
        if ag:
            ins = [
                [partials[slot - 1, h], arrived[h, 0], arrived[h, 1], residual, out_grad, gain]
                for h in range(HALVES)
            ]
            sums = None
            for h in range(HALVES):
                sums = norm_sums(pos, ins[h], half, slot - 1, h, sums, list(marks))
            grad = [None] * HALVES
            grad[0], held[0] = norm_out(
                pos, list(enumerate(ins)), half, slot - 1, sums, proj_out, []
            )
        for k in range(parts):
            gather_now, reduce_now = ag and k <= parts - 2, rs and k >= 1
            if not gather_now and not reduce_now:
                continue
            for h in range(HALVES):
                if k == 0 and h > 0:
                    if rs and slot > 1:
                        add_forward(slot, h, PIECES)
                    do_one([sent[h - 1, 1]])
                    grad[h], held[h] = norm_out(
                        pos, [(h, ins[h])], half, slot - 1, sums, None, list(marks)
                    )
                if reduce_now:
                    if slot == 0 and k == 1 and h > 0:
                        add_forward(0, h, 1)
                        do_one([sent[h - 1, 1]])
                    finish((slot, h), [sent[h - 1, 1]] if h > 0 else [])
                for flow in range(2):
                    if k == 0:
                        x = before = grad[h]
                    elif (h, flow) not in came:
                        x = first_block(pos, flow, partials[slot, h])
                    else:
                        x, held[h] = relay(
                            pos,
                            flow,
                            k,
                            partials[slot, h] if reduce_now else None,
                            came[h, flow],
                            held.get(h),
                            list(marks) + ([] if before is None else [before]),
                        )
                        before = x
                    came[h, flow] = lax.ppermute(
                        x,
                        ("tensor", "query"),
                        pairs(flow, 0 if reduce_now else k, parts - 2 if gather_now else k - 1),
                    )
                    sent[h, flow] = x
                    if slot == chunks - 1 and flow == 1 and slot > 0:
                        if (k, h) == (parts - 2, HALVES - 1):
                            load(1, [x])
                            continue
                        if (k, h) == (parts - 1, HALVES - 1):
                            load(QUARTERS - len(resident), [x])
                            continue
                    if slot == 0 and k == 2 and (h, flow) == (HALVES - 1, 1) and chunks > 1 and HALVES > 1:
                        add_forward(1, 1, PIECES)
                        do_one([x])
                        continue
                    if slot == 0 and k == parts - 1 and (h, flow) == (HALVES - 1, 1) and chunks > 1:
                        work.insert(0, ((1, 0), functools.partial(forward, 1, 0, 0, 1)))
                    if slot == 0 and work and work[0][0] == (1, 1):
                        continue
                    if k > 0 and (slot > 0 or k > 1) and not (slot == 1 and work and k == 1 and flow == 0):
                        if slot == chunks and flow == 0:
                            marks[:] = [touch(x)]
                        else:
                            do_one([x], slot == chunks)
                if k == 0 and slot == chunks and h == HALVES - 1:
                    marks[:] = [touch(sent[h, 1])]
        if ag:
            if slot + 1 < chunks:
                add_forward(slot + 1, 0, PIECES)
            if rs:
                blocks = [(h, held[h]) for h in range(HALVES)]
                for piece in range(PIECES):
                    work.append(
                        (
                            ("b", slot - 1),
                            functools.partial(backward, slot - 1, blocks, None, True, piece, PIECES),
                        )
                    )
            else:
                while work:
                    do_one(list(marks))
                marks[:] = [touch(came[0, 0])]
                held[0] = store_last(pos, (came[0, 0], came[0, 1]), held[0], list(marks))
            gathered.append(held[0])
        arrived = came
    last = chunks - 1
    sketch = sketch_slice(pos, gathered, segment_ids, kp, [])
    marks[:] = [backward(last, [(0, held[0])], None, HALVES == 1, 0, 1, [sketch])]
    for h in range(1, HALVES):
        marks[:] = [tie(marks[0], [came[h, 0]])]
        held[h] = store_last(pos, (came[h, 0], came[h, 1]), held[h], list(marks))
    terms = score_terms(pos, from_others(sketch, "query", queriers), queries, list(marks))
    for h in range(1, HALVES):
        marks[:] = [backward(last, [(h, held[h])], totals.get(last), h == HALVES - 1, 0, 1, [terms])]
    scores = score_sum(pos, from_others(terms, "tensor", parts), list(marks))
    return (result[0].reshape(1, tokens, -1), scores)


def solution(mesh):
    return jax.shard_map(
        body,
        mesh=mesh,
        in_specs=(
            P(("groups", "dp", "query"), None, "tensor"),
            P(("groups", "dp", "query"), "tensor", None),
            P(("groups", "dp", "query"), "tensor", None),
            P(),
            P("tensor", None),
            P(None, "tensor"),
            P(),
            P("query", "tensor"),
            P(("groups", "dp", "query"), None),
        ),
        out_specs=(P(("groups", "dp", "query"), None, "tensor"), P(("groups", "dp"), "query")),
        check_vma=False,
    )
```

```python
import functools

import jax
import jax.numpy as jnp
from jax import lax
from jax.experimental import pallas as pl
from jax.experimental.pallas import tpu as pltpu
from jax.sharding import PartitionSpec as P

EX_DEV = 4
EPS = 1e-05
CHUNKS = 2
HALVES = 2
PIECES = 2
SHORT, LONG = 0.2, 5.0
SMALL, LIMIT, LARGE = 6 * 1024 * 1024, 11 * 1024 * 1024, 24 * 1024 * 1024
QUARTERS = 4

F32, BF16 = jnp.float32, jnp.bfloat16
ANY = pl.BlockSpec(memory_space=pl.ANY)
TOKEN = jax.ShapeDtypeStruct((8, 128), F32)
TOKEN_SPEC = pl.BlockSpec((8, 128), lambda *_: (0, 0))


def divisor(total, wanted):
    size = min(total, wanted)
    while total % size:
        size //= 2
    return size


def cost(microseconds):
    return pl.CostEstimate(flops=0, bytes_accessed=int(microseconds * 3.6e6), transcendentals=0)


def in_hbm(x):
    return pltpu.with_memory_space_constraint(x, pltpu.HBM)


def project_rows(values, matrix):
    return lax.dot_general(
        values, matrix, (((1,), (1,)), ((), ())), preferred_element_type=F32
    )


def spread(values, first):
    k = values.shape[1]
    row = lax.broadcasted_iota(jnp.int32, (k, 2 * k), 0)
    col = lax.broadcasted_iota(jnp.int32, (k, 2 * k), 1)
    return jnp.dot(values, jnp.where(col == row + first, 1.0, 0.0).astype(BF16), preferred_element_type=F32)


def forward_extra(by_share, proj_in, chunk, held, after):
    parts, _, rows, depth = by_share.shape
    extra = 2 * proj_in.shape[0]
    at = held.shape[2] // extra - 1

    def kernel(x_ref, p_ref, *refs):
        part = project_rows(x_ref[...].reshape(parts * rows, depth), p_ref[...]).astype(BF16)
        refs[-1][...] = spread(part, 0).astype(BF16).reshape(parts, rows, extra)

    return pl.pallas_call(
        kernel,
        grid=(1,),
        in_specs=[
            pl.BlockSpec((parts, None, rows, depth), lambda i: (0, chunk, 0, 0)),
            pl.BlockSpec(proj_in.shape, lambda i: (0, 0)),
        ]
        + [ANY] * (1 + len(after)),
        out_specs=pl.BlockSpec((parts, rows, extra), lambda i: (0, 0, at)),
        out_shape=jax.ShapeDtypeStruct(held.shape, BF16),
        input_output_aliases={2: 0},
        compiler_params=pltpu.CompilerParams(vmem_limit_bytes=LIMIT),
        cost_estimate=cost(SHORT),
        name="forward_extra",
    )(by_share, proj_in, held, *after)


def forward_piece(by_share, w_out, chunk, halves, half_at, extra, piece, pieces, held, after):
    parts, _, rows, depth = by_share.shape
    half = w_out.shape[1] // halves
    span = half // pieces
    cols = divisor(span, 1024)
    steps = span // cols
    base = half_at * half + piece * span

    def kernel(x_ref, w_ref, *refs):
        out_ref, tok_ref, held_ref, sems = refs[-4:]
        i = pl.program_id(0)

        def copy(j):
            columns = pl.ds(base + j * cols, cols)
            return pltpu.make_async_copy(w_ref.at[:, columns], held_ref.at[j], sems.at[j])

        @pl.when(i == 0)
        def _():
            for j in range(steps):
                copy(j).start()

        for j in range(steps):

            @pl.when(i == j)
            def _():
                copy(j).wait()
                x = x_ref[...].reshape(parts * rows, depth)
                y = jnp.dot(x, held_ref[j], preferred_element_type=F32).astype(BF16)
                out_ref[...] = y.reshape(parts, rows, cols)

        tok_ref[...] = jnp.zeros_like(tok_ref)

    more = ([] if held is None else [held]) + after
    return pl.pallas_call(
        kernel,
        grid=(steps,),
        in_specs=[
            pl.BlockSpec(
                (parts, None, rows, depth), lambda i: (0, chunk, 0, 0), pipeline_mode=pl.Buffered(1)
            )
        ]
        + [ANY] * (1 + len(more)),
        out_specs=[
            pl.BlockSpec((parts, rows, cols), lambda i: (0, 0, piece * steps + i)),
            TOKEN_SPEC,
        ],
        out_shape=[jax.ShapeDtypeStruct((parts, rows, half + extra), BF16), TOKEN],
        scratch_shapes=[pltpu.VMEM((steps, depth, cols), BF16), pltpu.SemaphoreType.DMA((steps,))],
        input_output_aliases={} if held is None else {2: 0},
        compiler_params=pltpu.CompilerParams(vmem_limit_bytes=LARGE),
        cost_estimate=cost(SHORT),
        name="forward_piece",
    )(in_hbm(by_share), in_hbm(w_out), *more)


def load_weights(w_out, piece, pieces, after):
    rows = w_out.shape[0] // pieces
    width = w_out.shape[1]

    def kernel(w_ref, *refs):
        out_ref, sem = refs[-2:]
        copy = pltpu.make_async_copy(w_ref.at[pl.ds(piece * rows, rows)], out_ref, sem)
        copy.start()
        copy.wait()

    return pl.pallas_call(
        kernel,
        in_specs=[ANY] * (1 + len(after)),
        out_specs=pl.BlockSpec(memory_space=pltpu.VMEM),
        out_shape=pltpu.VMEM((rows, width), BF16),
        scratch_shapes=[pltpu.SemaphoreType.DMA],
        compiler_params=pltpu.CompilerParams(vmem_limit_bytes=SMALL),
        cost_estimate=cost(SHORT),
        name="load_weights",
    )(in_hbm(w_out), *after)


def backward_piece(blocks, weights, chunk, chunks, halves, piece, pieces, total, last, held, after):
    parts, rows, _ = blocks[0][1].shape
    some, width = weights[0].shape
    half, span = width // halves, some * len(weights)
    cols = divisor(some, 256)
    n, m = len(blocks), len(weights)

    def kernel(*refs):
        out_ref, tok_ref = refs[-2:]
        for j in range(m):

            def step(i, carry):
                here = pl.ds(pl.multiple_of(i * cols, cols), cols)
                there = pl.ds(pl.multiple_of(j * some + i * cols, cols), cols)
                y = None if total is None else refs[n + m][:, :, there].reshape(parts * rows, cols)
                for b, (at, _) in enumerate(blocks):
                    g = refs[b][...].reshape(parts * rows, half)
                    term = project_rows(g, refs[n + j][here, at * half : (at + 1) * half])
                    y = term if y is None else y + term
                out_ref[:, :, there] = y.astype(out_ref.dtype).reshape(parts, rows, cols)
                return carry

            lax.fori_loop(0, some // cols, step, 0)
        tok_ref[...] = jnp.zeros_like(tok_ref)

    once = pl.Buffered(1)
    here = pl.BlockSpec((parts, rows, span), lambda i: (0, 0, piece))
    if last:
        out_spec = pl.BlockSpec((parts, None, rows, span), lambda i: (0, chunk, 0, piece))
        out_shape = jax.ShapeDtypeStruct((parts, chunks, rows, span * pieces), BF16)
    else:
        out_spec, out_shape = here, jax.ShapeDtypeStruct((parts, rows, span * pieces), F32)
    sums = [] if total is None else [total]
    extra = ([] if held is None else [held]) + after
    return pl.pallas_call(
        kernel,
        grid=(1,),
        in_specs=[pl.BlockSpec((parts, rows, half), lambda i: (0, 0, 0), pipeline_mode=once)] * n
        + [pl.BlockSpec(memory_space=pltpu.VMEM)] * m
        + [pl.BlockSpec((parts, rows, span), lambda i: (0, 0, piece), pipeline_mode=once)] * len(sums)
        + [ANY] * len(extra),
        out_specs=[out_spec, TOKEN_SPEC],
        out_shape=[out_shape, TOKEN],
        input_output_aliases={} if held is None else {n + m + len(sums): 0},
        compiler_params=pltpu.CompilerParams(vmem_limit_bytes=LIMIT),
        cost_estimate=cost(SHORT),
        name="backward_piece",
    )(
        *[g for _, g in blocks],
        *[pltpu.with_memory_space_constraint(w, pltpu.VMEM) for w in weights],
        *sums,
        *extra,
    )


def relay(pos, flow, k, partial, came, held, after):
    rows, width = came.shape
    parts = (partial if held is None else held).shape[0]
    n_in = 1 + (partial is not None) + (held is not None) + len(after)

    def far(pos_ref, steps):
        way = pos_ref[1] if flow == 0 else -pos_ref[1]
        return lax.clamp(0, pos_ref[0] + way * steps, parts - 1)

    def kernel(pos_ref, *refs):
        came_ref, x_ref = refs[0], refs[n_in]
        place = pos_ref[2] if flow == 0 else parts - 1 - pos_ref[2]
        if held is not None:
            store = pltpu.make_async_copy(came_ref, refs[n_in + 1].at[far(pos_ref, -k)], refs[-1])
            pl.when(place >= k)(store.start)
        if partial is not None:

            @pl.when(place < k)
            def _():
                x_ref[...] = (came_ref[...].astype(F32) + refs[1][...].astype(F32)).astype(BF16)

            @pl.when(place >= k)
            def _():
                x_ref[...] = came_ref[...]

        else:
            x_ref[...] = came_ref[...]
        if held is not None:
            pl.when(place >= k)(store.wait)

    line = jax.ShapeDtypeStruct((rows, width), BF16)
    whole = pl.BlockSpec((rows, width), lambda i, w: (0, 0), pipeline_mode=pl.Buffered(1))
    args, specs, out_specs, out_shape, alias = [came], [whole], [whole], [line], {}
    if partial is not None:
        term = pl.BlockSpec(
            (None, rows, width),
            lambda i, w: (far(w, parts - k), 0, 0),
            pipeline_mode=pl.Buffered(1),
        )
        specs.append(term)
        args.append(partial)
    if held is not None:
        alias[1 + len(args)] = 1
        specs.append(ANY)
        args.append(held)
        out_specs.append(ANY)
        out_shape.append(jax.ShapeDtypeStruct(held.shape, BF16))
    outs = pl.pallas_call(
        kernel,
        grid_spec=pltpu.PrefetchScalarGridSpec(
            num_scalar_prefetch=1,
            grid=(1,),
            in_specs=specs + [ANY] * len(after),
            out_specs=out_specs,
            scratch_shapes=[pltpu.SemaphoreType.DMA] if held is not None else [],
        ),
        out_shape=out_shape,
        input_output_aliases=alias,
        compiler_params=pltpu.CompilerParams(vmem_limit_bytes=SMALL),
        cost_estimate=cost(LONG),
        name="relay",
    )(pos, *args, *after)
    return outs[0], (outs[1] if held is not None else None)


def store_last(pos, came, held, after):
    parts = held.shape[0]

    def kernel(pos_ref, a_ref, b_ref, *refs):
        out_ref, sem = refs[-2:]
        rank, way, place = pos_ref[0], pos_ref[1], pos_ref[2]
        ends = (
            (place == parts - 1, a_ref, rank - way * (parts - 1)),
            (place == 0, b_ref, rank + way * (parts - 1)),
        )
        for at_end, came_ref, at in ends:
            copy = pltpu.make_async_copy(came_ref, out_ref.at[lax.clamp(0, at, parts - 1)], sem)

            @pl.when(at_end)
            def _():
                copy.start()
                copy.wait()

    return pl.pallas_call(
        kernel,
        grid_spec=pltpu.PrefetchScalarGridSpec(
            num_scalar_prefetch=1,
            grid=(1,),
            in_specs=[pl.BlockSpec(held.shape[1:], lambda i, w: (0, 0))] * 2 + [ANY] * (1 + len(after)),
            out_specs=ANY,
            scratch_shapes=[pltpu.SemaphoreType.DMA],
        ),
        out_shape=jax.ShapeDtypeStruct(held.shape, BF16),
        input_output_aliases={3: 0},
        compiler_params=pltpu.CompilerParams(vmem_limit_bytes=SMALL),
        cost_estimate=cost(SHORT),
        name="store_last",
    )(pos, *came, held, *after)


def first_block(pos, flow, partial):
    parts, rows, width = partial.shape

    def there(i, w):
        way = w[1] if flow == 0 else -w[1]
        return lax.clamp(0, w[0] + way * (parts - 1), parts - 1), 0, 0

    def kernel(pos_ref, p_ref, out_ref):
        out_ref[...] = p_ref[...]

    return pl.pallas_call(
        kernel,
        grid_spec=pltpu.PrefetchScalarGridSpec(
            num_scalar_prefetch=1,
            grid=(1,),
            in_specs=[pl.BlockSpec((None, rows, width), there)],
            out_specs=pl.BlockSpec((rows, width), lambda i, w: (0, 0)),
        ),
        out_shape=jax.ShapeDtypeStruct((rows, width), BF16),
        compiler_params=pltpu.CompilerParams(vmem_limit_bytes=SMALL),
        cost_estimate=cost(SHORT),
        name="first_block",
    )(pos, partial)


def norm_terms(p_ref, a_ref, b_ref, res_ref, grad_ref, gain_ref, at):
    proj = p_ref[:, at].astype(F32) + a_ref[:, at].astype(F32) + b_ref[:, at].astype(F32)
    z = res_ref[:, at].astype(F32) + proj
    scaled = gain_ref[:, at].astype(F32) * grad_ref[:, at].astype(F32)
    return z, scaled


def norm_specs(ins, half, chunk, at):
    _, rows, wide = ins[0].shape
    once = pl.Buffered(1)
    whole = pl.BlockSpec((rows, wide), lambda i, r: (0, 0), pipeline_mode=once)
    own = pl.BlockSpec((None, rows, half), lambda i, r: (0, chunk, at), pipeline_mode=once)
    mine = pl.BlockSpec((None, rows, wide), lambda i, r: (r[0], 0, 0), pipeline_mode=once)
    return [mine, whole, whole, own, own, pl.BlockSpec((1, half), lambda i, r: (0, at))]


def norm_sums(pos, ins, half, chunk, at, sums, after):
    rows = ins[0].shape[1]
    cols = divisor(half, 1024)

    def kernel(pos_ref, *refs):
        square_ref, cross_ref = refs[-2:]

        def step(i, sums):
            z, scaled = norm_terms(*refs[:6], pl.ds(pl.multiple_of(i * cols, cols), cols))
            square, cross = sums
            for j in range(0, cols, 128):
                zj = z[:, j : j + 128]
                square = square + zj * zj
                cross = cross + zj * scaled[:, j : j + 128]
            return square, cross

        zero = jnp.zeros((rows, 128), F32)
        start = (zero, zero) if sums is None else (refs[6][...], refs[7][...])
        square_ref[...], cross_ref[...] = lax.fori_loop(0, half // cols, step, start)

    stat = pl.BlockSpec((rows, 128), lambda i, r: (0, 0))
    before = [] if sums is None else list(sums)
    return pl.pallas_call(
        kernel,
        grid_spec=pltpu.PrefetchScalarGridSpec(
            num_scalar_prefetch=1,
            grid=(1,),
            in_specs=norm_specs(ins, half, chunk, at) + [stat] * len(before) + [ANY] * len(after),
            out_specs=[stat, stat],
        ),
        out_shape=[jax.ShapeDtypeStruct((rows, 128), F32)] * 2,
        compiler_params=pltpu.CompilerParams(vmem_limit_bytes=LIMIT),
        cost_estimate=cost(LONG),
        name="norm_sums",
    )(pos, *ins, *before, *after)


def norm_out(pos, ins, half, chunk, sums, proj_out, after):
    parts, rows, wide = ins[0][1][0].shape
    cols = divisor(half, 1024)
    n, width = len(ins), ins[0][1][3].shape[2]
    with_b = proj_out

    def kernel(pos_ref, *refs):
        square_ref, cross_ref = refs[6 * n], refs[6 * n + 1]
        if with_b is None:
            out_ref, held_ref, sem = refs[-3:]
        else:
            out_ref, held_ref, rest_ref, sem = refs[-4:]
        inv = lax.rsqrt(jnp.sum(square_ref[...], axis=-1, keepdims=True) / width + EPS)
        slope = inv * inv * inv * (jnp.sum(cross_ref[...], axis=-1, keepdims=True) / width)
        for j in range(n):
            to_ref = out_ref if j == 0 else rest_ref.at[j - 1]

            def step(i, carry):
                here = pl.ds(pl.multiple_of(i * cols, cols), cols)
                z, scaled = norm_terms(*refs[6 * j : 6 * j + 6], here)
                to_ref[:, here] = (inv * scaled - z * slope).astype(BF16)
                return carry

            lax.fori_loop(0, half // cols, step, 0)
        if with_b is not None:
            p_ref = refs[6 * n + 2]
            b = project_rows(out_ref[:, :half], p_ref[:, :half])
            for j in range(1, n):
                b = b + project_rows(rest_ref[j - 1], p_ref[:, j * half : (j + 1) * half])
            a = sum(refs[j][:, half:].astype(F32) for j in range(3))
            out_ref[:, half:] = (a + spread(b.astype(BF16), b.shape[1])).astype(BF16)
        else:
            out_ref[:, half:] = jnp.zeros((rows, wide - half), BF16)
        own = pltpu.make_async_copy(out_ref, held_ref.at[pos_ref[0]], sem)
        own.start()
        own.wait()

    stat = pl.BlockSpec((rows, 128), lambda i, r: (0, 0))
    specs, args = [], []
    for at, one in ins:
        specs += norm_specs(one, half, chunk, at)
        args += one
    specs, args = specs + [stat, stat], args + list(sums)
    scratch = [pltpu.SemaphoreType.DMA]
    if with_b is not None:
        specs.append(pl.BlockSpec(proj_out.shape, lambda i, r: (0, 0)))
        args.append(proj_out)
        scratch = [pltpu.VMEM((max(1, n - 1), rows, half), BF16)] + scratch
    return pl.pallas_call(
        kernel,
        grid_spec=pltpu.PrefetchScalarGridSpec(
            num_scalar_prefetch=1,
            grid=(1,),
            in_specs=specs + [ANY] * len(after),
            out_specs=[pl.BlockSpec((rows, wide), lambda i, r: (0, 0)), ANY],
            scratch_shapes=scratch,
        ),
        out_shape=[
            jax.ShapeDtypeStruct((rows, wide), BF16),
            jax.ShapeDtypeStruct((parts, rows, wide), BF16),
        ],
        compiler_params=pltpu.CompilerParams(vmem_limit_bytes=LIMIT),
        cost_estimate=cost(SHORT),
        name="norm_out",
    )(pos, *args, *after)


def tie(value, after):
    def kernel(value_ref, *refs):
        refs[-1][...] = value_ref[...]

    whole = pl.BlockSpec(value.shape, lambda i: (0,) * value.ndim)
    return pl.pallas_call(
        kernel,
        grid=(1,),
        in_specs=[whole] + [ANY] * len(after),
        out_specs=whole,
        out_shape=jax.ShapeDtypeStruct(value.shape, value.dtype),
        compiler_params=pltpu.CompilerParams(vmem_limit_bytes=SMALL),
        cost_estimate=cost(SHORT),
        name="tie",
    )(value, *after)


def touch(x):
    def kernel(x_ref, out_ref):
        out_ref[...] = jnp.zeros_like(out_ref)

    return pl.pallas_call(
        kernel,
        grid=(1,),
        in_specs=[ANY],
        out_specs=TOKEN_SPEC,
        out_shape=TOKEN,
        compiler_params=pltpu.CompilerParams(vmem_limit_bytes=SMALL),
        cost_estimate=cost(SHORT),
        name="touch",
    )(x)


def from_others(value, axis, size):
    return [value] + [
        lax.ppermute(value, axis, [(d, (d + shift) % size) for d in range(size)])
        for shift in range(1, size)
    ]


def sketch_slice(pos, gathered, segment_ids, kp, after):
    parts, rows, wide = gathered[0].shape
    extra, mine = 2 * kp, kp // parts
    chunks, tokens = len(gathered), segment_ids.shape[1]

    def kernel(pos_ref, *refs):
        out_ref, sum_ref = refs[-2:]
        example = lax.broadcasted_iota(jnp.int32, (8, tokens), 0)
        by_row = jnp.where(refs[chunks][...] == example, 1.0, 0.0).astype(BF16)
        same = lax.broadcasted_iota(jnp.int32, (tokens, tokens), 0) == lax.broadcasted_iota(
            jnp.int32, (tokens, tokens), 1
        )
        weights = project_rows(jnp.where(same, 1.0, 0.0).astype(BF16), by_row)
        weights = weights.reshape(parts, chunks, rows, 8)
        for e in range(EX_DEV):
            total = None
            for c in range(chunks):
                both = refs[c][...].reshape(parts * rows, extra)
                weight = weights[:, c].reshape(parts * rows, 8)[:, e : e + 1]
                part = (both.astype(F32) * weight).astype(BF16)
                term = lax.dot_general(
                    part, both, (((0,), (0,)), ((), ())), preferred_element_type=F32
                )
                total = term if total is None else total + term
            sum_ref[e] = total
        low = lax.broadcasted_iota(jnp.int32, (1, extra), 1) < kp
        for r in range(parts):

            @pl.when(pos_ref[0] == r)
            def _():
                for e in range(EX_DEV):
                    for i in range(mine // 2):
                        at = kp + r * mine + 2 * i
                        left, right = sum_ref[e, at : at + 1, :], sum_ref[e, at + 1 : at + 2, :]
                        out_ref[e : e + 1, i * extra : (i + 1) * extra] = jnp.where(
                            low, left, pltpu.roll(right, kp, 1)
                        )

    return pl.pallas_call(
        kernel,
        grid_spec=pltpu.PrefetchScalarGridSpec(
            num_scalar_prefetch=1,
            grid=(1,),
            in_specs=[pl.BlockSpec((parts, rows, extra), lambda i, w: (0, 0, wide // extra - 1))] * chunks
            + [pl.BlockSpec(segment_ids.shape, lambda i, w: (0, 0))]
            + [ANY] * len(after),
            out_specs=pl.BlockSpec((EX_DEV, mine * kp), lambda i, w: (0, 0)),
            scratch_shapes=[pltpu.VMEM((EX_DEV, extra, extra), F32)],
        ),
        out_shape=jax.ShapeDtypeStruct((EX_DEV, mine * kp), F32),
        compiler_params=pltpu.CompilerParams(vmem_limit_bytes=LIMIT),
        cost_estimate=cost(SHORT),
        name="sketch_slice",
    )(pos, *gathered, segment_ids, *after)


def score_terms(pos, sketches, queries, after):
    size = len(sketches)
    n, depth = queries.shape

    def kernel(pos_ref, *refs):
        out_ref, all_ref = refs[-2:]
        for back in range(size):
            all_ref[lax.rem(pos_ref[3] - back + size, size)] = refs[back][...]
        for d in range(size):
            rest, total = all_ref[d], None
            for _ in range(3):
                part = rest.astype(BF16)
                rest = rest - part.astype(F32)
                term = project_rows(part, refs[size][...])
                total = term if total is None else total + term
            out_ref[d * EX_DEV : (d + 1) * EX_DEV, :] = total

    return pl.pallas_call(
        kernel,
        grid_spec=pltpu.PrefetchScalarGridSpec(
            num_scalar_prefetch=1,
            grid=(1,),
            in_specs=[pl.BlockSpec((EX_DEV, depth), lambda i, w: (0, 0))] * size
            + [pl.BlockSpec((n, depth), lambda i, w: (0, 0))]
            + [ANY] * len(after),
            out_specs=pl.BlockSpec((size * EX_DEV, n), lambda i, w: (0, 0)),
            scratch_shapes=[pltpu.VMEM((size, EX_DEV, depth), F32)],
        ),
        out_shape=jax.ShapeDtypeStruct((size * EX_DEV, n), F32),
        compiler_params=pltpu.CompilerParams(vmem_limit_bytes=LIMIT),
        cost_estimate=cost(SHORT),
        name="score_terms",
    )(pos, *sketches, queries, *after)


def score_sum(pos, terms, after):
    size = len(terms)
    shape = terms[0].shape

    def kernel(pos_ref, *refs):
        out_ref, all_ref = refs[-2:]
        for back in range(size):
            all_ref[lax.rem(pos_ref[0] - back + size, size)] = refs[back][...]
        total = all_ref[0]
        for d in range(1, size):
            total = total + all_ref[d]
        out_ref[...] = total

    whole = pl.BlockSpec(shape, lambda i, w: (0, 0))
    return pl.pallas_call(
        kernel,
        grid_spec=pltpu.PrefetchScalarGridSpec(
            num_scalar_prefetch=1,
            grid=(1,),
            in_specs=[whole] * size + [ANY] * len(after),
            out_specs=whole,
            scratch_shapes=[pltpu.VMEM((size,) + shape, F32)],
        ),
        out_shape=jax.ShapeDtypeStruct(shape, F32),
        compiler_params=pltpu.CompilerParams(vmem_limit_bytes=SMALL),
        cost_estimate=cost(SHORT),
        name="score_sum",
    )(pos, *terms, *after)


def body(inputs, residual, out_grad, norm_gain, w_out, proj_in, proj_out, queries, segment_ids):
    parts = lax.axis_size("tensor")
    rank = lax.axis_index("tensor")
    queriers = lax.axis_size("query")
    q_rank = lax.axis_index("query")
    tokens = inputs.shape[1]
    share = tokens // parts
    chunks = max(1, min(CHUNKS, share // 16))
    rows = share // chunks
    by_share = inputs.reshape(parts, chunks, rows, inputs.shape[2])
    gain = norm_gain.reshape(1, -1)
    half = w_out.shape[1] // HALVES
    kp = proj_out.shape[0]

    up = 1 - 2 * lax.rem(q_rank, 2)
    pos = jnp.stack([rank, up, jnp.where(up == 1, rank, parts - 1 - rank), q_rank]).astype(jnp.int32)

    def pairs(flow, low, high):
        out = []
        for q in range(queriers):
            way = 1 if (q % 2 == 0) == (flow == 0) else -1
            for t in range(parts):
                spot = t if way == 1 else parts - 1 - t
                if low <= spot <= min(high, parts - 2):
                    out.append((t * queriers + q, (t + way) * queriers + q))
        return out

    work, marks, resident = [], [], []
    partials, totals, result = {}, {}, [None]

    def forward(c, h, piece, pieces, after):
        partials[c, h], mark = forward_piece(
            by_share,
            w_out,
            c,
            HALVES,
            h,
            2 * kp,
            piece,
            pieces,
            partials.get((c, h)),
            after,
        )
        if h == 0 and piece == pieces - 1:
            partials[c, h] = forward_extra(by_share, proj_in, c, partials[c, h], [mark])
        return mark

    def backward(c, blocks, total, last, piece, pieces, after):
        held = result[0] if last else totals.get(c)
        some = resident[piece * QUARTERS // pieces : (piece + 1) * QUARTERS // pieces]
        done, mark = backward_piece(
            blocks, some, c, chunks, HALVES, piece, pieces, total, last, held, after
        )
        if last:
            result[0] = done
        else:
            totals[c] = done
        return mark

    def do_one(after, touching=False):
        if work:
            marks[:] = [work.pop(0)[1](after)]
        elif touching:
            marks[:] = [touch(after[0])]

    def finish(key, after):
        while any(k == key for k, _ in work):
            do_one(list(marks) + after)

    def load(count, after):
        for _ in range(count):
            resident.append(load_weights(w_out, len(resident), QUARTERS, after))
            after = [resident[-1]]
        marks[:] = after

    def add_forward(c, h, pieces):
        for piece in range(pieces):
            work.append(((c, h), functools.partial(forward, c, h, piece, pieces)))

    add_forward(0, 0, 1)
    finish((0, 0), [])
    gathered = []
    for slot in range(chunks + 1):
        rs, ag = slot < chunks, slot > 0
        came, held, sent, before = {}, {}, {}, None
        if ag:
            if slot == chunks:
                residual, out_grad, proj_out = in_hbm(residual), in_hbm(out_grad), in_hbm(proj_out)
            ins = [
                [partials[slot - 1, h], arrived[h, 0], arrived[h, 1], residual, out_grad, gain]
                for h in range(HALVES)
            ]
            sums = None
            for h in range(HALVES):
                sums = norm_sums(pos, ins[h], half, slot - 1, h, sums, list(marks))
            grad = [None] * HALVES
            grad[0], held[0] = norm_out(
                pos, list(enumerate(ins)), half, slot - 1, sums, proj_out, []
            )
        for k in range(parts):
            gather_now, reduce_now = ag and k <= parts - 2, rs and k >= 1
            if not gather_now and not reduce_now:
                continue
            for h in range(HALVES):
                if k == 0 and h > 0:
                    if rs and slot > 1:
                        add_forward(slot, h, PIECES)
                    do_one([sent[h - 1, 1]])
                    grad[h], held[h] = norm_out(
                        pos, [(h, ins[h])], half, slot - 1, sums, None, list(marks)
                    )
                if reduce_now:
                    if slot == 0 and k == 1 and h > 0:
                        add_forward(0, h, 1)
                        do_one([sent[h - 1, 1]])
                    finish((slot, h), [sent[h - 1, 1]] if h > 0 else [])
                for flow in range(2):
                    if k == 0:
                        x = before = grad[h]
                    elif (h, flow) not in came:
                        x = first_block(pos, flow, partials[slot, h])
                    else:
                        x, held[h] = relay(
                            pos,
                            flow,
                            k,
                            partials[slot, h] if reduce_now else None,
                            came[h, flow],
                            held.get(h),
                            list(marks) + ([] if before is None else [before]),
                        )
                        before = x
                    came[h, flow] = lax.ppermute(
                        x,
                        ("tensor", "query"),
                        pairs(flow, 0 if reduce_now else k, parts - 2 if gather_now else k - 1),
                    )
                    sent[h, flow] = x
                    if slot == chunks - 1 and flow == 1 and slot > 0:
                        if (k, h) == (parts - 2, HALVES - 1):
                            load(1, [x])
                            continue
                        if (k, h) == (parts - 1, HALVES - 1):
                            load(QUARTERS - len(resident), [x])
                            continue
                    if slot == 0 and k == 2 and (h, flow) == (HALVES - 1, 1) and chunks > 1 and HALVES > 1:
                        add_forward(1, 1, 2 * PIECES)
                        do_one([x])
                        continue
                    if slot == 0 and k == parts - 1 and (h, flow) == (0, 1):
                        do_one([x])
                        continue
                    if slot == 0 and k == parts - 1 and (h, flow) == (HALVES - 1, 1) and chunks > 1:
                        work.insert(0, ((1, 0), functools.partial(forward, 1, 0, 0, 1)))
                    if slot == 0 and work and work[0][0] == (1, 1):
                        continue
                    if k > 0 and (slot > 0 or k > 1) and not (slot == 1 and work and k == 1 and flow == 0):
                        if slot == chunks and flow == 0:
                            marks[:] = [touch(x)]
                        else:
                            do_one([x], slot == chunks)
                if k == 0 and slot == chunks and h == HALVES - 1:
                    marks[:] = [touch(sent[h, 1])]
        if ag:
            if slot + 1 < chunks:
                add_forward(slot + 1, 0, PIECES)
            if rs:
                blocks = [(h, held[h]) for h in range(HALVES)]
                for piece in range(PIECES):
                    work.append(
                        (
                            ("b", slot - 1),
                            functools.partial(backward, slot - 1, blocks, None, True, piece, PIECES),
                        )
                    )
            else:
                while work:
                    do_one(list(marks))
                marks[:] = [touch(came[0, 0])]
                held[0] = store_last(pos, (came[0, 0], came[0, 1]), held[0], list(marks))
            gathered.append(held[0])
        arrived = came
    last = chunks - 1
    sketch = sketch_slice(pos, gathered, segment_ids, kp, [])
    marks[:] = [backward(last, [(0, held[0])], None, HALVES == 1, 0, 1, [sketch])]
    for h in range(1, HALVES):
        marks[:] = [tie(marks[0], [came[h, 0]])]
        held[h] = store_last(pos, (came[h, 0], came[h, 1]), held[h], list(marks))
    terms = score_terms(pos, from_others(sketch, "query", queriers), queries, list(marks))
    for h in range(1, HALVES):
        marks[:] = [backward(last, [(h, held[h])], totals.get(last), h == HALVES - 1, 0, 1, [terms])]
    scores = score_sum(pos, from_others(terms, "tensor", parts), list(marks))
    return (result[0].reshape(1, tokens, -1), scores)


def solution(mesh):
    return jax.shard_map(
        body,
        mesh=mesh,
        in_specs=(
            P(("groups", "dp", "query"), None, "tensor"),
            P(("groups", "dp", "query"), "tensor", None),
            P(("groups", "dp", "query"), "tensor", None),
            P(),
            P("tensor", None),
            P(None, "tensor"),
            P(),
            P("query", "tensor"),
            P(("groups", "dp", "query"), None),
        ),
        out_specs=(P(("groups", "dp", "query"), None, "tensor"), P(("groups", "dp"), "query")),
        check_vma=False,
    )
```

```python
import functools

import jax
import jax.numpy as jnp
from jax import lax
from jax.experimental import pallas as pl
from jax.experimental.pallas import tpu as pltpu
from jax.sharding import PartitionSpec as P

EX_DEV = 4
EPS = 1e-05
CHUNKS = 2
HALVES = 2
PIECES = 2
SHORT, LONG = 0.2, 5.0
SMALL, LIMIT, LARGE = 5 * 1024 * 1024, 9 * 1024 * 1024, 24 * 1024 * 1024
QUARTERS = 4

F32, BF16 = jnp.float32, jnp.bfloat16
ANY = pl.BlockSpec(memory_space=pl.ANY)
TOKEN = jax.ShapeDtypeStruct((8, 128), F32)
TOKEN_SPEC = pl.BlockSpec((8, 128), lambda *_: (0, 0))


def divisor(total, wanted):
    size = min(total, wanted)
    while total % size:
        size //= 2
    return size


def cost(microseconds):
    return pl.CostEstimate(flops=0, bytes_accessed=int(microseconds * 3.6e6), transcendentals=0)


def in_hbm(x):
    return pltpu.with_memory_space_constraint(x, pltpu.HBM)


def project_rows(values, matrix):
    return lax.dot_general(
        values, matrix, (((1,), (1,)), ((), ())), preferred_element_type=F32
    )


def spread(values, first):
    k = values.shape[1]
    row = lax.broadcasted_iota(jnp.int32, (k, 2 * k), 0)
    col = lax.broadcasted_iota(jnp.int32, (k, 2 * k), 1)
    return jnp.dot(values, jnp.where(col == row + first, 1.0, 0.0).astype(BF16), preferred_element_type=F32)


def forward_extra(by_share, proj_in, chunk, held, after):
    parts, _, rows, depth = by_share.shape
    extra = 2 * proj_in.shape[0]
    at = held.shape[2] // extra - 1

    def kernel(x_ref, p_ref, *refs):
        part = project_rows(x_ref[...].reshape(parts * rows, depth), p_ref[...]).astype(BF16)
        refs[-1][...] = spread(part, 0).astype(BF16).reshape(parts, rows, extra)

    return pl.pallas_call(
        kernel,
        grid=(1,),
        in_specs=[
            pl.BlockSpec((parts, None, rows, depth), lambda i: (0, chunk, 0, 0)),
            pl.BlockSpec(proj_in.shape, lambda i: (0, 0)),
        ]
        + [ANY] * (1 + len(after)),
        out_specs=pl.BlockSpec((parts, rows, extra), lambda i: (0, 0, at)),
        out_shape=jax.ShapeDtypeStruct(held.shape, BF16),
        input_output_aliases={2: 0},
        compiler_params=pltpu.CompilerParams(vmem_limit_bytes=LIMIT),
        cost_estimate=cost(SHORT),
        name="forward_extra",
    )(by_share, proj_in, held, *after)


def forward_piece(by_share, w_out, chunk, halves, half_at, extra, piece, pieces, held, after):
    parts, _, rows, depth = by_share.shape
    half = w_out.shape[1] // halves
    span = half // pieces
    cols = divisor(span, max(256, span // 4))
    steps = span // cols
    base = half_at * half + piece * span

    def kernel(x_ref, w_ref, *refs):
        out_ref, tok_ref, held_ref, sems = refs[-4:]
        i = pl.program_id(0)

        def copy(j):
            columns = pl.ds(pl.multiple_of(base + j * cols, cols), cols)
            return pltpu.make_async_copy(w_ref.at[:, columns], held_ref.at[j], sems.at[j])

        @pl.when(i == 0)
        def _():
            for j in range(steps):
                copy(j).start()

        copy(i).wait()
        x = x_ref[...].reshape(parts * rows, depth)
        y = jnp.dot(x, held_ref[i], preferred_element_type=F32).astype(BF16)
        out_ref[...] = y.reshape(parts, rows, cols)
        tok_ref[...] = jnp.zeros_like(tok_ref)

    more = ([] if held is None else [held]) + after
    return pl.pallas_call(
        kernel,
        grid=(steps,),
        in_specs=[
            pl.BlockSpec(
                (parts, None, rows, depth), lambda i: (0, chunk, 0, 0), pipeline_mode=pl.Buffered(1)
            )
        ]
        + [ANY] * (1 + len(more)),
        out_specs=[
            pl.BlockSpec((parts, rows, cols), lambda i: (0, 0, piece * steps + i)),
            TOKEN_SPEC,
        ],
        out_shape=[jax.ShapeDtypeStruct((parts, rows, half + extra), BF16), TOKEN],
        scratch_shapes=[pltpu.VMEM((steps, depth, cols), BF16), pltpu.SemaphoreType.DMA((steps,))],
        input_output_aliases={} if held is None else {2: 0},
        compiler_params=pltpu.CompilerParams(vmem_limit_bytes=LARGE),
        cost_estimate=cost(SHORT),
        name="forward_piece",
    )(in_hbm(by_share) if chunk == 0 and half_at == 0 else by_share, in_hbm(w_out), *more)


def load_weights(w_out, piece, pieces, after):
    rows = w_out.shape[0] // pieces
    width = w_out.shape[1]

    def kernel(w_ref, *refs):
        out_ref, sem = refs[-2:]
        copy = pltpu.make_async_copy(w_ref.at[pl.ds(piece * rows, rows)], out_ref, sem)
        copy.start()
        copy.wait()

    return pl.pallas_call(
        kernel,
        in_specs=[ANY] * (1 + len(after)),
        out_specs=pl.BlockSpec(memory_space=pltpu.VMEM),
        out_shape=pltpu.VMEM((rows, width), BF16),
        scratch_shapes=[pltpu.SemaphoreType.DMA],
        compiler_params=pltpu.CompilerParams(vmem_limit_bytes=SMALL),
        cost_estimate=cost(SHORT),
        name="load_weights",
    )(in_hbm(w_out), *after)


def load_rows(residual, out_grad, chunk, rows, after):
    width = residual.shape[2]

    def kernel(*refs):
        out_refs, sems = refs[-3:-1], refs[-1]
        copies = [
            pltpu.make_async_copy(refs[j].at[0, pl.ds(chunk * rows, rows)], out_refs[j], sems.at[j])
            for j in range(2)
        ]
        for copy in copies:
            copy.start()
        for copy in copies:
            copy.wait()

    return pl.pallas_call(
        kernel,
        in_specs=[ANY] * (2 + len(after)),
        out_specs=[pl.BlockSpec(memory_space=pltpu.VMEM)] * 2,
        out_shape=[pltpu.VMEM((rows, width), BF16)] * 2,
        scratch_shapes=[pltpu.SemaphoreType.DMA((2,))],
        compiler_params=pltpu.CompilerParams(vmem_limit_bytes=SMALL),
        cost_estimate=cost(SHORT),
        name="load_rows",
    )(in_hbm(residual), in_hbm(out_grad), *after)


def in_vmem(x):
    return pltpu.with_memory_space_constraint(x, pltpu.VMEM)


def backward_piece(blocks, weights, chunk, chunks, halves, piece, pieces, total, last, held, after):
    parts, rows, _ = blocks[0][1].shape
    some, width = weights[0].shape
    half, span = width // halves, some * len(weights)
    cols = divisor(some, 256)
    n, m = len(blocks), len(weights)

    def kernel(*refs):
        out_ref, tok_ref = refs[-2:]
        for j in range(m):

            def step(i, carry):
                here = pl.ds(pl.multiple_of(i * cols, cols), cols)
                there = pl.ds(pl.multiple_of(j * some + i * cols, cols), cols)
                y = None if total is None else refs[n + m][:, :, there].reshape(parts * rows, cols)
                for b, (at, _) in enumerate(blocks):
                    g = refs[b][...].reshape(parts * rows, half)
                    term = project_rows(g, refs[n + j][here, at * half : (at + 1) * half])
                    y = term if y is None else y + term
                out_ref[:, :, there] = y.astype(out_ref.dtype).reshape(parts, rows, cols)
                return carry

            lax.fori_loop(0, some // cols, step, 0)
        tok_ref[...] = jnp.zeros_like(tok_ref)

    once = pl.Buffered(1)
    here = pl.BlockSpec((parts, rows, span), lambda i: (0, 0, piece))
    if last:
        out_spec = pl.BlockSpec((parts, None, rows, span), lambda i: (0, chunk, 0, piece))
        out_shape = jax.ShapeDtypeStruct((parts, chunks, rows, span * pieces), BF16)
    else:
        out_spec, out_shape = here, jax.ShapeDtypeStruct((parts, rows, span * pieces), F32)
    sums = [] if total is None else [total]
    extra = ([] if held is None else [held]) + after
    return pl.pallas_call(
        kernel,
        grid=(1,),
        in_specs=[pl.BlockSpec((parts, rows, half), lambda i: (0, 0, 0), pipeline_mode=once)] * n
        + [pl.BlockSpec(memory_space=pltpu.VMEM)] * m
        + [pl.BlockSpec((parts, rows, span), lambda i: (0, 0, piece), pipeline_mode=once)] * len(sums)
        + [ANY] * len(extra),
        out_specs=[out_spec, TOKEN_SPEC],
        out_shape=[out_shape, TOKEN],
        input_output_aliases={} if held is None else {n + m + len(sums): 0},
        compiler_params=pltpu.CompilerParams(vmem_limit_bytes=LIMIT),
        cost_estimate=cost(SHORT),
        name="backward_piece",
    )(
        *[g for _, g in blocks],
        *[in_vmem(w) for w in weights],
        *sums,
        *extra,
    )


def relay(pos, flow, k, partial, came, held, after):
    rows, width = came.shape
    parts = (partial if held is None else held).shape[0]
    n_in = 1 + (partial is not None) + (held is not None) + len(after)

    def far(pos_ref, steps):
        way = pos_ref[1] if flow == 0 else -pos_ref[1]
        return lax.clamp(0, pos_ref[0] + way * steps, parts - 1)

    def kernel(pos_ref, *refs):
        came_ref, x_ref = refs[0], refs[n_in]
        place = pos_ref[2] if flow == 0 else parts - 1 - pos_ref[2]
        if held is not None:
            store = pltpu.make_async_copy(came_ref, refs[n_in + 1].at[far(pos_ref, -k)], refs[-1])
            pl.when(place >= k)(store.start)
        if partial is not None:

            @pl.when(place < k)
            def _():
                x_ref[...] = (came_ref[...].astype(F32) + refs[1][...].astype(F32)).astype(BF16)

            @pl.when(place >= k)
            def _():
                x_ref[...] = came_ref[...]

        else:
            x_ref[...] = came_ref[...]
        if held is not None:
            pl.when(place >= k)(store.wait)

    line = jax.ShapeDtypeStruct((rows, width), BF16)
    whole = pl.BlockSpec((rows, width), lambda i, w: (0, 0), pipeline_mode=pl.Buffered(1))
    args, specs, out_specs, out_shape, alias = [came], [whole], [whole], [line], {}
    if partial is not None:
        term = pl.BlockSpec(
            (None, rows, width),
            lambda i, w: (far(w, parts - k), 0, 0),
            pipeline_mode=pl.Buffered(1),
        )
        specs.append(term)
        args.append(partial)
    if held is not None:
        alias[1 + len(args)] = 1
        specs.append(ANY)
        args.append(held)
        out_specs.append(ANY)
        out_shape.append(jax.ShapeDtypeStruct(held.shape, BF16))
    outs = pl.pallas_call(
        kernel,
        grid_spec=pltpu.PrefetchScalarGridSpec(
            num_scalar_prefetch=1,
            grid=(1,),
            in_specs=specs + [ANY] * len(after),
            out_specs=out_specs,
            scratch_shapes=[pltpu.SemaphoreType.DMA] if held is not None else [],
        ),
        out_shape=out_shape,
        input_output_aliases=alias,
        compiler_params=pltpu.CompilerParams(vmem_limit_bytes=SMALL),
        cost_estimate=cost(LONG),
        name="relay",
    )(pos, *args, *after)
    return outs[0], (outs[1] if held is not None else None)


def store_last(pos, came, held, after):
    parts = held.shape[0]

    def kernel(pos_ref, a_ref, b_ref, *refs):
        out_ref, sem = refs[-2:]
        rank, way, place = pos_ref[0], pos_ref[1], pos_ref[2]
        ends = (
            (place == parts - 1, a_ref, rank - way * (parts - 1)),
            (place == 0, b_ref, rank + way * (parts - 1)),
        )
        for at_end, came_ref, at in ends:
            copy = pltpu.make_async_copy(came_ref, out_ref.at[lax.clamp(0, at, parts - 1)], sem)

            @pl.when(at_end)
            def _():
                copy.start()
                copy.wait()

    return pl.pallas_call(
        kernel,
        grid_spec=pltpu.PrefetchScalarGridSpec(
            num_scalar_prefetch=1,
            grid=(1,),
            in_specs=[pl.BlockSpec(held.shape[1:], lambda i, w: (0, 0))] * 2 + [ANY] * (1 + len(after)),
            out_specs=ANY,
            scratch_shapes=[pltpu.SemaphoreType.DMA],
        ),
        out_shape=jax.ShapeDtypeStruct(held.shape, BF16),
        input_output_aliases={3: 0},
        compiler_params=pltpu.CompilerParams(vmem_limit_bytes=SMALL),
        cost_estimate=cost(SHORT),
        name="store_last",
    )(pos, *came, held, *after)


def first_block(pos, flow, partial):
    parts, rows, width = partial.shape

    def there(i, w):
        way = w[1] if flow == 0 else -w[1]
        return lax.clamp(0, w[0] + way * (parts - 1), parts - 1), 0, 0

    def kernel(pos_ref, p_ref, out_ref):
        out_ref[...] = p_ref[...]

    return pl.pallas_call(
        kernel,
        grid_spec=pltpu.PrefetchScalarGridSpec(
            num_scalar_prefetch=1,
            grid=(1,),
            in_specs=[pl.BlockSpec((None, rows, width), there)],
            out_specs=pl.BlockSpec((rows, width), lambda i, w: (0, 0)),
        ),
        out_shape=jax.ShapeDtypeStruct((rows, width), BF16),
        compiler_params=pltpu.CompilerParams(vmem_limit_bytes=SMALL),
        cost_estimate=cost(SHORT),
        name="first_block",
    )(pos, partial)


def norm_terms(p_ref, a_ref, b_ref, res_ref, grad_ref, gain_ref, at):
    proj = p_ref[:, at].astype(F32) + a_ref[:, at].astype(F32) + b_ref[:, at].astype(F32)
    z = res_ref[:, at].astype(F32) + proj
    scaled = gain_ref[:, at].astype(F32) * grad_ref[:, at].astype(F32)
    return z, scaled


def norm_specs(ins, half, chunk, at):
    _, rows, wide = ins[0].shape
    once = pl.Buffered(1)
    whole = pl.BlockSpec((rows, wide), lambda i, r: (0, 0), pipeline_mode=once)
    own = pl.BlockSpec((rows, half), lambda i, r: (0, at), pipeline_mode=once)
    mine = pl.BlockSpec((None, rows, wide), lambda i, r: (r[0], 0, 0), pipeline_mode=once)
    return [mine, whole, whole, own, own, pl.BlockSpec((1, half), lambda i, r: (0, at))]


def norm_sums(pos, ins, half, chunk, at, sums, after):
    rows = ins[0].shape[1]
    cols = divisor(half, 1024)

    def kernel(pos_ref, *refs):
        square_ref, cross_ref = refs[-2:]

        def step(i, sums):
            z, scaled = norm_terms(*refs[:6], pl.ds(pl.multiple_of(i * cols, cols), cols))
            square, cross = sums
            for j in range(0, cols, 128):
                zj = z[:, j : j + 128]
                square = square + zj * zj
                cross = cross + zj * scaled[:, j : j + 128]
            return square, cross

        zero = jnp.zeros((rows, 128), F32)
        start = (zero, zero) if sums is None else (refs[6][...], refs[7][...])
        square_ref[...], cross_ref[...] = lax.fori_loop(0, half // cols, step, start)

    stat = pl.BlockSpec((rows, 128), lambda i, r: (0, 0))
    before = [] if sums is None else list(sums)
    return pl.pallas_call(
        kernel,
        grid_spec=pltpu.PrefetchScalarGridSpec(
            num_scalar_prefetch=1,
            grid=(1,),
            in_specs=norm_specs(ins, half, chunk, at) + [stat] * len(before) + [ANY] * len(after),
            out_specs=[stat, stat],
        ),
        out_shape=[jax.ShapeDtypeStruct((rows, 128), F32)] * 2,
        compiler_params=pltpu.CompilerParams(vmem_limit_bytes=LIMIT),
        cost_estimate=cost(LONG),
        name="norm_sums",
    )(pos, *ins, *before, *after)


def norm_out(pos, ins, half, chunk, sums, proj_out, after):
    parts, rows, wide = ins[0][1][0].shape
    cols = divisor(half, 1024)
    n, width = len(ins), ins[0][1][3].shape[1]
    with_b = proj_out

    def kernel(pos_ref, *refs):
        square_ref, cross_ref = refs[6 * n], refs[6 * n + 1]
        if with_b is None:
            out_ref, held_ref, sem = refs[-3:]
        else:
            out_ref, held_ref, rest_ref, sem = refs[-4:]
        inv = lax.rsqrt(jnp.sum(square_ref[...], axis=-1, keepdims=True) / width + EPS)
        slope = inv * inv * inv * (jnp.sum(cross_ref[...], axis=-1, keepdims=True) / width)
        for j in range(n):
            to_ref = out_ref if j == 0 else rest_ref.at[j - 1]

            def step(i, carry):
                here = pl.ds(pl.multiple_of(i * cols, cols), cols)
                z, scaled = norm_terms(*refs[6 * j : 6 * j + 6], here)
                to_ref[:, here] = (inv * scaled - z * slope).astype(BF16)
                return carry

            lax.fori_loop(0, half // cols, step, 0)
        if with_b is not None:
            p_ref = refs[6 * n + 2]
            b = project_rows(out_ref[:, :half], p_ref[:, :half])
            for j in range(1, n):
                b = b + project_rows(rest_ref[j - 1], p_ref[:, j * half : (j + 1) * half])
            a = sum(refs[j][:, half:].astype(F32) for j in range(3))
            out_ref[:, half:] = (a + spread(b.astype(BF16), b.shape[1])).astype(BF16)
        else:
            out_ref[:, half:] = jnp.zeros((rows, wide - half), BF16)
        own = pltpu.make_async_copy(out_ref, held_ref.at[pos_ref[0]], sem)
        own.start()
        own.wait()

    stat = pl.BlockSpec((rows, 128), lambda i, r: (0, 0))
    specs, args = [], []
    for at, one in ins:
        specs += norm_specs(one, half, chunk, at)
        args += one
    specs, args = specs + [stat, stat], args + list(sums)
    scratch = [pltpu.SemaphoreType.DMA]
    if with_b is not None:
        specs.append(
            pl.BlockSpec(proj_out.shape, lambda i, r: (0, 0), pipeline_mode=pl.Buffered(1))
        )
        args.append(proj_out)
        scratch = [pltpu.VMEM((max(1, n - 1), rows, half), BF16)] + scratch
    return pl.pallas_call(
        kernel,
        grid_spec=pltpu.PrefetchScalarGridSpec(
            num_scalar_prefetch=1,
            grid=(1,),
            in_specs=specs + [ANY] * len(after),
            out_specs=[pl.BlockSpec((rows, wide), lambda i, r: (0, 0)), ANY],
            scratch_shapes=scratch,
        ),
        out_shape=[
            jax.ShapeDtypeStruct((rows, wide), BF16),
            jax.ShapeDtypeStruct((parts, rows, wide), BF16),
        ],
        compiler_params=pltpu.CompilerParams(vmem_limit_bytes=LIMIT),
        cost_estimate=cost(SHORT),
        name="norm_out",
    )(pos, *args, *after)


def tie(value, after):
    def kernel(value_ref, *refs):
        refs[-1][...] = value_ref[...]

    whole = pl.BlockSpec(value.shape, lambda i: (0,) * value.ndim)
    return pl.pallas_call(
        kernel,
        grid=(1,),
        in_specs=[whole] + [ANY] * len(after),
        out_specs=whole,
        out_shape=jax.ShapeDtypeStruct(value.shape, value.dtype),
        compiler_params=pltpu.CompilerParams(vmem_limit_bytes=SMALL),
        cost_estimate=cost(SHORT),
        name="tie",
    )(value, *after)


def touch(x):
    def kernel(x_ref, out_ref):
        out_ref[...] = jnp.zeros_like(out_ref)

    return pl.pallas_call(
        kernel,
        grid=(1,),
        in_specs=[ANY],
        out_specs=TOKEN_SPEC,
        out_shape=TOKEN,
        compiler_params=pltpu.CompilerParams(vmem_limit_bytes=SMALL),
        cost_estimate=cost(SHORT),
        name="touch",
    )(x)


def from_others(value, axis, size):
    return [value] + [
        lax.ppermute(value, axis, [(d, (d + shift) % size) for d in range(size)])
        for shift in range(1, size)
    ]


def sketch_slice(pos, gathered, segment_ids, kp, after):
    parts, rows, wide = gathered[0].shape
    extra, mine = 2 * kp, kp // parts
    chunks, tokens = len(gathered), segment_ids.shape[1]

    def kernel(pos_ref, *refs):
        out_ref, sum_ref = refs[-2:]
        example = lax.broadcasted_iota(jnp.int32, (8, tokens), 0)
        by_row = jnp.where(refs[chunks][...] == example, 1.0, 0.0).astype(BF16)
        same = lax.broadcasted_iota(jnp.int32, (tokens, tokens), 0) == lax.broadcasted_iota(
            jnp.int32, (tokens, tokens), 1
        )
        weights = project_rows(jnp.where(same, 1.0, 0.0).astype(BF16), by_row)
        weights = weights.reshape(parts, chunks, rows, 8)
        for e in range(EX_DEV):
            total = None
            for c in range(chunks):
                both = refs[c][...].reshape(parts * rows, extra)
                weight = weights[:, c].reshape(parts * rows, 8)[:, e : e + 1]
                part = (both.astype(F32) * weight).astype(BF16)
                term = lax.dot_general(
                    part, both, (((0,), (0,)), ((), ())), preferred_element_type=F32
                )
                total = term if total is None else total + term
            sum_ref[e] = total
        low = lax.broadcasted_iota(jnp.int32, (1, extra), 1) < kp
        for r in range(parts):

            @pl.when(pos_ref[0] == r)
            def _():
                for e in range(EX_DEV):
                    for i in range(mine // 2):
                        at = kp + r * mine + 2 * i
                        left, right = sum_ref[e, at : at + 1, :], sum_ref[e, at + 1 : at + 2, :]
                        out_ref[e : e + 1, i * extra : (i + 1) * extra] = jnp.where(
                            low, left, pltpu.roll(right, kp, 1)
                        )

    return pl.pallas_call(
        kernel,
        grid_spec=pltpu.PrefetchScalarGridSpec(
            num_scalar_prefetch=1,
            grid=(1,),
            in_specs=[pl.BlockSpec((parts, rows, extra), lambda i, w: (0, 0, wide // extra - 1))] * chunks
            + [pl.BlockSpec(segment_ids.shape, lambda i, w: (0, 0))]
            + [ANY] * len(after),
            out_specs=pl.BlockSpec((EX_DEV, mine * kp), lambda i, w: (0, 0)),
            scratch_shapes=[pltpu.VMEM((EX_DEV, extra, extra), F32)],
        ),
        out_shape=jax.ShapeDtypeStruct((EX_DEV, mine * kp), F32),
        compiler_params=pltpu.CompilerParams(vmem_limit_bytes=LIMIT),
        cost_estimate=cost(SHORT),
        name="sketch_slice",
    )(pos, *gathered, segment_ids, *after)


def score_terms(pos, sketches, queries, after):
    size = len(sketches)
    n, depth = queries.shape

    def kernel(pos_ref, *refs):
        out_ref, all_ref = refs[-2:]
        for back in range(size):
            all_ref[lax.rem(pos_ref[3] - back + size, size)] = refs[back][...]
        for d in range(size):
            rest, total = all_ref[d], None
            for _ in range(3):
                part = rest.astype(BF16)
                rest = rest - part.astype(F32)
                term = project_rows(part, refs[size][...])
                total = term if total is None else total + term
            out_ref[d * EX_DEV : (d + 1) * EX_DEV, :] = total

    return pl.pallas_call(
        kernel,
        grid_spec=pltpu.PrefetchScalarGridSpec(
            num_scalar_prefetch=1,
            grid=(1,),
            in_specs=[pl.BlockSpec((EX_DEV, depth), lambda i, w: (0, 0))] * size
            + [pl.BlockSpec((n, depth), lambda i, w: (0, 0))]
            + [ANY] * len(after),
            out_specs=pl.BlockSpec((size * EX_DEV, n), lambda i, w: (0, 0)),
            scratch_shapes=[pltpu.VMEM((size, EX_DEV, depth), F32)],
        ),
        out_shape=jax.ShapeDtypeStruct((size * EX_DEV, n), F32),
        compiler_params=pltpu.CompilerParams(vmem_limit_bytes=LIMIT),
        cost_estimate=cost(SHORT),
        name="score_terms",
    )(pos, *sketches, queries, *after)


def score_sum(pos, terms, after):
    size = len(terms)
    shape = terms[0].shape

    def kernel(pos_ref, *refs):
        out_ref, all_ref = refs[-2:]
        for back in range(size):
            all_ref[lax.rem(pos_ref[0] - back + size, size)] = refs[back][...]
        total = all_ref[0]
        for d in range(1, size):
            total = total + all_ref[d]
        out_ref[...] = total

    whole = pl.BlockSpec(shape, lambda i, w: (0, 0))
    return pl.pallas_call(
        kernel,
        grid_spec=pltpu.PrefetchScalarGridSpec(
            num_scalar_prefetch=1,
            grid=(1,),
            in_specs=[whole] * size + [ANY] * len(after),
            out_specs=whole,
            scratch_shapes=[pltpu.VMEM((size,) + shape, F32)],
        ),
        out_shape=jax.ShapeDtypeStruct(shape, F32),
        compiler_params=pltpu.CompilerParams(vmem_limit_bytes=SMALL),
        cost_estimate=cost(SHORT),
        name="score_sum",
    )(pos, *terms, *after)


def body(inputs, residual, out_grad, norm_gain, w_out, proj_in, proj_out, queries, segment_ids):
    parts = lax.axis_size("tensor")
    rank = lax.axis_index("tensor")
    queriers = lax.axis_size("query")
    q_rank = lax.axis_index("query")
    tokens = inputs.shape[1]
    share = tokens // parts
    chunks = max(1, min(CHUNKS, share // 16))
    rows = share // chunks
    by_share = inputs.reshape(parts, chunks, rows, inputs.shape[2])
    gain = norm_gain.reshape(1, -1)
    half = w_out.shape[1] // HALVES
    kp = proj_out.shape[0]

    up = 1 - 2 * lax.rem(q_rank, 2)
    pos = jnp.stack([rank, up, jnp.where(up == 1, rank, parts - 1 - rank), q_rank]).astype(jnp.int32)

    def pairs(flow, low, high):
        out = []
        for q in range(queriers):
            way = 1 if (q % 2 == 0) == (flow == 0) else -1
            for t in range(parts):
                spot = t if way == 1 else parts - 1 - t
                if low <= spot <= min(high, parts - 2):
                    out.append((t * queriers + q, (t + way) * queriers + q))
        return out

    work, marks, resident = [], [], []
    partials, totals, result = {}, {}, [None]

    def forward(c, h, piece, pieces, after):
        partials[c, h], mark = forward_piece(
            by_share,
            w_out,
            c,
            HALVES,
            h,
            2 * kp,
            piece,
            pieces,
            partials.get((c, h)),
            after,
        )
        if h == 0 and piece == pieces - 1:
            partials[c, h] = forward_extra(by_share, proj_in, c, partials[c, h], [mark])
        return mark

    def backward(c, blocks, total, last, piece, pieces, after):
        held = result[0] if last else totals.get(c)
        some = resident[piece * QUARTERS // pieces : (piece + 1) * QUARTERS // pieces]
        done, mark = backward_piece(
            blocks, some, c, chunks, HALVES, piece, pieces, total, last, held, after
        )
        if last:
            result[0] = done
        else:
            totals[c] = done
        return mark

    def do_one(after, touching=False):
        if work:
            marks[:] = [work.pop(0)[1](after)]
        elif touching:
            marks[:] = [touch(after[0])]

    def finish(key, after):
        while any(k == key for k, _ in work):
            do_one(list(marks) + after)

    def load(count, after):
        for _ in range(count):
            resident.append(load_weights(w_out, len(resident), QUARTERS, after))
            after = [resident[-1]]
        marks[:] = after

    def add_forward(c, h, pieces):
        for piece in range(pieces):
            work.append(((c, h), functools.partial(forward, c, h, piece, pieces)))

    add_forward(0, 0, 1)
    finish((0, 0), [])
    gathered = []
    for slot in range(chunks + 1):
        rs, ag = slot < chunks, slot > 0
        came, held, sent, before = {}, {}, {}, None
        if ag:
            if slot == chunks:
                proj_out = in_hbm(proj_out)
            res, grd = in_vmem(own_rows[0]), in_vmem(own_rows[1])
            ins = [
                [partials[slot - 1, h], arrived[h, 0], arrived[h, 1], res, grd, gain]
                for h in range(HALVES)
            ]
            sums = None
            for h in range(HALVES):
                sums = norm_sums(pos, ins[h], half, slot - 1, h, sums, list(marks))
            grad = [None] * HALVES
            grad[0], held[0] = norm_out(
                pos, list(enumerate(ins)), half, slot - 1, sums, proj_out, []
            )
        for k in range(parts):
            gather_now, reduce_now = ag and k <= parts - 2, rs and k >= 1
            if not gather_now and not reduce_now:
                continue
            for h in range(HALVES):
                if k == 0 and h > 0:
                    if rs and slot > 1:
                        add_forward(slot, h, PIECES)
                    do_one([sent[h - 1, 1]])
                    grad[h], held[h] = norm_out(
                        pos, [(h, ins[h])], half, slot - 1, sums, None, list(marks)
                    )
                if reduce_now:
                    if slot == 0 and k == 1 and h > 0:
                        add_forward(0, h, 1)
                        do_one([sent[h - 1, 1]])
                    finish((slot, h), [sent[h - 1, 1]] if h > 0 else [])
                for flow in range(2):
                    if k == 0:
                        x = before = grad[h]
                    elif (h, flow) not in came:
                        x = first_block(pos, flow, partials[slot, h])
                    else:
                        x, held[h] = relay(
                            pos,
                            flow,
                            k,
                            partials[slot, h] if reduce_now else None,
                            came[h, flow],
                            held.get(h),
                            list(marks) + ([] if before is None else [before]),
                        )
                        before = x
                    came[h, flow] = lax.ppermute(
                        x,
                        ("tensor", "query"),
                        pairs(flow, 0 if reduce_now else k, parts - 2 if gather_now else k - 1),
                    )
                    sent[h, flow] = x
                    if rs and (k, h, flow) == (parts - 1, HALVES - 1, 1):
                        own_rows = load_rows(residual, out_grad, slot, rows, [x])
                        x = own_rows[0]
                    if slot == chunks - 1 and flow == 1 and slot > 0:
                        if (k, h) == (parts - 2, HALVES - 1):
                            load(1, [x])
                            continue
                        if (k, h) == (parts - 1, HALVES - 1):
                            load(QUARTERS - len(resident), [x])
                            continue
                    if slot == 0 and k == 2 and (h, flow) == (HALVES - 1, 1) and chunks > 1 and HALVES > 1:
                        add_forward(1, 1, 2 * PIECES)
                        do_one([x])
                        continue
                    if slot == 0 and k == parts - 1 and (h, flow) == (0, 1):
                        do_one([x])
                        continue
                    if slot == 0 and k == parts - 1 and (h, flow) == (HALVES - 1, 1) and chunks > 1:
                        work.insert(0, ((1, 0), functools.partial(forward, 1, 0, 0, 1)))
                    if slot == 0 and work and work[0][0] == (1, 1):
                        continue
                    if k > 0 and (slot > 0 or k > 1) and not (slot == 1 and work and k == 1 and flow == 0):
                        if slot == chunks and flow == 0:
                            marks[:] = [touch(x)]
                        else:
                            do_one([x], slot == chunks)
                if k == 0 and slot == chunks and h == HALVES - 1:
                    marks[:] = [touch(sent[h, 1])]
        if ag:
            if slot + 1 < chunks:
                add_forward(slot + 1, 0, PIECES)
            if rs:
                blocks = [(h, held[h]) for h in range(HALVES)]
                for piece in range(PIECES):
                    work.append(
                        (
                            ("b", slot - 1),
                            functools.partial(backward, slot - 1, blocks, None, True, piece, PIECES),
                        )
                    )
            else:
                while work:
                    do_one(list(marks))
                marks[:] = [touch(came[0, 0])]
                held[0] = store_last(pos, (came[0, 0], came[0, 1]), held[0], list(marks))
            gathered.append(held[0])
        arrived = came
    last = chunks - 1
    sketch = sketch_slice(pos, gathered, segment_ids, kp, [])
    marks[:] = [backward(last, [(0, held[0])], None, HALVES == 1, 0, 1, [sketch])]
    for h in range(1, HALVES):
        marks[:] = [tie(marks[0], [came[h, 0]])]
        held[h] = store_last(pos, (came[h, 0], came[h, 1]), held[h], list(marks))
    terms = score_terms(pos, from_others(sketch, "query", queriers), queries, list(marks))
    for h in range(1, HALVES):
        marks[:] = [backward(last, [(h, held[h])], totals.get(last), h == HALVES - 1, 0, 1, [terms])]
    scores = score_sum(pos, from_others(terms, "tensor", parts), list(marks))
    return (result[0].reshape(1, tokens, -1), scores)


def solution(mesh):
    return jax.shard_map(
        body,
        mesh=mesh,
        in_specs=(
            P(("groups", "dp", "query"), None, "tensor"),
            P(("groups", "dp", "query"), "tensor", None),
            P(("groups", "dp", "query"), "tensor", None),
            P(),
            P("tensor", None),
            P(None, "tensor"),
            P(),
            P("query", "tensor"),
            P(("groups", "dp", "query"), None),
        ),
        out_specs=(P(("groups", "dp", "query"), None, "tensor"), P(("groups", "dp"), "query")),
        check_vma=False,
    )
```

```python
import functools

import jax
import jax.numpy as jnp
from jax import lax
from jax.experimental import pallas as pl
from jax.experimental.pallas import tpu as pltpu
from jax.sharding import PartitionSpec as P

EX_DEV = 4
EPS = 1e-05
CHUNKS = 2
HALVES = 2
PIECES = 2
SHORT, LONG = 0.2, 5.0
SMALL, LIMIT, LARGE = 5 * 1024 * 1024, 9 * 1024 * 1024, 24 * 1024 * 1024
QUARTERS = 4

F32, BF16 = jnp.float32, jnp.bfloat16
ANY = pl.BlockSpec(memory_space=pl.ANY)
TOKEN = jax.ShapeDtypeStruct((8, 128), F32)
TOKEN_SPEC = pl.BlockSpec((8, 128), lambda *_: (0, 0))


def divisor(total, wanted):
    size = min(total, wanted)
    while total % size:
        size //= 2
    return size


def cost(microseconds):
    return pl.CostEstimate(flops=0, bytes_accessed=int(microseconds * 3.6e6), transcendentals=0)


def in_hbm(x):
    return pltpu.with_memory_space_constraint(x, pltpu.HBM)


def project_rows(values, matrix):
    return lax.dot_general(
        values, matrix, (((1,), (1,)), ((), ())), preferred_element_type=F32
    )


def spread(values, first):
    k = values.shape[1]
    row = lax.broadcasted_iota(jnp.int32, (k, 2 * k), 0)
    col = lax.broadcasted_iota(jnp.int32, (k, 2 * k), 1)
    return jnp.dot(values, jnp.where(col == row + first, 1.0, 0.0).astype(BF16), preferred_element_type=F32)


def forward_extra(by_share, proj_in, chunk, held, after):
    parts, _, rows, depth = by_share.shape
    extra = 2 * proj_in.shape[0]
    at = held.shape[2] // extra - 1

    def kernel(x_ref, p_ref, *refs):
        part = project_rows(x_ref[...].reshape(parts * rows, depth), p_ref[...]).astype(BF16)
        refs[-1][...] = spread(part, 0).astype(BF16).reshape(parts, rows, extra)

    return pl.pallas_call(
        kernel,
        grid=(1,),
        in_specs=[
            pl.BlockSpec((parts, None, rows, depth), lambda i: (0, chunk, 0, 0)),
            pl.BlockSpec(proj_in.shape, lambda i: (0, 0)),
        ]
        + [ANY] * (1 + len(after)),
        out_specs=pl.BlockSpec((parts, rows, extra), lambda i: (0, 0, at)),
        out_shape=jax.ShapeDtypeStruct(held.shape, BF16),
        input_output_aliases={2: 0},
        compiler_params=pltpu.CompilerParams(vmem_limit_bytes=LIMIT),
        cost_estimate=cost(SHORT),
        name="forward_extra",
    )(by_share, proj_in, held, *after)


def forward_piece(by_share, w_out, chunk, halves, half_at, extra, piece, pieces, held, after):
    parts, _, rows, depth = by_share.shape
    half = w_out.shape[1] // halves
    span = half // pieces
    cols = divisor(span, max(256, span // 4))
    steps = span // cols
    base = half_at * half + piece * span

    def kernel(x_ref, w_ref, *refs):
        out_ref, tok_ref, held_ref, sems = refs[-4:]
        i = pl.program_id(0)

        def copy(j):
            columns = pl.ds(pl.multiple_of(base + j * cols, cols), cols)
            return pltpu.make_async_copy(w_ref.at[:, columns], held_ref.at[j], sems.at[j])

        @pl.when(i == 0)
        def _():
            for j in range(steps):
                copy(j).start()

        copy(i).wait()
        x = x_ref[...].reshape(parts * rows, depth)
        y = jnp.dot(x, held_ref[i], preferred_element_type=F32).astype(BF16)
        out_ref[...] = y.reshape(parts, rows, cols)
        tok_ref[...] = jnp.zeros_like(tok_ref)

    more = ([] if held is None else [held]) + after
    return pl.pallas_call(
        kernel,
        grid=(steps,),
        in_specs=[
            pl.BlockSpec(
                (parts, None, rows, depth), lambda i: (0, chunk, 0, 0), pipeline_mode=pl.Buffered(1)
            )
        ]
        + [ANY] * (1 + len(more)),
        out_specs=[
            pl.BlockSpec((parts, rows, cols), lambda i: (0, 0, piece * steps + i)),
            TOKEN_SPEC,
        ],
        out_shape=[jax.ShapeDtypeStruct((parts, rows, half + extra), BF16), TOKEN],
        scratch_shapes=[pltpu.VMEM((steps, depth, cols), BF16), pltpu.SemaphoreType.DMA((steps,))],
        input_output_aliases={} if held is None else {2: 0},
        compiler_params=pltpu.CompilerParams(vmem_limit_bytes=LARGE),
        cost_estimate=cost(SHORT),
        name="forward_piece",
    )(in_hbm(by_share) if chunk == 0 and half_at == 0 else by_share, in_hbm(w_out), *more)


def load_weights(w_out, piece, pieces, after):
    rows = w_out.shape[0] // pieces
    width = w_out.shape[1]

    def kernel(w_ref, *refs):
        out_ref, sem = refs[-2:]
        copy = pltpu.make_async_copy(w_ref.at[pl.ds(piece * rows, rows)], out_ref, sem)
        copy.start()
        copy.wait()

    return pl.pallas_call(
        kernel,
        in_specs=[ANY] * (1 + len(after)),
        out_specs=pl.BlockSpec(memory_space=pltpu.VMEM),
        out_shape=pltpu.VMEM((rows, width), BF16),
        scratch_shapes=[pltpu.SemaphoreType.DMA],
        compiler_params=pltpu.CompilerParams(vmem_limit_bytes=SMALL),
        cost_estimate=cost(SHORT),
        name="load_weights",
    )(in_hbm(w_out), *after)


def load_rows(residual, out_grad, chunk, rows, after):
    width = residual.shape[2]

    def kernel(*refs):
        out_refs, sems = refs[-3:-1], refs[-1]
        copies = [
            pltpu.make_async_copy(refs[j].at[0, pl.ds(chunk * rows, rows)], out_refs[j], sems.at[j])
            for j in range(2)
        ]
        for copy in copies:
            copy.start()
        for copy in copies:
            copy.wait()

    return pl.pallas_call(
        kernel,
        in_specs=[ANY] * (2 + len(after)),
        out_specs=[pl.BlockSpec(memory_space=pltpu.VMEM)] * 2,
        out_shape=[pltpu.VMEM((rows, width), BF16)] * 2,
        scratch_shapes=[pltpu.SemaphoreType.DMA((2,))],
        compiler_params=pltpu.CompilerParams(vmem_limit_bytes=SMALL),
        cost_estimate=cost(SHORT),
        name="load_rows",
    )(in_hbm(residual), in_hbm(out_grad), *after)


def in_vmem(x):
    return pltpu.with_memory_space_constraint(x, pltpu.VMEM)


def backward_piece(blocks, weights, chunk, chunks, halves, piece, pieces, total, last, held, after):
    parts, rows, _ = blocks[0][1].shape
    some, width = weights[0].shape
    half, span = width // halves, some * len(weights)
    cols = divisor(some, 256)
    n, m = len(blocks), len(weights)

    def kernel(*refs):
        out_ref, tok_ref = refs[-2:]
        for j in range(m):

            def step(i, carry):
                here = pl.ds(pl.multiple_of(i * cols, cols), cols)
                there = pl.ds(pl.multiple_of(j * some + i * cols, cols), cols)
                y = None if total is None else refs[n + m][:, :, there].reshape(parts * rows, cols)
                for b, (at, _) in enumerate(blocks):
                    g = refs[b][...].reshape(parts * rows, half)
                    term = project_rows(g, refs[n + j][here, at * half : (at + 1) * half])
                    y = term if y is None else y + term
                out_ref[:, :, there] = y.astype(out_ref.dtype).reshape(parts, rows, cols)
                return carry

            lax.fori_loop(0, some // cols, step, 0)
        tok_ref[...] = jnp.zeros_like(tok_ref)

    once = pl.Buffered(1)
    here = pl.BlockSpec((parts, rows, span), lambda i: (0, 0, piece))
    if last:
        out_spec = pl.BlockSpec((parts, None, rows, span), lambda i: (0, chunk, 0, piece))
        out_shape = jax.ShapeDtypeStruct((parts, chunks, rows, span * pieces), BF16)
    else:
        out_spec, out_shape = here, jax.ShapeDtypeStruct((parts, rows, span * pieces), F32)
    sums = [] if total is None else [total]
    extra = ([] if held is None else [held]) + after
    return pl.pallas_call(
        kernel,
        grid=(1,),
        in_specs=[pl.BlockSpec((parts, rows, half), lambda i: (0, 0, 0), pipeline_mode=once)] * n
        + [pl.BlockSpec(memory_space=pltpu.VMEM)] * m
        + [pl.BlockSpec((parts, rows, span), lambda i: (0, 0, piece), pipeline_mode=once)] * len(sums)
        + [ANY] * len(extra),
        out_specs=[out_spec, TOKEN_SPEC],
        out_shape=[out_shape, TOKEN],
        input_output_aliases={} if held is None else {n + m + len(sums): 0},
        compiler_params=pltpu.CompilerParams(vmem_limit_bytes=LIMIT),
        cost_estimate=cost(SHORT),
        name="backward_piece",
    )(
        *[g for _, g in blocks],
        *[in_vmem(w) for w in weights],
        *sums,
        *extra,
    )


def relay(pos, flow, k, partial, came, held, after):
    rows, width = came.shape
    parts = (partial if held is None else held).shape[0]
    n_in = 1 + (partial is not None) + (held is not None) + len(after)

    def far(pos_ref, steps):
        way = pos_ref[1] if flow == 0 else -pos_ref[1]
        return lax.clamp(0, pos_ref[0] + way * steps, parts - 1)

    def kernel(pos_ref, *refs):
        came_ref, x_ref = refs[0], refs[n_in]
        place = pos_ref[2] if flow == 0 else parts - 1 - pos_ref[2]
        if held is not None:
            store = pltpu.make_async_copy(came_ref, refs[n_in + 1].at[far(pos_ref, -k)], refs[-1])
            pl.when(place >= k)(store.start)
        if partial is not None:

            @pl.when(place < k)
            def _():
                x_ref[...] = (came_ref[...].astype(F32) + refs[1][...].astype(F32)).astype(BF16)

            @pl.when(place >= k)
            def _():
                x_ref[...] = came_ref[...]

        else:
            x_ref[...] = came_ref[...]
        if held is not None:
            pl.when(place >= k)(store.wait)

    line = jax.ShapeDtypeStruct((rows, width), BF16)
    whole = pl.BlockSpec((rows, width), lambda i, w: (0, 0), pipeline_mode=pl.Buffered(1))
    args, specs, out_specs, out_shape, alias = [came], [whole], [whole], [line], {}
    if partial is not None:
        term = pl.BlockSpec(
            (None, rows, width),
            lambda i, w: (far(w, parts - k), 0, 0),
            pipeline_mode=pl.Buffered(1),
        )
        specs.append(term)
        args.append(partial)
    if held is not None:
        alias[1 + len(args)] = 1
        specs.append(ANY)
        args.append(held)
        out_specs.append(ANY)
        out_shape.append(jax.ShapeDtypeStruct(held.shape, BF16))
    outs = pl.pallas_call(
        kernel,
        grid_spec=pltpu.PrefetchScalarGridSpec(
            num_scalar_prefetch=1,
            grid=(1,),
            in_specs=specs + [ANY] * len(after),
            out_specs=out_specs,
            scratch_shapes=[pltpu.SemaphoreType.DMA] if held is not None else [],
        ),
        out_shape=out_shape,
        input_output_aliases=alias,
        compiler_params=pltpu.CompilerParams(vmem_limit_bytes=SMALL),
        cost_estimate=cost(LONG),
        name="relay",
    )(pos, *args, *after)
    return outs[0], (outs[1] if held is not None else None)


def store_last(pos, came, held, after):
    parts = held.shape[0]

    def kernel(pos_ref, a_ref, b_ref, *refs):
        out_ref, sem = refs[-2:]
        rank, way, place = pos_ref[0], pos_ref[1], pos_ref[2]
        ends = (
            (place == parts - 1, a_ref, rank - way * (parts - 1)),
            (place == 0, b_ref, rank + way * (parts - 1)),
        )
        for at_end, came_ref, at in ends:
            copy = pltpu.make_async_copy(came_ref, out_ref.at[lax.clamp(0, at, parts - 1)], sem)

            @pl.when(at_end)
            def _():
                copy.start()
                copy.wait()

    return pl.pallas_call(
        kernel,
        grid_spec=pltpu.PrefetchScalarGridSpec(
            num_scalar_prefetch=1,
            grid=(1,),
            in_specs=[pl.BlockSpec(held.shape[1:], lambda i, w: (0, 0))] * 2 + [ANY] * (1 + len(after)),
            out_specs=ANY,
            scratch_shapes=[pltpu.SemaphoreType.DMA],
        ),
        out_shape=jax.ShapeDtypeStruct(held.shape, BF16),
        input_output_aliases={3: 0},
        compiler_params=pltpu.CompilerParams(vmem_limit_bytes=SMALL),
        cost_estimate=cost(SHORT),
        name="store_last",
    )(pos, *came, held, *after)


def first_block(pos, flow, partial):
    parts, rows, width = partial.shape

    def there(i, w):
        way = w[1] if flow == 0 else -w[1]
        return lax.clamp(0, w[0] + way * (parts - 1), parts - 1), 0, 0

    def kernel(pos_ref, p_ref, out_ref):
        out_ref[...] = p_ref[...]

    return pl.pallas_call(
        kernel,
        grid_spec=pltpu.PrefetchScalarGridSpec(
            num_scalar_prefetch=1,
            grid=(1,),
            in_specs=[pl.BlockSpec((None, rows, width), there)],
            out_specs=pl.BlockSpec((rows, width), lambda i, w: (0, 0)),
        ),
        out_shape=jax.ShapeDtypeStruct((rows, width), BF16),
        compiler_params=pltpu.CompilerParams(vmem_limit_bytes=SMALL),
        cost_estimate=cost(SHORT),
        name="first_block",
    )(pos, partial)


def norm_terms(p_ref, a_ref, b_ref, res_ref, grad_ref, gain_ref, at):
    proj = p_ref[:, at].astype(F32) + a_ref[:, at].astype(F32) + b_ref[:, at].astype(F32)
    z = res_ref[:, at].astype(F32) + proj
    scaled = gain_ref[:, at].astype(F32) * grad_ref[:, at].astype(F32)
    return z, scaled


def norm_specs(ins, half, chunk, at):
    _, rows, wide = ins[0].shape
    once = pl.Buffered(1)
    whole = pl.BlockSpec((rows, wide), lambda i, r: (0, 0), pipeline_mode=once)
    own = pl.BlockSpec((rows, half), lambda i, r: (0, at), pipeline_mode=once)
    mine = pl.BlockSpec((None, rows, wide), lambda i, r: (r[0], 0, 0), pipeline_mode=once)
    return [mine, whole, whole, own, own, pl.BlockSpec((1, half), lambda i, r: (0, at))]


def norm_sums(pos, ins, half, chunk, at, sums, after):
    rows = ins[0].shape[1]
    cols = divisor(half, 1024)

    def kernel(pos_ref, *refs):
        square_ref, cross_ref = refs[-2:]

        def step(i, sums):
            z, scaled = norm_terms(*refs[:6], pl.ds(pl.multiple_of(i * cols, cols), cols))
            square, cross = sums
            for j in range(0, cols, 128):
                zj = z[:, j : j + 128]
                square = square + zj * zj
                cross = cross + zj * scaled[:, j : j + 128]
            return square, cross

        zero = jnp.zeros((rows, 128), F32)
        start = (zero, zero) if sums is None else (refs[6][...], refs[7][...])
        square_ref[...], cross_ref[...] = lax.fori_loop(0, half // cols, step, start)

    stat = pl.BlockSpec((rows, 128), lambda i, r: (0, 0))
    before = [] if sums is None else list(sums)
    return pl.pallas_call(
        kernel,
        grid_spec=pltpu.PrefetchScalarGridSpec(
            num_scalar_prefetch=1,
            grid=(1,),
            in_specs=norm_specs(ins, half, chunk, at) + [stat] * len(before) + [ANY] * len(after),
            out_specs=[stat, stat],
        ),
        out_shape=[jax.ShapeDtypeStruct((rows, 128), F32)] * 2,
        compiler_params=pltpu.CompilerParams(vmem_limit_bytes=LIMIT),
        cost_estimate=cost(LONG),
        name="norm_sums",
    )(pos, *ins, *before, *after)


def norm_out(pos, ins, half, chunk, sums, proj_out, after):
    parts, rows, wide = ins[0][1][0].shape
    cols = divisor(half, 1024)
    n, width = len(ins), ins[0][1][3].shape[1]
    with_b = proj_out

    def kernel(pos_ref, *refs):
        square_ref, cross_ref = refs[6 * n], refs[6 * n + 1]
        if with_b is None:
            out_ref, held_ref, sem = refs[-3:]
        else:
            out_ref, held_ref, rest_ref, sem = refs[-4:]
        inv = lax.rsqrt(jnp.sum(square_ref[...], axis=-1, keepdims=True) / width + EPS)
        slope = inv * inv * inv * (jnp.sum(cross_ref[...], axis=-1, keepdims=True) / width)
        for j in range(n):
            to_ref = out_ref if j == 0 else rest_ref.at[j - 1]

            def step(i, carry):
                here = pl.ds(pl.multiple_of(i * cols, cols), cols)
                z, scaled = norm_terms(*refs[6 * j : 6 * j + 6], here)
                to_ref[:, here] = (inv * scaled - z * slope).astype(BF16)
                return carry

            lax.fori_loop(0, half // cols, step, 0)
        if with_b is not None:
            p_ref = refs[6 * n + 2]
            b = project_rows(out_ref[:, :half], p_ref[:, :half])
            for j in range(1, n):
                b = b + project_rows(rest_ref[j - 1], p_ref[:, j * half : (j + 1) * half])
            a = sum(refs[j][:, half:].astype(F32) for j in range(3))
            out_ref[:, half:] = (a + spread(b.astype(BF16), b.shape[1])).astype(BF16)
        else:
            out_ref[:, half:] = jnp.zeros((rows, wide - half), BF16)
        own = pltpu.make_async_copy(out_ref, held_ref.at[pos_ref[0]], sem)
        own.start()
        own.wait()

    stat = pl.BlockSpec((rows, 128), lambda i, r: (0, 0))
    specs, args = [], []
    for at, one in ins:
        specs += norm_specs(one, half, chunk, at)
        args += one
    specs, args = specs + [stat, stat], args + list(sums)
    scratch = [pltpu.SemaphoreType.DMA]
    if with_b is not None:
        specs.append(
            pl.BlockSpec(proj_out.shape, lambda i, r: (0, 0), pipeline_mode=pl.Buffered(1))
        )
        args.append(proj_out)
        scratch = [pltpu.VMEM((max(1, n - 1), rows, half), BF16)] + scratch
    return pl.pallas_call(
        kernel,
        grid_spec=pltpu.PrefetchScalarGridSpec(
            num_scalar_prefetch=1,
            grid=(1,),
            in_specs=specs + [ANY] * len(after),
            out_specs=[pl.BlockSpec((rows, wide), lambda i, r: (0, 0)), ANY],
            scratch_shapes=scratch,
        ),
        out_shape=[
            jax.ShapeDtypeStruct((rows, wide), BF16),
            jax.ShapeDtypeStruct((parts, rows, wide), BF16),
        ],
        compiler_params=pltpu.CompilerParams(vmem_limit_bytes=LIMIT),
        cost_estimate=cost(SHORT),
        name="norm_out",
    )(pos, *args, *after)


def tie(value, after):
    def kernel(value_ref, *refs):
        refs[-1][...] = value_ref[...]

    whole = pl.BlockSpec(value.shape, lambda i: (0,) * value.ndim)
    return pl.pallas_call(
        kernel,
        grid=(1,),
        in_specs=[whole] + [ANY] * len(after),
        out_specs=whole,
        out_shape=jax.ShapeDtypeStruct(value.shape, value.dtype),
        compiler_params=pltpu.CompilerParams(vmem_limit_bytes=SMALL),
        cost_estimate=cost(SHORT),
        name="tie",
    )(value, *after)


def touch(x):
    def kernel(x_ref, out_ref):
        out_ref[...] = jnp.zeros_like(out_ref)

    return pl.pallas_call(
        kernel,
        grid=(1,),
        in_specs=[ANY],
        out_specs=TOKEN_SPEC,
        out_shape=TOKEN,
        compiler_params=pltpu.CompilerParams(vmem_limit_bytes=SMALL),
        cost_estimate=cost(SHORT),
        name="touch",
    )(x)


def from_others(value, axis, size):
    return [value] + [
        lax.ppermute(value, axis, [(d, (d + shift) % size) for d in range(size)])
        for shift in range(1, size)
    ]


def sketch_slice(pos, gathered, segment_ids, kp, after):
    parts, rows, wide = gathered[0].shape
    extra, mine = 2 * kp, kp // parts
    chunks, tokens = len(gathered), segment_ids.shape[1]

    def kernel(pos_ref, *refs):
        out_ref, sum_ref = refs[-2:]
        example = lax.broadcasted_iota(jnp.int32, (8, tokens), 0)
        by_row = jnp.where(refs[chunks][...] == example, 1.0, 0.0).astype(BF16)
        same = lax.broadcasted_iota(jnp.int32, (tokens, tokens), 0) == lax.broadcasted_iota(
            jnp.int32, (tokens, tokens), 1
        )
        weights = project_rows(jnp.where(same, 1.0, 0.0).astype(BF16), by_row)
        weights = weights.reshape(parts, chunks, rows, 8)
        for e in range(EX_DEV):
            total = None
            for c in range(chunks):
                both = refs[c][...].reshape(parts * rows, extra)
                weight = weights[:, c].reshape(parts * rows, 8)[:, e : e + 1]
                part = (both.astype(F32) * weight).astype(BF16)
                term = lax.dot_general(
                    part, both, (((0,), (0,)), ((), ())), preferred_element_type=F32
                )
                total = term if total is None else total + term
            sum_ref[e] = total
        low = lax.broadcasted_iota(jnp.int32, (1, extra), 1) < kp
        for r in range(parts):

            @pl.when(pos_ref[0] == r)
            def _():
                for e in range(EX_DEV):
                    for i in range(mine // 2):
                        at = kp + r * mine + 2 * i
                        left, right = sum_ref[e, at : at + 1, :], sum_ref[e, at + 1 : at + 2, :]
                        out_ref[e : e + 1, i * extra : (i + 1) * extra] = jnp.where(
                            low, left, pltpu.roll(right, kp, 1)
                        )

    return pl.pallas_call(
        kernel,
        grid_spec=pltpu.PrefetchScalarGridSpec(
            num_scalar_prefetch=1,
            grid=(1,),
            in_specs=[pl.BlockSpec((parts, rows, extra), lambda i, w: (0, 0, wide // extra - 1))] * chunks
            + [pl.BlockSpec(segment_ids.shape, lambda i, w: (0, 0))]
            + [ANY] * len(after),
            out_specs=pl.BlockSpec((EX_DEV, mine * kp), lambda i, w: (0, 0)),
            scratch_shapes=[pltpu.VMEM((EX_DEV, extra, extra), F32)],
        ),
        out_shape=jax.ShapeDtypeStruct((EX_DEV, mine * kp), F32),
        compiler_params=pltpu.CompilerParams(vmem_limit_bytes=LIMIT),
        cost_estimate=cost(SHORT),
        name="sketch_slice",
    )(pos, *gathered, segment_ids, *after)


def score_terms(pos, sketches, queries, after):
    size = len(sketches)
    n, depth = queries.shape

    def kernel(pos_ref, *refs):
        out_ref, all_ref = refs[-2:]
        for back in range(size):
            all_ref[lax.rem(pos_ref[3] - back + size, size)] = refs[back][...]
        for d in range(size):
            rest, total = all_ref[d], None
            for _ in range(3):
                part = rest.astype(BF16)
                rest = rest - part.astype(F32)
                term = project_rows(part, refs[size][...])
                total = term if total is None else total + term
            out_ref[d * EX_DEV : (d + 1) * EX_DEV, :] = total

    return pl.pallas_call(
        kernel,
        grid_spec=pltpu.PrefetchScalarGridSpec(
            num_scalar_prefetch=1,
            grid=(1,),
            in_specs=[pl.BlockSpec((EX_DEV, depth), lambda i, w: (0, 0))] * size
            + [pl.BlockSpec((n, depth), lambda i, w: (0, 0))]
            + [ANY] * len(after),
            out_specs=pl.BlockSpec((size * EX_DEV, n), lambda i, w: (0, 0)),
            scratch_shapes=[pltpu.VMEM((size, EX_DEV, depth), F32)],
        ),
        out_shape=jax.ShapeDtypeStruct((size * EX_DEV, n), F32),
        compiler_params=pltpu.CompilerParams(vmem_limit_bytes=LIMIT),
        cost_estimate=cost(SHORT),
        name="score_terms",
    )(pos, *sketches, queries, *after)


def score_sum(pos, terms, after):
    size = len(terms)
    shape = terms[0].shape

    def kernel(pos_ref, *refs):
        out_ref, all_ref = refs[-2:]
        for back in range(size):
            all_ref[lax.rem(pos_ref[0] - back + size, size)] = refs[back][...]
        total = all_ref[0]
        for d in range(1, size):
            total = total + all_ref[d]
        out_ref[...] = total

    whole = pl.BlockSpec(shape, lambda i, w: (0, 0))
    return pl.pallas_call(
        kernel,
        grid_spec=pltpu.PrefetchScalarGridSpec(
            num_scalar_prefetch=1,
            grid=(1,),
            in_specs=[whole] * size + [ANY] * len(after),
            out_specs=whole,
            scratch_shapes=[pltpu.VMEM((size,) + shape, F32)],
        ),
        out_shape=jax.ShapeDtypeStruct(shape, F32),
        compiler_params=pltpu.CompilerParams(vmem_limit_bytes=SMALL),
        cost_estimate=cost(SHORT),
        name="score_sum",
    )(pos, *terms, *after)


def body(inputs, residual, out_grad, norm_gain, w_out, proj_in, proj_out, queries, segment_ids):
    parts = lax.axis_size("tensor")
    rank = lax.axis_index("tensor")
    queriers = lax.axis_size("query")
    q_rank = lax.axis_index("query")
    tokens = inputs.shape[1]
    share = tokens // parts
    chunks = max(1, min(CHUNKS, share // 16))
    rows = share // chunks
    by_share = inputs.reshape(parts, chunks, rows, inputs.shape[2])
    gain = norm_gain.reshape(1, -1)
    half = w_out.shape[1] // HALVES
    kp = proj_out.shape[0]

    up = 1 - 2 * lax.rem(q_rank, 2)
    pos = jnp.stack([rank, up, jnp.where(up == 1, rank, parts - 1 - rank), q_rank]).astype(jnp.int32)

    def pairs(flow, low, high):
        out = []
        for q in range(queriers):
            way = 1 if (q % 2 == 0) == (flow == 0) else -1
            for t in range(parts):
                spot = t if way == 1 else parts - 1 - t
                if low <= spot <= min(high, parts - 2):
                    out.append((t * queriers + q, (t + way) * queriers + q))
        return out

    work, marks, resident = [], [], []
    partials, totals, result = {}, {}, [None]

    def forward(c, h, piece, pieces, after):
        partials[c, h], mark = forward_piece(
            by_share,
            w_out,
            c,
            HALVES,
            h,
            2 * kp,
            piece,
            pieces,
            partials.get((c, h)),
            after,
        )
        if h == 0 and piece == pieces - 1:
            partials[c, h] = forward_extra(by_share, proj_in, c, partials[c, h], [mark])
        return mark

    def backward(c, blocks, total, last, piece, pieces, after):
        held = result[0] if last else totals.get(c)
        some = resident[piece * QUARTERS // pieces : (piece + 1) * QUARTERS // pieces]
        done, mark = backward_piece(
            blocks, some, c, chunks, HALVES, piece, pieces, total, last, held, after
        )
        if last:
            result[0] = done
        else:
            totals[c] = done
        return mark

    def do_one(after, touching=False):
        if work:
            marks[:] = [work.pop(0)[1](after)]
        elif touching:
            marks[:] = [touch(after[0])]

    def finish(key, after):
        while any(k == key for k, _ in work):
            do_one(list(marks) + after)

    def load(count, after):
        for _ in range(count):
            resident.append(load_weights(w_out, len(resident), QUARTERS, after))
            after = [resident[-1]]
        marks[:] = after

    def add_forward(c, h, pieces):
        for piece in range(pieces):
            work.append(((c, h), functools.partial(forward, c, h, piece, pieces)))

    add_forward(0, 0, 1)
    finish((0, 0), [])
    gathered = []
    for slot in range(chunks + 1):
        rs, ag = slot < chunks, slot > 0
        came, held, sent, before = {}, {}, {}, None
        if ag:
            res, grd = in_vmem(own_rows[0]), in_vmem(own_rows[1])
            ins = [
                [partials[slot - 1, h], arrived[h, 0], arrived[h, 1], res, grd, gain]
                for h in range(HALVES)
            ]
            sums = None
            for h in range(HALVES):
                sums = norm_sums(pos, ins[h], half, slot - 1, h, sums, list(marks))
            grad = [None] * HALVES
            grad[0], held[0] = norm_out(
                pos, list(enumerate(ins)), half, slot - 1, sums, proj_out, []
            )
        for k in range(parts):
            gather_now, reduce_now = ag and k <= parts - 2, rs and k >= 1
            if not gather_now and not reduce_now:
                continue
            for h in range(HALVES):
                if k == 0 and h > 0:
                    if rs and slot > 1:
                        add_forward(slot, h, PIECES)
                    do_one([sent[h - 1, 1]])
                    grad[h], held[h] = norm_out(
                        pos, [(h, ins[h])], half, slot - 1, sums, None, list(marks)
                    )
                if reduce_now:
                    if slot == 0 and k == 1 and h > 0:
                        add_forward(0, h, 1)
                        do_one([sent[h - 1, 1]])
                    finish((slot, h), [sent[h - 1, 1]] if h > 0 else [])
                for flow in range(2):
                    if k == 0:
                        x = before = grad[h]
                    elif (h, flow) not in came:
                        x = first_block(pos, flow, partials[slot, h])
                    else:
                        x, held[h] = relay(
                            pos,
                            flow,
                            k,
                            partials[slot, h] if reduce_now else None,
                            came[h, flow],
                            held.get(h),
                            list(marks) + ([] if before is None else [before]),
                        )
                        before = x
                    came[h, flow] = lax.ppermute(
                        x,
                        ("tensor", "query"),
                        pairs(flow, 0 if reduce_now else k, parts - 2 if gather_now else k - 1),
                    )
                    sent[h, flow] = x
                    if rs and (k, h, flow) == (parts - 1, HALVES - 1, 1):
                        own_rows = load_rows(residual, out_grad, slot, rows, [x])
                        x = own_rows[0]
                    if slot == chunks - 1 and flow == 1 and slot > 0:
                        if (k, h) == (parts - 2, HALVES - 1):
                            load(1, [x])
                            continue
                        if (k, h) == (parts - 1, HALVES - 1):
                            load(QUARTERS - len(resident), [x])
                            continue
                    if slot == 0 and k == 2 and (h, flow) == (HALVES - 1, 1) and chunks > 1 and HALVES > 1:
                        add_forward(1, 1, 2 * PIECES)
                        do_one([x])
                        continue
                    if slot == 0 and k == parts - 1 and (h, flow) == (0, 1):
                        do_one([x])
                        continue
                    if slot == 0 and k == parts - 1 and (h, flow) == (HALVES - 1, 1) and chunks > 1:
                        work.insert(0, ((1, 0), functools.partial(forward, 1, 0, 0, 1)))
                    if slot == 0 and work and work[0][0] == (1, 1):
                        continue
                    if k > 0 and (slot > 0 or k > 1) and not (slot == 1 and work and k == 1 and flow == 0):
                        if slot == chunks and (h, flow, k) != (HALVES - 1, 1, parts - 2):
                            marks[:] = [touch(x)]
                        else:
                            do_one([x], slot == chunks)
                if k == 0 and slot == chunks and h == HALVES - 1:
                    marks[:] = [touch(sent[h, 1])]
        if ag:
            if slot + 1 < chunks:
                add_forward(slot + 1, 0, PIECES)
            if rs:
                blocks = [(h, held[h]) for h in range(HALVES)]
                for piece in range(PIECES):
                    work.append(
                        (
                            ("b", slot - 1),
                            functools.partial(backward, slot - 1, blocks, None, True, piece, PIECES),
                        )
                    )
            else:
                while work:
                    do_one(list(marks))
                marks[:] = [tie(marks[0], [came[0, 0]])]
                held[0] = store_last(pos, (came[0, 0], came[0, 1]), held[0], list(marks))
            gathered.append(held[0])
        arrived = came
    last = chunks - 1
    sketch = sketch_slice(pos, gathered, segment_ids, kp, [])
    marks[:] = [backward(last, [(0, held[0])], None, HALVES == 1, 0, 1, [sketch])]
    for h in range(1, HALVES):
        marks[:] = [tie(marks[0], [came[h, 0]])]
        held[h] = store_last(pos, (came[h, 0], came[h, 1]), held[h], list(marks))
    terms = score_terms(pos, from_others(sketch, "query", queriers), queries, list(marks))
    for h in range(1, HALVES):
        marks[:] = [backward(last, [(h, held[h])], totals.get(last), h == HALVES - 1, 0, 1, [terms])]
    scores = score_sum(pos, from_others(terms, "tensor", parts), list(marks))
    return (result[0].reshape(1, tokens, -1), scores)


def solution(mesh):
    return jax.shard_map(
        body,
        mesh=mesh,
        in_specs=(
            P(("groups", "dp", "query"), None, "tensor"),
            P(("groups", "dp", "query"), "tensor", None),
            P(("groups", "dp", "query"), "tensor", None),
            P(),
            P("tensor", None),
            P(None, "tensor"),
            P(),
            P("query", "tensor"),
            P(("groups", "dp", "query"), None),
        ),
        out_specs=(P(("groups", "dp", "query"), None, "tensor"), P(("groups", "dp"), "query")),
        check_vma=False,
    )
```

```python
import functools

import jax
import jax.numpy as jnp
from jax import lax
from jax.experimental import pallas as pl
from jax.experimental.pallas import tpu as pltpu
from jax.sharding import PartitionSpec as P

EX_DEV = 4
EPS = 1e-05
CHUNKS = 2
HALVES = 2
PIECES = 2
SHORT, LONG = 0.2, 5.0
SMALL, LIMIT, LARGE = 5 * 1024 * 1024, 9 * 1024 * 1024, 24 * 1024 * 1024
QUARTERS = 4

F32, BF16 = jnp.float32, jnp.bfloat16
ANY = pl.BlockSpec(memory_space=pl.ANY)
TOKEN = jax.ShapeDtypeStruct((8, 128), F32)
TOKEN_SPEC = pl.BlockSpec((8, 128), lambda *_: (0, 0))


def divisor(total, wanted):
    size = min(total, wanted)
    while total % size:
        size //= 2
    return size


def cost(microseconds):
    return pl.CostEstimate(flops=0, bytes_accessed=int(microseconds * 3.6e6), transcendentals=0)


def in_hbm(x):
    return pltpu.with_memory_space_constraint(x, pltpu.HBM)


def project_rows(values, matrix):
    return lax.dot_general(
        values, matrix, (((1,), (1,)), ((), ())), preferred_element_type=F32
    )


def spread(values, first):
    k = values.shape[1]
    row = lax.broadcasted_iota(jnp.int32, (k, 2 * k), 0)
    col = lax.broadcasted_iota(jnp.int32, (k, 2 * k), 1)
    return jnp.dot(values, jnp.where(col == row + first, 1.0, 0.0).astype(BF16), preferred_element_type=F32)


def forward_extra(by_share, proj_in, chunk, held, after):
    parts, _, rows, depth = by_share.shape
    extra = 2 * proj_in.shape[0]
    at = held.shape[2] // extra - 1

    def kernel(x_ref, p_ref, *refs):
        part = project_rows(x_ref[...].reshape(parts * rows, depth), p_ref[...]).astype(BF16)
        refs[-1][...] = spread(part, 0).astype(BF16).reshape(parts, rows, extra)

    return pl.pallas_call(
        kernel,
        grid=(1,),
        in_specs=[
            pl.BlockSpec((parts, None, rows, depth), lambda i: (0, chunk, 0, 0)),
            pl.BlockSpec(proj_in.shape, lambda i: (0, 0)),
        ]
        + [ANY] * (1 + len(after)),
        out_specs=pl.BlockSpec((parts, rows, extra), lambda i: (0, 0, at)),
        out_shape=jax.ShapeDtypeStruct(held.shape, BF16),
        input_output_aliases={2: 0},
        compiler_params=pltpu.CompilerParams(vmem_limit_bytes=LIMIT),
        cost_estimate=cost(SHORT),
        name="forward_extra",
    )(by_share, proj_in, held, *after)


def forward_piece(by_share, w_out, chunk, halves, half_at, extra, piece, pieces, held, after):
    parts, _, rows, depth = by_share.shape
    half = w_out.shape[1] // halves
    span = half // pieces
    cols = divisor(span, max(256, span // 4))
    steps = span // cols
    base = half_at * half + piece * span

    def kernel(x_ref, w_ref, *refs):
        out_ref, tok_ref, held_ref, sems = refs[-4:]
        i = pl.program_id(0)

        def copy(j):
            columns = pl.ds(pl.multiple_of(base + j * cols, cols), cols)
            return pltpu.make_async_copy(w_ref.at[:, columns], held_ref.at[j], sems.at[j])

        @pl.when(i == 0)
        def _():
            for j in range(steps):
                copy(j).start()

        copy(i).wait()
        x = x_ref[...].reshape(parts * rows, depth)
        y = jnp.dot(x, held_ref[i], preferred_element_type=F32).astype(BF16)
        out_ref[...] = y.reshape(parts, rows, cols)
        tok_ref[...] = jnp.zeros_like(tok_ref)

    more = ([] if held is None else [held]) + after
    return pl.pallas_call(
        kernel,
        grid=(steps,),
        in_specs=[
            pl.BlockSpec(
                (parts, None, rows, depth), lambda i: (0, chunk, 0, 0), pipeline_mode=pl.Buffered(1)
            )
        ]
        + [ANY] * (1 + len(more)),
        out_specs=[
            pl.BlockSpec((parts, rows, cols), lambda i: (0, 0, piece * steps + i)),
            TOKEN_SPEC,
        ],
        out_shape=[jax.ShapeDtypeStruct((parts, rows, half + extra), BF16), TOKEN],
        scratch_shapes=[pltpu.VMEM((steps, depth, cols), BF16), pltpu.SemaphoreType.DMA((steps,))],
        input_output_aliases={} if held is None else {2: 0},
        compiler_params=pltpu.CompilerParams(vmem_limit_bytes=LARGE),
        cost_estimate=cost(SHORT),
        name="forward_piece",
    )(in_hbm(by_share) if chunk == 0 and half_at == 0 else by_share, in_hbm(w_out), *more)


def load_weights(w_out, piece, pieces, after):
    rows = w_out.shape[0] // pieces
    width = w_out.shape[1]

    def kernel(w_ref, *refs):
        out_ref, sem = refs[-2:]
        copy = pltpu.make_async_copy(w_ref.at[pl.ds(piece * rows, rows)], out_ref, sem)
        copy.start()
        copy.wait()

    return pl.pallas_call(
        kernel,
        in_specs=[ANY] * (1 + len(after)),
        out_specs=pl.BlockSpec(memory_space=pltpu.VMEM),
        out_shape=pltpu.VMEM((rows, width), BF16),
        scratch_shapes=[pltpu.SemaphoreType.DMA],
        compiler_params=pltpu.CompilerParams(vmem_limit_bytes=SMALL),
        cost_estimate=cost(SHORT),
        name="load_weights",
    )(in_hbm(w_out), *after)


def load_rows(residual, out_grad, chunk, rows, after):
    width = residual.shape[2]

    def kernel(*refs):
        out_refs, sems = refs[-3:-1], refs[-1]
        copies = [
            pltpu.make_async_copy(refs[j].at[0, pl.ds(chunk * rows, rows)], out_refs[j], sems.at[j])
            for j in range(2)
        ]
        for copy in copies:
            copy.start()
        for copy in copies:
            copy.wait()

    return pl.pallas_call(
        kernel,
        in_specs=[ANY] * (2 + len(after)),
        out_specs=[pl.BlockSpec(memory_space=pltpu.VMEM)] * 2,
        out_shape=[pltpu.VMEM((rows, width), BF16)] * 2,
        scratch_shapes=[pltpu.SemaphoreType.DMA((2,))],
        compiler_params=pltpu.CompilerParams(vmem_limit_bytes=SMALL),
        cost_estimate=cost(SHORT),
        name="load_rows",
    )(in_hbm(residual), in_hbm(out_grad), *after)


def in_vmem(x):
    return pltpu.with_memory_space_constraint(x, pltpu.VMEM)


def backward_piece(blocks, weights, chunk, chunks, halves, piece, pieces, total, last, held, after):
    parts, rows, _ = blocks[0][1].shape
    some, width = weights[0].shape
    half, span = width // halves, some * len(weights)
    cols = divisor(some, 256)
    n, m = len(blocks), len(weights)

    def kernel(*refs):
        out_ref, tok_ref = refs[-2:]
        for j in range(m):

            def step(i, carry):
                here = pl.ds(pl.multiple_of(i * cols, cols), cols)
                there = pl.ds(pl.multiple_of(j * some + i * cols, cols), cols)
                y = None if total is None else refs[n + m][:, :, there].reshape(parts * rows, cols)
                for b, (at, _) in enumerate(blocks):
                    g = refs[b][...].reshape(parts * rows, half)
                    term = project_rows(g, refs[n + j][here, at * half : (at + 1) * half])
                    y = term if y is None else y + term
                out_ref[:, :, there] = y.astype(out_ref.dtype).reshape(parts, rows, cols)
                return carry

            lax.fori_loop(0, some // cols, step, 0)
        tok_ref[...] = jnp.zeros_like(tok_ref)

    once = pl.Buffered(1)
    here = pl.BlockSpec((parts, rows, span), lambda i: (0, 0, piece))
    if last:
        out_spec = pl.BlockSpec((parts, None, rows, span), lambda i: (0, chunk, 0, piece))
        out_shape = jax.ShapeDtypeStruct((parts, chunks, rows, span * pieces), BF16)
    else:
        out_spec, out_shape = here, jax.ShapeDtypeStruct((parts, rows, span * pieces), F32)
    sums = [] if total is None else [total]
    extra = ([] if held is None else [held]) + after
    return pl.pallas_call(
        kernel,
        grid=(1,),
        in_specs=[pl.BlockSpec((parts, rows, half), lambda i: (0, 0, 0), pipeline_mode=once)] * n
        + [pl.BlockSpec(memory_space=pltpu.VMEM)] * m
        + [pl.BlockSpec((parts, rows, span), lambda i: (0, 0, piece), pipeline_mode=once)] * len(sums)
        + [ANY] * len(extra),
        out_specs=[out_spec, TOKEN_SPEC],
        out_shape=[out_shape, TOKEN],
        input_output_aliases={} if held is None else {n + m + len(sums): 0},
        compiler_params=pltpu.CompilerParams(vmem_limit_bytes=LIMIT),
        cost_estimate=cost(SHORT),
        name="backward_piece",
    )(
        *[g for _, g in blocks],
        *[in_vmem(w) for w in weights],
        *sums,
        *extra,
    )


def relay(pos, flow, k, partial, came, held, after):
    rows, width = came.shape
    parts = (partial if held is None else held).shape[0]
    n_in = 1 + (partial is not None) + (held is not None) + len(after)

    def far(pos_ref, steps):
        way = pos_ref[1] if flow == 0 else -pos_ref[1]
        return lax.clamp(0, pos_ref[0] + way * steps, parts - 1)

    def kernel(pos_ref, *refs):
        came_ref, x_ref = refs[0], refs[n_in]
        place = pos_ref[2] if flow == 0 else parts - 1 - pos_ref[2]
        if held is not None:
            store = pltpu.make_async_copy(came_ref, refs[n_in + 1].at[far(pos_ref, -k)], refs[-1])
            pl.when(place >= k)(store.start)
        if partial is not None:

            @pl.when(place < k)
            def _():
                x_ref[...] = (came_ref[...].astype(F32) + refs[1][...].astype(F32)).astype(BF16)

            @pl.when(place >= k)
            def _():
                x_ref[...] = came_ref[...]

        else:
            x_ref[...] = came_ref[...]
        if held is not None:
            pl.when(place >= k)(store.wait)

    line = jax.ShapeDtypeStruct((rows, width), BF16)
    whole = pl.BlockSpec((rows, width), lambda i, w: (0, 0), pipeline_mode=pl.Buffered(1))
    args, specs, out_specs, out_shape, alias = [came], [whole], [whole], [line], {}
    if partial is not None:
        term = pl.BlockSpec(
            (None, rows, width),
            lambda i, w: (far(w, parts - k), 0, 0),
            pipeline_mode=pl.Buffered(1),
        )
        specs.append(term)
        args.append(partial)
    if held is not None:
        alias[1 + len(args)] = 1
        specs.append(ANY)
        args.append(held)
        out_specs.append(ANY)
        out_shape.append(jax.ShapeDtypeStruct(held.shape, BF16))
    outs = pl.pallas_call(
        kernel,
        grid_spec=pltpu.PrefetchScalarGridSpec(
            num_scalar_prefetch=1,
            grid=(1,),
            in_specs=specs + [ANY] * len(after),
            out_specs=out_specs,
            scratch_shapes=[pltpu.SemaphoreType.DMA] if held is not None else [],
        ),
        out_shape=out_shape,
        input_output_aliases=alias,
        compiler_params=pltpu.CompilerParams(vmem_limit_bytes=SMALL),
        cost_estimate=cost(LONG),
        name="relay",
    )(pos, *args, *after)
    return outs[0], (outs[1] if held is not None else None)


def store_last(pos, came, held, after):
    parts = held.shape[0]

    def kernel(pos_ref, a_ref, b_ref, *refs):
        out_ref, sem = refs[-2:]
        rank, way, place = pos_ref[0], pos_ref[1], pos_ref[2]
        ends = (
            (place == parts - 1, a_ref, rank - way * (parts - 1)),
            (place == 0, b_ref, rank + way * (parts - 1)),
        )
        for at_end, came_ref, at in ends:
            copy = pltpu.make_async_copy(came_ref, out_ref.at[lax.clamp(0, at, parts - 1)], sem)

            @pl.when(at_end)
            def _():
                copy.start()
                copy.wait()

    return pl.pallas_call(
        kernel,
        grid_spec=pltpu.PrefetchScalarGridSpec(
            num_scalar_prefetch=1,
            grid=(1,),
            in_specs=[pl.BlockSpec(held.shape[1:], lambda i, w: (0, 0))] * 2 + [ANY] * (1 + len(after)),
            out_specs=ANY,
            scratch_shapes=[pltpu.SemaphoreType.DMA],
        ),
        out_shape=jax.ShapeDtypeStruct(held.shape, BF16),
        input_output_aliases={3: 0},
        compiler_params=pltpu.CompilerParams(vmem_limit_bytes=SMALL),
        cost_estimate=cost(SHORT),
        name="store_last",
    )(pos, *came, held, *after)


def first_block(pos, flow, partial):
    parts, rows, width = partial.shape

    def there(i, w):
        way = w[1] if flow == 0 else -w[1]
        return lax.clamp(0, w[0] + way * (parts - 1), parts - 1), 0, 0

    def kernel(pos_ref, p_ref, out_ref):
        out_ref[...] = p_ref[...]

    return pl.pallas_call(
        kernel,
        grid_spec=pltpu.PrefetchScalarGridSpec(
            num_scalar_prefetch=1,
            grid=(1,),
            in_specs=[pl.BlockSpec((None, rows, width), there)],
            out_specs=pl.BlockSpec((rows, width), lambda i, w: (0, 0)),
        ),
        out_shape=jax.ShapeDtypeStruct((rows, width), BF16),
        compiler_params=pltpu.CompilerParams(vmem_limit_bytes=SMALL),
        cost_estimate=cost(SHORT),
        name="first_block",
    )(pos, partial)


def norm_terms(p_ref, a_ref, b_ref, res_ref, grad_ref, gain_ref, at):
    proj = p_ref[:, at].astype(F32) + a_ref[:, at].astype(F32) + b_ref[:, at].astype(F32)
    z = res_ref[:, at].astype(F32) + proj
    scaled = gain_ref[:, at].astype(F32) * grad_ref[:, at].astype(F32)
    return z, scaled


def norm_specs(ins, half, chunk, at):
    _, rows, wide = ins[0].shape
    once = pl.Buffered(1)
    whole = pl.BlockSpec((rows, wide), lambda i, r: (0, 0), pipeline_mode=once)
    own = pl.BlockSpec((rows, half), lambda i, r: (0, at), pipeline_mode=once)
    mine = pl.BlockSpec((None, rows, wide), lambda i, r: (r[0], 0, 0), pipeline_mode=once)
    return [mine, whole, whole, own, own, pl.BlockSpec((1, half), lambda i, r: (0, at))]


def norm_sums(pos, ins, half, chunk, at, sums, after):
    rows = ins[0].shape[1]
    cols = divisor(half, 1024)

    def kernel(pos_ref, *refs):
        square_ref, cross_ref = refs[-2:]

        def step(i, sums):
            z, scaled = norm_terms(*refs[:6], pl.ds(pl.multiple_of(i * cols, cols), cols))
            square, cross = sums
            for j in range(0, cols, 128):
                zj = z[:, j : j + 128]
                square = square + zj * zj
                cross = cross + zj * scaled[:, j : j + 128]
            return square, cross

        zero = jnp.zeros((rows, 128), F32)
        start = (zero, zero) if sums is None else (refs[6][...], refs[7][...])
        square_ref[...], cross_ref[...] = lax.fori_loop(0, half // cols, step, start)

    stat = pl.BlockSpec((rows, 128), lambda i, r: (0, 0))
    before = [] if sums is None else list(sums)
    return pl.pallas_call(
        kernel,
        grid_spec=pltpu.PrefetchScalarGridSpec(
            num_scalar_prefetch=1,
            grid=(1,),
            in_specs=norm_specs(ins, half, chunk, at) + [stat] * len(before) + [ANY] * len(after),
            out_specs=[stat, stat],
        ),
        out_shape=[jax.ShapeDtypeStruct((rows, 128), F32)] * 2,
        compiler_params=pltpu.CompilerParams(vmem_limit_bytes=LIMIT),
        cost_estimate=cost(LONG),
        name="norm_sums",
    )(pos, *ins, *before, *after)


def norm_out(pos, ins, half, chunk, sums, proj_out, after):
    parts, rows, wide = ins[0][1][0].shape
    cols = divisor(half, 1024)
    n, width = len(ins), ins[0][1][3].shape[1]
    with_b = proj_out

    def kernel(pos_ref, *refs):
        square_ref, cross_ref = refs[6 * n], refs[6 * n + 1]
        if with_b is None:
            out_ref, held_ref, sem = refs[-3:]
        else:
            out_ref, held_ref, rest_ref, sem = refs[-4:]
        inv = lax.rsqrt(jnp.sum(square_ref[...], axis=-1, keepdims=True) / width + EPS)
        slope = inv * inv * inv * (jnp.sum(cross_ref[...], axis=-1, keepdims=True) / width)
        for j in range(n):
            to_ref = out_ref if j == 0 else rest_ref.at[j - 1]

            def step(i, carry):
                here = pl.ds(pl.multiple_of(i * cols, cols), cols)
                z, scaled = norm_terms(*refs[6 * j : 6 * j + 6], here)
                to_ref[:, here] = (inv * scaled - z * slope).astype(BF16)
                return carry

            lax.fori_loop(0, half // cols, step, 0)
        if with_b is not None:
            p_ref = refs[6 * n + 2]
            b = project_rows(out_ref[:, :half], p_ref[:, :half])
            for j in range(1, n):
                b = b + project_rows(rest_ref[j - 1], p_ref[:, j * half : (j + 1) * half])
            a = sum(refs[6 * (n - 1) + j][:, half:].astype(F32) for j in range(3))
            out_ref[:, half:] = (a + spread(b.astype(BF16), b.shape[1])).astype(BF16)
        else:
            out_ref[:, half:] = jnp.zeros((rows, wide - half), BF16)
        own = pltpu.make_async_copy(out_ref, held_ref.at[pos_ref[0]], sem)
        own.start()
        own.wait()

    stat = pl.BlockSpec((rows, 128), lambda i, r: (0, 0))
    specs, args = [], []
    for at, one in ins:
        specs += norm_specs(one, half, chunk, at)
        args += one
    specs, args = specs + [stat, stat], args + list(sums)
    scratch = [pltpu.SemaphoreType.DMA]
    if with_b is not None:
        specs.append(
            pl.BlockSpec(proj_out.shape, lambda i, r: (0, 0), pipeline_mode=pl.Buffered(1))
        )
        args.append(proj_out)
        scratch = [pltpu.VMEM((max(1, n - 1), rows, half), BF16)] + scratch
    return pl.pallas_call(
        kernel,
        grid_spec=pltpu.PrefetchScalarGridSpec(
            num_scalar_prefetch=1,
            grid=(1,),
            in_specs=specs + [ANY] * len(after),
            out_specs=[pl.BlockSpec((rows, wide), lambda i, r: (0, 0)), ANY],
            scratch_shapes=scratch,
        ),
        out_shape=[
            jax.ShapeDtypeStruct((rows, wide), BF16),
            jax.ShapeDtypeStruct((parts, rows, wide), BF16),
        ],
        compiler_params=pltpu.CompilerParams(vmem_limit_bytes=LIMIT),
        cost_estimate=cost(SHORT),
        name="norm_out",
    )(pos, *args, *after)


def tie(value, after):
    def kernel(value_ref, *refs):
        refs[-1][...] = value_ref[...]

    whole = pl.BlockSpec(value.shape, lambda i: (0,) * value.ndim)
    return pl.pallas_call(
        kernel,
        grid=(1,),
        in_specs=[whole] + [ANY] * len(after),
        out_specs=whole,
        out_shape=jax.ShapeDtypeStruct(value.shape, value.dtype),
        compiler_params=pltpu.CompilerParams(vmem_limit_bytes=SMALL),
        cost_estimate=cost(SHORT),
        name="tie",
    )(value, *after)


def touch(x):
    def kernel(x_ref, out_ref):
        out_ref[...] = jnp.zeros_like(out_ref)

    return pl.pallas_call(
        kernel,
        grid=(1,),
        in_specs=[ANY],
        out_specs=TOKEN_SPEC,
        out_shape=TOKEN,
        compiler_params=pltpu.CompilerParams(vmem_limit_bytes=SMALL),
        cost_estimate=cost(SHORT),
        name="touch",
    )(x)


def from_others(value, axis, size):
    return [value] + [
        lax.ppermute(value, axis, [(d, (d + shift) % size) for d in range(size)])
        for shift in range(1, size)
    ]


def sketch_slice(pos, gathered, segment_ids, kp, after):
    parts, rows, wide = gathered[0].shape
    extra, mine = 2 * kp, kp // parts
    chunks, tokens = len(gathered), segment_ids.shape[1]

    def kernel(pos_ref, *refs):
        out_ref, sum_ref = refs[-2:]
        example = lax.broadcasted_iota(jnp.int32, (8, tokens), 0)
        by_row = jnp.where(refs[chunks][...] == example, 1.0, 0.0).astype(BF16)
        same = lax.broadcasted_iota(jnp.int32, (tokens, tokens), 0) == lax.broadcasted_iota(
            jnp.int32, (tokens, tokens), 1
        )
        weights = project_rows(jnp.where(same, 1.0, 0.0).astype(BF16), by_row)
        weights = weights.reshape(parts, chunks, rows, 8)
        for e in range(EX_DEV):
            total = None
            for c in range(chunks):
                both = refs[c][...].reshape(parts * rows, extra)
                weight = weights[:, c].reshape(parts * rows, 8)[:, e : e + 1]
                part = (both.astype(F32) * weight).astype(BF16)
                term = lax.dot_general(
                    part, both, (((0,), (0,)), ((), ())), preferred_element_type=F32
                )
                total = term if total is None else total + term
            sum_ref[e] = total
        low = lax.broadcasted_iota(jnp.int32, (1, extra), 1) < kp
        for r in range(parts):

            @pl.when(pos_ref[0] == r)
            def _():
                for e in range(EX_DEV):
                    for i in range(mine // 2):
                        at = kp + r * mine + 2 * i
                        left, right = sum_ref[e, at : at + 1, :], sum_ref[e, at + 1 : at + 2, :]
                        out_ref[e : e + 1, i * extra : (i + 1) * extra] = jnp.where(
                            low, left, pltpu.roll(right, kp, 1)
                        )

    return pl.pallas_call(
        kernel,
        grid_spec=pltpu.PrefetchScalarGridSpec(
            num_scalar_prefetch=1,
            grid=(1,),
            in_specs=[pl.BlockSpec((parts, rows, extra), lambda i, w: (0, 0, wide // extra - 1))] * chunks
            + [pl.BlockSpec(segment_ids.shape, lambda i, w: (0, 0))]
            + [ANY] * len(after),
            out_specs=pl.BlockSpec((EX_DEV, mine * kp), lambda i, w: (0, 0)),
            scratch_shapes=[pltpu.VMEM((EX_DEV, extra, extra), F32)],
        ),
        out_shape=jax.ShapeDtypeStruct((EX_DEV, mine * kp), F32),
        compiler_params=pltpu.CompilerParams(vmem_limit_bytes=LIMIT),
        cost_estimate=cost(SHORT),
        name="sketch_slice",
    )(pos, *gathered, segment_ids, *after)


def score_terms(pos, sketches, queries, after):
    size = len(sketches)
    n, depth = queries.shape

    def kernel(pos_ref, *refs):
        out_ref, all_ref, parts_ref = refs[-3:]
        for back in range(size):
            all_ref[lax.rem(pos_ref[3] - back + size, size)] = refs[back][...]
        for d in range(size):
            rest = all_ref[d]
            for t in range(3):
                part = rest.astype(BF16).astype(F32)
                rest = rest - part
                at = (t * size + d) * EX_DEV
                parts_ref[at : at + EX_DEV, :] = part
        terms = project_rows(parts_ref[...].astype(BF16), refs[size][...])
        n_out = size * EX_DEV
        out_ref[...] = terms[:n_out] + terms[n_out : 2 * n_out] + terms[2 * n_out :]

    return pl.pallas_call(
        kernel,
        grid_spec=pltpu.PrefetchScalarGridSpec(
            num_scalar_prefetch=1,
            grid=(1,),
            in_specs=[pl.BlockSpec((EX_DEV, depth), lambda i, w: (0, 0))] * size
            + [pl.BlockSpec((n, depth), lambda i, w: (0, 0))]
            + [ANY] * len(after),
            out_specs=pl.BlockSpec((size * EX_DEV, n), lambda i, w: (0, 0)),
            scratch_shapes=[
                pltpu.VMEM((size, EX_DEV, depth), F32),
                pltpu.VMEM((3 * size * EX_DEV, depth), F32),
            ],
        ),
        out_shape=jax.ShapeDtypeStruct((size * EX_DEV, n), F32),
        compiler_params=pltpu.CompilerParams(vmem_limit_bytes=LIMIT),
        cost_estimate=cost(SHORT),
        name="score_terms",
    )(pos, *sketches, queries, *after)


def score_sum(pos, terms, after):
    size = len(terms)
    shape = terms[0].shape

    def kernel(pos_ref, *refs):
        out_ref, all_ref = refs[-2:]
        for back in range(size):
            all_ref[lax.rem(pos_ref[0] - back + size, size)] = refs[back][...]
        total = all_ref[0]
        for d in range(1, size):
            total = total + all_ref[d]
        out_ref[...] = total

    whole = pl.BlockSpec(shape, lambda i, w: (0, 0))
    return pl.pallas_call(
        kernel,
        grid_spec=pltpu.PrefetchScalarGridSpec(
            num_scalar_prefetch=1,
            grid=(1,),
            in_specs=[whole] * size + [ANY] * len(after),
            out_specs=whole,
            scratch_shapes=[pltpu.VMEM((size,) + shape, F32)],
        ),
        out_shape=jax.ShapeDtypeStruct(shape, F32),
        compiler_params=pltpu.CompilerParams(vmem_limit_bytes=SMALL),
        cost_estimate=cost(SHORT),
        name="score_sum",
    )(pos, *terms, *after)


def body(inputs, residual, out_grad, norm_gain, w_out, proj_in, proj_out, queries, segment_ids):
    parts = lax.axis_size("tensor")
    rank = lax.axis_index("tensor")
    queriers = lax.axis_size("query")
    q_rank = lax.axis_index("query")
    tokens = inputs.shape[1]
    share = tokens // parts
    chunks = max(1, min(CHUNKS, share // 16))
    rows = share // chunks
    by_share = inputs.reshape(parts, chunks, rows, inputs.shape[2])
    gain = norm_gain.reshape(1, -1)
    half = w_out.shape[1] // HALVES
    kp = proj_out.shape[0]

    up = 1 - 2 * lax.rem(q_rank, 2)
    pos = jnp.stack([rank, up, jnp.where(up == 1, rank, parts - 1 - rank), q_rank]).astype(jnp.int32)

    def pairs(flow, low, high):
        out = []
        for q in range(queriers):
            way = 1 if (q % 2 == 0) == (flow == 0) else -1
            for t in range(parts):
                spot = t if way == 1 else parts - 1 - t
                if low <= spot <= min(high, parts - 2):
                    out.append((t * queriers + q, (t + way) * queriers + q))
        return out

    work, marks, resident = [], [], []
    partials, totals, result = {}, {}, [None]

    def forward(c, h, piece, pieces, after):
        partials[c, h], mark = forward_piece(
            by_share,
            w_out,
            c,
            HALVES,
            h,
            2 * kp,
            piece,
            pieces,
            partials.get((c, h)),
            after,
        )
        if h == HALVES - 1 and piece == pieces - 1:
            partials[c, h] = forward_extra(by_share, proj_in, c, partials[c, h], [mark])
        return mark

    def backward(c, blocks, total, last, piece, pieces, after):
        held = result[0] if last else totals.get(c)
        some = resident[piece * QUARTERS // pieces : (piece + 1) * QUARTERS // pieces]
        done, mark = backward_piece(
            blocks, some, c, chunks, HALVES, piece, pieces, total, last, held, after
        )
        if last:
            result[0] = done
        else:
            totals[c] = done
        return mark

    def do_one(after, touching=False):
        if work:
            marks[:] = [work.pop(0)[1](after)]
        elif touching:
            marks[:] = [touch(after[0])]

    def finish(key, after):
        while any(k == key for k, _ in work):
            do_one(list(marks) + after)

    def load(count, after):
        for _ in range(count):
            resident.append(load_weights(w_out, len(resident), QUARTERS, after))
            after = [resident[-1]]
        marks[:] = after

    def add_forward(c, h, pieces):
        for piece in range(pieces):
            work.append(((c, h), functools.partial(forward, c, h, piece, pieces)))

    add_forward(0, 0, 1)
    finish((0, 0), [])
    gathered = []
    for slot in range(chunks + 1):
        rs, ag = slot < chunks, slot > 0
        came, held, sent, before = {}, {}, {}, None
        if ag:
            res, grd = in_vmem(own_rows[0]), in_vmem(own_rows[1])
            ins = [
                [partials[slot - 1, h], arrived[h, 0], arrived[h, 1], res, grd, gain]
                for h in range(HALVES)
            ]
            sums = None
            for h in range(HALVES):
                sums = norm_sums(pos, ins[h], half, slot - 1, h, sums, list(marks))
            grad = [None] * HALVES
            grad[0], held[0] = norm_out(
                pos, list(enumerate(ins)), half, slot - 1, sums, proj_out, []
            )
        for k in range(parts):
            gather_now, reduce_now = ag and k <= parts - 2, rs and k >= 1
            if not gather_now and not reduce_now:
                continue
            for h in range(HALVES):
                if k == 0 and h > 0:
                    if rs and slot > 1:
                        add_forward(slot, h, PIECES)
                    do_one([sent[h - 1, 1]])
                    grad[h], held[h] = norm_out(
                        pos, [(h, ins[h])], half, slot - 1, sums, None, list(marks)
                    )
                if reduce_now:
                    if slot == 0 and k == 1 and h > 0:
                        add_forward(0, h, 1)
                        do_one([sent[h - 1, 1]])
                    finish((slot, h), [sent[h - 1, 1]] if h > 0 else [])
                for flow in range(2):
                    if k == 0:
                        x = before = grad[h]
                    elif (h, flow) not in came:
                        x = first_block(pos, flow, partials[slot, h])
                    else:
                        x, held[h] = relay(
                            pos,
                            flow,
                            k,
                            partials[slot, h] if reduce_now else None,
                            came[h, flow],
                            held.get(h),
                            list(marks) + ([] if before is None else [before]),
                        )
                        before = x
                    came[h, flow] = lax.ppermute(
                        x,
                        ("tensor", "query"),
                        pairs(flow, 0 if reduce_now else k, parts - 2 if gather_now else k - 1),
                    )
                    sent[h, flow] = x
                    if rs and (k, h, flow) == (parts - 1, HALVES - 1, 1):
                        own_rows = load_rows(residual, out_grad, slot, rows, [x])
                        x = own_rows[0]
                    if slot == chunks - 1 and flow == 1 and slot > 0:
                        if (k, h) == (parts - 2, HALVES - 1):
                            load(1, [x])
                            continue
                        if (k, h) == (parts - 1, HALVES - 1):
                            load(QUARTERS - len(resident), [x])
                            continue
                    if slot == 0 and k == 2 and (h, flow) == (HALVES - 1, 1) and chunks > 1 and HALVES > 1:
                        add_forward(1, 1, 2 * PIECES)
                        do_one([x])
                        continue
                    if slot == 0 and k == parts - 1 and (h, flow) == (0, 1):
                        do_one([x])
                        continue
                    if slot == 0 and k == parts - 1 and (h, flow) == (HALVES - 1, 1) and chunks > 1:
                        work.insert(0, ((1, 0), functools.partial(forward, 1, 0, 0, 1)))
                    if slot == 0 and work and work[0][0] == (1, 1):
                        continue
                    if k > 0 and (slot > 0 or k > 1) and not (slot == 1 and work and k == 1 and flow == 0):
                        if slot == chunks and (h, flow, k) != (HALVES - 1, 1, parts - 2):
                            marks[:] = [touch(x)]
                        else:
                            do_one([x], slot == chunks)
                if k == 0 and slot == chunks and h == HALVES - 1:
                    marks[:] = [touch(sent[h, 1])]
        if ag:
            if slot + 1 < chunks:
                add_forward(slot + 1, 0, PIECES)
            if rs:
                blocks = [(h, held[h]) for h in range(HALVES)]
                for piece in range(PIECES):
                    work.append(
                        (
                            ("b", slot - 1),
                            functools.partial(backward, slot - 1, blocks, None, True, piece, PIECES),
                        )
                    )
            else:
                while work:
                    do_one(list(marks))
                marks[:] = [tie(marks[0], [came[0, 0]])]
                held[0] = store_last(pos, (came[0, 0], came[0, 1]), held[0], list(marks))
            gathered.append(held[0])
        arrived = came
    last = chunks - 1
    sketch = sketch_slice(pos, gathered, segment_ids, kp, [])
    marks[:] = [backward(last, [(0, held[0])], None, HALVES == 1, 0, 1, [sketch])]
    for h in range(1, HALVES):
        marks[:] = [tie(marks[0], [came[h, 0]])]
        held[h] = store_last(pos, (came[h, 0], came[h, 1]), held[h], list(marks))
    terms = score_terms(pos, from_others(sketch, "query", queriers), queries, list(marks))
    for h in range(1, HALVES):
        marks[:] = [backward(last, [(h, held[h])], totals.get(last), h == HALVES - 1, 0, 1, [terms])]
    scores = score_sum(pos, from_others(terms, "tensor", parts), list(marks))
    return (result[0].reshape(1, tokens, -1), scores)


def solution(mesh):
    return jax.shard_map(
        body,
        mesh=mesh,
        in_specs=(
            P(("groups", "dp", "query"), None, "tensor"),
            P(("groups", "dp", "query"), "tensor", None),
            P(("groups", "dp", "query"), "tensor", None),
            P(),
            P("tensor", None),
            P(None, "tensor"),
            P(),
            P("query", "tensor"),
            P(("groups", "dp", "query"), None),
        ),
        out_specs=(P(("groups", "dp", "query"), None, "tensor"), P(("groups", "dp"), "query")),
        check_vma=False,
    )
```

```python
import functools

import jax
import jax.numpy as jnp
from jax import lax
from jax.experimental import pallas as pl
from jax.experimental.pallas import tpu as pltpu
from jax.sharding import PartitionSpec as P

EX_DEV = 4
EPS = 1e-05
CHUNKS = 2
HALVES = 2
PIECES = 2
SHORT, LONG = 0.2, 5.0
SMALL, LIMIT, LARGE = 5 * 1024 * 1024, 9 * 1024 * 1024, 24 * 1024 * 1024
QUARTERS = 4

F32, BF16 = jnp.float32, jnp.bfloat16
ANY = pl.BlockSpec(memory_space=pl.ANY)
TOKEN = jax.ShapeDtypeStruct((8, 128), F32)
TOKEN_SPEC = pl.BlockSpec((8, 128), lambda *_: (0, 0))


def divisor(total, wanted):
    size = min(total, wanted)
    while total % size:
        size //= 2
    return size


def cost(microseconds):
    return pl.CostEstimate(flops=0, bytes_accessed=int(microseconds * 3.6e6), transcendentals=0)


def in_hbm(x):
    return pltpu.with_memory_space_constraint(x, pltpu.HBM)


def project_rows(values, matrix):
    return lax.dot_general(
        values, matrix, (((1,), (1,)), ((), ())), preferred_element_type=F32
    )


def spread(values, first):
    k = values.shape[1]
    row = lax.broadcasted_iota(jnp.int32, (k, 2 * k), 0)
    col = lax.broadcasted_iota(jnp.int32, (k, 2 * k), 1)
    return jnp.dot(values, jnp.where(col == row + first, 1.0, 0.0).astype(BF16), preferred_element_type=F32)


def forward_extra(by_share, proj_in, chunk, held, after):
    parts, _, rows, depth = by_share.shape
    extra = 2 * proj_in.shape[0]
    at = held.shape[2] // extra - 1

    def kernel(x_ref, p_ref, *refs):
        part = project_rows(x_ref[...].reshape(parts * rows, depth), p_ref[...]).astype(BF16)
        refs[-1][...] = spread(part, 0).astype(BF16).reshape(parts, rows, extra)

    return pl.pallas_call(
        kernel,
        grid=(1,),
        in_specs=[
            pl.BlockSpec((parts, None, rows, depth), lambda i: (0, chunk, 0, 0)),
            pl.BlockSpec(proj_in.shape, lambda i: (0, 0)),
        ]
        + [ANY] * (1 + len(after)),
        out_specs=pl.BlockSpec((parts, rows, extra), lambda i: (0, 0, at)),
        out_shape=jax.ShapeDtypeStruct(held.shape, BF16),
        input_output_aliases={2: 0},
        compiler_params=pltpu.CompilerParams(vmem_limit_bytes=LIMIT),
        cost_estimate=cost(SHORT),
        name="forward_extra",
    )(by_share, proj_in, held, *after)


def forward_piece(by_share, w_out, chunk, halves, half_at, extra, piece, pieces, held, after):
    parts, _, rows, depth = by_share.shape
    half = w_out.shape[1] // halves
    span = half // pieces
    cols = divisor(span, max(256, span // 4))
    steps = span // cols
    base = half_at * half + piece * span

    def kernel(x_ref, w_ref, *refs):
        out_ref, tok_ref, held_ref, sems = refs[-4:]
        i = pl.program_id(0)

        def copy(j):
            columns = pl.ds(pl.multiple_of(base + j * cols, cols), cols)
            return pltpu.make_async_copy(w_ref.at[:, columns], held_ref.at[j], sems.at[j])

        @pl.when(i == 0)
        def _():
            for j in range(steps):
                copy(j).start()

        copy(i).wait()
        x = x_ref[...].reshape(parts * rows, depth)
        y = jnp.dot(x, held_ref[i], preferred_element_type=F32).astype(BF16)
        out_ref[...] = y.reshape(parts, rows, cols)
        tok_ref[...] = jnp.zeros_like(tok_ref)

    more = ([] if held is None else [held]) + after
    return pl.pallas_call(
        kernel,
        grid=(steps,),
        in_specs=[
            pl.BlockSpec(
                (parts, None, rows, depth), lambda i: (0, chunk, 0, 0), pipeline_mode=pl.Buffered(1)
            )
        ]
        + [ANY] * (1 + len(more)),
        out_specs=[
            pl.BlockSpec((parts, rows, cols), lambda i: (0, 0, piece * steps + i)),
            TOKEN_SPEC,
        ],
        out_shape=[jax.ShapeDtypeStruct((parts, rows, half + extra), BF16), TOKEN],
        scratch_shapes=[pltpu.VMEM((steps, depth, cols), BF16), pltpu.SemaphoreType.DMA((steps,))],
        input_output_aliases={} if held is None else {2: 0},
        compiler_params=pltpu.CompilerParams(vmem_limit_bytes=LARGE),
        cost_estimate=cost(SHORT),
        name="forward_piece",
    )(in_hbm(by_share) if chunk == 0 and half_at == 0 else by_share, in_hbm(w_out), *more)


def load_weights(w_out, piece, pieces, after):
    rows = w_out.shape[0] // pieces
    width = w_out.shape[1]

    def kernel(w_ref, *refs):
        out_ref, sem = refs[-2:]
        copy = pltpu.make_async_copy(w_ref.at[pl.ds(piece * rows, rows)], out_ref, sem)
        copy.start()
        copy.wait()

    return pl.pallas_call(
        kernel,
        in_specs=[ANY] * (1 + len(after)),
        out_specs=pl.BlockSpec(memory_space=pltpu.VMEM),
        out_shape=pltpu.VMEM((rows, width), BF16),
        scratch_shapes=[pltpu.SemaphoreType.DMA],
        compiler_params=pltpu.CompilerParams(vmem_limit_bytes=SMALL),
        cost_estimate=cost(SHORT),
        name="load_weights",
    )(in_hbm(w_out), *after)


def load_rows(residual, out_grad, chunk, rows, after):
    width = residual.shape[2]

    def kernel(*refs):
        out_refs, sems = refs[-3:-1], refs[-1]
        copies = [
            pltpu.make_async_copy(refs[j].at[0, pl.ds(chunk * rows, rows)], out_refs[j], sems.at[j])
            for j in range(2)
        ]
        for copy in copies:
            copy.start()
        for copy in copies:
            copy.wait()

    return pl.pallas_call(
        kernel,
        in_specs=[ANY] * (2 + len(after)),
        out_specs=[pl.BlockSpec(memory_space=pltpu.VMEM)] * 2,
        out_shape=[pltpu.VMEM((rows, width), BF16)] * 2,
        scratch_shapes=[pltpu.SemaphoreType.DMA((2,))],
        compiler_params=pltpu.CompilerParams(vmem_limit_bytes=SMALL),
        cost_estimate=cost(SHORT),
        name="load_rows",
    )(in_hbm(residual), in_hbm(out_grad), *after)


def in_vmem(x):
    return pltpu.with_memory_space_constraint(x, pltpu.VMEM)


def backward_piece(blocks, weights, chunk, chunks, halves, piece, pieces, total, last, held, after):
    parts, rows, _ = blocks[0][1].shape
    some, width = weights[0].shape
    half, span = width // halves, some * len(weights)
    cols = divisor(some, 256)
    n, m = len(blocks), len(weights)

    def kernel(*refs):
        out_ref, tok_ref = refs[-2:]
        for j in range(m):

            def step(i, carry):
                here = pl.ds(pl.multiple_of(i * cols, cols), cols)
                there = pl.ds(pl.multiple_of(j * some + i * cols, cols), cols)
                y = None if total is None else refs[n + m][:, :, there].reshape(parts * rows, cols)
                for b, (at, _) in enumerate(blocks):
                    g = refs[b][...].reshape(parts * rows, half)
                    term = project_rows(g, refs[n + j][here, at * half : (at + 1) * half])
                    y = term if y is None else y + term
                out_ref[:, :, there] = y.astype(out_ref.dtype).reshape(parts, rows, cols)
                return carry

            lax.fori_loop(0, some // cols, step, 0)
        tok_ref[...] = jnp.zeros_like(tok_ref)

    once = pl.Buffered(1)
    here = pl.BlockSpec((parts, rows, span), lambda i: (0, 0, piece))
    if last:
        out_spec = pl.BlockSpec((parts, None, rows, span), lambda i: (0, chunk, 0, piece))
        out_shape = jax.ShapeDtypeStruct((parts, chunks, rows, span * pieces), BF16)
    else:
        out_spec, out_shape = here, jax.ShapeDtypeStruct((parts, rows, span * pieces), F32)
    sums = [] if total is None else [total]
    extra = ([] if held is None else [held]) + after
    return pl.pallas_call(
        kernel,
        grid=(1,),
        in_specs=[pl.BlockSpec((parts, rows, half), lambda i: (0, 0, 0), pipeline_mode=once)] * n
        + [pl.BlockSpec(memory_space=pltpu.VMEM)] * m
        + [pl.BlockSpec((parts, rows, span), lambda i: (0, 0, piece), pipeline_mode=once)] * len(sums)
        + [ANY] * len(extra),
        out_specs=[out_spec, TOKEN_SPEC],
        out_shape=[out_shape, TOKEN],
        input_output_aliases={} if held is None else {n + m + len(sums): 0},
        compiler_params=pltpu.CompilerParams(vmem_limit_bytes=LIMIT),
        cost_estimate=cost(SHORT),
        name="backward_piece",
    )(
        *[g for _, g in blocks],
        *[in_vmem(w) for w in weights],
        *sums,
        *extra,
    )


def relay(pos, flow, k, partial, came, held, after):
    rows, width = came.shape
    parts = (partial if held is None else held).shape[0]
    n_in = 1 + (partial is not None) + (held is not None) + len(after)

    def far(pos_ref, steps):
        way = pos_ref[1] if flow == 0 else -pos_ref[1]
        return lax.clamp(0, pos_ref[0] + way * steps, parts - 1)

    def kernel(pos_ref, *refs):
        came_ref, x_ref = refs[0], refs[n_in]
        place = pos_ref[2] if flow == 0 else parts - 1 - pos_ref[2]
        if held is not None:
            store = pltpu.make_async_copy(came_ref, refs[n_in + 1].at[far(pos_ref, -k)], refs[-1])
            pl.when(place >= k)(store.start)
        if partial is not None:

            @pl.when(place < k)
            def _():
                x_ref[...] = (came_ref[...].astype(F32) + refs[1][...].astype(F32)).astype(BF16)

            @pl.when(place >= k)
            def _():
                x_ref[...] = came_ref[...]

        else:
            x_ref[...] = came_ref[...]
        if held is not None:
            pl.when(place >= k)(store.wait)

    line = jax.ShapeDtypeStruct((rows, width), BF16)
    whole = pl.BlockSpec((rows, width), lambda i, w: (0, 0), pipeline_mode=pl.Buffered(1))
    args, specs, out_specs, out_shape, alias = [came], [whole], [whole], [line], {}
    if partial is not None:
        term = pl.BlockSpec(
            (None, rows, width),
            lambda i, w: (far(w, parts - k), 0, 0),
            pipeline_mode=pl.Buffered(1),
        )
        specs.append(term)
        args.append(partial)
    if held is not None:
        alias[1 + len(args)] = 1
        specs.append(ANY)
        args.append(held)
        out_specs.append(ANY)
        out_shape.append(jax.ShapeDtypeStruct(held.shape, BF16))
    outs = pl.pallas_call(
        kernel,
        grid_spec=pltpu.PrefetchScalarGridSpec(
            num_scalar_prefetch=1,
            grid=(1,),
            in_specs=specs + [ANY] * len(after),
            out_specs=out_specs,
            scratch_shapes=[pltpu.SemaphoreType.DMA] if held is not None else [],
        ),
        out_shape=out_shape,
        input_output_aliases=alias,
        compiler_params=pltpu.CompilerParams(vmem_limit_bytes=SMALL),
        cost_estimate=cost(LONG),
        name="relay",
    )(pos, *args, *after)
    return outs[0], (outs[1] if held is not None else None)


def store_last(pos, came, held, after):
    parts = held.shape[0]

    def kernel(pos_ref, a_ref, b_ref, *refs):
        out_ref, sem = refs[-2:]
        rank, way, place = pos_ref[0], pos_ref[1], pos_ref[2]
        ends = (
            (place == parts - 1, a_ref, rank - way * (parts - 1)),
            (place == 0, b_ref, rank + way * (parts - 1)),
        )
        for at_end, came_ref, at in ends:
            copy = pltpu.make_async_copy(came_ref, out_ref.at[lax.clamp(0, at, parts - 1)], sem)

            @pl.when(at_end)
            def _():
                copy.start()
                copy.wait()

    return pl.pallas_call(
        kernel,
        grid_spec=pltpu.PrefetchScalarGridSpec(
            num_scalar_prefetch=1,
            grid=(1,),
            in_specs=[pl.BlockSpec(held.shape[1:], lambda i, w: (0, 0))] * 2 + [ANY] * (1 + len(after)),
            out_specs=ANY,
            scratch_shapes=[pltpu.SemaphoreType.DMA],
        ),
        out_shape=jax.ShapeDtypeStruct(held.shape, BF16),
        input_output_aliases={3: 0},
        compiler_params=pltpu.CompilerParams(vmem_limit_bytes=SMALL),
        cost_estimate=cost(SHORT),
        name="store_last",
    )(pos, *came, held, *after)


def first_block(pos, flow, partial):
    parts, rows, width = partial.shape

    def there(i, w):
        way = w[1] if flow == 0 else -w[1]
        return lax.clamp(0, w[0] + way * (parts - 1), parts - 1), 0, 0

    def kernel(pos_ref, p_ref, out_ref):
        out_ref[...] = p_ref[...]

    return pl.pallas_call(
        kernel,
        grid_spec=pltpu.PrefetchScalarGridSpec(
            num_scalar_prefetch=1,
            grid=(1,),
            in_specs=[pl.BlockSpec((None, rows, width), there)],
            out_specs=pl.BlockSpec((rows, width), lambda i, w: (0, 0)),
        ),
        out_shape=jax.ShapeDtypeStruct((rows, width), BF16),
        compiler_params=pltpu.CompilerParams(vmem_limit_bytes=SMALL),
        cost_estimate=cost(SHORT),
        name="first_block",
    )(pos, partial)


def norm_terms(p_ref, a_ref, b_ref, res_ref, grad_ref, gain_ref, at):
    proj = p_ref[:, at].astype(F32) + a_ref[:, at].astype(F32) + b_ref[:, at].astype(F32)
    z = res_ref[:, at].astype(F32) + proj
    scaled = gain_ref[:, at].astype(F32) * grad_ref[:, at].astype(F32)
    return z, scaled


def norm_specs(ins, half, chunk, at):
    _, rows, wide = ins[0].shape
    once = pl.Buffered(1)
    whole = pl.BlockSpec((rows, wide), lambda i, r: (0, 0), pipeline_mode=once)
    own = pl.BlockSpec((rows, half), lambda i, r: (0, at), pipeline_mode=once)
    mine = pl.BlockSpec((None, rows, wide), lambda i, r: (r[0], 0, 0), pipeline_mode=once)
    return [mine, whole, whole, own, own, pl.BlockSpec((1, half), lambda i, r: (0, at))]


def norm_sums(pos, ins, half, chunk, at, sums, after):
    rows = ins[0].shape[1]
    cols = divisor(half, 1024)

    def kernel(pos_ref, *refs):
        square_ref, cross_ref = refs[-2:]

        def step(i, sums):
            z, scaled = norm_terms(*refs[:6], pl.ds(pl.multiple_of(i * cols, cols), cols))
            square, cross = sums
            for j in range(0, cols, 128):
                zj = z[:, j : j + 128]
                square = square + zj * zj
                cross = cross + zj * scaled[:, j : j + 128]
            return square, cross

        zero = jnp.zeros((rows, 128), F32)
        start = (zero, zero) if sums is None else (refs[6][...], refs[7][...])
        square_ref[...], cross_ref[...] = lax.fori_loop(0, half // cols, step, start)

    stat = pl.BlockSpec((rows, 128), lambda i, r: (0, 0))
    before = [] if sums is None else list(sums)
    return pl.pallas_call(
        kernel,
        grid_spec=pltpu.PrefetchScalarGridSpec(
            num_scalar_prefetch=1,
            grid=(1,),
            in_specs=norm_specs(ins, half, chunk, at) + [stat] * len(before) + [ANY] * len(after),
            out_specs=[stat, stat],
        ),
        out_shape=[jax.ShapeDtypeStruct((rows, 128), F32)] * 2,
        compiler_params=pltpu.CompilerParams(vmem_limit_bytes=LIMIT),
        cost_estimate=cost(LONG),
        name="norm_sums",
    )(pos, *ins, *before, *after)


def norm_out(pos, ins, half, chunk, sums, proj_out, after):
    parts, rows, wide = ins[0][1][0].shape
    cols = divisor(half, 1024)
    n, width = len(ins), ins[0][1][3].shape[1]
    with_b = proj_out

    def kernel(pos_ref, *refs):
        square_ref, cross_ref = refs[6 * n], refs[6 * n + 1]
        if with_b is None:
            out_ref, held_ref, sem = refs[-3:]
        else:
            out_ref, held_ref, rest_ref, sem = refs[-4:]
        inv = lax.rsqrt(jnp.sum(square_ref[...], axis=-1, keepdims=True) / width + EPS)
        slope = inv * inv * inv * (jnp.sum(cross_ref[...], axis=-1, keepdims=True) / width)
        for j in range(n):
            to_ref = out_ref if j == 0 else rest_ref.at[j - 1]

            def step(i, carry):
                here = pl.ds(pl.multiple_of(i * cols, cols), cols)
                z, scaled = norm_terms(*refs[6 * j : 6 * j + 6], here)
                to_ref[:, here] = (inv * scaled - z * slope).astype(BF16)
                return carry

            lax.fori_loop(0, half // cols, step, 0)
        if with_b is not None:
            p_ref = refs[6 * n + 2]
            b = project_rows(out_ref[:, :half], p_ref[:, :half])
            for j in range(1, n):
                b = b + project_rows(rest_ref[j - 1], p_ref[:, j * half : (j + 1) * half])
            a = sum(refs[6 * (n - 1) + j][:, half:].astype(F32) for j in range(3))
            out_ref[:, half:] = (a + spread(b.astype(BF16), b.shape[1])).astype(BF16)
        else:
            out_ref[:, half:] = jnp.zeros((rows, wide - half), BF16)
        own = pltpu.make_async_copy(out_ref, held_ref.at[pos_ref[0]], sem)
        own.start()
        own.wait()

    stat = pl.BlockSpec((rows, 128), lambda i, r: (0, 0))
    specs, args = [], []
    for at, one in ins:
        specs += norm_specs(one, half, chunk, at)
        args += one
    specs, args = specs + [stat, stat], args + list(sums)
    scratch = [pltpu.SemaphoreType.DMA]
    if with_b is not None:
        specs.append(
            pl.BlockSpec(proj_out.shape, lambda i, r: (0, 0), pipeline_mode=pl.Buffered(1))
        )
        args.append(proj_out)
        scratch = [pltpu.VMEM((max(1, n - 1), rows, half), BF16)] + scratch
    return pl.pallas_call(
        kernel,
        grid_spec=pltpu.PrefetchScalarGridSpec(
            num_scalar_prefetch=1,
            grid=(1,),
            in_specs=specs + [ANY] * len(after),
            out_specs=[pl.BlockSpec((rows, wide), lambda i, r: (0, 0)), ANY],
            scratch_shapes=scratch,
        ),
        out_shape=[
            jax.ShapeDtypeStruct((rows, wide), BF16),
            jax.ShapeDtypeStruct((parts, rows, wide), BF16),
        ],
        compiler_params=pltpu.CompilerParams(vmem_limit_bytes=LIMIT),
        cost_estimate=cost(SHORT),
        name="norm_out",
    )(pos, *args, *after)


def tie(value, after):
    def kernel(value_ref, *refs):
        refs[-1][...] = value_ref[...]

    whole = pl.BlockSpec(value.shape, lambda i: (0,) * value.ndim)
    return pl.pallas_call(
        kernel,
        grid=(1,),
        in_specs=[whole] + [ANY] * len(after),
        out_specs=whole,
        out_shape=jax.ShapeDtypeStruct(value.shape, value.dtype),
        compiler_params=pltpu.CompilerParams(vmem_limit_bytes=SMALL),
        cost_estimate=cost(SHORT),
        name="tie",
    )(value, *after)


def touch(x):
    def kernel(x_ref, out_ref):
        out_ref[...] = jnp.zeros_like(out_ref)

    return pl.pallas_call(
        kernel,
        grid=(1,),
        in_specs=[ANY],
        out_specs=TOKEN_SPEC,
        out_shape=TOKEN,
        compiler_params=pltpu.CompilerParams(vmem_limit_bytes=SMALL),
        cost_estimate=cost(SHORT),
        name="touch",
    )(x)


def from_others(value, axis, size):
    return [value] + [
        lax.ppermute(value, axis, [(d, (d + shift) % size) for d in range(size)])
        for shift in range(1, size)
    ]


def sketch_slice(pos, gathered, segment_ids, kp, after):
    parts, rows, wide = gathered[0].shape
    extra, mine = 2 * kp, kp // parts
    chunks, tokens = len(gathered), segment_ids.shape[1]

    def kernel(pos_ref, *refs):
        out_ref, sum_ref = refs[-2:]
        example = lax.broadcasted_iota(jnp.int32, (8, tokens), 0)
        by_row = jnp.where(refs[chunks][...] == example, 1.0, 0.0).astype(BF16)
        same = lax.broadcasted_iota(jnp.int32, (tokens, tokens), 0) == lax.broadcasted_iota(
            jnp.int32, (tokens, tokens), 1
        )
        weights = project_rows(jnp.where(same, 1.0, 0.0).astype(BF16), by_row)
        weights = weights.reshape(parts, chunks, rows, 8)
        for e in range(EX_DEV):
            total = None
            for c in range(chunks):
                both = refs[c][...].reshape(parts * rows, extra)
                weight = weights[:, c].reshape(parts * rows, 8)[:, e : e + 1]
                part = (both.astype(F32) * weight).astype(BF16)
                term = lax.dot_general(
                    part, both, (((0,), (0,)), ((), ())), preferred_element_type=F32
                )
                total = term if total is None else total + term
            sum_ref[e] = total
        low = lax.broadcasted_iota(jnp.int32, (1, extra), 1) < kp
        for r in range(parts):

            @pl.when(pos_ref[0] == r)
            def _():
                for e in range(EX_DEV):
                    for i in range(mine // 2):
                        at = kp + r * mine + 2 * i
                        left, right = sum_ref[e, at : at + 1, :], sum_ref[e, at + 1 : at + 2, :]
                        out_ref[e : e + 1, i * extra : (i + 1) * extra] = jnp.where(
                            low, left, pltpu.roll(right, kp, 1)
                        )

    return pl.pallas_call(
        kernel,
        grid_spec=pltpu.PrefetchScalarGridSpec(
            num_scalar_prefetch=1,
            grid=(1,),
            in_specs=[pl.BlockSpec((parts, rows, extra), lambda i, w: (0, 0, wide // extra - 1))] * chunks
            + [pl.BlockSpec(segment_ids.shape, lambda i, w: (0, 0))]
            + [ANY] * len(after),
            out_specs=pl.BlockSpec((EX_DEV, mine * kp), lambda i, w: (0, 0)),
            scratch_shapes=[pltpu.VMEM((EX_DEV, extra, extra), F32)],
        ),
        out_shape=jax.ShapeDtypeStruct((EX_DEV, mine * kp), F32),
        compiler_params=pltpu.CompilerParams(vmem_limit_bytes=LIMIT),
        cost_estimate=cost(SHORT),
        name="sketch_slice",
    )(pos, *gathered, segment_ids, *after)


def score_terms(pos, sketches, queries, after):
    size = len(sketches)
    n, depth = queries.shape

    def kernel(pos_ref, *refs):
        out_ref, all_ref, parts_ref = refs[-3:]
        for back in range(size):
            all_ref[lax.rem(pos_ref[3] - back + size, size)] = refs[back][...]
        for d in range(size):
            rest = all_ref[d]
            for t in range(3):
                part = rest.astype(BF16).astype(F32)
                rest = rest - part
                at = (t * size + d) * EX_DEV
                parts_ref[at : at + EX_DEV, :] = part
        terms = project_rows(parts_ref[...].astype(BF16), refs[size][...])
        n_out = size * EX_DEV
        out_ref[...] = terms[:n_out] + terms[n_out : 2 * n_out] + terms[2 * n_out :]

    return pl.pallas_call(
        kernel,
        grid_spec=pltpu.PrefetchScalarGridSpec(
            num_scalar_prefetch=1,
            grid=(1,),
            in_specs=[pl.BlockSpec((EX_DEV, depth), lambda i, w: (0, 0))] * size
            + [pl.BlockSpec((n, depth), lambda i, w: (0, 0))]
            + [ANY] * len(after),
            out_specs=pl.BlockSpec((size * EX_DEV, n), lambda i, w: (0, 0)),
            scratch_shapes=[
                pltpu.VMEM((size, EX_DEV, depth), F32),
                pltpu.VMEM((3 * size * EX_DEV, depth), F32),
            ],
        ),
        out_shape=jax.ShapeDtypeStruct((size * EX_DEV, n), F32),
        compiler_params=pltpu.CompilerParams(vmem_limit_bytes=LIMIT),
        cost_estimate=cost(SHORT),
        name="score_terms",
    )(pos, *sketches, queries, *after)


def score_sum(pos, terms, after):
    size = len(terms)
    shape = terms[0].shape

    def kernel(pos_ref, *refs):
        out_ref, all_ref = refs[-2:]
        for back in range(size):
            all_ref[lax.rem(pos_ref[0] - back + size, size)] = refs[back][...]
        total = all_ref[0]
        for d in range(1, size):
            total = total + all_ref[d]
        out_ref[...] = total

    whole = pl.BlockSpec(shape, lambda i, w: (0, 0))
    return pl.pallas_call(
        kernel,
        grid_spec=pltpu.PrefetchScalarGridSpec(
            num_scalar_prefetch=1,
            grid=(1,),
            in_specs=[whole] * size + [ANY] * len(after),
            out_specs=whole,
            scratch_shapes=[pltpu.VMEM((size,) + shape, F32)],
        ),
        out_shape=jax.ShapeDtypeStruct(shape, F32),
        compiler_params=pltpu.CompilerParams(vmem_limit_bytes=SMALL),
        cost_estimate=cost(SHORT),
        name="score_sum",
    )(pos, *terms, *after)


def body(inputs, residual, out_grad, norm_gain, w_out, proj_in, proj_out, queries, segment_ids):
    parts = lax.axis_size("tensor")
    rank = lax.axis_index("tensor")
    queriers = lax.axis_size("query")
    q_rank = lax.axis_index("query")
    tokens = inputs.shape[1]
    share = tokens // parts
    chunks = max(1, min(CHUNKS, share // 16))
    rows = share // chunks
    by_share = inputs.reshape(parts, chunks, rows, inputs.shape[2])
    gain = norm_gain.reshape(1, -1)
    half = w_out.shape[1] // HALVES
    kp = proj_out.shape[0]

    up = 1 - 2 * lax.rem(q_rank, 2)
    pos = jnp.stack([rank, up, jnp.where(up == 1, rank, parts - 1 - rank), q_rank]).astype(jnp.int32)

    def pairs(flow, low, high):
        out = []
        for q in range(queriers):
            way = 1 if (q % 2 == 0) == (flow == 0) else -1
            for t in range(parts):
                spot = t if way == 1 else parts - 1 - t
                if low <= spot <= min(high, parts - 2):
                    out.append((t * queriers + q, (t + way) * queriers + q))
        return out

    work, marks, resident = [], [], []
    partials, totals, result = {}, {}, [None]

    def forward(c, h, piece, pieces, after):
        partials[c, h], mark = forward_piece(
            by_share,
            w_out,
            c,
            HALVES,
            h,
            2 * kp,
            piece,
            pieces,
            partials.get((c, h)),
            after,
        )
        if h == HALVES - 1 and piece == pieces - 1:
            partials[c, h] = forward_extra(by_share, proj_in, c, partials[c, h], [mark])
        return mark

    def backward(c, blocks, total, last, piece, pieces, after):
        held = result[0] if last else totals.get(c)
        some = resident[piece * QUARTERS // pieces : (piece + 1) * QUARTERS // pieces]
        done, mark = backward_piece(
            blocks, some, c, chunks, HALVES, piece, pieces, total, last, held, after
        )
        if last:
            result[0] = done
        else:
            totals[c] = done
        return mark

    def do_one(after, touching=False):
        if work:
            marks[:] = [work.pop(0)[1](after)]
        elif touching:
            marks[:] = [touch(after[0])]

    def finish(key, after):
        while any(k == key for k, _ in work):
            do_one(list(marks) + after)

    def load(count, after):
        for _ in range(count):
            resident.append(load_weights(w_out, len(resident), QUARTERS, after))
            after = [resident[-1]]
        marks[:] = after

    def add_forward(c, h, pieces):
        for piece in range(pieces):
            work.append(((c, h), functools.partial(forward, c, h, piece, pieces)))

    add_forward(0, 0, 1)
    finish((0, 0), [])
    gathered = []
    for slot in range(chunks + 1):
        rs, ag = slot < chunks, slot > 0
        came, held, sent, before = {}, {}, {}, None
        if ag:
            res, grd = in_vmem(own_rows[0]), in_vmem(own_rows[1])
            ins = [
                [partials[slot - 1, h], arrived[h, 0], arrived[h, 1], res, grd, gain]
                for h in range(HALVES)
            ]
            sums = None
            for h in range(HALVES):
                sums = norm_sums(pos, ins[h], half, slot - 1, h, sums, list(marks))
            grad = [None] * HALVES
            grad[0], held[0] = norm_out(
                pos, list(enumerate(ins)), half, slot - 1, sums, proj_out, []
            )
        for k in range(parts):
            gather_now, reduce_now = ag and k <= parts - 2, rs and k >= 1
            if not gather_now and not reduce_now:
                continue
            for h in range(HALVES):
                if k == 0 and h > 0:
                    if rs and slot > 1:
                        add_forward(slot, h, PIECES)
                    do_one([sent[h - 1, 1]])
                    grad[h], held[h] = norm_out(
                        pos, [(h, ins[h])], half, slot - 1, sums, None, list(marks)
                    )
                if reduce_now:
                    if slot == 0 and k == 1 and h > 0:
                        add_forward(0, h, 1)
                        do_one([sent[h - 1, 1]])
                    finish((slot, h), [sent[h - 1, 1]] if h > 0 else [])
                for flow in range(2):
                    if k == 0:
                        x = before = grad[h]
                    elif (h, flow) not in came:
                        x = first_block(pos, flow, partials[slot, h])
                    else:
                        x, held[h] = relay(
                            pos,
                            flow,
                            k,
                            partials[slot, h] if reduce_now else None,
                            came[h, flow],
                            held.get(h),
                            list(marks) + ([] if before is None else [before]),
                        )
                        before = x
                    came[h, flow] = lax.ppermute(
                        x,
                        ("tensor", "query"),
                        pairs(flow, 0 if reduce_now else k, parts - 2 if gather_now else k - 1),
                    )
                    sent[h, flow] = x
                    if rs and (k, h, flow) == (parts - (1 if slot == 0 else 2), HALVES - 1, 1):
                        own_rows = load_rows(residual, out_grad, slot, rows, [x])
                        x = own_rows[0]
                    if slot == chunks - 1 and flow == 1 and slot > 0:
                        if (k, h) == (parts - 2, HALVES - 1):
                            load(1, [x])
                            continue
                        if (k, h) == (parts - 1, HALVES - 1):
                            load(QUARTERS - len(resident), [x])
                            continue
                    if slot == 0 and k == 2 and (h, flow) == (HALVES - 1, 1) and chunks > 1 and HALVES > 1:
                        add_forward(1, 1, 2 * PIECES)
                        do_one([x])
                        continue
                    if slot == 0 and k == parts - 1 and (h, flow) == (0, 1):
                        do_one([x])
                        continue
                    if slot == 0 and k == parts - 1 and (h, flow) == (HALVES - 1, 1) and chunks > 1:
                        work.insert(0, ((1, 0), functools.partial(forward, 1, 0, 0, 1)))
                    if slot == 0 and work and work[0][0] == (1, 1):
                        continue
                    if k > 0 and (slot > 0 or k > 1) and not (slot == 1 and work and k == 1 and flow == 0):
                        if slot == chunks and (h, flow, k) != (HALVES - 1, 1, parts - 2):
                            marks[:] = [touch(x)]
                        else:
                            do_one([x], slot == chunks)
                if k == 0 and slot == chunks and h == HALVES - 1:
                    marks[:] = [touch(sent[h, 1])]
        if ag:
            if slot + 1 < chunks:
                add_forward(slot + 1, 0, PIECES)
            if rs:
                blocks = [(h, held[h]) for h in range(HALVES)]
                for piece in range(PIECES):
                    work.append(
                        (
                            ("b", slot - 1),
                            functools.partial(backward, slot - 1, blocks, None, True, piece, PIECES),
                        )
                    )
            else:
                while work:
                    do_one(list(marks))
                marks[:] = [tie(marks[0], [came[0, 0]])]
                held[0] = store_last(pos, (came[0, 0], came[0, 1]), held[0], list(marks))
            gathered.append(held[0])
        arrived = came
    last = chunks - 1
    sketch = sketch_slice(pos, gathered, segment_ids, kp, [])
    marks[:] = [backward(last, [(0, held[0])], None, HALVES == 1, 0, 1, [sketch])]
    for h in range(1, HALVES):
        marks[:] = [tie(marks[0], [came[h, 0]])]
        held[h] = store_last(pos, (came[h, 0], came[h, 1]), held[h], list(marks))
    terms = score_terms(pos, from_others(sketch, "query", queriers), queries, list(marks))
    for h in range(1, HALVES):
        marks[:] = [backward(last, [(h, held[h])], totals.get(last), h == HALVES - 1, 0, 1, [terms])]
    scores = score_sum(pos, from_others(terms, "tensor", parts), list(marks))
    return (result[0].reshape(1, tokens, -1), scores)


def solution(mesh):
    return jax.shard_map(
        body,
        mesh=mesh,
        in_specs=(
            P(("groups", "dp", "query"), None, "tensor"),
            P(("groups", "dp", "query"), "tensor", None),
            P(("groups", "dp", "query"), "tensor", None),
            P(),
            P("tensor", None),
            P(None, "tensor"),
            P(),
            P("query", "tensor"),
            P(("groups", "dp", "query"), None),
        ),
        out_specs=(P(("groups", "dp", "query"), None, "tensor"), P(("groups", "dp"), "query")),
        check_vma=False,
    )
```

```python
import functools

import jax
import jax.numpy as jnp
from jax import lax
from jax.experimental import pallas as pl
from jax.experimental.pallas import tpu as pltpu
from jax.sharding import PartitionSpec as P

EX_DEV = 4
EPS = 1e-05
CHUNKS = 2
HALVES = 2
PIECES = 2
SHORT, LONG = 0.2, 5.0
SMALL, LIMIT, LARGE = 5 * 1024 * 1024, 9 * 1024 * 1024, 24 * 1024 * 1024
QUARTERS = 4

F32, BF16 = jnp.float32, jnp.bfloat16
ANY = pl.BlockSpec(memory_space=pl.ANY)
TOKEN = jax.ShapeDtypeStruct((8, 128), F32)
TOKEN_SPEC = pl.BlockSpec((8, 128), lambda *_: (0, 0))


def divisor(total, wanted):
    size = min(total, wanted)
    while total % size:
        size //= 2
    return size


def cost(microseconds):
    return pl.CostEstimate(flops=0, bytes_accessed=int(microseconds * 3.6e6), transcendentals=0)


def in_hbm(x):
    return pltpu.with_memory_space_constraint(x, pltpu.HBM)


def project_rows(values, matrix):
    return lax.dot_general(
        values, matrix, (((1,), (1,)), ((), ())), preferred_element_type=F32
    )


def spread(values, first):
    k = values.shape[1]
    row = lax.broadcasted_iota(jnp.int32, (k, 2 * k), 0)
    col = lax.broadcasted_iota(jnp.int32, (k, 2 * k), 1)
    return jnp.dot(values, jnp.where(col == row + first, 1.0, 0.0).astype(BF16), preferred_element_type=F32)


def forward_extra(by_share, proj_in, chunk, held, after):
    parts, _, rows, depth = by_share.shape
    extra = 2 * proj_in.shape[0]
    at = held.shape[2] // extra - 1

    def kernel(x_ref, p_ref, *refs):
        part = project_rows(x_ref[...].reshape(parts * rows, depth), p_ref[...]).astype(BF16)
        refs[-1][...] = spread(part, 0).astype(BF16).reshape(parts, rows, extra)

    return pl.pallas_call(
        kernel,
        grid=(1,),
        in_specs=[
            pl.BlockSpec((parts, None, rows, depth), lambda i: (0, chunk, 0, 0)),
            pl.BlockSpec(proj_in.shape, lambda i: (0, 0)),
        ]
        + [ANY] * (1 + len(after)),
        out_specs=pl.BlockSpec((parts, rows, extra), lambda i: (0, 0, at)),
        out_shape=jax.ShapeDtypeStruct(held.shape, BF16),
        input_output_aliases={2: 0},
        compiler_params=pltpu.CompilerParams(vmem_limit_bytes=LIMIT),
        cost_estimate=cost(SHORT),
        name="forward_extra",
    )(by_share, proj_in, held, *after)


def forward_piece(by_share, w_out, chunk, halves, half_at, extra, piece, pieces, held, after):
    parts, _, rows, depth = by_share.shape
    half = w_out.shape[1] // halves
    span = half // pieces
    cols = divisor(span, max(256, span // 8))
    steps = span // cols
    base = half_at * half + piece * span

    def kernel(x_ref, w_ref, *refs):
        out_ref, tok_ref, held_ref, sems = refs[-4:]
        i = pl.program_id(0)

        def copy(j):
            columns = pl.ds(pl.multiple_of(base + j * cols, cols), cols)
            return pltpu.make_async_copy(w_ref.at[:, columns], held_ref.at[j], sems.at[j])

        @pl.when(i == 0)
        def _():
            for j in range(steps):
                copy(j).start()

        copy(i).wait()
        x = x_ref[...].reshape(parts * rows, depth)
        y = jnp.dot(x, held_ref[i], preferred_element_type=F32).astype(BF16)
        out_ref[...] = y.reshape(parts, rows, cols)
        tok_ref[...] = jnp.zeros_like(tok_ref)

    more = ([] if held is None else [held]) + after
    return pl.pallas_call(
        kernel,
        grid=(steps,),
        in_specs=[
            pl.BlockSpec(
                (parts, None, rows, depth), lambda i: (0, chunk, 0, 0), pipeline_mode=pl.Buffered(1)
            )
        ]
        + [ANY] * (1 + len(more)),
        out_specs=[
            pl.BlockSpec((parts, rows, cols), lambda i: (0, 0, piece * steps + i)),
            TOKEN_SPEC,
        ],
        out_shape=[jax.ShapeDtypeStruct((parts, rows, half + extra), BF16), TOKEN],
        scratch_shapes=[pltpu.VMEM((steps, depth, cols), BF16), pltpu.SemaphoreType.DMA((steps,))],
        input_output_aliases={} if held is None else {2: 0},
        compiler_params=pltpu.CompilerParams(vmem_limit_bytes=LARGE),
        cost_estimate=cost(SHORT),
        name="forward_piece",
    )(in_hbm(by_share) if chunk == 0 and half_at == 0 else by_share, in_hbm(w_out), *more)


def load_weights(w_out, piece, pieces, after):
    rows = w_out.shape[0] // pieces
    width = w_out.shape[1]

    def kernel(w_ref, *refs):
        out_ref, sem = refs[-2:]
        copy = pltpu.make_async_copy(w_ref.at[pl.ds(piece * rows, rows)], out_ref, sem)
        copy.start()
        copy.wait()

    return pl.pallas_call(
        kernel,
        in_specs=[ANY] * (1 + len(after)),
        out_specs=pl.BlockSpec(memory_space=pltpu.VMEM),
        out_shape=pltpu.VMEM((rows, width), BF16),
        scratch_shapes=[pltpu.SemaphoreType.DMA],
        compiler_params=pltpu.CompilerParams(vmem_limit_bytes=SMALL),
        cost_estimate=cost(SHORT),
        name="load_weights",
    )(in_hbm(w_out), *after)


def load_rows(residual, out_grad, chunk, rows, after):
    width = residual.shape[2]

    def kernel(*refs):
        out_refs, sems = refs[-3:-1], refs[-1]
        copies = [
            pltpu.make_async_copy(refs[j].at[0, pl.ds(chunk * rows, rows)], out_refs[j], sems.at[j])
            for j in range(2)
        ]
        for copy in copies:
            copy.start()
        for copy in copies:
            copy.wait()

    return pl.pallas_call(
        kernel,
        in_specs=[ANY] * (2 + len(after)),
        out_specs=[pl.BlockSpec(memory_space=pltpu.VMEM)] * 2,
        out_shape=[pltpu.VMEM((rows, width), BF16)] * 2,
        scratch_shapes=[pltpu.SemaphoreType.DMA((2,))],
        compiler_params=pltpu.CompilerParams(vmem_limit_bytes=SMALL),
        cost_estimate=cost(SHORT),
        name="load_rows",
    )(in_hbm(residual), in_hbm(out_grad), *after)


def in_vmem(x):
    return pltpu.with_memory_space_constraint(x, pltpu.VMEM)


def backward_piece(blocks, weights, chunk, chunks, halves, piece, pieces, total, last, held, after):
    parts, rows, _ = blocks[0][1].shape
    some, width = weights[0].shape
    half, span = width // halves, some * len(weights)
    cols = divisor(some, 256)
    n, m = len(blocks), len(weights)

    def kernel(*refs):
        out_ref, tok_ref = refs[-2:]
        for j in range(m):

            def step(i, carry):
                here = pl.ds(pl.multiple_of(i * cols, cols), cols)
                there = pl.ds(pl.multiple_of(j * some + i * cols, cols), cols)
                y = None if total is None else refs[n + m][:, :, there].reshape(parts * rows, cols)
                for b, (at, _) in enumerate(blocks):
                    g = refs[b][...].reshape(parts * rows, half)
                    term = project_rows(g, refs[n + j][here, at * half : (at + 1) * half])
                    y = term if y is None else y + term
                out_ref[:, :, there] = y.astype(out_ref.dtype).reshape(parts, rows, cols)
                return carry

            lax.fori_loop(0, some // cols, step, 0)
        tok_ref[...] = jnp.zeros_like(tok_ref)

    once = pl.Buffered(1)
    here = pl.BlockSpec((parts, rows, span), lambda i: (0, 0, piece))
    if last:
        out_spec = pl.BlockSpec((parts, None, rows, span), lambda i: (0, chunk, 0, piece))
        out_shape = jax.ShapeDtypeStruct((parts, chunks, rows, span * pieces), BF16)
    else:
        out_spec, out_shape = here, jax.ShapeDtypeStruct((parts, rows, span * pieces), F32)
    sums = [] if total is None else [total]
    extra = ([] if held is None else [held]) + after
    return pl.pallas_call(
        kernel,
        grid=(1,),
        in_specs=[pl.BlockSpec((parts, rows, half), lambda i: (0, 0, 0), pipeline_mode=once)] * n
        + [pl.BlockSpec(memory_space=pltpu.VMEM)] * m
        + [pl.BlockSpec((parts, rows, span), lambda i: (0, 0, piece), pipeline_mode=once)] * len(sums)
        + [ANY] * len(extra),
        out_specs=[out_spec, TOKEN_SPEC],
        out_shape=[out_shape, TOKEN],
        input_output_aliases={} if held is None else {n + m + len(sums): 0},
        compiler_params=pltpu.CompilerParams(vmem_limit_bytes=LIMIT),
        cost_estimate=cost(SHORT),
        name="backward_piece",
    )(
        *[g for _, g in blocks],
        *[in_vmem(w) for w in weights],
        *sums,
        *extra,
    )


def relay(pos, flow, k, partial, came, held, after):
    rows, width = came.shape
    parts = (partial if held is None else held).shape[0]
    n_in = 1 + (partial is not None) + (held is not None) + len(after)

    def far(pos_ref, steps):
        way = pos_ref[1] if flow == 0 else -pos_ref[1]
        return lax.clamp(0, pos_ref[0] + way * steps, parts - 1)

    def kernel(pos_ref, *refs):
        came_ref, x_ref = refs[0], refs[n_in]
        place = pos_ref[2] if flow == 0 else parts - 1 - pos_ref[2]
        if held is not None:
            store = pltpu.make_async_copy(came_ref, refs[n_in + 1].at[far(pos_ref, -k)], refs[-1])
            pl.when(place >= k)(store.start)
        if partial is not None:

            @pl.when(place < k)
            def _():
                x_ref[...] = (came_ref[...].astype(F32) + refs[1][...].astype(F32)).astype(BF16)

            @pl.when(place >= k)
            def _():
                x_ref[...] = came_ref[...]

        else:
            x_ref[...] = came_ref[...]
        if held is not None:
            pl.when(place >= k)(store.wait)

    line = jax.ShapeDtypeStruct((rows, width), BF16)
    whole = pl.BlockSpec((rows, width), lambda i, w: (0, 0), pipeline_mode=pl.Buffered(1))
    args, specs, out_specs, out_shape, alias = [came], [whole], [whole], [line], {}
    if partial is not None:
        term = pl.BlockSpec(
            (None, rows, width),
            lambda i, w: (far(w, parts - k), 0, 0),
            pipeline_mode=pl.Buffered(1),
        )
        specs.append(term)
        args.append(partial)
    if held is not None:
        alias[1 + len(args)] = 1
        specs.append(ANY)
        args.append(held)
        out_specs.append(ANY)
        out_shape.append(jax.ShapeDtypeStruct(held.shape, BF16))
    outs = pl.pallas_call(
        kernel,
        grid_spec=pltpu.PrefetchScalarGridSpec(
            num_scalar_prefetch=1,
            grid=(1,),
            in_specs=specs + [ANY] * len(after),
            out_specs=out_specs,
            scratch_shapes=[pltpu.SemaphoreType.DMA] if held is not None else [],
        ),
        out_shape=out_shape,
        input_output_aliases=alias,
        compiler_params=pltpu.CompilerParams(vmem_limit_bytes=SMALL),
        cost_estimate=cost(LONG),
        name="relay",
    )(pos, *args, *after)
    return outs[0], (outs[1] if held is not None else None)


def store_last(pos, came, held, after):
    parts = held.shape[0]

    def kernel(pos_ref, a_ref, b_ref, *refs):
        out_ref, sem = refs[-2:]
        rank, way, place = pos_ref[0], pos_ref[1], pos_ref[2]
        ends = (
            (place == parts - 1, a_ref, rank - way * (parts - 1)),
            (place == 0, b_ref, rank + way * (parts - 1)),
        )
        for at_end, came_ref, at in ends:
            copy = pltpu.make_async_copy(came_ref, out_ref.at[lax.clamp(0, at, parts - 1)], sem)

            @pl.when(at_end)
            def _():
                copy.start()
                copy.wait()

    return pl.pallas_call(
        kernel,
        grid_spec=pltpu.PrefetchScalarGridSpec(
            num_scalar_prefetch=1,
            grid=(1,),
            in_specs=[pl.BlockSpec(held.shape[1:], lambda i, w: (0, 0))] * 2 + [ANY] * (1 + len(after)),
            out_specs=ANY,
            scratch_shapes=[pltpu.SemaphoreType.DMA],
        ),
        out_shape=jax.ShapeDtypeStruct(held.shape, BF16),
        input_output_aliases={3: 0},
        compiler_params=pltpu.CompilerParams(vmem_limit_bytes=SMALL),
        cost_estimate=cost(SHORT),
        name="store_last",
    )(pos, *came, held, *after)


def first_block(pos, flow, partial):
    parts, rows, width = partial.shape

    def there(i, w):
        way = w[1] if flow == 0 else -w[1]
        return lax.clamp(0, w[0] + way * (parts - 1), parts - 1), 0, 0

    def kernel(pos_ref, p_ref, out_ref):
        out_ref[...] = p_ref[...]

    return pl.pallas_call(
        kernel,
        grid_spec=pltpu.PrefetchScalarGridSpec(
            num_scalar_prefetch=1,
            grid=(1,),
            in_specs=[pl.BlockSpec((None, rows, width), there)],
            out_specs=pl.BlockSpec((rows, width), lambda i, w: (0, 0)),
        ),
        out_shape=jax.ShapeDtypeStruct((rows, width), BF16),
        compiler_params=pltpu.CompilerParams(vmem_limit_bytes=SMALL),
        cost_estimate=cost(SHORT),
        name="first_block",
    )(pos, partial)


def norm_terms(p_ref, a_ref, b_ref, res_ref, grad_ref, gain_ref, at):
    proj = p_ref[:, at].astype(F32) + a_ref[:, at].astype(F32) + b_ref[:, at].astype(F32)
    z = res_ref[:, at].astype(F32) + proj
    scaled = gain_ref[:, at].astype(F32) * grad_ref[:, at].astype(F32)
    return z, scaled


def norm_specs(ins, half, chunk, at):
    _, rows, wide = ins[0].shape
    once = pl.Buffered(1)
    whole = pl.BlockSpec((rows, wide), lambda i, r: (0, 0), pipeline_mode=once)
    own = pl.BlockSpec((rows, half), lambda i, r: (0, at), pipeline_mode=once)
    mine = pl.BlockSpec((None, rows, wide), lambda i, r: (r[0], 0, 0), pipeline_mode=once)
    return [mine, whole, whole, own, own, pl.BlockSpec((1, half), lambda i, r: (0, at))]


def norm_sums(pos, ins, half, chunk, at, sums, after):
    rows = ins[0].shape[1]
    cols = divisor(half, 1024)

    def kernel(pos_ref, *refs):
        square_ref, cross_ref = refs[-2:]

        def step(i, sums):
            z, scaled = norm_terms(*refs[:6], pl.ds(pl.multiple_of(i * cols, cols), cols))
            square, cross = sums
            for j in range(0, cols, 128):
                zj = z[:, j : j + 128]
                square = square + zj * zj
                cross = cross + zj * scaled[:, j : j + 128]
            return square, cross

        zero = jnp.zeros((rows, 128), F32)
        start = (zero, zero) if sums is None else (refs[6][...], refs[7][...])
        square_ref[...], cross_ref[...] = lax.fori_loop(0, half // cols, step, start)

    stat = pl.BlockSpec((rows, 128), lambda i, r: (0, 0))
    before = [] if sums is None else list(sums)
    return pl.pallas_call(
        kernel,
        grid_spec=pltpu.PrefetchScalarGridSpec(
            num_scalar_prefetch=1,
            grid=(1,),
            in_specs=norm_specs(ins, half, chunk, at) + [stat] * len(before) + [ANY] * len(after),
            out_specs=[stat, stat],
        ),
        out_shape=[jax.ShapeDtypeStruct((rows, 128), F32)] * 2,
        compiler_params=pltpu.CompilerParams(vmem_limit_bytes=LIMIT),
        cost_estimate=cost(LONG),
        name="norm_sums",
    )(pos, *ins, *before, *after)


def norm_out(pos, ins, half, chunk, sums, proj_out, after):
    parts, rows, wide = ins[0][1][0].shape
    cols = divisor(half, 1024)
    n, width = len(ins), ins[0][1][3].shape[1]
    with_b = proj_out

    def kernel(pos_ref, *refs):
        square_ref, cross_ref = refs[6 * n], refs[6 * n + 1]
        if with_b is None:
            out_ref, held_ref, sem = refs[-3:]
        else:
            out_ref, held_ref, rest_ref, sem = refs[-4:]
        inv = lax.rsqrt(jnp.sum(square_ref[...], axis=-1, keepdims=True) / width + EPS)
        slope = inv * inv * inv * (jnp.sum(cross_ref[...], axis=-1, keepdims=True) / width)
        for j in range(n):
            to_ref = out_ref if j == 0 else rest_ref.at[j - 1]

            def step(i, carry):
                here = pl.ds(pl.multiple_of(i * cols, cols), cols)
                z, scaled = norm_terms(*refs[6 * j : 6 * j + 6], here)
                to_ref[:, here] = (inv * scaled - z * slope).astype(BF16)
                return carry

            lax.fori_loop(0, half // cols, step, 0)
        if with_b is not None:
            p_ref = refs[6 * n + 2]
            b = project_rows(out_ref[:, :half], p_ref[:, :half])
            for j in range(1, n):
                b = b + project_rows(rest_ref[j - 1], p_ref[:, j * half : (j + 1) * half])
            a = sum(refs[6 * (n - 1) + j][:, half:].astype(F32) for j in range(3))
            out_ref[:, half:] = (a + spread(b.astype(BF16), b.shape[1])).astype(BF16)
        else:
            out_ref[:, half:] = jnp.zeros((rows, wide - half), BF16)
        own = pltpu.make_async_copy(out_ref, held_ref.at[pos_ref[0]], sem)
        own.start()
        own.wait()

    stat = pl.BlockSpec((rows, 128), lambda i, r: (0, 0))
    specs, args = [], []
    for at, one in ins:
        specs += norm_specs(one, half, chunk, at)
        args += one
    specs, args = specs + [stat, stat], args + list(sums)
    scratch = [pltpu.SemaphoreType.DMA]
    if with_b is not None:
        specs.append(
            pl.BlockSpec(proj_out.shape, lambda i, r: (0, 0), pipeline_mode=pl.Buffered(1))
        )
        args.append(proj_out)
        scratch = [pltpu.VMEM((max(1, n - 1), rows, half), BF16)] + scratch
    return pl.pallas_call(
        kernel,
        grid_spec=pltpu.PrefetchScalarGridSpec(
            num_scalar_prefetch=1,
            grid=(1,),
            in_specs=specs + [ANY] * len(after),
            out_specs=[pl.BlockSpec((rows, wide), lambda i, r: (0, 0)), ANY],
            scratch_shapes=scratch,
        ),
        out_shape=[
            jax.ShapeDtypeStruct((rows, wide), BF16),
            jax.ShapeDtypeStruct((parts, rows, wide), BF16),
        ],
        compiler_params=pltpu.CompilerParams(vmem_limit_bytes=LIMIT),
        cost_estimate=cost(SHORT),
        name="norm_out",
    )(pos, *args, *after)


def tie(value, after):
    def kernel(value_ref, *refs):
        refs[-1][...] = value_ref[...]

    whole = pl.BlockSpec(value.shape, lambda i: (0,) * value.ndim)
    return pl.pallas_call(
        kernel,
        grid=(1,),
        in_specs=[whole] + [ANY] * len(after),
        out_specs=whole,
        out_shape=jax.ShapeDtypeStruct(value.shape, value.dtype),
        compiler_params=pltpu.CompilerParams(vmem_limit_bytes=SMALL),
        cost_estimate=cost(SHORT),
        name="tie",
    )(value, *after)


def touch(x):
    def kernel(x_ref, out_ref):
        out_ref[...] = jnp.zeros_like(out_ref)

    return pl.pallas_call(
        kernel,
        grid=(1,),
        in_specs=[ANY],
        out_specs=TOKEN_SPEC,
        out_shape=TOKEN,
        compiler_params=pltpu.CompilerParams(vmem_limit_bytes=SMALL),
        cost_estimate=cost(SHORT),
        name="touch",
    )(x)


def from_others(value, axis, size):
    return [value] + [
        lax.ppermute(value, axis, [(d, (d + shift) % size) for d in range(size)])
        for shift in range(1, size)
    ]


def sketch_slice(pos, gathered, segment_ids, kp, after):
    parts, rows, wide = gathered[0].shape
    extra, mine = 2 * kp, kp // parts
    chunks, tokens = len(gathered), segment_ids.shape[1]

    def kernel(pos_ref, *refs):
        out_ref, sum_ref = refs[-2:]
        example = lax.broadcasted_iota(jnp.int32, (8, tokens), 0)
        by_row = jnp.where(refs[chunks][...] == example, 1.0, 0.0).astype(BF16)
        same = lax.broadcasted_iota(jnp.int32, (tokens, tokens), 0) == lax.broadcasted_iota(
            jnp.int32, (tokens, tokens), 1
        )
        weights = project_rows(jnp.where(same, 1.0, 0.0).astype(BF16), by_row)
        weights = weights.reshape(parts, chunks, rows, 8)
        for e in range(EX_DEV):
            total = None
            for c in range(chunks):
                both = refs[c][...].reshape(parts * rows, extra)
                weight = weights[:, c].reshape(parts * rows, 8)[:, e : e + 1]
                part = (both.astype(F32) * weight).astype(BF16)
                term = lax.dot_general(
                    part, both, (((0,), (0,)), ((), ())), preferred_element_type=F32
                )
                total = term if total is None else total + term
            sum_ref[e] = total
        low = lax.broadcasted_iota(jnp.int32, (1, extra), 1) < kp
        for r in range(parts):

            @pl.when(pos_ref[0] == r)
            def _():
                for e in range(EX_DEV):
                    for i in range(mine // 2):
                        at = kp + r * mine + 2 * i
                        left, right = sum_ref[e, at : at + 1, :], sum_ref[e, at + 1 : at + 2, :]
                        out_ref[e : e + 1, i * extra : (i + 1) * extra] = jnp.where(
                            low, left, pltpu.roll(right, kp, 1)
                        )

    return pl.pallas_call(
        kernel,
        grid_spec=pltpu.PrefetchScalarGridSpec(
            num_scalar_prefetch=1,
            grid=(1,),
            in_specs=[pl.BlockSpec((parts, rows, extra), lambda i, w: (0, 0, wide // extra - 1))] * chunks
            + [pl.BlockSpec(segment_ids.shape, lambda i, w: (0, 0))]
            + [ANY] * len(after),
            out_specs=pl.BlockSpec((EX_DEV, mine * kp), lambda i, w: (0, 0)),
            scratch_shapes=[pltpu.VMEM((EX_DEV, extra, extra), F32)],
        ),
        out_shape=jax.ShapeDtypeStruct((EX_DEV, mine * kp), F32),
        compiler_params=pltpu.CompilerParams(vmem_limit_bytes=LIMIT),
        cost_estimate=cost(SHORT),
        name="sketch_slice",
    )(pos, *gathered, segment_ids, *after)


def score_terms(pos, sketches, queries, after):
    size = len(sketches)
    n, depth = queries.shape

    def kernel(pos_ref, *refs):
        out_ref, all_ref, parts_ref = refs[-3:]
        for back in range(size):
            all_ref[lax.rem(pos_ref[3] - back + size, size)] = refs[back][...]
        for d in range(size):
            rest = all_ref[d]
            for t in range(3):
                part = rest.astype(BF16).astype(F32)
                rest = rest - part
                at = (t * size + d) * EX_DEV
                parts_ref[at : at + EX_DEV, :] = part
        terms = project_rows(parts_ref[...].astype(BF16), refs[size][...])
        n_out = size * EX_DEV
        out_ref[...] = terms[:n_out] + terms[n_out : 2 * n_out] + terms[2 * n_out :]

    return pl.pallas_call(
        kernel,
        grid_spec=pltpu.PrefetchScalarGridSpec(
            num_scalar_prefetch=1,
            grid=(1,),
            in_specs=[pl.BlockSpec((EX_DEV, depth), lambda i, w: (0, 0))] * size
            + [pl.BlockSpec((n, depth), lambda i, w: (0, 0))]
            + [ANY] * len(after),
            out_specs=pl.BlockSpec((size * EX_DEV, n), lambda i, w: (0, 0)),
            scratch_shapes=[
                pltpu.VMEM((size, EX_DEV, depth), F32),
                pltpu.VMEM((3 * size * EX_DEV, depth), F32),
            ],
        ),
        out_shape=jax.ShapeDtypeStruct((size * EX_DEV, n), F32),
        compiler_params=pltpu.CompilerParams(vmem_limit_bytes=LIMIT),
        cost_estimate=cost(SHORT),
        name="score_terms",
    )(pos, *sketches, queries, *after)


def score_sum(pos, terms, after):
    size = len(terms)
    shape = terms[0].shape

    def kernel(pos_ref, *refs):
        out_ref, all_ref = refs[-2:]
        for back in range(size):
            all_ref[lax.rem(pos_ref[0] - back + size, size)] = refs[back][...]
        total = all_ref[0]
        for d in range(1, size):
            total = total + all_ref[d]
        out_ref[...] = total

    whole = pl.BlockSpec(shape, lambda i, w: (0, 0))
    return pl.pallas_call(
        kernel,
        grid_spec=pltpu.PrefetchScalarGridSpec(
            num_scalar_prefetch=1,
            grid=(1,),
            in_specs=[whole] * size + [ANY] * len(after),
            out_specs=whole,
            scratch_shapes=[pltpu.VMEM((size,) + shape, F32)],
        ),
        out_shape=jax.ShapeDtypeStruct(shape, F32),
        compiler_params=pltpu.CompilerParams(vmem_limit_bytes=SMALL),
        cost_estimate=cost(SHORT),
        name="score_sum",
    )(pos, *terms, *after)


def body(inputs, residual, out_grad, norm_gain, w_out, proj_in, proj_out, queries, segment_ids):
    parts = lax.axis_size("tensor")
    rank = lax.axis_index("tensor")
    queriers = lax.axis_size("query")
    q_rank = lax.axis_index("query")
    tokens = inputs.shape[1]
    share = tokens // parts
    chunks = max(1, min(CHUNKS, share // 16))
    rows = share // chunks
    by_share = inputs.reshape(parts, chunks, rows, inputs.shape[2])
    gain = norm_gain.reshape(1, -1)
    half = w_out.shape[1] // HALVES
    kp = proj_out.shape[0]

    up = 1 - 2 * lax.rem(q_rank, 2)
    pos = jnp.stack([rank, up, jnp.where(up == 1, rank, parts - 1 - rank), q_rank]).astype(jnp.int32)

    def pairs(flow, low, high):
        out = []
        for q in range(queriers):
            way = 1 if (q % 2 == 0) == (flow == 0) else -1
            for t in range(parts):
                spot = t if way == 1 else parts - 1 - t
                if low <= spot <= min(high, parts - 2):
                    out.append((t * queriers + q, (t + way) * queriers + q))
        return out

    work, marks, resident = [], [], []
    partials, totals, result = {}, {}, [None]

    def forward(c, h, piece, pieces, after):
        partials[c, h], mark = forward_piece(
            by_share,
            w_out,
            c,
            HALVES,
            h,
            2 * kp,
            piece,
            pieces,
            partials.get((c, h)),
            after,
        )
        if h == HALVES - 1 and piece == pieces - 1:
            partials[c, h] = forward_extra(by_share, proj_in, c, partials[c, h], [mark])
        return mark

    def backward(c, blocks, total, last, piece, pieces, after):
        held = result[0] if last else totals.get(c)
        some = resident[piece * QUARTERS // pieces : (piece + 1) * QUARTERS // pieces]
        done, mark = backward_piece(
            blocks, some, c, chunks, HALVES, piece, pieces, total, last, held, after
        )
        if last:
            result[0] = done
        else:
            totals[c] = done
        return mark

    def do_one(after, touching=False):
        if work:
            marks[:] = [work.pop(0)[1](after)]
        elif touching:
            marks[:] = [touch(after[0])]

    def finish(key, after):
        while any(k == key for k, _ in work):
            do_one(list(marks) + after)

    def load(count, after):
        for _ in range(count):
            resident.append(load_weights(w_out, len(resident), QUARTERS, after))
            after = [resident[-1]]
        marks[:] = after

    def add_forward(c, h, pieces):
        for piece in range(pieces):
            work.append(((c, h), functools.partial(forward, c, h, piece, pieces)))

    add_forward(0, 0, 1)
    finish((0, 0), [])
    gathered = []
    for slot in range(chunks + 1):
        rs, ag = slot < chunks, slot > 0
        came, held, sent, before = {}, {}, {}, None
        if ag:
            res, grd = in_vmem(own_rows[0]), in_vmem(own_rows[1])
            ins = [
                [partials[slot - 1, h], arrived[h, 0], arrived[h, 1], res, grd, gain]
                for h in range(HALVES)
            ]
            sums = None
            for h in range(HALVES):
                sums = norm_sums(pos, ins[h], half, slot - 1, h, sums, list(marks))
            grad = [None] * HALVES
            grad[0], held[0] = norm_out(
                pos, list(enumerate(ins)), half, slot - 1, sums, proj_out, []
            )
        for k in range(parts):
            gather_now, reduce_now = ag and k <= parts - 2, rs and k >= 1
            if not gather_now and not reduce_now:
                continue
            for h in range(HALVES):
                if k == 0 and h > 0:
                    if rs and slot > 1:
                        add_forward(slot, h, PIECES)
                    do_one([sent[h - 1, 1]])
                    grad[h], held[h] = norm_out(
                        pos, [(h, ins[h])], half, slot - 1, sums, None, list(marks)
                    )
                if reduce_now:
                    if slot == 0 and k == 1 and h > 0:
                        add_forward(0, h, 1)
                        do_one([sent[h - 1, 1]])
                    finish((slot, h), [sent[h - 1, 1]] if h > 0 else [])
                for flow in range(2):
                    if k == 0:
                        x = before = grad[h]
                    elif (h, flow) not in came:
                        x = first_block(pos, flow, partials[slot, h])
                    else:
                        x, held[h] = relay(
                            pos,
                            flow,
                            k,
                            partials[slot, h] if reduce_now else None,
                            came[h, flow],
                            held.get(h),
                            list(marks) + ([] if before is None else [before]),
                        )
                        before = x
                    came[h, flow] = lax.ppermute(
                        x,
                        ("tensor", "query"),
                        pairs(flow, 0 if reduce_now else k, parts - 2 if gather_now else k - 1),
                    )
                    sent[h, flow] = x
                    if rs and (k, h, flow) == (parts - (1 if slot == 0 else 2), HALVES - 1, 1):
                        own_rows = load_rows(residual, out_grad, slot, rows, [x])
                        x = own_rows[0]
                    if slot == chunks - 1 and flow == 1 and slot > 0:
                        if (k, h) == (parts - 2, HALVES - 1):
                            load(1, [x])
                            continue
                        if (k, h) == (parts - 1, HALVES - 1):
                            load(QUARTERS - len(resident), [x])
                            continue
                    if slot == 0 and k == 2 and (h, flow) == (HALVES - 1, 1) and chunks > 1 and HALVES > 1:
                        add_forward(1, 1, 2 * PIECES)
                        do_one([x])
                        continue
                    if slot == 0 and k == parts - 1 and (h, flow) == (0, 1):
                        do_one([x])
                        continue
                    if slot == 0 and k == parts - 1 and (h, flow) == (HALVES - 1, 1) and chunks > 1:
                        work.insert(0, ((1, 0), functools.partial(forward, 1, 0, 0, 1)))
                    if slot == 0 and work and work[0][0] == (1, 1):
                        continue
                    if k > 0 and (slot > 0 or k > 1) and not (slot == 1 and work and k == 1 and flow == 0):
                        if slot == chunks and (h, flow, k) != (HALVES - 1, 1, parts - 2):
                            marks[:] = [touch(x)]
                        else:
                            do_one([x], slot == chunks)
                if k == 0 and slot == chunks and h == HALVES - 1:
                    marks[:] = [touch(sent[h, 1])]
        if ag:
            if slot + 1 < chunks:
                add_forward(slot + 1, 0, PIECES)
            if rs:
                blocks = [(h, held[h]) for h in range(HALVES)]
                for piece in range(PIECES):
                    work.append(
                        (
                            ("b", slot - 1),
                            functools.partial(backward, slot - 1, blocks, None, True, piece, PIECES),
                        )
                    )
            else:
                while work:
                    do_one(list(marks))
                marks[:] = [tie(marks[0], [came[0, 0]])]
                held[0] = store_last(pos, (came[0, 0], came[0, 1]), held[0], list(marks))
            gathered.append(held[0])
        arrived = came
    last = chunks - 1
    sketch = sketch_slice(pos, gathered, segment_ids, kp, [])
    marks[:] = [backward(last, [(0, held[0])], None, HALVES == 1, 0, 1, [sketch])]
    for h in range(1, HALVES):
        marks[:] = [tie(marks[0], [came[h, 0]])]
        held[h] = store_last(pos, (came[h, 0], came[h, 1]), held[h], list(marks))
    terms = score_terms(pos, from_others(sketch, "query", queriers), queries, list(marks))
    for h in range(1, HALVES):
        marks[:] = [backward(last, [(h, held[h])], totals.get(last), h == HALVES - 1, 0, 1, [terms])]
    scores = score_sum(pos, from_others(terms, "tensor", parts), list(marks))
    return (result[0].reshape(1, tokens, -1), scores)


def solution(mesh):
    return jax.shard_map(
        body,
        mesh=mesh,
        in_specs=(
            P(("groups", "dp", "query"), None, "tensor"),
            P(("groups", "dp", "query"), "tensor", None),
            P(("groups", "dp", "query"), "tensor", None),
            P(),
            P("tensor", None),
            P(None, "tensor"),
            P(),
            P("query", "tensor"),
            P(("groups", "dp", "query"), None),
        ),
        out_specs=(P(("groups", "dp", "query"), None, "tensor"), P(("groups", "dp"), "query")),
        check_vma=False,
    )
```
